32 devices in a mesh: rep: 2 (over y), node: 4 (over x, core), local: 4 (over z).
Axes of the slice: x: 2, y: 2, z: 4, core: 2. Of those that a mesh axis runs over, the one named last changes fastest.
Arguments:
- tokens: bfloat16 [256, 7168], P(('rep', 'node', 'local')), parts along dimension 0, may hold values from -6 to 6
- group_ids: int32 [256, 4], P(('rep', 'node', 'local')), parts along dimension 0, may hold values from 0 to 3, as said below
- route_weights: bfloat16 [256, 4], P(('rep', 'node', 'local')), parts along dimension 0, may hold values from 0.049804688 to 0.59765625
- gate_experts: bfloat16 [4, 7168, 2048], P('node', None, 'local'), may hold values from -0.0625 to 0.0625
- up_experts: bfloat16 [4, 7168, 2048], P('node', None, 'local'), may hold values from -0.0625 to 0.0625
- down_experts: bfloat16 [4, 2048, 7168], P('node', 'local'), may hold values from -0.125 to 0.125
- gate_shared: bfloat16 [7168, 2048], P(None, 'local'), may hold values from -0.0625 to 0.0625
- up_shared: bfloat16 [7168, 2048], P(None, 'local'), may hold values from -0.0625 to 0.0625
- down_shared: bfloat16 [2048, 7168], P('local'), may hold values from -0.125 to 0.125
Outputs:
- layer_out: bfloat16 [256, 7168], P(('rep', 'node', 'local')), parts along dimension 0
The draws below stay inside these ranges and needn't reach their ends.
There are 2 independent parts, one for each index of `rep`. The reference program is written for one: setup_inputs(seed, part) draws one part's arguments, and reference() takes and returns one part's arrays. A program takes and returns all parts, laid end to end along the dimension named above; an argument that names none is the same for every part. Nothing has to cross between parts.
Inputs may be any that keep to these rules, and one draw needn't show every extreme that they name: `group_ids`: each row names 4 different groups. Of the 8 rows of one device, each group is named by exactly 8 rows.
All inputs are finite; a program needn't handle non-finite values.
Results may differ from the reference program's by a relative error of at most 0.01.
Values may be sent and summed in bfloat16 or wider, within the bound.
No kernel may reach another device: no remote copies, remote signals or barrier semaphores. Data moves between devices by JAX's collectives and lax.ppermute only.
A program may use at most 128 MiB of HBM per device.

```python
import math
import jax
import jax.numpy as jnp
from jax import lax

D = 7168
FF_E = 2048
FF_S = 2048
TOPG = 4
ROWS = 8
EXPERTS = 4
TOKENS = 128
EXPERT_BLOCK = 512
SHARED_BLOCK = 512
N_NODE = 4
N_LOCAL = 4


def draw_group_ids(key, part):
    key = jax.random.fold_in(key, 7)
    block_count = N_NODE * N_LOCAL
    row_index = jnp.arange(ROWS, dtype=jnp.int32)
    offsets = jnp.arange(TOPG, dtype=jnp.int32)

    def one_block(block_key):
        key_order, key_column, key_row = jax.random.split(block_key, 3)
        group_order = jax.random.permutation(key_order, N_NODE).astype(jnp.int32)
        table = group_order[(row_index[:, None] + offsets[None, :]) % N_NODE]
        column_score = jax.random.randint(key_column, (ROWS, TOPG), 0, 4096) * TOPG + offsets[None, :]
        table = jnp.take_along_axis(table, jnp.argsort(column_score, axis=1), axis=1)
        return table[jax.random.permutation(key_row, ROWS)]
    tables = jax.vmap(one_block)(jax.random.split(key, block_count))
    return tables.reshape(block_count * ROWS, TOPG).astype(jnp.int32)


def shard_levels(stream_key, extent, pieces, least, top_value):
    def one(axis_at, parts):
        draws = jax.random.uniform(jax.random.fold_in(jax.random.fold_in(stream_key, 6), axis_at), (parts,), jnp.float32, least / len(pieces), top_value / len(pieces))
        return jnp.repeat(jnp.exp(draws), extent[axis_at] // parts).reshape((-1,) + (1,) * (len(extent) - axis_at - 1))

    gain = one(*pieces[0])
    for cut in pieces[1:]:
        gain = gain * one(*cut)
    return gain


def bell_draw(key, shape, deviation, limit, shards=(), held_as=jnp.bfloat16):
    entries = jax.random.normal(key, shape, jnp.float32) * deviation
    if len(shards) > 0:
        entries = shard_levels(key, shape, shards, -0.22, 0.18) * entries
    return jnp.clip(entries, min=-limit, max=limit).astype(held_as)


def setup_inputs(seed: int = 0, part: int = 0) -> dict:
    key_of = jax.random.split(jax.random.key(seed), 10)
    part_keys = jax.random.split(jax.random.fold_in(key_of[9], part), 10)
    tokens = bell_draw(part_keys[0], (TOKENS, D), 1.0, 6.0, ((0, 16),))
    group_ids = draw_group_ids(jax.random.fold_in(jax.random.fold_in(key_of[9], part), 71), part)
    route_weights = jnp.clip(jnp.exp(math.log(0.59765625) - 2.4849066 * jax.random.uniform(part_keys[2], (TOKENS, TOPG), jnp.float32) ** shard_levels(part_keys[2], (TOKENS, TOPG), ((0, 16),), -0.2, 0.2)), 0.049804688, 0.59765625).astype(jnp.bfloat16)
    gate_experts = bell_draw(key_of[3], (EXPERTS, D, FF_E), D ** -0.5, 0.0625, ((0, 4), (2, 4)))
    up_experts = bell_draw(key_of[4], (EXPERTS, D, FF_E), D ** -0.5, 0.0625, ((0, 4), (2, 4)))
    down_experts = bell_draw(key_of[5], (EXPERTS, FF_E, D), FF_E ** -0.5, 0.125, ((0, 4), (1, 4)))
    gate_shared = bell_draw(key_of[6], (D, FF_S), D ** -0.5, 0.0625, ((1, 4),))
    up_shared = bell_draw(key_of[7], (D, FF_S), D ** -0.5, 0.0625, ((1, 4),))
    down_shared = bell_draw(key_of[8], (FF_S, D), FF_S ** -0.5, 0.125, ((0, 4),))
    return {"tokens": tokens, "group_ids": group_ids, "route_weights": route_weights, "gate_experts": gate_experts, "up_experts": up_experts, "down_experts": down_experts, "gate_shared": gate_shared, "up_shared": up_shared, "down_shared": down_shared}


def reference(tokens, group_ids, route_weights, gate_experts, up_experts, down_experts, gate_shared, up_shared, down_shared):
    per_expert = TOKENS * TOPG // N_NODE
    weights = route_weights.astype(jnp.float32)
    expert_range = jnp.arange(EXPERTS, dtype=jnp.int32)

    def one_expert(running, expert):
        hit = group_ids == expert
        row_hit = jnp.any(hit, axis=1)
        row_weight = jnp.sum(jnp.where(hit, weights, jnp.zeros_like(weights)), axis=1)
        order = jnp.argsort(jnp.where(row_hit, 0, 1).astype(jnp.int32), stable=True).astype(jnp.int32)
        picked = order[:per_expert]
        rows = tokens[picked]
        gate_value = jnp.dot(rows, gate_experts[expert], preferred_element_type=jnp.float32)
        up_value = jnp.dot(rows, up_experts[expert], preferred_element_type=jnp.float32)
        activation = (jax.nn.silu(gate_value) * up_value).astype(jnp.bfloat16)
        down_matrix = down_experts[expert]
        expert_out = jnp.zeros((per_expert, D), jnp.float32)
        for block_number in range(N_LOCAL):
            lower = block_number * EXPERT_BLOCK
            partial_sum = jnp.dot(activation[:, lower:lower + EXPERT_BLOCK], down_matrix[lower:lower + EXPERT_BLOCK], preferred_element_type=jnp.float32)
            partial_sum = lax.optimization_barrier(partial_sum.astype(jnp.bfloat16))
            expert_out = expert_out + partial_sum.astype(jnp.float32)
        running = running.at[picked].add(expert_out * row_weight[picked][:, None])
        return running, None

    routed, _ = lax.scan(one_expert, jnp.zeros((TOKENS, D), jnp.float32), expert_range)
    gate_value = jnp.dot(tokens, gate_shared, preferred_element_type=jnp.float32)
    up_value = jnp.dot(tokens, up_shared, preferred_element_type=jnp.float32)
    shared_act = (jax.nn.silu(gate_value) * up_value).astype(jnp.bfloat16)
    shared = jnp.zeros((TOKENS, D), jnp.float32)
    for shard_number in range(N_LOCAL):
        lower = shard_number * SHARED_BLOCK
        partial_sum = jnp.dot(shared_act[:, lower:lower + SHARED_BLOCK], down_shared[lower:lower + SHARED_BLOCK], preferred_element_type=jnp.float32)
        partial_sum = lax.optimization_barrier(partial_sum.astype(jnp.bfloat16))
        shared = shared + partial_sum.astype(jnp.float32)
    return (routed + shared).astype(jnp.bfloat16)
```

```python
import functools

import jax
import jax.numpy as jnp
from jax import lax
from jax.experimental import pallas as pl
from jax.experimental.pallas import tpu as pltpu
from jax.sharding import PartitionSpec as P

LANES = 128
ROW_BLOCK = 128
F32 = jnp.float32
BF16 = jnp.bfloat16


def pack_kernel(tokens_ref, groups_ref, weights_ref, out_ref):
    rows, width = tokens_ref.shape
    out_ref[:, :width] = tokens_ref[...]
    lane = lax.broadcasted_iota(jnp.int32, (rows, LANES), 1)
    dense = jnp.zeros((rows, LANES), F32)
    for k in range(groups_ref.shape[1]):
        dense += jnp.where(
            lane == groups_ref[:, k : k + 1], weights_ref[:, k : k + 1].astype(F32), 0.0
        )
    out_ref[:, width:] = dense.astype(BF16)


def pack_rows(tokens, group_ids, route_weights):
    rows, width = tokens.shape
    return pl.pallas_call(
        pack_kernel,
        out_shape=jax.ShapeDtypeStruct((rows, width + LANES), BF16),
        name="pack_rows",
    )(tokens, group_ids, route_weights)


def expert_kernel(
    share, place_ref, x_ref, gate_ref, up_ref, down_ref, sgate_ref, sup_ref, sdown_ref,
    out_ref, sgu, sd, acc, act, sems,
):
    width = down_ref.shape[1]
    hidden = gate_ref.shape[1]
    rows = x_ref.shape[0]
    step = 512
    node = place_ref[0]
    column = pl.multiple_of((node // share) * LANES, LANES)
    copies = [
        pltpu.make_async_copy(sgate_ref.at[:, pl.ds(column, LANES)], sgu.at[:, pl.ds(0, LANES)], sems.at[0]),
        pltpu.make_async_copy(sup_ref.at[:, pl.ds(column, LANES)], sgu.at[:, pl.ds(LANES, LANES)], sems.at[1]),
        pltpu.make_async_copy(sdown_ref.at[pl.ds(column, LANES), :], sd, sems.at[2]),
    ]

    @pl.when(pl.program_id(0) == 0)
    def _():
        for copy in copies:
            copy.start()

    acc[...] = jnp.zeros_like(acc)

    def first(i, carry):
        at = pl.multiple_of(i * step, step)
        x = x_ref[:, pl.ds(at, step)]
        acc[:, :hidden] += jnp.dot(x, gate_ref[pl.ds(at, step), :], preferred_element_type=F32)
        acc[:, hidden : 2 * hidden] += jnp.dot(x, up_ref[pl.ds(at, step), :], preferred_element_type=F32)
        return carry

    lax.fori_loop(0, width // step, first, 0)

    @pl.when(pl.program_id(0) == 0)
    def _():
        for copy in copies:
            copy.wait()

    def second(i, carry):
        at = pl.multiple_of(i * step, step)
        acc[:, 2 * hidden :] += jnp.dot(
            x_ref[:, pl.ds(at, step)], sgu[pl.ds(at, step), :], preferred_element_type=F32
        )
        return carry

    lax.fori_loop(0, width // step, second, 0)

    lane = lax.broadcasted_iota(jnp.int32, (rows, LANES), 1)
    weight = jnp.sum(
        jnp.where(lane == node, x_ref[:, pl.ds(width, LANES)].astype(F32), 0.0), axis=1, keepdims=True
    )
    gate = acc[:, :hidden]
    act[:, :hidden] = (gate / (1.0 + jnp.exp(-gate)) * acc[:, hidden : 2 * hidden] * weight).astype(BF16)
    gate = acc[:, 2 * hidden : 2 * hidden + LANES]
    shared = gate / (1.0 + jnp.exp(-gate)) * acc[:, 2 * hidden + LANES :]
    if share > 1:
        shared = jnp.where(lane // (LANES // share) == node % share, shared, 0.0)
    act[:, hidden:] = shared.astype(BF16)

    def third(i, carry):
        at = pl.multiple_of(i * step, step)
        total = jnp.dot(act[:, :hidden], down_ref[:, pl.ds(at, step)], preferred_element_type=F32)
        total += jnp.dot(act[:, hidden:], sd[:, pl.ds(at, step)], preferred_element_type=F32)
        out_ref[:, pl.ds(at, step)] = total.astype(BF16)
        return carry

    lax.fori_loop(0, width // step, third, 0)


def expert_rows(place, x, gate, up, down, sgate, sup, sdown, node_count):
    rows, packed = x.shape
    hidden, width = down.shape
    share = max(1, LANES * node_count // sgate.shape[1])
    block = min(rows, ROW_BLOCK)
    vmem = pl.BlockSpec(memory_space=pltpu.VMEM)
    hbm = pl.BlockSpec(memory_space=pl.ANY)
    if rows == block:
        x_spec, out_spec = vmem, vmem
    else:
        x_spec = pl.BlockSpec((block, packed), lambda i: (i, 0))
        out_spec = pl.BlockSpec((block, width), lambda i: (i, 0))
    gate, up, down = (pltpu.with_memory_space_constraint(w, pltpu.VMEM) for w in (gate, up, down))
    return pl.pallas_call(
        functools.partial(expert_kernel, share),
        grid=(rows // block,),
        in_specs=[pl.BlockSpec(memory_space=pltpu.SMEM), x_spec, vmem, vmem, vmem, hbm, hbm, hbm],
        out_specs=out_spec,
        out_shape=jax.ShapeDtypeStruct((rows, width), BF16),
        scratch_shapes=[
            pltpu.VMEM((width, 2 * LANES), BF16),
            pltpu.VMEM((LANES, width), BF16),
            pltpu.VMEM((block, 2 * hidden + 2 * LANES), F32),
            pltpu.VMEM((block, hidden + LANES), BF16),
            pltpu.SemaphoreType.DMA((3,)),
        ],
        compiler_params=pltpu.CompilerParams(vmem_limit_bytes=24 << 20),
        name="expert_rows",
    )(place, x, gate, up, down, sgate, sup, sdown)


def add_rows(*terms):
    total = terms[0].astype(F32)
    for term in terms[1:]:
        total = total + term.astype(F32)
    return total.astype(BF16)


def per_device(
    tokens,
    group_ids,
    route_weights,
    gate_experts,
    up_experts,
    down_experts,
    gate_shared,
    up_shared,
    down_shared,
):
    rows, width = tokens.shape
    node_count = lax.axis_size("node")
    local_count = lax.axis_size("local")
    x_count = node_count // 2
    small = node_count % 2 == 0 and x_count * local_count <= 8
    place = lax.axis_index("node").reshape(1)
    packed = pack_rows(tokens, group_ids, route_weights)

    def shift_local(value, k):
        return lax.ppermute(value, "local", [(i, (i + k) % local_count) for i in range(local_count)])

    def shift_x(value, k):
        return lax.ppermute(
            value, "node", [(i, (i + 2 * k) % node_count) for i in range(node_count)]
        )

    def swap_core(value):
        return lax.ppermute(value, "node", [(i, i ^ 1) for i in range(node_count)])

    if small:
        blocks = [packed] + [shift_local(packed, k) for k in range(1, local_count)]
        blocks = blocks + [shift_x(b, j) for j in range(1, x_count) for b in blocks]
        blocks = blocks + [swap_core(b) for b in blocks]
        x = jnp.concatenate(blocks, axis=0)
    else:
        x = lax.all_gather(packed, ("node", "local"), axis=0, tiled=True)
    part = expert_rows(
        place, x, gate_experts[0], up_experts[0], down_experts[0],
        gate_shared, up_shared, down_shared, node_count,
    )
    if not small:
        return lax.psum_scatter(part, ("node", "local"), scatter_dimension=0, tiled=True)
    half = x_count * local_count * rows
    part = add_rows(part[:half], swap_core(part[half:]))
    span = local_count * rows
    part = add_rows(
        part[:span],
        *(shift_x(part[j * span : (j + 1) * span], -j) for j in range(1, x_count)),
    )
    return add_rows(
        part[:rows],
        *(shift_local(part[k * rows : (k + 1) * rows], -k) for k in range(1, local_count)),
    )


def solution(mesh):
    in_specs = (
        P(("rep", "node", "local"), None),
        P(("rep", "node", "local"), None),
        P(("rep", "node", "local"), None),
        P("node", None, "local"),
        P("node", None, "local"),
        P("node", "local", None),
        P(None, "local"),
        P(None, "local"),
        P("local", None),
    )
    out_specs = P(("rep", "node", "local"), None)
    return jax.shard_map(
        per_device, mesh=mesh, in_specs=in_specs, out_specs=out_specs, check_vma=False
    )
```

```python
import functools

import jax
import jax.numpy as jnp
from jax import lax
from jax.experimental import pallas as pl
from jax.experimental.pallas import tpu as pltpu
from jax.sharding import PartitionSpec as P

LANES = 128
ROW_BLOCK = 128
F32 = jnp.float32
BF16 = jnp.bfloat16
VMEM_SPEC = pl.BlockSpec(memory_space=pltpu.VMEM)
SMEM_SPEC = pl.BlockSpec(memory_space=pltpu.SMEM)
ANY_SPEC = pl.BlockSpec(memory_space=pl.ANY)


def pack_kernel(tokens_ref, groups_ref, weights_ref, out_ref):
    rows, width = tokens_ref.shape
    out_ref[:, :width] = tokens_ref[...]
    groups = groups_ref[...].T
    weights = weights_ref[...].astype(F32).T
    lane = lax.broadcasted_iota(jnp.int32, (rows, LANES), 1)
    dense = jnp.zeros((rows, LANES), F32)
    for k in range(groups.shape[1]):
        dense += jnp.where(lane == groups[:, k : k + 1], weights[:, k : k + 1], 0.0)
    out_ref[:, width:] = dense.astype(BF16)


def pack_rows(tokens, group_ids, route_weights):
    rows, width = tokens.shape
    return pl.pallas_call(
        pack_kernel,
        out_shape=jax.ShapeDtypeStruct((rows, width + LANES), BF16),
        name="pack_rows",
    )(tokens, group_ids.T, route_weights.T)


def in_hbm(value):
    return pltpu.with_memory_space_constraint(value, pltpu.HBM)


def run_copies(copies):
    for copy in copies:
        copy.start()
    for copy in copies:
        copy.wait()


def load_first_kernel(share, place_ref, after_ref, gate_ref, up_ref, sgate_ref, sup_ref, out_ref, sems):
    del after_ref
    width, hidden = gate_ref.shape
    column = pl.multiple_of((place_ref[0] // share) * LANES, LANES)
    parts = 4
    piece = width // parts
    copies = []
    for i in range(parts):
        at = pl.ds(i * piece, piece)
        for source, lower, size in (
            (gate_ref.at[at, :], 0, hidden),
            (up_ref.at[at, :], hidden, hidden),
            (sgate_ref.at[at, pl.ds(column, LANES)], 2 * hidden, LANES),
            (sup_ref.at[at, pl.ds(column, LANES)], 2 * hidden + LANES, LANES),
        ):
            copies.append(
                pltpu.make_async_copy(source, out_ref.at[at, pl.ds(lower, size)], sems.at[len(copies)])
            )
    run_copies(copies)


def load_first(place, after, gate, up, sgate, sup, share):
    width, hidden = gate.shape
    shape = (width, 2 * hidden + 2 * LANES)
    gate, up, sgate, sup = (in_hbm(w) for w in (gate, up, sgate, sup))
    return pl.pallas_call(
        functools.partial(load_first_kernel, share),
        in_specs=[SMEM_SPEC] + [ANY_SPEC] * 5,
        out_specs=VMEM_SPEC,
        out_shape=pltpu.VMEM(shape, BF16),
        scratch_shapes=[pltpu.SemaphoreType.DMA((16,))],
        cost_estimate=pl.CostEstimate(flops=0, bytes_accessed=4 * shape[0] * shape[1], transcendentals=0),
        compiler_params=pltpu.CompilerParams(vmem_limit_bytes=1 << 20),
        name="load_first",
    )(place, after, gate, up, sgate, sup)


def load_second_kernel(share, place_ref, after_ref, down_ref, sdown_ref, out_ref, sems):
    del after_ref
    hidden, width = down_ref.shape
    column = pl.multiple_of((place_ref[0] // share) * LANES, LANES)
    copies = []
    for i in range(0, hidden, LANES):
        copies.append(
            pltpu.make_async_copy(down_ref.at[pl.ds(i, LANES), :], out_ref.at[pl.ds(i, LANES), :], sems.at[len(copies)])
        )
    copies.append(
        pltpu.make_async_copy(sdown_ref.at[pl.ds(column, LANES), :], out_ref.at[pl.ds(hidden, LANES), :], sems.at[len(copies)])
    )
    run_copies(copies)


def load_second(place, after, down, sdown, share):
    hidden, width = down.shape
    shape = (hidden + LANES, width)
    down, sdown = in_hbm(down), in_hbm(sdown)
    return pl.pallas_call(
        functools.partial(load_second_kernel, share),
        in_specs=[SMEM_SPEC] + [ANY_SPEC] * 3,
        out_specs=VMEM_SPEC,
        out_shape=pltpu.VMEM(shape, BF16),
        scratch_shapes=[pltpu.SemaphoreType.DMA((hidden // LANES + 1,))],
        cost_estimate=pl.CostEstimate(flops=0, bytes_accessed=4 * shape[0] * shape[1], transcendentals=0),
        compiler_params=pltpu.CompilerParams(vmem_limit_bytes=1 << 20),
        name="load_second",
    )(place, after, down, sdown)


def expert_kernel(share, place_ref, x_ref, first_ref, second_ref, out_ref, act):
    total_hidden, width = second_ref.shape
    hidden = total_hidden - LANES
    rows = x_ref.shape[0]
    node = place_ref[0]
    lane = lax.broadcasted_iota(jnp.int32, (rows, LANES), 1)
    weight = jnp.sum(
        jnp.where(lane == node, x_ref[:, width:].astype(F32), 0.0), axis=1, keepdims=True
    )
    tile = 2 * LANES
    x = x_ref[:, :width]

    def silu(v):
        return v / (1.0 + jnp.exp(-v))

    for at in range(0, hidden, tile):
        gate = jnp.dot(x, first_ref[:, at : at + tile], preferred_element_type=F32)
        up = jnp.dot(x, first_ref[:, hidden + at : hidden + at + tile], preferred_element_type=F32)
        act[:, at : at + tile] = (silu(gate) * up * weight).astype(BF16)
    both = jnp.dot(x, first_ref[:, 2 * hidden :], preferred_element_type=F32)
    shared = silu(both[:, :LANES]) * both[:, LANES:]
    if share > 1:
        shared = jnp.where(lane // (LANES // share) == node % share, shared, 0.0)
    act[:, hidden:] = shared.astype(BF16)

    step = 1024

    def third(i, carry):
        at = pl.multiple_of(i * step, step)
        total = jnp.dot(act[...], second_ref[:, pl.ds(at, step)], preferred_element_type=F32)
        out_ref[:, pl.ds(at, step)] = total.astype(BF16)
        return carry

    lax.fori_loop(0, width // step, third, 0)


def expert_rows(place, x, first, second, share):
    rows, packed = x.shape
    width = second.shape[1]
    block = min(rows, ROW_BLOCK)
    if rows == block:
        x_spec, out_spec = VMEM_SPEC, VMEM_SPEC
    else:
        x_spec = pl.BlockSpec((block, packed), lambda i: (i, 0))
        out_spec = pl.BlockSpec((block, width), lambda i: (i, 0))
    return pl.pallas_call(
        functools.partial(expert_kernel, share),
        grid=(rows // block,),
        in_specs=[SMEM_SPEC, x_spec, VMEM_SPEC, VMEM_SPEC],
        out_specs=out_spec,
        out_shape=jax.ShapeDtypeStruct((rows, width), BF16),
        scratch_shapes=[pltpu.VMEM((block, second.shape[0]), BF16)],
        compiler_params=pltpu.CompilerParams(vmem_limit_bytes=20 << 20),
        name="expert_rows",
    )(place, x, first, second)


def f32_sum(*terms):
    return functools.reduce(lambda a, b: a + b, (t.astype(F32) for t in terms))


def per_device(
    tokens,
    group_ids,
    route_weights,
    gate_experts,
    up_experts,
    down_experts,
    gate_shared,
    up_shared,
    down_shared,
):
    rows, width = tokens.shape
    node_count = lax.axis_size("node")
    local_count = lax.axis_size("local")
    share = max(1, LANES * node_count // gate_shared.shape[1])
    place = lax.axis_index("node").reshape(1)
    packed = pack_rows(tokens, group_ids, route_weights)

    if node_count != 4 or local_count != 4:
        first = load_first(place, packed, gate_experts[0], up_experts[0], gate_shared, up_shared, share)
        second = load_second(place, packed, down_experts[0], down_shared, share)
        x = lax.all_gather(packed, ("node", "local"), axis=0, tiled=True)
        part = expert_rows(place, x, first, second, share)
        return lax.psum_scatter(part, ("node", "local"), scatter_dimension=0, tiled=True)

    def swap(value, axis, bit):
        return lax.ppermute(value, axis, [(i, i ^ bit) for i in range(4)])

    def swap_z2(value):
        return swap(value, "local", 2)

    def swap_z1(value):
        return swap(value, "local", 1)

    def swap_x(value):
        return swap(value, "node", 2)

    def swap_core(value):
        return swap(value, "node", 1)

    cut = width // 2
    two = 2 * rows
    got = swap_z2(packed)
    first = load_first(place, packed, gate_experts[0], up_experts[0], gate_shared, up_shared, share)
    got, first = lax.optimization_barrier((got, first))
    rows_1 = jnp.concatenate([packed, got], axis=0)
    a1, b1 = rows_1[:, :cut], rows_1[:, cut:]
    a2 = jnp.concatenate([a1, swap_z1(a1)], axis=0)
    b2 = jnp.concatenate([b1, swap_x(b1)], axis=0)
    a_got = swap_x(a2)
    b3 = swap_z1(b2)
    second = load_second(place, a2, down_experts[0], down_shared, share)
    a_got, b3, second = lax.optimization_barrier((a_got, b3, second))
    a3 = jnp.concatenate([a2, a_got], axis=0)
    b3 = jnp.concatenate([b2[:two], b3[:two], b2[two:], b3[two:]], axis=0)
    rows_3 = jnp.concatenate([a3, b3], axis=1)
    x = jnp.concatenate([rows_3, swap_core(rows_3)], axis=0)

    part = expert_rows(place, x, first, second, share)

    half = 8 * rows
    mine, other = part[:half], swap_core(part[half:])
    four = 4 * rows
    a_send = f32_sum(mine[four:, :cut], other[four:, :cut]).astype(BF16)
    b_mine, b_other = mine[:, cut:], other[:, cut:]

    def odd(value):
        return jnp.concatenate([value[two:four], value[four + two :]], axis=0)

    def even(value):
        return jnp.concatenate([value[:two], value[four : four + two]], axis=0)

    b_send = f32_sum(odd(b_mine), odd(b_other)).astype(BF16)
    a_got = swap_x(a_send)
    b_got = swap_z1(b_send)
    a_sum = f32_sum(mine[:four, :cut], other[:four, :cut], a_got)
    b_sum = f32_sum(even(b_mine), even(b_other), b_got)
    a_got = swap_z1(a_sum[two:].astype(BF16))
    b_got = swap_x(b_sum[two:].astype(BF16))
    a_sum = f32_sum(a_sum[:two], a_got)
    b_sum = f32_sum(b_sum[:two], b_got)
    total = jnp.concatenate([a_sum, b_sum], axis=1)
    got = swap_z2(total[rows:].astype(BF16))
    return f32_sum(total[:rows], got).astype(BF16)


def solution(mesh):
    in_specs = (
        P(("rep", "node", "local"), None),
        P(("rep", "node", "local"), None),
        P(("rep", "node", "local"), None),
        P("node", None, "local"),
        P("node", None, "local"),
        P("node", "local", None),
        P(None, "local"),
        P(None, "local"),
        P("local", None),
    )
    out_specs = P(("rep", "node", "local"), None)
    return jax.shard_map(
        per_device, mesh=mesh, in_specs=in_specs, out_specs=out_specs, check_vma=False
    )
```

```python
import functools

import jax
import jax.numpy as jnp
from jax import lax
from jax.experimental import pallas as pl
from jax.experimental.pallas import tpu as pltpu
from jax.sharding import PartitionSpec as P

LANES = 128
ROW_BLOCK = 128
F32 = jnp.float32
BF16 = jnp.bfloat16
VMEM_SPEC = pl.BlockSpec(memory_space=pltpu.VMEM)
SMEM_SPEC = pl.BlockSpec(memory_space=pltpu.SMEM)
ANY_SPEC = pl.BlockSpec(memory_space=pl.ANY)


def in_hbm(value):
    return pltpu.with_memory_space_constraint(value, pltpu.HBM)


def run_copies(copies):
    for copy in copies:
        copy.start()
    for copy in copies:
        copy.wait()


def after(value, *done):
    return lax.optimization_barrier((value, *done))[0]


def shared_column(place_ref, share):
    return pl.multiple_of((place_ref[0] // share) * LANES, LANES)


def load_gate_kernel(
    share, place_ref, groups_ref, weights_ref, gate_ref, sgate_ref, sup_ref, out_ref, dense_ref, sems
):
    width, hidden = gate_ref.shape
    column = shared_column(place_ref, share)
    parts = 4
    piece = width // parts
    copies = []
    for i in range(parts):
        at = pl.ds(i * piece, piece)
        for source, lower, size in (
            (gate_ref.at[at, :], 0, hidden),
            (sgate_ref.at[at, pl.ds(column, LANES)], hidden, LANES),
            (sup_ref.at[at, pl.ds(column, LANES)], hidden + LANES, LANES),
        ):
            copies.append(
                pltpu.make_async_copy(source, out_ref.at[at, pl.ds(lower, size)], sems.at[len(copies)])
            )
    for copy in copies:
        copy.start()
    groups = groups_ref[...].T
    weights = weights_ref[...].astype(F32).T
    lane = lax.broadcasted_iota(jnp.int32, dense_ref.shape, 1)
    dense = jnp.zeros(dense_ref.shape, F32)
    for k in range(groups.shape[1]):
        dense += jnp.where(lane == groups[:, k : k + 1], weights[:, k : k + 1], 0.0)
    dense_ref[...] = dense.astype(BF16)
    for copy in copies:
        copy.wait()


def load_gate(place, group_ids, route_weights, gate, sgate, sup, share):
    width, hidden = gate.shape
    shape = (width, hidden + 2 * LANES)
    return pl.pallas_call(
        functools.partial(load_gate_kernel, share),
        in_specs=[SMEM_SPEC] + [VMEM_SPEC] * 2 + [ANY_SPEC] * 3,
        out_specs=[VMEM_SPEC] * 2,
        out_shape=[pltpu.VMEM(shape, BF16), pltpu.VMEM((group_ids.shape[0], LANES), BF16)],
        scratch_shapes=[pltpu.SemaphoreType.DMA((12,))],
        cost_estimate=pl.CostEstimate(flops=0, bytes_accessed=4 * shape[0] * shape[1], transcendentals=0),
        compiler_params=pltpu.CompilerParams(vmem_limit_bytes=1 << 20),
        name="load_gate",
    )(place, group_ids.T, route_weights.T, in_hbm(gate), in_hbm(sgate), in_hbm(sup))


def load_up_kernel(up_ref, out_ref, sems):
    width = up_ref.shape[0]
    parts = 8
    piece = width // parts
    run_copies(
        [
            pltpu.make_async_copy(
                up_ref.at[pl.ds(i * piece, piece), :], out_ref.at[pl.ds(i * piece, piece), :], sems.at[i]
            )
            for i in range(parts)
        ]
    )


def load_up(up):
    width, hidden = up.shape
    return pl.pallas_call(
        load_up_kernel,
        in_specs=[ANY_SPEC],
        out_specs=VMEM_SPEC,
        out_shape=pltpu.VMEM((width, hidden), BF16),
        scratch_shapes=[pltpu.SemaphoreType.DMA((8,))],
        cost_estimate=pl.CostEstimate(flops=0, bytes_accessed=4 * width * hidden, transcendentals=0),
        compiler_params=pltpu.CompilerParams(vmem_limit_bytes=1 << 20),
        name="load_up",
    )(in_hbm(up))


def silu(v):
    return v / (1.0 + jnp.exp(-v))


def activate(share, node, x, first_ref, up_ref, weight, act):
    width, hidden = up_ref.shape
    tile = min(2 * LANES, hidden)
    for at in range(0, hidden, tile):
        gate = jnp.dot(x, first_ref[:, at : at + tile], preferred_element_type=F32)
        up = jnp.dot(x, up_ref[:, at : at + tile], preferred_element_type=F32)
        act[:, at : at + tile] = (silu(gate) * up * weight).astype(BF16)
    both = jnp.dot(x, first_ref[:, hidden:], preferred_element_type=F32)
    shared = silu(both[:, :LANES]) * both[:, LANES:]
    if share > 1:
        lane = lax.broadcasted_iota(jnp.int32, shared.shape, 1)
        shared = jnp.where(lane // (LANES // share) == node % share, shared, 0.0)
    act[:, hidden:] = shared.astype(BF16)


def row_weight(node, dense):
    lane = lax.broadcasted_iota(jnp.int32, dense.shape, 1)
    return jnp.sum(jnp.where(lane == node, dense.astype(F32), 0.0), axis=1, keepdims=True)


def down_copies(share, place_ref, down_ref, sdown_ref, second, sems):
    hidden, width = down_ref.shape
    column = shared_column(place_ref, share)
    parts = 4
    piece = width // parts
    copies = []
    for i in range(parts):
        at = pl.ds(i * piece, piece)
        copies.append(
            pltpu.make_async_copy(down_ref.at[:, at], second.at[pl.ds(0, hidden), at], sems.at[2 * i])
        )
        copies.append(
            pltpu.make_async_copy(
                sdown_ref.at[pl.ds(column, LANES), at], second.at[pl.ds(hidden, LANES), at], sems.at[2 * i + 1]
            )
        )
    return copies


def split_kernel(
    share, place_ref, a0_ref, b0_ref, a1_ref, b1_ref, first_ref, up_ref, down_ref, sdown_ref,
    own_a_ref, own_b_ref, other_a_ref, other_b_ref, x, act, second, sems,
):
    copies = down_copies(share, place_ref, down_ref, sdown_ref, second, sems)
    for copy in copies:
        copy.start()
    width = up_ref.shape[0]
    half, cut = a0_ref.shape
    quarter = half // 4
    order = (0, 2, 1, 3)
    for c, (a_ref, b_ref) in enumerate(((a0_ref, b0_ref), (a1_ref, b1_ref))):
        x[c * half : (c + 1) * half, :cut] = a_ref[...]
        for i, j in enumerate(order):
            x[c * half + i * quarter : c * half + (i + 1) * quarter, cut:] = b_ref[
                j * quarter : (j + 1) * quarter, :
            ]
    node = place_ref[0]
    weight = row_weight(node, x[:, width:])
    activate(share, node, x[:, :width], first_ref, up_ref, weight, act)
    parts = 4
    piece = width // parts
    for i in range(parts):
        copies[2 * i].wait()
        copies[2 * i + 1].wait()
        total = jnp.dot(
            act[...], second[:, i * piece : (i + 1) * piece], preferred_element_type=F32
        ).astype(BF16)
        if i < parts // 2:
            at = slice(i * piece, (i + 1) * piece)
            own_a_ref[:, at] = total[:half]
            other_a_ref[:, at] = total[half:]
        else:
            at = slice(i * piece - cut, (i + 1) * piece - cut)
            for k, j in enumerate(order):
                to = slice(k * quarter, (k + 1) * quarter)
                own_b_ref[to, at] = total[j * quarter : (j + 1) * quarter]
                other_b_ref[to, at] = total[half + j * quarter : half + (j + 1) * quarter]


def split_rows(place, pieces, first, up, down, sdown, share):
    half, cut = pieces[0].shape
    hidden, width = down.shape
    out = jax.ShapeDtypeStruct((half, cut), BF16)
    return pl.pallas_call(
        functools.partial(split_kernel, share),
        in_specs=[SMEM_SPEC] + [VMEM_SPEC] * 6 + [ANY_SPEC] * 2,
        out_specs=[VMEM_SPEC] * 4,
        out_shape=[out] * 4,
        scratch_shapes=[
            pltpu.VMEM((2 * half, width + LANES), BF16),
            pltpu.VMEM((2 * half, hidden + LANES), BF16),
            pltpu.VMEM((hidden + LANES, width), BF16),
            pltpu.SemaphoreType.DMA((8,)),
        ],
        compiler_params=pltpu.CompilerParams(vmem_limit_bytes=28 << 20),
        name="split_rows",
    )(place, *pieces, first, up, in_hbm(down), in_hbm(sdown))


def block_kernel(share, place_ref, x_ref, first_ref, up_ref, down_ref, sdown_ref, out_ref, act, second, sems):
    copies = down_copies(share, place_ref, down_ref, sdown_ref, second, sems)

    @pl.when(pl.program_id(0) == 0)
    def _():
        run_copies(copies)

    width = up_ref.shape[0]
    node = place_ref[0]
    weight = row_weight(node, x_ref[:, width:])
    activate(share, node, x_ref[:, :width], first_ref, up_ref, weight, act)
    parts = 4
    piece = width // parts
    for i in range(parts):
        at = slice(i * piece, (i + 1) * piece)
        out_ref[:, at] = jnp.dot(act[...], second[:, at], preferred_element_type=F32).astype(BF16)


def block_rows(place, x, first, up, down, sdown, share):
    rows, packed = x.shape
    hidden, width = down.shape
    block = min(rows, ROW_BLOCK)
    return pl.pallas_call(
        functools.partial(block_kernel, share),
        grid=(rows // block,),
        in_specs=[SMEM_SPEC, pl.BlockSpec((block, packed), lambda i: (i, 0))] + [VMEM_SPEC] * 2 + [ANY_SPEC] * 2,
        out_specs=pl.BlockSpec((block, width), lambda i: (i, 0)),
        out_shape=jax.ShapeDtypeStruct((rows, width), BF16),
        scratch_shapes=[
            pltpu.VMEM((block, hidden + LANES), BF16),
            pltpu.VMEM((hidden + LANES, width), BF16),
            pltpu.SemaphoreType.DMA((8,)),
        ],
        compiler_params=pltpu.CompilerParams(vmem_limit_bytes=28 << 20),
        name="block_rows",
    )(place, x, first, up, in_hbm(down), in_hbm(sdown))


def f32_sum(*terms):
    return functools.reduce(lambda a, b: a + b, (t.astype(F32) for t in terms))


def swap(value, axis, bit):
    return lax.ppermute(value, axis, [(i, i ^ bit) for i in range(4)])


swap_z2 = functools.partial(swap, axis="local", bit=2)
swap_z1 = functools.partial(swap, axis="local", bit=1)
swap_x = functools.partial(swap, axis="node", bit=2)
swap_core = functools.partial(swap, axis="node", bit=1)


def stack(*values):
    return jnp.concatenate(values, axis=0)


def per_device(
    tokens,
    group_ids,
    route_weights,
    gate_experts,
    up_experts,
    down_experts,
    gate_shared,
    up_shared,
    down_shared,
):
    rows, width = tokens.shape
    node_count = lax.axis_size("node")
    local_count = lax.axis_size("local")
    share = max(1, LANES * node_count // gate_shared.shape[1])
    place = lax.axis_index("node").reshape(1)
    gate, up, down = gate_experts[0], up_experts[0], down_experts[0]
    first, dense = load_gate(place, group_ids, route_weights, gate, gate_shared, up_shared, share)

    if node_count != 4 or local_count != 4:
        up = load_up(up)
        x = lax.all_gather(
            jnp.concatenate([tokens, dense], axis=1), ("node", "local"), axis=0, tiled=True
        )
        part = block_rows(place, x, first, up, down, down_shared, share)
        return lax.psum_scatter(part, ("node", "local"), scatter_dimension=0, tiled=True)

    cut = width // 2
    got_dense = swap_z2(dense)
    got, first = lax.optimization_barrier((swap_z2(tokens), first))
    a = stack(tokens[:, :cut], got[:, :cut])
    b = jnp.concatenate(
        [stack(tokens[:, cut:], got[:, cut:]), stack(dense, got_dense)], axis=1
    )
    b = stack(b, swap_x(b))
    a = stack(a, swap_z1(a))
    b_got = swap_z1(b)
    a_got = swap_x(a)
    up = load_up(after(up, a, b))
    a_got, b_got, up = lax.optimization_barrier((a_got, b_got, up))
    a = stack(a, a_got)
    b = stack(b, b_got)
    pieces = (a, b, swap_core(a), swap_core(b))

    own_a, own_b, other_a, other_b = split_rows(place, pieces, first, up, down, down_shared, share)

    def scatter(own, other, swap_first, swap_second):
        got = swap_core(other)
        send = f32_sum(own[4 * rows :], got[4 * rows :]).astype(BF16)
        total = f32_sum(own[: 4 * rows], got[: 4 * rows], swap_first(send))
        total = f32_sum(total[: 2 * rows], swap_second(total[2 * rows :].astype(BF16)))
        return f32_sum(total[:rows], swap_z2(total[rows:].astype(BF16))).astype(BF16)

    a = scatter(own_a, other_a, swap_x, swap_z1)
    b = scatter(own_b, other_b, swap_z1, swap_x)
    return jnp.concatenate([a, b], axis=1)


def solution(mesh):
    in_specs = (
        P(("rep", "node", "local"), None),
        P(("rep", "node", "local"), None),
        P(("rep", "node", "local"), None),
        P("node", None, "local"),
        P("node", None, "local"),
        P("node", "local", None),
        P(None, "local"),
        P(None, "local"),
        P("local", None),
    )
    out_specs = P(("rep", "node", "local"), None)
    return jax.shard_map(
        per_device, mesh=mesh, in_specs=in_specs, out_specs=out_specs, check_vma=False
    )
```

```python
import functools

import jax
import jax.numpy as jnp
from jax import lax
from jax.experimental import pallas as pl
from jax.experimental.pallas import tpu as pltpu
from jax.sharding import PartitionSpec as P

LANES = 128
ROW_BLOCK = 128
F32 = jnp.float32
BF16 = jnp.bfloat16
VMEM_SPEC = pl.BlockSpec(memory_space=pltpu.VMEM)
SMEM_SPEC = pl.BlockSpec(memory_space=pltpu.SMEM)
ANY_SPEC = pl.BlockSpec(memory_space=pl.ANY)


def in_hbm(value):
    return pltpu.with_memory_space_constraint(value, pltpu.HBM)


def run_copies(copies):
    for copy in copies:
        copy.start()
    for copy in copies:
        copy.wait()


def after(value, *done):
    return lax.optimization_barrier((value, *done))[0]


def shared_column(place_ref, share):
    return pl.multiple_of((place_ref[0] // share) * LANES, LANES)


def dense_kernel(groups_ref, weights_ref, out_ref):
    groups = groups_ref[...].T
    weights = weights_ref[...].astype(F32).T
    lane = lax.broadcasted_iota(jnp.int32, out_ref.shape, 1)
    dense = jnp.zeros(out_ref.shape, F32)
    for k in range(groups.shape[1]):
        dense += jnp.where(lane == groups[:, k : k + 1], weights[:, k : k + 1], 0.0)
    out_ref[...] = dense.astype(BF16)


def dense_weights(group_ids, route_weights):
    return pl.pallas_call(
        dense_kernel,
        out_shape=jax.ShapeDtypeStruct((group_ids.shape[0], LANES), BF16),
        name="dense_weights",
    )(group_ids.T, route_weights.T)


def load_gate_kernel(share, place_ref, gate_ref, sgate_ref, sup_ref, out_ref, sems):
    width, hidden = gate_ref.shape
    column = shared_column(place_ref, share)
    parts = 4
    piece = width // parts
    copies = []
    for i in range(parts):
        at = pl.ds(i * piece, piece)
        for source, lower, size in (
            (gate_ref.at[at, :], 0, hidden),
            (sgate_ref.at[at, pl.ds(column, LANES)], hidden, LANES),
            (sup_ref.at[at, pl.ds(column, LANES)], hidden + LANES, LANES),
        ):
            copies.append(
                pltpu.make_async_copy(source, out_ref.at[at, pl.ds(lower, size)], sems.at[len(copies)])
            )
    run_copies(copies)


def load_gate(place, gate, sgate, sup, share):
    width, hidden = gate.shape
    shape = (width, hidden + 2 * LANES)
    return pl.pallas_call(
        functools.partial(load_gate_kernel, share),
        in_specs=[SMEM_SPEC] + [ANY_SPEC] * 3,
        out_specs=VMEM_SPEC,
        out_shape=pltpu.VMEM(shape, BF16),
        scratch_shapes=[pltpu.SemaphoreType.DMA((12,))],
        cost_estimate=pl.CostEstimate(flops=0, bytes_accessed=4 * shape[0] * shape[1], transcendentals=0),
        compiler_params=pltpu.CompilerParams(vmem_limit_bytes=1 << 20),
        name="load_gate",
    )(place, in_hbm(gate), in_hbm(sgate), in_hbm(sup))


def load_up_kernel(up_ref, out_ref, sems):
    width = up_ref.shape[0]
    parts = 8
    piece = width // parts
    run_copies(
        [
            pltpu.make_async_copy(
                up_ref.at[pl.ds(i * piece, piece), :], out_ref.at[pl.ds(i * piece, piece), :], sems.at[i]
            )
            for i in range(parts)
        ]
    )


def load_up(up):
    width, hidden = up.shape
    return pl.pallas_call(
        load_up_kernel,
        in_specs=[ANY_SPEC],
        out_specs=VMEM_SPEC,
        out_shape=pltpu.VMEM((width, hidden), BF16),
        scratch_shapes=[pltpu.SemaphoreType.DMA((8,))],
        cost_estimate=pl.CostEstimate(flops=0, bytes_accessed=4 * width * hidden, transcendentals=0),
        compiler_params=pltpu.CompilerParams(vmem_limit_bytes=1 << 20),
        name="load_up",
    )(in_hbm(up))


def silu(v):
    return v / (1.0 + jnp.exp(-v))


def activate(share, node, x, first_ref, up_ref, weight, act):
    width, hidden = up_ref.shape
    tile = min(2 * LANES, hidden)
    for at in range(0, hidden, tile):
        gate = jnp.dot(x, first_ref[:, at : at + tile], preferred_element_type=F32)
        up = jnp.dot(x, up_ref[:, at : at + tile], preferred_element_type=F32)
        act[:, at : at + tile] = (silu(gate) * up * weight).astype(BF16)
    both = jnp.dot(x, first_ref[:, hidden:], preferred_element_type=F32)
    shared = silu(both[:, :LANES]) * both[:, LANES:]
    if share > 1:
        lane = lax.broadcasted_iota(jnp.int32, shared.shape, 1)
        shared = jnp.where(lane // (LANES // share) == node % share, shared, 0.0)
    act[:, hidden:] = shared.astype(BF16)


def row_weight(node, dense):
    lane = lax.broadcasted_iota(jnp.int32, dense.shape, 1)
    return jnp.sum(jnp.where(lane == node, dense.astype(F32), 0.0), axis=1, keepdims=True)


def down_copies(share, place_ref, down_ref, sdown_ref, second, sems):
    hidden, width = down_ref.shape
    column = shared_column(place_ref, share)
    parts = 4
    piece = width // parts
    copies = []
    for i in range(parts):
        at = pl.ds(i * piece, piece)
        copies.append(
            pltpu.make_async_copy(down_ref.at[:, at], second.at[pl.ds(0, hidden), at], sems.at[2 * i])
        )
        copies.append(
            pltpu.make_async_copy(
                sdown_ref.at[pl.ds(column, LANES), at], second.at[pl.ds(hidden, LANES), at], sems.at[2 * i + 1]
            )
        )
    return copies


def regroup(value, outer, inner):
    rows = value.shape[0] // (outer * inner)
    return jnp.concatenate(
        [
            value[(o * inner + i) * rows : (o * inner + i + 1) * rows]
            for i in range(inner)
            for o in range(outer)
        ],
        axis=0,
    )


def split_kernel(
    share, place_ref, a0_ref, b0_ref, a1_ref, b1_ref, first_ref, up_ref, down_ref, sdown_ref,
    own_a_ref, own_b_ref, other_a_ref, other_b_ref, x, act, second, sems,
):
    copies = down_copies(share, place_ref, down_ref, sdown_ref, second, sems)
    for copy in copies:
        copy.start()
    width = up_ref.shape[0]
    half, cut = a0_ref.shape
    for c, (a_ref, b_ref) in enumerate(((a0_ref, b0_ref), (a1_ref, b1_ref))):
        rows = slice(c * half, (c + 1) * half)
        x[rows, :cut] = a_ref[...]
        x[rows, cut:] = regroup(b_ref[...].astype(F32), 4, 2).astype(BF16)
    node = place_ref[0]
    weight = row_weight(node, x[:, width:])
    activate(share, node, x[:, :width], first_ref, up_ref, weight, act)
    parts = len(copies) // 2
    piece = width // parts
    cut = own_a_ref.shape[1]
    for i in range(parts):
        copies[2 * i].wait()
        copies[2 * i + 1].wait()
        lower, upper = i * piece, (i + 1) * piece
        for at, to in ((lower, min(upper, cut)), (max(lower, cut), upper)):
            if at >= to:
                continue
            total = jnp.dot(act[...], second[:, at:to], preferred_element_type=F32)
            if to <= cut:
                own_a_ref[:, at:to] = total[:half].astype(BF16)
                other_a_ref[:, at:to] = total[half:].astype(BF16)
            else:
                own_b_ref[:, at - cut : to - cut] = regroup(total[:half], 2, 4).astype(BF16)
                other_b_ref[:, at - cut : to - cut] = regroup(total[half:], 2, 4).astype(BF16)


def split_rows(place, pieces, first, up, down, sdown, cut, share):
    half = pieces[0].shape[0]
    hidden, width = down.shape
    out_a = jax.ShapeDtypeStruct((half, cut), BF16)
    out_b = jax.ShapeDtypeStruct((half, width - cut), BF16)
    return pl.pallas_call(
        functools.partial(split_kernel, share),
        in_specs=[SMEM_SPEC] + [VMEM_SPEC] * 6 + [ANY_SPEC] * 2,
        out_specs=[VMEM_SPEC] * 4,
        out_shape=[out_a, out_b] * 2,
        scratch_shapes=[
            pltpu.VMEM((2 * half, width + LANES), BF16),
            pltpu.VMEM((2 * half, hidden + LANES), BF16),
            pltpu.VMEM((hidden + LANES, width), BF16),
            pltpu.SemaphoreType.DMA((8,)),
        ],
        compiler_params=pltpu.CompilerParams(vmem_limit_bytes=28 << 20),
        name="split_rows",
    )(place, *pieces, first, up, in_hbm(down), in_hbm(sdown))


def block_kernel(share, place_ref, x_ref, first_ref, up_ref, down_ref, sdown_ref, out_ref, act, second, sems):
    copies = down_copies(share, place_ref, down_ref, sdown_ref, second, sems)

    @pl.when(pl.program_id(0) == 0)
    def _():
        run_copies(copies)

    width = up_ref.shape[0]
    node = place_ref[0]
    weight = row_weight(node, x_ref[:, width:])
    activate(share, node, x_ref[:, :width], first_ref, up_ref, weight, act)
    parts = 4
    piece = width // parts
    for i in range(parts):
        at = slice(i * piece, (i + 1) * piece)
        out_ref[:, at] = jnp.dot(act[...], second[:, at], preferred_element_type=F32).astype(BF16)


def block_rows(place, x, first, up, down, sdown, share):
    rows, packed = x.shape
    hidden, width = down.shape
    block = min(rows, ROW_BLOCK)
    return pl.pallas_call(
        functools.partial(block_kernel, share),
        grid=(rows // block,),
        in_specs=[SMEM_SPEC, pl.BlockSpec((block, packed), lambda i: (i, 0))] + [VMEM_SPEC] * 2 + [ANY_SPEC] * 2,
        out_specs=pl.BlockSpec((block, width), lambda i: (i, 0)),
        out_shape=jax.ShapeDtypeStruct((rows, width), BF16),
        scratch_shapes=[
            pltpu.VMEM((block, hidden + LANES), BF16),
            pltpu.VMEM((hidden + LANES, width), BF16),
            pltpu.SemaphoreType.DMA((8,)),
        ],
        compiler_params=pltpu.CompilerParams(vmem_limit_bytes=28 << 20),
        name="block_rows",
    )(place, x, first, up, in_hbm(down), in_hbm(sdown))


def f32_sum(*terms):
    return functools.reduce(lambda a, b: a + b, (t.astype(F32) for t in terms))


def swap(value, axis, bit):
    return lax.ppermute(value, axis, [(i, i ^ bit) for i in range(4)])


swap_x = functools.partial(swap, axis="node", bit=2)
swap_core = functools.partial(swap, axis="node", bit=1)


def swap_z(value, k):
    return swap(value, "local", k)


def stack(*values):
    return jnp.concatenate(values, axis=0)


def per_device(
    tokens,
    group_ids,
    route_weights,
    gate_experts,
    up_experts,
    down_experts,
    gate_shared,
    up_shared,
    down_shared,
):
    rows, width = tokens.shape
    node_count = lax.axis_size("node")
    local_count = lax.axis_size("local")
    share = max(1, LANES * node_count // gate_shared.shape[1])
    place = lax.axis_index("node").reshape(1)
    gate, up, down = gate_experts[0], up_experts[0], down_experts[0]
    dense = dense_weights(group_ids, route_weights)

    if node_count != 4 or local_count != 4:
        first = load_gate(place, gate, gate_shared, up_shared, share)
        up = load_up(up)
        x = lax.all_gather(
            jnp.concatenate([tokens, dense], axis=1), ("node", "local"), axis=0, tiled=True
        )
        part = block_rows(place, x, first, up, down, down_shared, share)
        return lax.psum_scatter(part, ("node", "local"), scatter_dimension=0, tiled=True)

    steps = (3, 2, 1)
    cut = width * 39 // 56 // LANES * LANES
    across = swap_x(tokens)
    a = tokens[:, :cut]
    got = {k: swap_z(a, k) for k in steps}
    dense_across = swap_x(dense)
    first = load_gate(after(place, dense), gate, gate_shared, up_shared, share)
    across, dense_across, got, first = lax.optimization_barrier((across, dense_across, got, first))
    far = stack(got[1], got[2], got[3])
    b = jnp.concatenate(
        [stack(tokens[:, cut:], across[:, cut:]), stack(dense, dense_across)], axis=1
    )
    b_got = {k: swap_z(b, k) for k in steps}
    far_across = swap_x(far)
    up = load_up(after(up, far, b))
    far_across, b_got, up = lax.optimization_barrier((far_across, b_got, up))
    a = stack(a, far, across[:, :cut], far_across)
    b = stack(b, b_got[1], b_got[2], b_got[3])
    pieces = (a, b, swap_core(a), swap_core(b))

    cut = width * 36 // 56 // LANES * LANES
    own_a, own_b, other_a, other_b = split_rows(place, pieces, first, up, down, down_shared, cut, share)

    four, two = 4 * rows, 2 * rows
    a_got = swap_core(other_a)
    b_got = swap_core(other_b)
    a_sum = f32_sum(own_a[:four], a_got[:four], swap_x(f32_sum(own_a[four:], a_got[four:]).astype(BF16)))
    b_sum = f32_sum(own_b[:two], b_got[:two])
    for k in steps:
        at = slice(k * two, (k + 1) * two)
        b_sum = f32_sum(b_sum, swap_z(f32_sum(own_b[at], b_got[at]).astype(BF16), k))
    a = a_sum[:rows]
    for k in steps:
        a = f32_sum(a, swap_z(a_sum[k * rows : (k + 1) * rows].astype(BF16), k))
    b = f32_sum(b_sum[:rows], swap_x(b_sum[rows:].astype(BF16)))
    return jnp.concatenate([a.astype(BF16), b.astype(BF16)], axis=1)


def solution(mesh):
    in_specs = (
        P(("rep", "node", "local"), None),
        P(("rep", "node", "local"), None),
        P(("rep", "node", "local"), None),
        P("node", None, "local"),
        P("node", None, "local"),
        P("node", "local", None),
        P(None, "local"),
        P(None, "local"),
        P("local", None),
    )
    out_specs = P(("rep", "node", "local"), None)
    return jax.shard_map(
        per_device, mesh=mesh, in_specs=in_specs, out_specs=out_specs, check_vma=False
    )
```

```python
import functools

import jax
import jax.numpy as jnp
from jax import lax
from jax.experimental import pallas as pl
from jax.experimental.pallas import tpu as pltpu
from jax.sharding import PartitionSpec as P

LANES = 128
ROW_BLOCK = 128
F32 = jnp.float32
BF16 = jnp.bfloat16
VMEM_SPEC = pl.BlockSpec(memory_space=pltpu.VMEM)
SMEM_SPEC = pl.BlockSpec(memory_space=pltpu.SMEM)
ANY_SPEC = pl.BlockSpec(memory_space=pl.ANY)


def in_hbm(value):
    return pltpu.with_memory_space_constraint(value, pltpu.HBM)


def run_copies(copies):
    for copy in copies:
        copy.start()
    for copy in copies:
        copy.wait()


def after(value, *done):
    return lax.optimization_barrier((value, *done))[0]


def pack_kernel(tokens_ref, groups_ref, weights_ref, packed_ref, tail_ref):
    rows, width = tokens_ref.shape
    packed_ref[:, :width] = tokens_ref[...]
    tail_ref[...] = tokens_ref[:, width - tail_ref.shape[1] :]
    groups = groups_ref[...].T
    weights = weights_ref[...].astype(F32).T
    lane = lax.broadcasted_iota(jnp.int32, (rows, LANES), 1)
    dense = jnp.zeros((rows, LANES), F32)
    for k in range(groups.shape[1]):
        dense += jnp.where(lane == groups[:, k : k + 1], weights[:, k : k + 1], 0.0)
    packed_ref[:, width:] = dense.astype(BF16)


def pack_rows(tokens, group_ids, route_weights, tail):
    rows, width = tokens.shape
    return pl.pallas_call(
        pack_kernel,
        out_specs=[VMEM_SPEC] * 2,
        out_shape=[pltpu.VMEM((rows, width + LANES), BF16), pltpu.VMEM((rows, tail), BF16)],
        name="pack_rows",
    )(tokens, group_ids.T, route_weights.T)


def load_kernel(weight_ref, out_ref, sems):
    parts = sems.shape[0]
    piece = weight_ref.shape[0] // parts
    run_copies(
        [
            pltpu.make_async_copy(
                weight_ref.at[pl.ds(i * piece, piece), :], out_ref.at[pl.ds(i * piece, piece), :], sems.at[i]
            )
            for i in range(parts)
        ]
    )


def load_weight(weight):
    return pl.pallas_call(
        load_kernel,
        in_specs=[ANY_SPEC],
        out_specs=VMEM_SPEC,
        out_shape=pltpu.VMEM(weight.shape, BF16),
        scratch_shapes=[pltpu.SemaphoreType.DMA((8,))],
        cost_estimate=pl.CostEstimate(flops=0, bytes_accessed=4 * weight.size, transcendentals=0),
        compiler_params=pltpu.CompilerParams(vmem_limit_bytes=1 << 20),
        name="load_weight",
    )(in_hbm(weight))


def silu(v):
    return v / (1.0 + jnp.exp(-v))


def activate(share, node, x, gate_ref, up_ref, weight, act):
    width, hidden = up_ref.shape
    tile = min(2 * LANES, hidden)
    for at in range(0, hidden, tile):
        gate = jnp.dot(x, gate_ref[:, at : at + tile], preferred_element_type=F32)
        up = jnp.dot(x, up_ref[:, at : at + tile], preferred_element_type=F32)
        act[:, at : at + tile] = (silu(gate) * up * weight).astype(BF16)


def activate_shared(share, node, x, first_shared, act):
    both = jnp.dot(x, first_shared[...], preferred_element_type=F32)
    shared = silu(both[:, :LANES]) * both[:, LANES:]
    if share > 1:
        lane = lax.broadcasted_iota(jnp.int32, shared.shape, 1)
        shared = jnp.where(lane // (LANES // share) == node % share, shared, 0.0)
    act[:, act.shape[1] - LANES :] = shared.astype(BF16)


def row_weight(node, dense):
    lane = lax.broadcasted_iota(jnp.int32, dense.shape, 1)
    return jnp.sum(jnp.where(lane == node, dense.astype(F32), 0.0), axis=1, keepdims=True)


DOWN_PARTS = 4


def weight_copies(share, place_ref, sgate_ref, sup_ref, down_ref, sdown_ref, first_shared, second, sems):
    hidden, width = down_ref.shape
    column = pl.multiple_of((place_ref[0] // share) * LANES, LANES)
    own = pl.ds(column, LANES)
    pairs = [
        (sgate_ref.at[:, own], first_shared.at[:, pl.ds(0, LANES)]),
        (sup_ref.at[:, own], first_shared.at[:, pl.ds(LANES, LANES)]),
    ]
    piece = width // DOWN_PARTS
    for i in range(DOWN_PARTS):
        at = pl.ds(i * piece, piece)
        pairs.append((down_ref.at[:, at], second.at[pl.ds(0, hidden), at]))
        pairs.append((sdown_ref.at[own, at], second.at[pl.ds(hidden, LANES), at]))
    return [pltpu.make_async_copy(a, b, sems.at[i]) for i, (a, b) in enumerate(pairs)]


def weight_scratch(hidden, width):
    return [
        pltpu.VMEM((width, 2 * LANES), BF16),
        pltpu.VMEM((hidden + LANES, width), BF16),
        pltpu.SemaphoreType.DMA((2 + 2 * DOWN_PARTS,)),
    ]


def split_kernel(
    share, place_ref, b0_ref, a0_ref, b1_ref, a1_ref, gate_ref, up_ref, sgate_ref, sup_ref, down_ref, sdown_ref,
    own_b_ref, own_a_ref, other_b_ref, other_a_ref, x, act, first_shared, second, sems,
):
    copies = weight_copies(
        share, place_ref, sgate_ref, sup_ref, down_ref, sdown_ref, first_shared, second, sems
    )
    for copy in copies:
        copy.start()
    width = up_ref.shape[0]
    half = a0_ref.shape[0]
    cut = width - a0_ref.shape[1]
    group, eighth = half // 4, half // 8
    for c, (b_ref, a_ref) in enumerate(((b0_ref, a0_ref), (b1_ref, a1_ref))):
        a = a_ref[...].astype(F32)
        for k in range(4):
            rows = pl.ds(pl.multiple_of(c * half + (place_ref[1] ^ k) * group, group), group)
            pair = [a[x_at * 4 * eighth + k * eighth :][:eighth] for x_at in range(2)]
            x[rows, cut:width] = jnp.concatenate(pair, axis=0).astype(BF16)
            x[rows, :cut] = b_ref[k * group : (k + 1) * group, :cut]
            x[rows, width:] = b_ref[k * group : (k + 1) * group, cut:]
    node = place_ref[0]
    weight = row_weight(node, x[:, width:])
    activate(share, node, x[:, :width], gate_ref, up_ref, weight, act)
    copies[0].wait()
    copies[1].wait()
    activate_shared(share, node, x[:, :width], first_shared, act)
    piece = width // DOWN_PARTS
    cut = own_b_ref.shape[1]
    for i in range(DOWN_PARTS):
        copies[2 + 2 * i].wait()
        copies[3 + 2 * i].wait()
        lower, upper = i * piece, (i + 1) * piece
        for at, to in ((lower, min(upper, cut)), (max(lower, cut), upper)):
            if at >= to:
                continue
            total = jnp.dot(act[...], second[:, at:to], preferred_element_type=F32)
            if to <= cut:
                own_b_ref[:, at:to] = total[:half].astype(BF16)
                other_b_ref[:, at:to] = total[half:].astype(BF16)
            else:
                own_a_ref[:, at - cut : to - cut] = total[:half].astype(BF16)
                other_a_ref[:, at - cut : to - cut] = total[half:].astype(BF16)


def split_rows(place, pieces, gate, up, sgate, sup, down, sdown, cut, share):
    half = pieces[0].shape[0]
    hidden, width = down.shape
    out_b = jax.ShapeDtypeStruct((half, cut), BF16)
    out_a = jax.ShapeDtypeStruct((half, width - cut), BF16)
    return pl.pallas_call(
        functools.partial(split_kernel, share),
        in_specs=[SMEM_SPEC] + [VMEM_SPEC] * 6 + [ANY_SPEC] * 4,
        out_specs=[VMEM_SPEC] * 4,
        out_shape=[out_b, out_a] * 2,
        scratch_shapes=[
            pltpu.VMEM((2 * half, width + LANES), BF16),
            pltpu.VMEM((2 * half, hidden + LANES), BF16),
        ]
        + weight_scratch(hidden, width),
        compiler_params=pltpu.CompilerParams(vmem_limit_bytes=30 << 20),
        name="split_rows",
    )(place, *pieces, gate, up, *(in_hbm(w) for w in (sgate, sup, down, sdown)))


def block_kernel(
    share, place_ref, x_ref, gate_ref, up_ref, sgate_ref, sup_ref, down_ref, sdown_ref,
    out_ref, act, first_shared, second, sems,
):
    copies = weight_copies(
        share, place_ref, sgate_ref, sup_ref, down_ref, sdown_ref, first_shared, second, sems
    )

    @pl.when(pl.program_id(0) == 0)
    def _():
        run_copies(copies)

    width = up_ref.shape[0]
    node = place_ref[0]
    weight = row_weight(node, x_ref[:, width:])
    x = x_ref[:, :width]
    activate(share, node, x, gate_ref, up_ref, weight, act)
    activate_shared(share, node, x, first_shared, act)
    piece = width // DOWN_PARTS
    for i in range(DOWN_PARTS):
        at = slice(i * piece, (i + 1) * piece)
        out_ref[:, at] = jnp.dot(act[...], second[:, at], preferred_element_type=F32).astype(BF16)


def block_rows(place, x, gate, up, sgate, sup, down, sdown, share):
    rows, packed = x.shape
    hidden, width = down.shape
    block = min(rows, ROW_BLOCK)
    return pl.pallas_call(
        functools.partial(block_kernel, share),
        grid=(rows // block,),
        in_specs=[SMEM_SPEC, pl.BlockSpec((block, packed), lambda i: (i, 0))] + [VMEM_SPEC] * 2 + [ANY_SPEC] * 4,
        out_specs=pl.BlockSpec((block, width), lambda i: (i, 0)),
        out_shape=jax.ShapeDtypeStruct((rows, width), BF16),
        scratch_shapes=[pltpu.VMEM((block, hidden + LANES), BF16)] + weight_scratch(hidden, width),
        compiler_params=pltpu.CompilerParams(vmem_limit_bytes=30 << 20),
        name="block_rows",
    )(place, x, gate, up, *(in_hbm(w) for w in (sgate, sup, down, sdown)))


def f32_sum(*terms):
    return functools.reduce(lambda a, b: a + b, (t.astype(F32) for t in terms))


def swap(value, axis, bit):
    return lax.ppermute(value, axis, [(i, i ^ bit) for i in range(4)])


swap_x = functools.partial(swap, axis="node", bit=2)
swap_core = functools.partial(swap, axis="node", bit=1)


def swap_z(value, k):
    return swap(value, "local", k)


def stack(*values):
    return jnp.concatenate(values, axis=0)


def per_device(
    tokens,
    group_ids,
    route_weights,
    gate_experts,
    up_experts,
    down_experts,
    gate_shared,
    up_shared,
    down_shared,
):
    rows, width = tokens.shape
    node_count = lax.axis_size("node")
    local_count = lax.axis_size("local")
    share = max(1, LANES * node_count // gate_shared.shape[1])
    place = jnp.stack([lax.axis_index("node"), lax.axis_index("local")])
    gate, up, down = gate_experts[0], up_experts[0], down_experts[0]
    rest = (gate_shared, up_shared, down, down_shared)
    cut = width * 17 // 56 // LANES * LANES
    packed, a = pack_rows(tokens, group_ids, route_weights, width - cut)

    if node_count != 4 or local_count != 4:
        x = lax.all_gather(packed, ("node", "local"), axis=0, tiled=True)
        part = block_rows(place, x, load_weight(gate), load_weight(up), *rest, share)
        return lax.psum_scatter(part, ("node", "local"), scatter_dimension=0, tiled=True)

    steps = (3, 2, 1)
    across = swap_x(packed)
    got = {k: swap_z(a, k) for k in steps}
    gate = load_weight(after(gate, a))
    got[1], gate = lax.optimization_barrier((got[1], gate))
    near_across = swap_x(got[1])
    across, got[2], got[3], gate = lax.optimization_barrier((across, got[2], got[3], gate))
    b = stack(packed, across)
    b = jnp.concatenate([b[:, :cut], b[:, width:]], axis=1)
    b_got = {k: swap_z(b, k) for k in steps}
    far = stack(got[2], got[3])
    far_across = swap_x(far)
    up = load_weight(after(up, far, b))
    b_got, far_across, up = lax.optimization_barrier((b_got, far_across, up))
    a = stack(a, got[1], far, across[:, cut:width], near_across, far_across)
    b = stack(b, b_got[1], b_got[2], b_got[3])
    pieces = (b, a, swap_core(b), swap_core(a))

    cut = width * 20 // 56 // LANES * LANES
    own_b, own_a, other_b, other_a = split_rows(place, pieces, gate, up, *rest, cut, share)

    def by_place(value):
        return value.reshape(4, 2, rows, -1)

    def exchange(value):
        return f32_sum(*lax.all_to_all(value.astype(BF16), "local", 0, 0))

    b_got = swap_core(other_b)
    a_got = swap_core(other_a)
    b_got = after(b_got, a_got)
    own_a, a_got = by_place(own_a), by_place(a_got)
    a_cross = swap_x(f32_sum(own_a[:, 1], a_got[:, 1]).astype(BF16))
    b_sum = exchange(by_place(f32_sum(own_b, b_got)))
    b = f32_sum(b_sum[0], swap_x(b_sum[1].astype(BF16)))
    a = exchange(f32_sum(own_a[:, 0], a_got[:, 0], a_cross))
    return jnp.concatenate([b.astype(BF16), a.astype(BF16)], axis=1)


def solution(mesh):
    in_specs = (
        P(("rep", "node", "local"), None),
        P(("rep", "node", "local"), None),
        P(("rep", "node", "local"), None),
        P("node", None, "local"),
        P("node", None, "local"),
        P("node", "local", None),
        P(None, "local"),
        P(None, "local"),
        P("local", None),
    )
    out_specs = P(("rep", "node", "local"), None)
    return jax.shard_map(
        per_device, mesh=mesh, in_specs=in_specs, out_specs=out_specs, check_vma=False
    )
```

```python
import functools

import jax
import jax.numpy as jnp
from jax import lax
from jax.experimental import pallas as pl
from jax.experimental.pallas import tpu as pltpu
from jax.sharding import PartitionSpec as P

LANES = 128
ROW_BLOCK = 128
F32 = jnp.float32
BF16 = jnp.bfloat16
VMEM_SPEC = pl.BlockSpec(memory_space=pltpu.VMEM)
SMEM_SPEC = pl.BlockSpec(memory_space=pltpu.SMEM)
ANY_SPEC = pl.BlockSpec(memory_space=pl.ANY)


def in_hbm(value):
    return pltpu.with_memory_space_constraint(value, pltpu.HBM)


def run_copies(copies):
    for copy in copies:
        copy.start()
    for copy in copies:
        copy.wait()


def after(value, *done):
    return lax.optimization_barrier((value, *done))[0]


def pack_kernel(tokens_ref, groups_ref, weights_ref, packed_ref, tail_ref):
    rows, width = tokens_ref.shape
    packed_ref[:, :width] = tokens_ref[...]
    tail_ref[...] = tokens_ref[:, width - tail_ref.shape[1] :]
    groups = groups_ref[...].T
    weights = weights_ref[...].astype(F32).T
    lane = lax.broadcasted_iota(jnp.int32, (rows, LANES), 1)
    dense = jnp.zeros((rows, LANES), F32)
    for k in range(groups.shape[1]):
        dense += jnp.where(lane == groups[:, k : k + 1], weights[:, k : k + 1], 0.0)
    packed_ref[:, width:] = dense.astype(BF16)


def pack_rows(tokens, group_ids, route_weights, tail):
    rows, width = tokens.shape
    return pl.pallas_call(
        pack_kernel,
        out_specs=[VMEM_SPEC] * 2,
        out_shape=[pltpu.VMEM((rows, width + LANES), BF16), pltpu.VMEM((rows, tail), BF16)],
        name="pack_rows",
    )(tokens, group_ids.T, route_weights.T)


def load_gate_kernel(share, place_ref, gate_ref, sgate_ref, sup_ref, out_ref, sems):
    width, hidden = gate_ref.shape
    column = pl.multiple_of((place_ref[0] // share) * LANES, LANES)
    parts = 4
    piece = width // parts
    copies = []
    for i in range(parts):
        at = pl.ds(i * piece, piece)
        for source, lower, size in (
            (gate_ref.at[at, :], 0, hidden),
            (sgate_ref.at[at, pl.ds(column, LANES)], hidden, LANES),
            (sup_ref.at[at, pl.ds(column, LANES)], hidden + LANES, LANES),
        ):
            copies.append(
                pltpu.make_async_copy(source, out_ref.at[at, pl.ds(lower, size)], sems.at[len(copies)])
            )
    run_copies(copies)


def load_gate(place, gate, sgate, sup, share):
    width, hidden = gate.shape
    shape = (width, hidden + 2 * LANES)
    return pl.pallas_call(
        functools.partial(load_gate_kernel, share),
        in_specs=[SMEM_SPEC] + [ANY_SPEC] * 3,
        out_specs=VMEM_SPEC,
        out_shape=pltpu.VMEM(shape, BF16),
        scratch_shapes=[pltpu.SemaphoreType.DMA((12,))],
        cost_estimate=pl.CostEstimate(flops=0, bytes_accessed=4 * shape[0] * shape[1], transcendentals=0),
        compiler_params=pltpu.CompilerParams(vmem_limit_bytes=1 << 20),
        name="load_gate",
    )(place, in_hbm(gate), in_hbm(sgate), in_hbm(sup))


def load_up_kernel(up_ref, out_ref, sems):
    width = up_ref.shape[0]
    parts = 8
    piece = width // parts
    run_copies(
        [
            pltpu.make_async_copy(
                up_ref.at[pl.ds(i * piece, piece), :], out_ref.at[pl.ds(i * piece, piece), :], sems.at[i]
            )
            for i in range(parts)
        ]
    )


def load_up(up):
    width, hidden = up.shape
    return pl.pallas_call(
        load_up_kernel,
        in_specs=[ANY_SPEC],
        out_specs=VMEM_SPEC,
        out_shape=pltpu.VMEM((width, hidden), BF16),
        scratch_shapes=[pltpu.SemaphoreType.DMA((8,))],
        cost_estimate=pl.CostEstimate(flops=0, bytes_accessed=4 * width * hidden, transcendentals=0),
        compiler_params=pltpu.CompilerParams(vmem_limit_bytes=1 << 20),
        name="load_up",
    )(in_hbm(up))


def silu(v):
    return v / (1.0 + jnp.exp(-v))


def activate(share, node, x, first_ref, up_ref, weight, act):
    width, hidden = up_ref.shape
    tile = min(2 * LANES, hidden)
    for at in range(0, hidden, tile):
        gate = jnp.dot(x, first_ref[:, at : at + tile], preferred_element_type=F32)
        up = jnp.dot(x, up_ref[:, at : at + tile], preferred_element_type=F32)
        act[:, at : at + tile] = (silu(gate) * up * weight).astype(BF16)
    both = jnp.dot(x, first_ref[:, hidden:], preferred_element_type=F32)
    shared = silu(both[:, :LANES]) * both[:, LANES:]
    if share > 1:
        lane = lax.broadcasted_iota(jnp.int32, shared.shape, 1)
        shared = jnp.where(lane // (LANES // share) == node % share, shared, 0.0)
    act[:, hidden:] = shared.astype(BF16)


def row_weight(node, dense):
    lane = lax.broadcasted_iota(jnp.int32, dense.shape, 1)
    return jnp.sum(jnp.where(lane == node, dense.astype(F32), 0.0), axis=1, keepdims=True)


DOWN_PARTS = 4


def down_copies(share, place_ref, down_ref, sdown_ref, second, sems):
    hidden, width = down_ref.shape
    column = pl.multiple_of((place_ref[0] // share) * LANES, LANES)
    piece = width // DOWN_PARTS
    copies = []
    for i in range(DOWN_PARTS):
        at = pl.ds(i * piece, piece)
        copies.append(
            pltpu.make_async_copy(down_ref.at[:, at], second.at[pl.ds(0, hidden), at], sems.at[2 * i])
        )
        copies.append(
            pltpu.make_async_copy(
                sdown_ref.at[pl.ds(column, LANES), at], second.at[pl.ds(hidden, LANES), at], sems.at[2 * i + 1]
            )
        )
    return copies


def down_scratch(rows, hidden, width):
    return [
        pltpu.VMEM((rows, hidden + LANES), BF16),
        pltpu.VMEM((hidden + LANES, width), BF16),
        pltpu.SemaphoreType.DMA((2 * DOWN_PARTS,)),
    ]


def regroup(value, outer, inner):
    rows = value.shape[0] // (outer * inner)
    return jnp.concatenate(
        [
            value[(o * inner + i) * rows : (o * inner + i + 1) * rows]
            for i in range(inner)
            for o in range(outer)
        ],
        axis=0,
    )


def split_kernel(
    share, place_ref, b0_ref, a0_ref, b1_ref, a1_ref, first_ref, up_ref, down_ref, sdown_ref,
    own_b_ref, own_a_ref, other_b_ref, other_a_ref, x, act, second, sems,
):
    copies = down_copies(share, place_ref, down_ref, sdown_ref, second, sems)
    for copy in copies:
        copy.start()
    width = up_ref.shape[0]
    half = a0_ref.shape[0]
    cut = width - a0_ref.shape[1]
    for c, (b_ref, a_ref) in enumerate(((b0_ref, a0_ref), (b1_ref, a1_ref))):
        rows = slice(c * half, (c + 1) * half)
        b = regroup(b_ref[...].astype(F32), 4, 2).astype(BF16)
        x[rows, :cut] = b[:, :cut]
        x[rows, cut:width] = a_ref[...]
        x[rows, width:] = b[:, cut:]
    node = place_ref[0]
    weight = row_weight(node, x[:, width:])
    activate(share, node, x[:, :width], first_ref, up_ref, weight, act)
    piece = width // DOWN_PARTS
    cut = own_b_ref.shape[1]
    for i in range(DOWN_PARTS):
        copies[2 * i].wait()
        copies[2 * i + 1].wait()
        lower, upper = i * piece, (i + 1) * piece
        for at, to in ((lower, min(upper, cut)), (max(lower, cut), upper)):
            if at >= to:
                continue
            total = jnp.dot(act[...], second[:, at:to], preferred_element_type=F32)
            if to <= cut:
                own_b_ref[:, at:to] = regroup(total[:half], 2, 4).astype(BF16)
                other_b_ref[:, at:to] = regroup(total[half:], 2, 4).astype(BF16)
            else:
                own_a_ref[:, at - cut : to - cut] = total[:half].astype(BF16)
                other_a_ref[:, at - cut : to - cut] = total[half:].astype(BF16)


def split_rows(place, pieces, first, up, down, sdown, cut, share):
    half = pieces[0].shape[0]
    hidden, width = down.shape
    out_b = jax.ShapeDtypeStruct((half, cut), BF16)
    out_a = jax.ShapeDtypeStruct((half, width - cut), BF16)
    return pl.pallas_call(
        functools.partial(split_kernel, share),
        in_specs=[SMEM_SPEC] + [VMEM_SPEC] * 6 + [ANY_SPEC] * 2,
        out_specs=[VMEM_SPEC] * 4,
        out_shape=[out_b, out_a] * 2,
        scratch_shapes=[pltpu.VMEM((2 * half, width + LANES), BF16)] + down_scratch(2 * half, hidden, width),
        compiler_params=pltpu.CompilerParams(vmem_limit_bytes=28 << 20),
        name="split_rows",
    )(place, *pieces, first, up, in_hbm(down), in_hbm(sdown))


def block_kernel(share, place_ref, x_ref, first_ref, up_ref, down_ref, sdown_ref, out_ref, act, second, sems):
    copies = down_copies(share, place_ref, down_ref, sdown_ref, second, sems)

    @pl.when(pl.program_id(0) == 0)
    def _():
        run_copies(copies)

    width = up_ref.shape[0]
    node = place_ref[0]
    weight = row_weight(node, x_ref[:, width:])
    activate(share, node, x_ref[:, :width], first_ref, up_ref, weight, act)
    piece = width // DOWN_PARTS
    for i in range(DOWN_PARTS):
        at = slice(i * piece, (i + 1) * piece)
        out_ref[:, at] = jnp.dot(act[...], second[:, at], preferred_element_type=F32).astype(BF16)


def block_rows(place, x, first, up, down, sdown, share):
    rows, packed = x.shape
    hidden, width = down.shape
    block = min(rows, ROW_BLOCK)
    return pl.pallas_call(
        functools.partial(block_kernel, share),
        grid=(rows // block,),
        in_specs=[SMEM_SPEC, pl.BlockSpec((block, packed), lambda i: (i, 0))] + [VMEM_SPEC] * 2 + [ANY_SPEC] * 2,
        out_specs=pl.BlockSpec((block, width), lambda i: (i, 0)),
        out_shape=jax.ShapeDtypeStruct((rows, width), BF16),
        scratch_shapes=down_scratch(block, hidden, width),
        compiler_params=pltpu.CompilerParams(vmem_limit_bytes=28 << 20),
        name="block_rows",
    )(place, x, first, up, in_hbm(down), in_hbm(sdown))


def f32_sum(*terms):
    return functools.reduce(lambda a, b: a + b, (t.astype(F32) for t in terms))


def swap(value, axis, bit):
    return lax.ppermute(value, axis, [(i, i ^ bit) for i in range(4)])


swap_x = functools.partial(swap, axis="node", bit=2)
swap_core = functools.partial(swap, axis="node", bit=1)


def swap_z(value, k):
    return swap(value, "local", k)


def stack(*values):
    return jnp.concatenate(values, axis=0)


def per_device(
    tokens,
    group_ids,
    route_weights,
    gate_experts,
    up_experts,
    down_experts,
    gate_shared,
    up_shared,
    down_shared,
):
    rows, width = tokens.shape
    node_count = lax.axis_size("node")
    local_count = lax.axis_size("local")
    share = max(1, LANES * node_count // gate_shared.shape[1])
    place = lax.axis_index("node").reshape(1)
    gate, up, down = gate_experts[0], up_experts[0], down_experts[0]
    cut = width * 17 // 56 // LANES * LANES
    packed, a = pack_rows(tokens, group_ids, route_weights, width - cut)

    if node_count != 4 or local_count != 4:
        x = lax.all_gather(packed, ("node", "local"), axis=0, tiled=True)
        first = load_gate(place, gate, gate_shared, up_shared, share)
        part = block_rows(place, x, first, load_up(up), down, down_shared, share)
        return lax.psum_scatter(part, ("node", "local"), scatter_dimension=0, tiled=True)

    steps = (1, 2, 3)
    across = swap_x(packed)
    got = {k: swap_z(a, k) for k in steps}
    first = load_gate(after(place, a), gate, gate_shared, up_shared, share)
    got[1], first = lax.optimization_barrier((got[1], first))
    far = {1: swap_x(got[1])}
    got[2] = after(got[2], got[1])
    far[2] = swap_x(got[2])
    got[3] = after(got[3], got[2])
    far[3] = swap_x(got[3])
    b = stack(packed, across)
    b = jnp.concatenate([b[:, :cut], b[:, width:]], axis=1)
    b = after(b, got[3])
    b_got = {k: swap_z(b, k) for k in steps}
    up = load_up(after(up, got[3], b))
    far, b_got, up = lax.optimization_barrier((far, b_got, up))
    a = stack(a, got[1], got[2], got[3], across[:, cut:width], far[1], far[2], far[3])
    b = stack(b, b_got[1], b_got[2], b_got[3])
    pieces = (b, a, swap_core(b), swap_core(a))

    cut = width * 20 // 56 // LANES * LANES
    own_b, own_a, other_b, other_a = split_rows(place, pieces, first, up, down, down_shared, cut, share)

    four, two = 4 * rows, 2 * rows
    a_got = swap_core(other_a)
    a_cross = swap_x(f32_sum(own_a[four:], a_got[four:]).astype(BF16))
    b_got = swap_core(after(other_b, a_got))
    b_far = [
        swap_z(f32_sum(own_b[k * two : (k + 1) * two], b_got[k * two : (k + 1) * two]).astype(BF16), k)
        for k in steps
    ]
    a_cross, b_far = lax.optimization_barrier((a_cross, b_far))
    a_sum = f32_sum(own_a[:four], a_got[:four], a_cross)
    a = f32_sum(a_sum[:rows], *(swap_z(a_sum[k * rows : (k + 1) * rows].astype(BF16), k) for k in steps))
    b_sum = f32_sum(own_b[:two], b_got[:two], *b_far)
    b = f32_sum(b_sum[:rows], swap_x(b_sum[rows:].astype(BF16)))
    return jnp.concatenate([b.astype(BF16), a.astype(BF16)], axis=1)


def solution(mesh):
    in_specs = (
        P(("rep", "node", "local"), None),
        P(("rep", "node", "local"), None),
        P(("rep", "node", "local"), None),
        P("node", None, "local"),
        P("node", None, "local"),
        P("node", "local", None),
        P(None, "local"),
        P(None, "local"),
        P("local", None),
    )
    out_specs = P(("rep", "node", "local"), None)
    return jax.shard_map(
        per_device, mesh=mesh, in_specs=in_specs, out_specs=out_specs, check_vma=False
    )
```

```python
import functools

import jax
import jax.numpy as jnp
from jax import lax
from jax.experimental import pallas as pl
from jax.experimental.pallas import tpu as pltpu
from jax.sharding import PartitionSpec as P

LANES = 128
ROW_BLOCK = 128
F32 = jnp.float32
BF16 = jnp.bfloat16
VMEM_SPEC = pl.BlockSpec(memory_space=pltpu.VMEM)
SMEM_SPEC = pl.BlockSpec(memory_space=pltpu.SMEM)
ANY_SPEC = pl.BlockSpec(memory_space=pl.ANY)


def in_hbm(value):
    return pltpu.with_memory_space_constraint(value, pltpu.HBM)


def run_copies(copies):
    for copy in copies:
        copy.start()
    for copy in copies:
        copy.wait()


def after(value, *done):
    return lax.optimization_barrier((value, *done))[0]


def pack_kernel(tokens_ref, groups_ref, weights_ref, packed_ref):
    rows, width = tokens_ref.shape
    packed_ref[:, :width] = tokens_ref[...]
    groups = groups_ref[...].T
    weights = weights_ref[...].astype(F32).T
    lane = lax.broadcasted_iota(jnp.int32, (rows, LANES), 1)
    dense = jnp.zeros((rows, LANES), F32)
    for k in range(groups.shape[1]):
        dense += jnp.where(lane == groups[:, k : k + 1], weights[:, k : k + 1], 0.0)
    packed_ref[:, width:] = dense.astype(BF16)


def pack_rows(tokens, group_ids, route_weights):
    rows, width = tokens.shape
    return pl.pallas_call(
        pack_kernel,
        out_specs=VMEM_SPEC,
        out_shape=pltpu.VMEM((rows, width + LANES), BF16),
        name="pack_rows",
    )(tokens, group_ids.T, route_weights.T)


def load_gate_kernel(share, place_ref, gate_ref, sgate_ref, sup_ref, out_ref, sems):
    width, hidden = gate_ref.shape
    column = pl.multiple_of((place_ref[0] // share) * LANES, LANES)
    parts = 4
    piece = width // parts
    copies = []
    for i in range(parts):
        at = pl.ds(i * piece, piece)
        for source, lower, size in (
            (gate_ref.at[at, :], 0, hidden),
            (sgate_ref.at[at, pl.ds(column, LANES)], hidden, LANES),
            (sup_ref.at[at, pl.ds(column, LANES)], hidden + LANES, LANES),
        ):
            copies.append(
                pltpu.make_async_copy(source, out_ref.at[at, pl.ds(lower, size)], sems.at[len(copies)])
            )
    run_copies(copies)


def load_gate(place, gate, sgate, sup, share):
    width, hidden = gate.shape
    shape = (width, hidden + 2 * LANES)
    return pl.pallas_call(
        functools.partial(load_gate_kernel, share),
        in_specs=[SMEM_SPEC] + [ANY_SPEC] * 3,
        out_specs=VMEM_SPEC,
        out_shape=pltpu.VMEM(shape, BF16),
        scratch_shapes=[pltpu.SemaphoreType.DMA((12,))],
        cost_estimate=pl.CostEstimate(flops=0, bytes_accessed=4 * shape[0] * shape[1], transcendentals=0),
        compiler_params=pltpu.CompilerParams(vmem_limit_bytes=1 << 20),
        name="load_gate",
    )(place, in_hbm(gate), in_hbm(sgate), in_hbm(sup))


def load_up_kernel(up_ref, out_ref, sems):
    width = up_ref.shape[0]
    parts = 8
    piece = width // parts
    run_copies(
        [
            pltpu.make_async_copy(
                up_ref.at[pl.ds(i * piece, piece), :], out_ref.at[pl.ds(i * piece, piece), :], sems.at[i]
            )
            for i in range(parts)
        ]
    )


def load_up(up):
    width, hidden = up.shape
    return pl.pallas_call(
        load_up_kernel,
        in_specs=[ANY_SPEC],
        out_specs=VMEM_SPEC,
        out_shape=pltpu.VMEM((width, hidden), BF16),
        scratch_shapes=[pltpu.SemaphoreType.DMA((8,))],
        cost_estimate=pl.CostEstimate(flops=0, bytes_accessed=4 * width * hidden, transcendentals=0),
        compiler_params=pltpu.CompilerParams(vmem_limit_bytes=1 << 20),
        name="load_up",
    )(in_hbm(up))


def silu(v):
    return v / (1.0 + jnp.exp(-v))


def activate(share, node, x, first_ref, up_ref, weight, act):
    width, hidden = up_ref.shape
    tile = min(2 * LANES, hidden)
    for at in range(0, hidden, tile):
        gate = jnp.dot(x, first_ref[:, at : at + tile], preferred_element_type=F32)
        up = jnp.dot(x, up_ref[:, at : at + tile], preferred_element_type=F32)
        act[:, at : at + tile] = (silu(gate) * up * weight).astype(BF16)
    both = jnp.dot(x, first_ref[:, hidden:], preferred_element_type=F32)
    shared = silu(both[:, :LANES]) * both[:, LANES:]
    if share > 1:
        lane = lax.broadcasted_iota(jnp.int32, shared.shape, 1)
        shared = jnp.where(lane // (LANES // share) == node % share, shared, 0.0)
    act[:, hidden:] = shared.astype(BF16)


def row_weight(node, dense):
    lane = lax.broadcasted_iota(jnp.int32, dense.shape, 1)
    return jnp.sum(jnp.where(lane == node, dense.astype(F32), 0.0), axis=1, keepdims=True)


DOWN_PARTS = 4


def down_copies(share, place_ref, down_ref, sdown_ref, second, sems):
    hidden, width = down_ref.shape
    column = pl.multiple_of((place_ref[0] // share) * LANES, LANES)
    piece = width // DOWN_PARTS
    copies = []
    for i in range(DOWN_PARTS):
        at = pl.ds(i * piece, piece)
        copies.append(
            pltpu.make_async_copy(down_ref.at[:, at], second.at[pl.ds(0, hidden), at], sems.at[2 * i])
        )
        copies.append(
            pltpu.make_async_copy(
                sdown_ref.at[pl.ds(column, LANES), at], second.at[pl.ds(hidden, LANES), at], sems.at[2 * i + 1]
            )
        )
    return copies


def down_scratch(rows, hidden, width):
    return [
        pltpu.VMEM((rows, hidden + LANES), BF16),
        pltpu.VMEM((hidden + LANES, width), BF16),
        pltpu.SemaphoreType.DMA((2 * DOWN_PARTS,)),
    ]


def pair_kernel(
    share, place_ref, own_ref, other_ref, first_ref, up_ref, down_ref, sdown_ref,
    own_out_ref, other_out_ref, x, act, second, sems,
):
    copies = down_copies(share, place_ref, down_ref, sdown_ref, second, sems)
    for copy in copies:
        copy.start()
    width = up_ref.shape[0]
    half = own_ref.shape[0]
    x[:half, :] = own_ref[...]
    x[half:, :] = other_ref[...]
    node = place_ref[0]
    weight = row_weight(node, x[:, width:])
    activate(share, node, x[:, :width], first_ref, up_ref, weight, act)
    piece = width // DOWN_PARTS
    for i in range(DOWN_PARTS):
        copies[2 * i].wait()
        copies[2 * i + 1].wait()
        at = slice(i * piece, (i + 1) * piece)
        total = jnp.dot(act[...], second[:, at], preferred_element_type=F32).astype(BF16)
        own_out_ref[:, at] = total[:half]
        other_out_ref[:, at] = total[half:]


def pair_rows(place, own, other, first, up, down, sdown, share):
    half = own.shape[0]
    hidden, width = down.shape
    out = jax.ShapeDtypeStruct((half, width), BF16)
    return pl.pallas_call(
        functools.partial(pair_kernel, share),
        in_specs=[SMEM_SPEC] + [VMEM_SPEC] * 4 + [ANY_SPEC] * 2,
        out_specs=[VMEM_SPEC] * 2,
        out_shape=[out] * 2,
        scratch_shapes=[pltpu.VMEM((2 * half, width + LANES), BF16)] + down_scratch(2 * half, hidden, width),
        compiler_params=pltpu.CompilerParams(vmem_limit_bytes=28 << 20),
        name="pair_rows",
    )(place, own, other, first, up, in_hbm(down), in_hbm(sdown))


def block_kernel(share, place_ref, x_ref, first_ref, up_ref, down_ref, sdown_ref, out_ref, act, second, sems):
    copies = down_copies(share, place_ref, down_ref, sdown_ref, second, sems)

    @pl.when(pl.program_id(0) == 0)
    def _():
        run_copies(copies)

    width = up_ref.shape[0]
    node = place_ref[0]
    weight = row_weight(node, x_ref[:, width:])
    activate(share, node, x_ref[:, :width], first_ref, up_ref, weight, act)
    piece = width // DOWN_PARTS
    for i in range(DOWN_PARTS):
        at = slice(i * piece, (i + 1) * piece)
        out_ref[:, at] = jnp.dot(act[...], second[:, at], preferred_element_type=F32).astype(BF16)


def block_rows(place, x, first, up, down, sdown, share):
    rows, packed = x.shape
    hidden, width = down.shape
    block = min(rows, ROW_BLOCK)
    return pl.pallas_call(
        functools.partial(block_kernel, share),
        grid=(rows // block,),
        in_specs=[SMEM_SPEC, pl.BlockSpec((block, packed), lambda i: (i, 0))] + [VMEM_SPEC] * 2 + [ANY_SPEC] * 2,
        out_specs=pl.BlockSpec((block, width), lambda i: (i, 0)),
        out_shape=jax.ShapeDtypeStruct((rows, width), BF16),
        scratch_shapes=down_scratch(block, hidden, width),
        compiler_params=pltpu.CompilerParams(vmem_limit_bytes=28 << 20),
        name="block_rows",
    )(place, x, first, up, in_hbm(down), in_hbm(sdown))


def f32_sum(*terms):
    return functools.reduce(lambda a, b: a + b, (t.astype(F32) for t in terms))


def flipped(value, even, odd):
    pairs = []
    for node in range(4):
        for local in range(4):
            node_bits, local_bits = odd if node % 2 else even
            pairs.append((node * 4 + local, (node ^ node_bits) * 4 + (local ^ local_bits)))
    return lax.ppermute(value, ("node", "local"), pairs)


X, Z1, Z2, CORE = (2, 0), (0, 1), (0, 2), (1, 0)
PHASES = ((Z2, X), (Z1, Z2), (X, Z1))


def stack(*values):
    return jnp.concatenate(values, axis=0)


def per_device(
    tokens,
    group_ids,
    route_weights,
    gate_experts,
    up_experts,
    down_experts,
    gate_shared,
    up_shared,
    down_shared,
):
    rows, width = tokens.shape
    node_count = lax.axis_size("node")
    local_count = lax.axis_size("local")
    share = max(1, LANES * node_count // gate_shared.shape[1])
    place = lax.axis_index("node").reshape(1)
    gate, up, down = gate_experts[0], up_experts[0], down_experts[0]
    packed = pack_rows(tokens, group_ids, route_weights)

    if node_count != 4 or local_count != 4:
        x = lax.all_gather(packed, ("node", "local"), axis=0, tiled=True)
        first = load_gate(place, gate, gate_shared, up_shared, share)
        part = block_rows(place, x, first, load_up(up), down, down_shared, share)
        return lax.psum_scatter(part, ("node", "local"), scatter_dimension=0, tiled=True)

    own = stack(packed, flipped(packed, *PHASES[0]))
    got = flipped(own, *PHASES[1])
    first = load_gate(after(place, own), gate, gate_shared, up_shared, share)
    got, first = lax.optimization_barrier((got, first))
    own = stack(own, got)
    got = flipped(own, *PHASES[2])
    up = load_up(after(up, own))
    got, up = lax.optimization_barrier((got, up))
    own = stack(own, got)
    other = flipped(own, CORE, CORE)

    own, other = pair_rows(place, own, other, first, up, down, down_shared, share)

    total = [own, flipped(other, CORE, CORE)]
    for phase in reversed(PHASES):
        half = total[0].shape[0] // 2
        sent = f32_sum(*(t[half:] for t in total)).astype(BF16)
        total = [f32_sum(*(t[:half] for t in total)), flipped(sent, *phase)]
    return f32_sum(*total).astype(BF16)


def solution(mesh):
    in_specs = (
        P(("rep", "node", "local"), None),
        P(("rep", "node", "local"), None),
        P(("rep", "node", "local"), None),
        P("node", None, "local"),
        P("node", None, "local"),
        P("node", "local", None),
        P(None, "local"),
        P(None, "local"),
        P("local", None),
    )
    out_specs = P(("rep", "node", "local"), None)
    return jax.shard_map(
        per_device, mesh=mesh, in_specs=in_specs, out_specs=out_specs, check_vma=False
    )
```

```python
import functools

import jax
import jax.numpy as jnp
from jax import lax
from jax.experimental import pallas as pl
from jax.experimental.pallas import tpu as pltpu
from jax.sharding import PartitionSpec as P

LANES = 128
ROW_BLOCK = 128
F32 = jnp.float32
BF16 = jnp.bfloat16
VMEM_SPEC = pl.BlockSpec(memory_space=pltpu.VMEM)
SMEM_SPEC = pl.BlockSpec(memory_space=pltpu.SMEM)
ANY_SPEC = pl.BlockSpec(memory_space=pl.ANY)


def in_hbm(value):
    return pltpu.with_memory_space_constraint(value, pltpu.HBM)


def run_copies(copies):
    for copy in copies:
        copy.start()
    for copy in copies:
        copy.wait()


def after(value, *done):
    return lax.optimization_barrier((value, *done))[0]


def pack_kernel(tokens_ref, groups_ref, weights_ref, packed_ref):
    rows, width = tokens_ref.shape
    packed_ref[:, :width] = tokens_ref[...]
    groups = groups_ref[...].T
    weights = weights_ref[...].astype(F32).T
    lane = lax.broadcasted_iota(jnp.int32, (rows, LANES), 1)
    dense = jnp.zeros((rows, LANES), F32)
    for k in range(groups.shape[1]):
        dense += jnp.where(lane == groups[:, k : k + 1], weights[:, k : k + 1], 0.0)
    packed_ref[:, width:] = dense.astype(BF16)


def pack_rows(tokens, group_ids, route_weights):
    rows, width = tokens.shape
    return pl.pallas_call(
        pack_kernel,
        out_specs=VMEM_SPEC,
        out_shape=pltpu.VMEM((rows, width + LANES), BF16),
        name="pack_rows",
    )(tokens, group_ids.T, route_weights.T)


def load_gate_kernel(share, place_ref, gate_ref, sgate_ref, sup_ref, out_ref, sems):
    width, hidden = gate_ref.shape
    column = pl.multiple_of((place_ref[0] // share) * LANES, LANES)
    parts = 4
    piece = width // parts
    copies = []
    for i in range(parts):
        at = pl.ds(i * piece, piece)
        for source, lower, size in (
            (gate_ref.at[at, :], 0, hidden),
            (sgate_ref.at[at, pl.ds(column, LANES)], hidden, LANES),
            (sup_ref.at[at, pl.ds(column, LANES)], hidden + LANES, LANES),
        ):
            copies.append(
                pltpu.make_async_copy(source, out_ref.at[at, pl.ds(lower, size)], sems.at[len(copies)])
            )
    run_copies(copies)


def load_gate(place, gate, sgate, sup, share):
    width, hidden = gate.shape
    shape = (width, hidden + 2 * LANES)
    return pl.pallas_call(
        functools.partial(load_gate_kernel, share),
        in_specs=[SMEM_SPEC] + [ANY_SPEC] * 3,
        out_specs=VMEM_SPEC,
        out_shape=pltpu.VMEM(shape, BF16),
        scratch_shapes=[pltpu.SemaphoreType.DMA((12,))],
        cost_estimate=pl.CostEstimate(flops=0, bytes_accessed=4 * shape[0] * shape[1], transcendentals=0),
        compiler_params=pltpu.CompilerParams(vmem_limit_bytes=1 << 20),
        name="load_gate",
    )(place, in_hbm(gate), in_hbm(sgate), in_hbm(sup))


def silu(v):
    return v / (1.0 + jnp.exp(-v))


def row_weight(node, dense):
    lane = lax.broadcasted_iota(jnp.int32, dense.shape, 1)
    return jnp.sum(jnp.where(lane == node, dense.astype(F32), 0.0), axis=1, keepdims=True)


DOWN_PARTS = 4
IN_FLIGHT = 3


def up_tile(hidden):
    return min(2 * LANES, hidden)


def stream_scratch(rows, hidden, width):
    copies = hidden // up_tile(hidden) + 2 * DOWN_PARTS
    return [
        pltpu.VMEM((rows, hidden), F32),
        pltpu.VMEM((rows, hidden + LANES), BF16),
        pltpu.VMEM((width, hidden), BF16),
        pltpu.VMEM((hidden + LANES, width), BF16),
        pltpu.SemaphoreType.DMA((copies,)),
    ]


def stream_copies(share, place_ref, up_ref, down_ref, sdown_ref, up, second, sems):
    width, hidden = up_ref.shape
    column = pl.multiple_of((place_ref[0] // share) * LANES, LANES)
    tile, piece = up_tile(hidden), width // DOWN_PARTS
    groups = [[(up_ref.at[:, pl.ds(at, tile)], up.at[:, pl.ds(at, tile)])] for at in range(0, hidden, tile)]
    for i in range(DOWN_PARTS):
        at = pl.ds(i * piece, piece)
        groups.append(
            [
                (down_ref.at[:, at], second.at[pl.ds(0, hidden), at]),
                (sdown_ref.at[pl.ds(column, LANES), at], second.at[pl.ds(hidden, LANES), at]),
            ]
        )
    count = iter(range(sems.shape[0]))
    return [[pltpu.make_async_copy(a, b, sems.at[next(count)]) for a, b in group] for group in groups]


def start_group(groups, i):
    if i < len(groups):
        for copy in groups[i]:
            copy.start()


def wait_group(groups, i):
    for copy in groups[i]:
        copy.wait()


def ffn(share, place_ref, x, first_ref, take, gate, act, up, second, store):
    width, hidden = up.shape
    node = place_ref[0]
    rows = x[:, :width]
    tile, piece = up_tile(hidden), width // DOWN_PARTS
    for at in range(0, hidden, tile):
        gate[:, at : at + tile] = jnp.dot(rows, first_ref[:, at : at + tile], preferred_element_type=F32)
    both = jnp.dot(rows, first_ref[:, hidden:], preferred_element_type=F32)
    shared = silu(both[:, :LANES]) * both[:, LANES:]
    if share > 1:
        lane = lax.broadcasted_iota(jnp.int32, shared.shape, 1)
        shared = jnp.where(lane // (LANES // share) == node % share, shared, 0.0)
    act[:, hidden:] = shared.astype(BF16)
    weight = row_weight(node, x[:, width:])
    tiles = hidden // tile
    for i in range(tiles):
        at = slice(i * tile, (i + 1) * tile)
        take(i)
        value = jnp.dot(rows, up[:, at], preferred_element_type=F32)
        act[:, at] = (silu(gate[:, at]) * value * weight).astype(BF16)
    for i in range(DOWN_PARTS):
        at = slice(i * piece, (i + 1) * piece)
        take(tiles + i)
        store(at, jnp.dot(act[...], second[:, at], preferred_element_type=F32).astype(BF16))


def pair_kernel(
    share, place_ref, own0_ref, own1_ref, other0_ref, other1_ref, first_ref, up_ref, down_ref, sdown_ref,
    own0_out_ref, own1_out_ref, other0_out_ref, other1_out_ref, x, gate, act, up, second, sems,
):
    groups = stream_copies(share, place_ref, up_ref, down_ref, sdown_ref, up, second, sems)
    for i in range(IN_FLIGHT):
        start_group(groups, i)
    half, cut = own0_ref.shape
    x[:half, :cut] = own0_ref[...]
    x[:half, cut:] = own1_ref[...]
    x[half:, :cut] = other0_ref[...]
    x[half:, cut:] = other1_ref[...]

    def take(i):
        wait_group(groups, i)
        start_group(groups, i + IN_FLIGHT)

    def store(at, total):
        own, other = (own0_out_ref, other0_out_ref) if at.stop <= cut else (own1_out_ref, other1_out_ref)
        at = slice(at.start % cut, at.start % cut + at.stop - at.start)
        own[:, at] = total[:half]
        other[:, at] = total[half:]

    ffn(share, place_ref, x, first_ref, take, gate, act, up, second, store)


def pair_rows(place, pieces, first, up, down, sdown, share):
    half, cut = pieces[0].shape
    hidden, width = down.shape
    out = jax.ShapeDtypeStruct((half, cut), BF16)
    return pl.pallas_call(
        functools.partial(pair_kernel, share),
        in_specs=[SMEM_SPEC] + [VMEM_SPEC] * 5 + [ANY_SPEC] * 3,
        out_specs=[VMEM_SPEC] * 4,
        out_shape=[out] * 4,
        scratch_shapes=[pltpu.VMEM((2 * half, width + LANES), BF16)] + stream_scratch(2 * half, hidden, width),
        compiler_params=pltpu.CompilerParams(vmem_limit_bytes=26 << 20),
        name="pair_rows",
    )(place, *pieces, first, in_hbm(up), in_hbm(down), in_hbm(sdown))


def block_kernel(
    share, place_ref, x_ref, first_ref, up_ref, down_ref, sdown_ref, out_ref, gate, act, up, second, sems
):
    groups = stream_copies(share, place_ref, up_ref, down_ref, sdown_ref, up, second, sems)

    @pl.when(pl.program_id(0) == 0)
    def _():
        for i in range(len(groups)):
            start_group(groups, i)
        for i in range(len(groups)):
            wait_group(groups, i)

    def store(at, total):
        out_ref[:, at] = total

    ffn(share, place_ref, x_ref, first_ref, lambda i: None, gate, act, up, second, store)


def block_rows(place, x, first, up, down, sdown, share):
    rows, packed = x.shape
    hidden, width = down.shape
    block = min(rows, ROW_BLOCK)
    return pl.pallas_call(
        functools.partial(block_kernel, share),
        grid=(rows // block,),
        in_specs=[SMEM_SPEC, pl.BlockSpec((block, packed), lambda i: (i, 0)), VMEM_SPEC] + [ANY_SPEC] * 3,
        out_specs=pl.BlockSpec((block, width), lambda i: (i, 0)),
        out_shape=jax.ShapeDtypeStruct((rows, width), BF16),
        scratch_shapes=stream_scratch(block, hidden, width),
        compiler_params=pltpu.CompilerParams(vmem_limit_bytes=26 << 20),
        name="block_rows",
    )(place, x, first, in_hbm(up), in_hbm(down), in_hbm(sdown))


def f32_sum(*terms):
    return functools.reduce(lambda a, b: a + b, (t.astype(F32) for t in terms))


def flipped(value, even, odd):
    pairs = []
    for node in range(4):
        for local in range(4):
            node_bits, local_bits = odd if node % 2 else even
            pairs.append((node * 4 + local, (node ^ node_bits) * 4 + (local ^ local_bits)))
    return lax.ppermute(value, ("node", "local"), pairs)


X, Z1, Z2, CORE = (2, 0), (0, 1), (0, 2), (1, 0)
PHASES = ((Z2, X), (Z1, Z2), (X, Z1))


def stack(*values):
    return jnp.concatenate(values, axis=0)


def per_device(
    tokens,
    group_ids,
    route_weights,
    gate_experts,
    up_experts,
    down_experts,
    gate_shared,
    up_shared,
    down_shared,
):
    rows, width = tokens.shape
    node_count = lax.axis_size("node")
    local_count = lax.axis_size("local")
    share = max(1, LANES * node_count // gate_shared.shape[1])
    place = lax.axis_index("node").reshape(1)
    gate, up, down = gate_experts[0], up_experts[0], down_experts[0]
    packed = pack_rows(tokens, group_ids, route_weights)

    if node_count != 4 or local_count != 4:
        x = lax.all_gather(packed, ("node", "local"), axis=0, tiled=True)
        first = load_gate(place, gate, gate_shared, up_shared, share)
        part = block_rows(place, x, first, up, down, down_shared, share)
        return lax.psum_scatter(part, ("node", "local"), scatter_dimension=0, tiled=True)

    cut = width // 2
    own = [packed[:, :cut], packed[:, cut:]]
    for phase in PHASES[:2]:
        own = [stack(part, flipped(part, *phase)) for part in own]
    got = [flipped(part, *PHASES[2]) for part in own]
    first = load_gate(after(place, *own), gate, gate_shared, up_shared, share)
    got, first = lax.optimization_barrier((got, first))
    own = [stack(part, add) for part, add in zip(own, got)]
    other = [flipped(part, CORE, CORE) for part in own]

    outs = pair_rows(place, own + other, first, up, down, down_shared, share)

    done = []
    for own, other in zip(outs[:2], outs[2:]):
        total = [own, flipped(other, CORE, CORE)]
        for phase in reversed(PHASES):
            half = total[0].shape[0] // 2
            sent = f32_sum(*(t[half:] for t in total)).astype(BF16)
            total = [f32_sum(*(t[:half] for t in total)), flipped(sent, *phase)]
        done.append(f32_sum(*total).astype(BF16))
    return jnp.concatenate(done, axis=1)


def solution(mesh):
    in_specs = (
        P(("rep", "node", "local"), None),
        P(("rep", "node", "local"), None),
        P(("rep", "node", "local"), None),
        P("node", None, "local"),
        P("node", None, "local"),
        P("node", "local", None),
        P(None, "local"),
        P(None, "local"),
        P("local", None),
    )
    out_specs = P(("rep", "node", "local"), None)
    return jax.shard_map(
        per_device, mesh=mesh, in_specs=in_specs, out_specs=out_specs, check_vma=False
    )
```

```python
import functools

import jax
import jax.numpy as jnp
from jax import lax
from jax.experimental import pallas as pl
from jax.experimental.pallas import tpu as pltpu
from jax.sharding import PartitionSpec as P

LANES = 128
ROW_BLOCK = 128
F32 = jnp.float32
BF16 = jnp.bfloat16
VMEM_SPEC = pl.BlockSpec(memory_space=pltpu.VMEM)
SMEM_SPEC = pl.BlockSpec(memory_space=pltpu.SMEM)
ANY_SPEC = pl.BlockSpec(memory_space=pl.ANY)


def in_hbm(value):
    return pltpu.with_memory_space_constraint(value, pltpu.HBM)


def run_copies(copies):
    for copy in copies:
        copy.start()
    for copy in copies:
        copy.wait()


def after(value, *done):
    return lax.optimization_barrier((value, *done))[0]


def pack_kernel(tokens_ref, groups_ref, weights_ref, packed_ref):
    rows, width = tokens_ref.shape
    packed_ref[:, :width] = tokens_ref[...]
    groups = groups_ref[...].T
    weights = weights_ref[...].astype(F32).T
    lane = lax.broadcasted_iota(jnp.int32, (rows, LANES), 1)
    dense = jnp.zeros((rows, LANES), F32)
    for k in range(groups.shape[1]):
        dense += jnp.where(lane == groups[:, k : k + 1], weights[:, k : k + 1], 0.0)
    packed_ref[:, width:] = dense.astype(BF16)


def pack_rows(tokens, group_ids, route_weights):
    rows, width = tokens.shape
    return pl.pallas_call(
        pack_kernel,
        out_specs=VMEM_SPEC,
        out_shape=pltpu.VMEM((rows, width + LANES), BF16),
        name="pack_rows",
    )(tokens, group_ids.T, route_weights.T)


def load_gate_kernel(share, place_ref, gate_ref, sgate_ref, sup_ref, out_ref, sems):
    width, hidden = gate_ref.shape
    column = pl.multiple_of((place_ref[0] // share) * LANES, LANES)
    parts = 4
    piece = width // parts
    copies = []
    for i in range(parts):
        at = pl.ds(i * piece, piece)
        for source, lower, size in (
            (gate_ref.at[at, :], 0, hidden),
            (sgate_ref.at[at, pl.ds(column, LANES)], hidden, LANES),
            (sup_ref.at[at, pl.ds(column, LANES)], hidden + LANES, LANES),
        ):
            copies.append(
                pltpu.make_async_copy(source, out_ref.at[at, pl.ds(lower, size)], sems.at[len(copies)])
            )
    run_copies(copies)


def load_gate(place, gate, sgate, sup, share):
    width, hidden = gate.shape
    shape = (width, hidden + 2 * LANES)
    return pl.pallas_call(
        functools.partial(load_gate_kernel, share),
        in_specs=[SMEM_SPEC] + [ANY_SPEC] * 3,
        out_specs=VMEM_SPEC,
        out_shape=pltpu.VMEM(shape, BF16),
        scratch_shapes=[pltpu.SemaphoreType.DMA((12,))],
        cost_estimate=pl.CostEstimate(flops=0, bytes_accessed=4 * shape[0] * shape[1], transcendentals=0),
        compiler_params=pltpu.CompilerParams(vmem_limit_bytes=1 << 20),
        name="load_gate",
    )(place, in_hbm(gate), in_hbm(sgate), in_hbm(sup))


def load_up_kernel(up_ref, out_ref, sems):
    width = up_ref.shape[0]
    parts = 8
    piece = width // parts
    run_copies(
        [
            pltpu.make_async_copy(
                up_ref.at[pl.ds(i * piece, piece), :], out_ref.at[pl.ds(i * piece, piece), :], sems.at[i]
            )
            for i in range(parts)
        ]
    )


def load_up(up):
    width, hidden = up.shape
    return pl.pallas_call(
        load_up_kernel,
        in_specs=[ANY_SPEC],
        out_specs=VMEM_SPEC,
        out_shape=pltpu.VMEM((width, hidden), BF16),
        scratch_shapes=[pltpu.SemaphoreType.DMA((8,))],
        cost_estimate=pl.CostEstimate(flops=0, bytes_accessed=4 * width * hidden, transcendentals=0),
        compiler_params=pltpu.CompilerParams(vmem_limit_bytes=1 << 20),
        name="load_up",
    )(in_hbm(up))


def silu(v):
    return v / (1.0 + jnp.exp(-v))


def row_weight(node, dense):
    lane = lax.broadcasted_iota(jnp.int32, dense.shape, 1)
    return jnp.sum(jnp.where(lane == node, dense.astype(F32), 0.0), axis=1, keepdims=True)


DOWN_PARTS = 4


def down_scratch(rows, hidden, width):
    return [
        pltpu.VMEM((rows, hidden + LANES), BF16),
        pltpu.VMEM((hidden + LANES, width), BF16),
        pltpu.SemaphoreType.DMA((2 * DOWN_PARTS,)),
    ]


def down_copies(share, place_ref, down_ref, sdown_ref, second, sems):
    hidden, width = down_ref.shape
    column = pl.multiple_of((place_ref[0] // share) * LANES, LANES)
    piece = width // DOWN_PARTS
    groups = []
    for i in range(DOWN_PARTS):
        at = pl.ds(i * piece, piece)
        groups.append(
            [
                pltpu.make_async_copy(down_ref.at[:, at], second.at[pl.ds(0, hidden), at], sems.at[2 * i]),
                pltpu.make_async_copy(
                    sdown_ref.at[pl.ds(column, LANES), at],
                    second.at[pl.ds(hidden, LANES), at],
                    sems.at[2 * i + 1],
                ),
            ]
        )
    return groups


def start_group(groups, i):
    for copy in groups[i]:
        copy.start()


def wait_group(groups, i):
    for copy in groups[i]:
        copy.wait()


def ffn(share, place_ref, x, first_ref, up_ref, act, second, take, store):
    width, hidden = up_ref.shape
    node = place_ref[0]
    rows = x[:, :width]
    weight = row_weight(node, x[:, width:])
    tile, piece = min(2 * LANES, hidden), width // DOWN_PARTS
    for at in range(0, hidden, tile):
        gate = jnp.dot(rows, first_ref[:, at : at + tile], preferred_element_type=F32)
        up = jnp.dot(rows, up_ref[:, at : at + tile], preferred_element_type=F32)
        act[:, at : at + tile] = (silu(gate) * up * weight).astype(BF16)
    both = jnp.dot(rows, first_ref[:, hidden:], preferred_element_type=F32)
    shared = silu(both[:, :LANES]) * both[:, LANES:]
    if share > 1:
        lane = lax.broadcasted_iota(jnp.int32, shared.shape, 1)
        shared = jnp.where(lane // (LANES // share) == node % share, shared, 0.0)
    act[:, hidden:] = shared.astype(BF16)
    for i in range(DOWN_PARTS):
        at = slice(i * piece, (i + 1) * piece)
        take(i)
        store(at, jnp.dot(act[...], second[:, at], preferred_element_type=F32))


def regroup(value, outer, inner):
    rows = value.shape[0] // (outer * inner)
    return jnp.concatenate(
        [
            value[(o * inner + i) * rows : (o * inner + i + 1) * rows]
            for i in range(inner)
            for o in range(outer)
        ],
        axis=0,
    )


def reorder(value, turn):
    value = value.astype(F32)
    return jnp.where(turn == 1, regroup(value, 2, 4), regroup(value, 4, 2)).astype(BF16)


def pair_kernel(
    share, place_ref, own0_ref, own1_ref, other0_ref, other1_ref, first_ref, up_ref, down_ref, sdown_ref,
    own0_out_ref, own1_out_ref, other0_out_ref, other1_out_ref, x, act, second, sems,
):
    groups = down_copies(share, place_ref, down_ref, sdown_ref, second, sems)
    for i in range(DOWN_PARTS):
        start_group(groups, i)
    half, cut = own0_ref.shape
    x[:half, :cut] = own0_ref[...]
    odd = place_ref[0] % 2
    x[:half, cut:] = reorder(own1_ref[...], odd)
    x[half:, :cut] = other0_ref[...]
    x[half:, cut:] = reorder(other1_ref[...], 1 - odd)

    def store(at, total):
        if at.stop <= cut:
            own0_out_ref[:, at] = total[:half].astype(BF16)
            other0_out_ref[:, at] = total[half:].astype(BF16)
        else:
            at = slice(at.start - cut, at.stop - cut)
            own1_out_ref[:, at] = reorder(total[:half], 1 - odd)
            other1_out_ref[:, at] = reorder(total[half:], odd)

    ffn(share, place_ref, x, first_ref, up_ref, act, second, functools.partial(wait_group, groups), store)


def pair_rows(place, pieces, first, up, down, sdown, share):
    half, cut = pieces[0].shape
    hidden, width = down.shape
    out = jax.ShapeDtypeStruct((half, cut), BF16)
    return pl.pallas_call(
        functools.partial(pair_kernel, share),
        in_specs=[SMEM_SPEC] + [VMEM_SPEC] * 6 + [ANY_SPEC] * 2,
        out_specs=[VMEM_SPEC] * 4,
        out_shape=[out] * 4,
        scratch_shapes=[pltpu.VMEM((2 * half, width + LANES), BF16)] + down_scratch(2 * half, hidden, width),
        compiler_params=pltpu.CompilerParams(vmem_limit_bytes=24 << 20),
        name="pair_rows",
    )(place, *pieces, first, up, in_hbm(down), in_hbm(sdown))


def block_kernel(
    share, place_ref, x_ref, first_ref, up_ref, down_ref, sdown_ref, out_ref, act, second, sems
):
    groups = down_copies(share, place_ref, down_ref, sdown_ref, second, sems)

    @pl.when(pl.program_id(0) == 0)
    def _():
        for i in range(DOWN_PARTS):
            start_group(groups, i)
        for i in range(DOWN_PARTS):
            wait_group(groups, i)

    def store(at, total):
        out_ref[:, at] = total.astype(BF16)

    ffn(share, place_ref, x_ref, first_ref, up_ref, act, second, lambda i: None, store)


def block_rows(place, x, first, up, down, sdown, share):
    rows, packed = x.shape
    hidden, width = down.shape
    block = min(rows, ROW_BLOCK)
    return pl.pallas_call(
        functools.partial(block_kernel, share),
        grid=(rows // block,),
        in_specs=[SMEM_SPEC, pl.BlockSpec((block, packed), lambda i: (i, 0))] + [VMEM_SPEC] * 2 + [ANY_SPEC] * 2,
        out_specs=pl.BlockSpec((block, width), lambda i: (i, 0)),
        out_shape=jax.ShapeDtypeStruct((rows, width), BF16),
        scratch_shapes=down_scratch(block, hidden, width),
        compiler_params=pltpu.CompilerParams(vmem_limit_bytes=24 << 20),
        name="block_rows",
    )(place, x, first, up, in_hbm(down), in_hbm(sdown))


def f32_sum(*terms):
    return functools.reduce(lambda a, b: a + b, (t.astype(F32) for t in terms))


def flipped(value, even, odd):
    pairs = []
    for node in range(4):
        for local in range(4):
            node_bits, local_bits = odd if node % 2 else even
            pairs.append((node * 4 + local, (node ^ node_bits) * 4 + (local ^ local_bits)))
    return lax.ppermute(value, ("node", "local"), pairs)


X, Z1, Z2, CORE = (2, 0), (0, 1), (0, 2), (1, 0)
PHASES = ((Z2, X), (Z1, Z2), (X, Z1))


def stack(*values):
    return jnp.concatenate(values, axis=0)


def per_device(
    tokens,
    group_ids,
    route_weights,
    gate_experts,
    up_experts,
    down_experts,
    gate_shared,
    up_shared,
    down_shared,
):
    rows, width = tokens.shape
    node_count = lax.axis_size("node")
    local_count = lax.axis_size("local")
    share = max(1, LANES * node_count // gate_shared.shape[1])
    place = lax.axis_index("node").reshape(1)
    gate, up, down = gate_experts[0], up_experts[0], down_experts[0]
    packed = pack_rows(tokens, group_ids, route_weights)

    if node_count != 4 or local_count != 4:
        x = lax.all_gather(packed, ("node", "local"), axis=0, tiled=True)
        first = load_gate(place, gate, gate_shared, up_shared, share)
        part = block_rows(place, x, first, load_up(up), down, down_shared, share)
        return lax.psum_scatter(part, ("node", "local"), scatter_dimension=0, tiled=True)

    cut = width // 2
    own = [packed[:, :cut], packed[:, cut:]]
    loads = (
        lambda *ready: None,
        lambda *ready: load_up(after(up, *ready)),
        lambda *ready: load_gate(after(place, *ready), gate, gate_shared, up_shared, share),
    )
    loaded = []
    for phase, load in zip(PHASES, loads):
        got = [flipped(part, *pairs) for part, pairs in zip(own, (phase, phase[::-1]))]
        weights = load(*own)
        if weights is not None:
            got, weights = lax.optimization_barrier((got, weights))
            loaded.append(weights)
        own = [stack(part, add) for part, add in zip(own, got)]
    up, first = loaded
    other = [flipped(part, CORE, CORE) for part in own]

    outs = pair_rows(place, own + other, first, up, down, down_shared, share)

    totals = [[own, flipped(other, CORE, CORE)] for own, other in zip(outs[:2], outs[2:])]
    for phase in reversed(PHASES):
        for i, pairs in enumerate((phase, phase[::-1])):
            total = totals[i]
            half = total[0].shape[0] // 2
            sent = f32_sum(*(t[half:] for t in total)).astype(BF16)
            totals[i] = [f32_sum(*(t[:half] for t in total)), flipped(sent, *pairs)]
    return jnp.concatenate([f32_sum(*total).astype(BF16) for total in totals], axis=1)


def solution(mesh):
    in_specs = (
        P(("rep", "node", "local"), None),
        P(("rep", "node", "local"), None),
        P(("rep", "node", "local"), None),
        P("node", None, "local"),
        P("node", None, "local"),
        P("node", "local", None),
        P(None, "local"),
        P(None, "local"),
        P("local", None),
    )
    out_specs = P(("rep", "node", "local"), None)
    return jax.shard_map(
        per_device, mesh=mesh, in_specs=in_specs, out_specs=out_specs, check_vma=False
    )
```

```python
import functools

import jax
import jax.numpy as jnp
from jax import lax
from jax.experimental import pallas as pl
from jax.experimental.pallas import tpu as pltpu
from jax.sharding import PartitionSpec as P

LANES = 128
ROW_BLOCK = 128
F32 = jnp.float32
BF16 = jnp.bfloat16
VMEM_SPEC = pl.BlockSpec(memory_space=pltpu.VMEM)
SMEM_SPEC = pl.BlockSpec(memory_space=pltpu.SMEM)
ANY_SPEC = pl.BlockSpec(memory_space=pl.ANY)


def in_hbm(value):
    return pltpu.with_memory_space_constraint(value, pltpu.HBM)


def run_copies(copies):
    for copy in copies:
        copy.start()
    for copy in copies:
        copy.wait()


def after(value, *done):
    return lax.optimization_barrier((value, *done))[0]


def pack_kernel(tokens_ref, groups_ref, weights_ref, packed_ref):
    rows, width = tokens_ref.shape
    packed_ref[:, :width] = tokens_ref[...]
    groups = groups_ref[...].T
    weights = weights_ref[...].astype(F32).T
    lane = lax.broadcasted_iota(jnp.int32, (rows, LANES), 1)
    dense = jnp.zeros((rows, LANES), F32)
    for k in range(groups.shape[1]):
        dense += jnp.where(lane == groups[:, k : k + 1], weights[:, k : k + 1], 0.0)
    packed_ref[:, width:] = dense.astype(BF16)


def pack_rows(tokens, group_ids, route_weights):
    rows, width = tokens.shape
    return pl.pallas_call(
        pack_kernel,
        out_specs=VMEM_SPEC,
        out_shape=pltpu.VMEM((rows, width + LANES), BF16),
        name="pack_rows",
    )(tokens, group_ids.T, route_weights.T)


def load_gate_kernel(share, place_ref, gate_ref, sgate_ref, sup_ref, out_ref, sems):
    width, hidden = gate_ref.shape
    column = pl.multiple_of((place_ref[0] // share) * LANES, LANES)
    parts = 4
    piece = width // parts
    copies = []
    for i in range(parts):
        at = pl.ds(i * piece, piece)
        for source, lower, size in (
            (gate_ref.at[at, :], 0, hidden),
            (sgate_ref.at[at, pl.ds(column, LANES)], hidden, LANES),
            (sup_ref.at[at, pl.ds(column, LANES)], hidden + LANES, LANES),
        ):
            copies.append(
                pltpu.make_async_copy(source, out_ref.at[at, pl.ds(lower, size)], sems.at[len(copies)])
            )
    run_copies(copies)


def load_gate(place, gate, sgate, sup, share):
    width, hidden = gate.shape
    shape = (width, hidden + 2 * LANES)
    return pl.pallas_call(
        functools.partial(load_gate_kernel, share),
        in_specs=[SMEM_SPEC] + [ANY_SPEC] * 3,
        out_specs=VMEM_SPEC,
        out_shape=pltpu.VMEM(shape, BF16),
        scratch_shapes=[pltpu.SemaphoreType.DMA((12,))],
        cost_estimate=pl.CostEstimate(flops=0, bytes_accessed=4 * shape[0] * shape[1], transcendentals=0),
        compiler_params=pltpu.CompilerParams(vmem_limit_bytes=1 << 20),
        name="load_gate",
    )(place, in_hbm(gate), in_hbm(sgate), in_hbm(sup))


def load_up_kernel(up_ref, out_ref, sems):
    width = up_ref.shape[0]
    parts = 8
    piece = width // parts
    run_copies(
        [
            pltpu.make_async_copy(
                up_ref.at[pl.ds(i * piece, piece), :], out_ref.at[pl.ds(i * piece, piece), :], sems.at[i]
            )
            for i in range(parts)
        ]
    )


def load_up(up):
    width, hidden = up.shape
    return pl.pallas_call(
        load_up_kernel,
        in_specs=[ANY_SPEC],
        out_specs=VMEM_SPEC,
        out_shape=pltpu.VMEM((width, hidden), BF16),
        scratch_shapes=[pltpu.SemaphoreType.DMA((8,))],
        cost_estimate=pl.CostEstimate(flops=0, bytes_accessed=4 * width * hidden, transcendentals=0),
        compiler_params=pltpu.CompilerParams(vmem_limit_bytes=1 << 20),
        name="load_up",
    )(in_hbm(up))


def silu(v):
    return v / (1.0 + jnp.exp(-v))


def row_weight(node, dense):
    lane = lax.broadcasted_iota(jnp.int32, dense.shape, 1)
    return jnp.sum(jnp.where(lane == node, dense.astype(F32), 0.0), axis=1, keepdims=True)


DOWN_PARTS = 4


def down_scratch(rows, hidden, width):
    return [
        pltpu.VMEM((rows, hidden + LANES), BF16),
        pltpu.VMEM((hidden + LANES, width), BF16),
        pltpu.SemaphoreType.DMA((2 * DOWN_PARTS,)),
    ]


def down_copies(share, place_ref, down_ref, sdown_ref, second, sems):
    hidden, width = down_ref.shape
    column = pl.multiple_of((place_ref[0] // share) * LANES, LANES)
    piece = width // DOWN_PARTS
    groups = []
    for i in range(DOWN_PARTS):
        at = pl.ds(i * piece, piece)
        groups.append(
            [
                pltpu.make_async_copy(down_ref.at[:, at], second.at[pl.ds(0, hidden), at], sems.at[2 * i]),
                pltpu.make_async_copy(
                    sdown_ref.at[pl.ds(column, LANES), at],
                    second.at[pl.ds(hidden, LANES), at],
                    sems.at[2 * i + 1],
                ),
            ]
        )
    return groups


def start_group(groups, i):
    for copy in groups[i]:
        copy.start()


def wait_group(groups, i):
    for copy in groups[i]:
        copy.wait()


def ffn(share, place_ref, x, first_ref, up_ref, act, second, take, store):
    width, hidden = up_ref.shape
    node = place_ref[0]
    rows = x[:, :width]
    weight = row_weight(node, x[:, width:])
    tile, piece = min(2 * LANES, hidden), width // DOWN_PARTS
    for at in range(0, hidden, tile):
        gate = jnp.dot(rows, first_ref[:, at : at + tile], preferred_element_type=F32)
        up = jnp.dot(rows, up_ref[:, at : at + tile], preferred_element_type=F32)
        act[:, at : at + tile] = (silu(gate) * up * weight).astype(BF16)
    both = jnp.dot(rows, first_ref[:, hidden:], preferred_element_type=F32)
    shared = silu(both[:, :LANES]) * both[:, LANES:]
    if share > 1:
        lane = lax.broadcasted_iota(jnp.int32, shared.shape, 1)
        shared = jnp.where(lane // (LANES // share) == node % share, shared, 0.0)
    act[:, hidden:] = shared.astype(BF16)
    for i in range(DOWN_PARTS):
        at = slice(i * piece, (i + 1) * piece)
        take(i)
        store(at, jnp.dot(act[...], second[:, at], preferred_element_type=F32))


def regroup(value, outer, inner):
    rows = value.shape[0] // (outer * inner)
    return jnp.concatenate(
        [
            value[(o * inner + i) * rows : (o * inner + i + 1) * rows]
            for i in range(inner)
            for o in range(outer)
        ],
        axis=0,
    )


def reorder(value, turn):
    value = value.astype(F32)
    return jnp.where(turn == 1, regroup(value, 2, 4), regroup(value, 4, 2)).astype(BF16)


def pair_kernel(
    share, place_ref, own0_ref, own1_ref, other0_ref, other1_ref, first_ref, up_ref, down_ref, sdown_ref,
    own0_out_ref, own1_out_ref, other0_out_ref, other1_out_ref, x, act, second, sems,
):
    groups = down_copies(share, place_ref, down_ref, sdown_ref, second, sems)
    for i in range(DOWN_PARTS):
        start_group(groups, i)
    half, cut = own0_ref.shape
    x[:half, :cut] = own0_ref[...]
    odd = place_ref[0] % 2
    x[:half, cut:] = reorder(own1_ref[...], odd)
    x[half:, :cut] = other0_ref[...]
    x[half:, cut:] = reorder(other1_ref[...], 1 - odd)

    def store(at, total):
        if at.stop <= cut:
            own0_out_ref[:, at] = total[:half].astype(BF16)
            other0_out_ref[:, at] = total[half:].astype(BF16)
        else:
            at = slice(at.start - cut, at.stop - cut)
            own1_out_ref[:, at] = reorder(total[:half], 1 - odd)
            other1_out_ref[:, at] = reorder(total[half:], odd)

    ffn(share, place_ref, x, first_ref, up_ref, act, second, functools.partial(wait_group, groups), store)


def pair_rows(place, pieces, first, up, down, sdown, share):
    half, cut = pieces[0].shape
    hidden, width = down.shape
    out = jax.ShapeDtypeStruct((half, cut), BF16)
    return pl.pallas_call(
        functools.partial(pair_kernel, share),
        in_specs=[SMEM_SPEC] + [VMEM_SPEC] * 6 + [ANY_SPEC] * 2,
        out_specs=[VMEM_SPEC] * 4,
        out_shape=[out] * 4,
        scratch_shapes=[pltpu.VMEM((2 * half, width + LANES), BF16)] + down_scratch(2 * half, hidden, width),
        compiler_params=pltpu.CompilerParams(vmem_limit_bytes=24 << 20),
        name="pair_rows",
    )(place, *pieces, first, up, in_hbm(down), in_hbm(sdown))


def block_kernel(
    share, place_ref, x_ref, first_ref, up_ref, down_ref, sdown_ref, out_ref, act, second, sems
):
    groups = down_copies(share, place_ref, down_ref, sdown_ref, second, sems)

    @pl.when(pl.program_id(0) == 0)
    def _():
        for i in range(DOWN_PARTS):
            start_group(groups, i)
        for i in range(DOWN_PARTS):
            wait_group(groups, i)

    def store(at, total):
        out_ref[:, at] = total.astype(BF16)

    ffn(share, place_ref, x_ref, first_ref, up_ref, act, second, lambda i: None, store)


def block_rows(place, x, first, up, down, sdown, share):
    rows, packed = x.shape
    hidden, width = down.shape
    block = min(rows, ROW_BLOCK)
    return pl.pallas_call(
        functools.partial(block_kernel, share),
        grid=(rows // block,),
        in_specs=[SMEM_SPEC, pl.BlockSpec((block, packed), lambda i: (i, 0))] + [VMEM_SPEC] * 2 + [ANY_SPEC] * 2,
        out_specs=pl.BlockSpec((block, width), lambda i: (i, 0)),
        out_shape=jax.ShapeDtypeStruct((rows, width), BF16),
        scratch_shapes=down_scratch(block, hidden, width),
        compiler_params=pltpu.CompilerParams(vmem_limit_bytes=24 << 20),
        name="block_rows",
    )(place, x, first, up, in_hbm(down), in_hbm(sdown))


def f32_sum(*terms):
    return functools.reduce(lambda a, b: a + b, (t.astype(F32) for t in terms))


def flipped(value, even, odd):
    pairs = []
    for node in range(4):
        for local in range(4):
            node_bits, local_bits = odd if node % 2 else even
            pairs.append((node * 4 + local, (node ^ node_bits) * 4 + (local ^ local_bits)))
    return lax.ppermute(value, ("node", "local"), pairs)


X, Z1, Z2, CORE = (2, 0), (0, 1), (0, 2), (1, 0)
PHASES = ((Z2, X), (Z1, Z2), (X, Z1))


def stack(*values):
    return jnp.concatenate(values, axis=0)


def per_device(
    tokens,
    group_ids,
    route_weights,
    gate_experts,
    up_experts,
    down_experts,
    gate_shared,
    up_shared,
    down_shared,
):
    rows, width = tokens.shape
    node_count = lax.axis_size("node")
    local_count = lax.axis_size("local")
    share = max(1, LANES * node_count // gate_shared.shape[1])
    place = lax.axis_index("node").reshape(1)
    gate, up, down = gate_experts[0], up_experts[0], down_experts[0]
    packed = pack_rows(tokens, group_ids, route_weights)

    if node_count != 4 or local_count != 4:
        x = lax.all_gather(packed, ("node", "local"), axis=0, tiled=True)
        first = load_gate(place, gate, gate_shared, up_shared, share)
        part = block_rows(place, x, first, load_up(up), down, down_shared, share)
        return lax.psum_scatter(part, ("node", "local"), scatter_dimension=0, tiled=True)

    cut = width // 2
    own = [packed[:, :cut], packed[:, cut:]]
    loads = (
        lambda *ready: None,
        lambda *ready: load_gate(after(place, *ready), gate, gate_shared, up_shared, share),
        lambda *ready: load_up(after(up, *ready)),
    )
    loaded = []
    for phase, load in zip(PHASES, loads):
        got = [flipped(part, *pairs) for part, pairs in zip(own, (phase, phase[::-1]))]
        weights = load(*own)
        if weights is not None:
            got, weights = lax.optimization_barrier((got, weights))
            loaded.append(weights)
        own = [stack(part, add) for part, add in zip(own, got)]
    first, up = loaded
    other = [flipped(part, CORE, CORE) for part in own]

    outs = pair_rows(place, own + other, first, up, down, down_shared, share)

    totals = [[own, flipped(other, CORE, CORE)] for own, other in zip(outs[:2], outs[2:])]
    for phase in reversed(PHASES):
        for i, pairs in enumerate((phase, phase[::-1])):
            total = totals[i]
            half = total[0].shape[0] // 2
            sent = f32_sum(*(t[half:] for t in total)).astype(BF16)
            totals[i] = [f32_sum(*(t[:half] for t in total)), flipped(sent, *pairs)]
    return jnp.concatenate([f32_sum(*total).astype(BF16) for total in totals], axis=1)


def solution(mesh):
    in_specs = (
        P(("rep", "node", "local"), None),
        P(("rep", "node", "local"), None),
        P(("rep", "node", "local"), None),
        P("node", None, "local"),
        P("node", None, "local"),
        P("node", "local", None),
        P(None, "local"),
        P(None, "local"),
        P("local", None),
    )
    out_specs = P(("rep", "node", "local"), None)
    return jax.shard_map(
        per_device, mesh=mesh, in_specs=in_specs, out_specs=out_specs, check_vma=False
    )
```

```python
import functools

import jax
import jax.numpy as jnp
from jax import lax
from jax.experimental import pallas as pl
from jax.experimental.pallas import tpu as pltpu
from jax.sharding import PartitionSpec as P

LANES = 128
ROW_BLOCK = 128
F32 = jnp.float32
BF16 = jnp.bfloat16
VMEM_SPEC = pl.BlockSpec(memory_space=pltpu.VMEM)
SMEM_SPEC = pl.BlockSpec(memory_space=pltpu.SMEM)
ANY_SPEC = pl.BlockSpec(memory_space=pl.ANY)


def in_hbm(value):
    return pltpu.with_memory_space_constraint(value, pltpu.HBM)


def run_copies(copies):
    for copy in copies:
        copy.start()
    for copy in copies:
        copy.wait()


def after(value, *done):
    return lax.optimization_barrier((value, *done))[0]


def pack_kernel(tokens_ref, groups_ref, weights_ref, packed_ref):
    rows, width = tokens_ref.shape
    packed_ref[:, :width] = tokens_ref[...]
    groups = groups_ref[...].T
    weights = weights_ref[...].astype(F32).T
    lane = lax.broadcasted_iota(jnp.int32, (rows, LANES), 1)
    dense = jnp.zeros((rows, LANES), F32)
    for k in range(groups.shape[1]):
        dense += jnp.where(lane == groups[:, k : k + 1], weights[:, k : k + 1], 0.0)
    packed_ref[:, width:] = dense.astype(BF16)


def pack_rows(tokens, group_ids, route_weights):
    rows, width = tokens.shape
    return pl.pallas_call(
        pack_kernel,
        out_specs=VMEM_SPEC,
        out_shape=pltpu.VMEM((rows, width + LANES), BF16),
        name="pack_rows",
    )(tokens, group_ids.T, route_weights.T)


def load_gate_kernel(share, place_ref, gate_ref, sgate_ref, sup_ref, out_ref, sems):
    width, hidden = gate_ref.shape
    column = pl.multiple_of((place_ref[0] // share) * LANES, LANES)
    parts = 4
    piece = width // parts
    copies = []
    for i in range(parts):
        at = pl.ds(i * piece, piece)
        for source, lower, size in (
            (gate_ref.at[at, :], 0, hidden),
            (sgate_ref.at[at, pl.ds(column, LANES)], hidden, LANES),
            (sup_ref.at[at, pl.ds(column, LANES)], hidden + LANES, LANES),
        ):
            copies.append(
                pltpu.make_async_copy(source, out_ref.at[at, pl.ds(lower, size)], sems.at[len(copies)])
            )
    run_copies(copies)


def load_gate(place, gate, sgate, sup, share):
    width, hidden = gate.shape
    shape = (width, hidden + 2 * LANES)
    return pl.pallas_call(
        functools.partial(load_gate_kernel, share),
        in_specs=[SMEM_SPEC] + [ANY_SPEC] * 3,
        out_specs=VMEM_SPEC,
        out_shape=pltpu.VMEM(shape, BF16),
        scratch_shapes=[pltpu.SemaphoreType.DMA((12,))],
        cost_estimate=pl.CostEstimate(flops=0, bytes_accessed=4 * shape[0] * shape[1], transcendentals=0),
        compiler_params=pltpu.CompilerParams(vmem_limit_bytes=1 << 20),
        name="load_gate",
    )(place, in_hbm(gate), in_hbm(sgate), in_hbm(sup))


def load_up_kernel(up_ref, out_ref, sems):
    width = up_ref.shape[0]
    parts = 8
    piece = width // parts
    run_copies(
        [
            pltpu.make_async_copy(
                up_ref.at[pl.ds(i * piece, piece), :], out_ref.at[pl.ds(i * piece, piece), :], sems.at[i]
            )
            for i in range(parts)
        ]
    )


def load_up(up):
    width, hidden = up.shape
    return pl.pallas_call(
        load_up_kernel,
        in_specs=[ANY_SPEC],
        out_specs=VMEM_SPEC,
        out_shape=pltpu.VMEM((width, hidden), BF16),
        scratch_shapes=[pltpu.SemaphoreType.DMA((8,))],
        cost_estimate=pl.CostEstimate(flops=0, bytes_accessed=4 * width * hidden, transcendentals=0),
        compiler_params=pltpu.CompilerParams(vmem_limit_bytes=1 << 20),
        name="load_up",
    )(in_hbm(up))


def silu(v):
    return v / (1.0 + jnp.exp(-v))


def row_weight(node, dense):
    lane = lax.broadcasted_iota(jnp.int32, dense.shape, 1)
    return jnp.sum(jnp.where(lane == node, dense.astype(F32), 0.0), axis=1, keepdims=True)


DOWN_PARTS = 7


def down_scratch(rows, hidden, width):
    return [
        pltpu.VMEM((rows, hidden + LANES), BF16),
        pltpu.VMEM((hidden + LANES, width), BF16),
        pltpu.SemaphoreType.DMA((2 * DOWN_PARTS,)),
    ]


def down_copies(share, place_ref, down_ref, sdown_ref, second, sems):
    hidden, width = down_ref.shape
    column = pl.multiple_of((place_ref[0] // share) * LANES, LANES)
    piece = width // DOWN_PARTS
    groups = []
    for i in range(DOWN_PARTS):
        at = pl.ds(i * piece, piece)
        groups.append(
            [
                pltpu.make_async_copy(down_ref.at[:, at], second.at[pl.ds(0, hidden), at], sems.at[2 * i]),
                pltpu.make_async_copy(
                    sdown_ref.at[pl.ds(column, LANES), at],
                    second.at[pl.ds(hidden, LANES), at],
                    sems.at[2 * i + 1],
                ),
            ]
        )
    return groups


def start_group(groups, i):
    for copy in groups[i]:
        copy.start()


def wait_group(groups, i):
    for copy in groups[i]:
        copy.wait()


def ffn(share, place_ref, x, first_ref, up_ref, act, second, take, store):
    width, hidden = up_ref.shape
    node = place_ref[0]
    rows = x[:, :width]
    weight = row_weight(node, x[:, width:])
    tile, piece = min(2 * LANES, hidden), width // DOWN_PARTS
    for at in range(0, hidden, tile):
        gate = jnp.dot(rows, first_ref[:, at : at + tile], preferred_element_type=F32)
        up = jnp.dot(rows, up_ref[:, at : at + tile], preferred_element_type=F32)
        act[:, at : at + tile] = (silu(gate) * up * weight).astype(BF16)
    both = jnp.dot(rows, first_ref[:, hidden:], preferred_element_type=F32)
    shared = silu(both[:, :LANES]) * both[:, LANES:]
    if share > 1:
        lane = lax.broadcasted_iota(jnp.int32, shared.shape, 1)
        shared = jnp.where(lane // (LANES // share) == node % share, shared, 0.0)
    act[:, hidden:] = shared.astype(BF16)
    for i in range(DOWN_PARTS):
        at = slice(i * piece, (i + 1) * piece)
        take(i)
        store(at, jnp.dot(act[...], second[:, at], preferred_element_type=F32))


def reorder(value):
    quarter = value.shape[0] // 4
    return jnp.concatenate([value[i * quarter : (i + 1) * quarter] for i in (0, 2, 1, 3)], axis=0)


def pair_kernel(
    share, place_ref, own0_ref, own1_ref, other0_ref, other1_ref, first_ref, up_ref, down_ref, sdown_ref,
    own0_out_ref, own1_out_ref, other0_out_ref, other1_out_ref, x, act, second, sems,
):
    groups = down_copies(share, place_ref, down_ref, sdown_ref, second, sems)
    for i in range(DOWN_PARTS):
        start_group(groups, i)
    half, cut = own0_ref.shape
    x[:half, :cut] = own0_ref[...]
    x[:half, cut:] = reorder(own1_ref[...])
    x[half:, :cut] = other0_ref[...]
    x[half:, cut:] = reorder(other1_ref[...])

    def store(at, total):
        total = total.astype(BF16)
        if at.stop <= cut:
            own0_out_ref[:, at] = total[:half]
            other0_out_ref[:, at] = total[half:]
        else:
            at = slice(at.start - cut, at.stop - cut)
            own1_out_ref[:, at] = reorder(total[:half])
            other1_out_ref[:, at] = reorder(total[half:])

    ffn(share, place_ref, x, first_ref, up_ref, act, second, functools.partial(wait_group, groups), store)


def pair_rows(place, pieces, first, up, down, sdown, share):
    half, cut = pieces[0].shape
    hidden, width = down.shape
    outs = [jax.ShapeDtypeStruct((half, columns), BF16) for columns in (cut, width - cut)] * 2
    return pl.pallas_call(
        functools.partial(pair_kernel, share),
        in_specs=[SMEM_SPEC] + [VMEM_SPEC] * 6 + [ANY_SPEC] * 2,
        out_specs=[VMEM_SPEC] * 4,
        out_shape=outs,
        scratch_shapes=[pltpu.VMEM((2 * half, width + LANES), BF16)] + down_scratch(2 * half, hidden, width),
        compiler_params=pltpu.CompilerParams(vmem_limit_bytes=24 << 20),
        name="pair_rows",
    )(place, *pieces, first, up, in_hbm(down), in_hbm(sdown))


def block_kernel(
    share, place_ref, x_ref, first_ref, up_ref, down_ref, sdown_ref, out_ref, act, second, sems
):
    groups = down_copies(share, place_ref, down_ref, sdown_ref, second, sems)

    @pl.when(pl.program_id(0) == 0)
    def _():
        for i in range(DOWN_PARTS):
            start_group(groups, i)
        for i in range(DOWN_PARTS):
            wait_group(groups, i)

    def store(at, total):
        out_ref[:, at] = total.astype(BF16)

    ffn(share, place_ref, x_ref, first_ref, up_ref, act, second, lambda i: None, store)


def block_rows(place, x, first, up, down, sdown, share):
    rows, packed = x.shape
    hidden, width = down.shape
    block = min(rows, ROW_BLOCK)
    return pl.pallas_call(
        functools.partial(block_kernel, share),
        grid=(rows // block,),
        in_specs=[SMEM_SPEC, pl.BlockSpec((block, packed), lambda i: (i, 0))] + [VMEM_SPEC] * 2 + [ANY_SPEC] * 2,
        out_specs=pl.BlockSpec((block, width), lambda i: (i, 0)),
        out_shape=jax.ShapeDtypeStruct((rows, width), BF16),
        scratch_shapes=down_scratch(block, hidden, width),
        compiler_params=pltpu.CompilerParams(vmem_limit_bytes=24 << 20),
        name="block_rows",
    )(place, x, first, up, in_hbm(down), in_hbm(sdown))


def f32_sum(*terms):
    return functools.reduce(lambda a, b: a + b, (t.astype(F32) for t in terms))


def flipped(value, bits):
    axis = 0 if bits[0] else 1
    return lax.ppermute(value, ("node", "local")[axis], [(i, i ^ bits[axis]) for i in range(4)])


X, Z1, Z2, CORE = (2, 0), (0, 1), (0, 2), (1, 0)
PHASES = ((Z2, Z2), (Z1, X), (X, Z1))


def stack(*values):
    return jnp.concatenate(values, axis=0)


def per_device(
    tokens,
    group_ids,
    route_weights,
    gate_experts,
    up_experts,
    down_experts,
    gate_shared,
    up_shared,
    down_shared,
):
    rows, width = tokens.shape
    node_count = lax.axis_size("node")
    local_count = lax.axis_size("local")
    share = max(1, LANES * node_count // gate_shared.shape[1])
    place = lax.axis_index("node").reshape(1)
    gate, up, down = gate_experts[0], up_experts[0], down_experts[0]
    packed = pack_rows(tokens, group_ids, route_weights)

    if node_count != 4 or local_count != 4:
        x = lax.all_gather(packed, ("node", "local"), axis=0, tiled=True)
        first = load_gate(place, gate, gate_shared, up_shared, share)
        part = block_rows(place, x, first, load_up(up), down, down_shared, share)
        return lax.psum_scatter(part, ("node", "local"), scatter_dimension=0, tiled=True)

    cut = width * 4 // 7 // LANES * LANES
    own = [packed[:, :cut], packed[:, cut:]]
    loads = (
        lambda *ready: None,
        lambda *ready: load_gate(after(place, *ready), gate, gate_shared, up_shared, share),
        lambda *ready: load_up(after(up, *ready)),
    )
    loaded = []
    for phase, load in zip(PHASES, loads):
        got = [flipped(part, pairs) for part, pairs in zip(own, phase)]
        weights = load(*own)
        if weights is not None:
            got, weights = lax.optimization_barrier((got, weights))
            loaded.append(weights)
        own = [stack(part, add) for part, add in zip(own, got)]
    first, up = loaded
    other = [flipped(part, CORE) for part in own]

    outs = pair_rows(place, own + other, first, up, down, down_shared, share)

    totals = [[own, flipped(other, CORE)] for own, other in zip(outs[:2], outs[2:])]
    for phase in reversed(PHASES):
        for i, pairs in enumerate(phase):
            total = totals[i]
            half = total[0].shape[0] // 2
            sent = f32_sum(*(t[half:] for t in total)).astype(BF16)
            totals[i] = [f32_sum(*(t[:half] for t in total)), flipped(sent, pairs)]
    return jnp.concatenate([f32_sum(*total).astype(BF16) for total in totals], axis=1)


def solution(mesh):
    in_specs = (
        P(("rep", "node", "local"), None),
        P(("rep", "node", "local"), None),
        P(("rep", "node", "local"), None),
        P("node", None, "local"),
        P("node", None, "local"),
        P("node", "local", None),
        P(None, "local"),
        P(None, "local"),
        P("local", None),
    )
    out_specs = P(("rep", "node", "local"), None)
    return jax.shard_map(
        per_device, mesh=mesh, in_specs=in_specs, out_specs=out_specs, check_vma=False
    )
```

```python
import functools

import jax
import jax.numpy as jnp
from jax import lax
from jax.experimental import pallas as pl
from jax.experimental.pallas import tpu as pltpu
from jax.sharding import PartitionSpec as P

LANES = 128
ROW_BLOCK = 128
F32 = jnp.float32
BF16 = jnp.bfloat16
VMEM_SPEC = pl.BlockSpec(memory_space=pltpu.VMEM)
SMEM_SPEC = pl.BlockSpec(memory_space=pltpu.SMEM)
ANY_SPEC = pl.BlockSpec(memory_space=pl.ANY)


def in_hbm(value):
    return pltpu.with_memory_space_constraint(value, pltpu.HBM)


def run_copies(copies):
    for copy in copies:
        copy.start()
    for copy in copies:
        copy.wait()


def after(value, *done):
    return lax.optimization_barrier((value, *done))[0]


def pack_kernel(tokens_ref, groups_ref, weights_ref, packed_ref):
    rows, width = tokens_ref.shape
    packed_ref[:, :width] = tokens_ref[...]
    groups = groups_ref[...].T
    weights = weights_ref[...].astype(F32).T
    lane = lax.broadcasted_iota(jnp.int32, (rows, LANES), 1)
    dense = jnp.zeros((rows, LANES), F32)
    for k in range(groups.shape[1]):
        dense += jnp.where(lane == groups[:, k : k + 1], weights[:, k : k + 1], 0.0)
    packed_ref[:, width:] = dense.astype(BF16)


def pack_rows(tokens, group_ids, route_weights):
    rows, width = tokens.shape
    return pl.pallas_call(
        pack_kernel,
        out_specs=VMEM_SPEC,
        out_shape=pltpu.VMEM((rows, width + LANES), BF16),
        name="pack_rows",
    )(tokens, group_ids.T, route_weights.T)


def load_gate_kernel(share, place_ref, gate_ref, sgate_ref, sup_ref, out_ref, sems):
    width, hidden = gate_ref.shape
    column = pl.multiple_of((place_ref[0] // share) * LANES, LANES)
    parts = 4
    piece = width // parts
    copies = []
    for i in range(parts):
        at = pl.ds(i * piece, piece)
        for source, lower, size in (
            (gate_ref.at[at, :], 0, hidden),
            (sgate_ref.at[at, pl.ds(column, LANES)], hidden, LANES),
            (sup_ref.at[at, pl.ds(column, LANES)], hidden + LANES, LANES),
        ):
            copies.append(
                pltpu.make_async_copy(source, out_ref.at[at, pl.ds(lower, size)], sems.at[len(copies)])
            )
    run_copies(copies)


def load_gate(place, gate, sgate, sup, share):
    width, hidden = gate.shape
    shape = (width, hidden + 2 * LANES)
    return pl.pallas_call(
        functools.partial(load_gate_kernel, share),
        in_specs=[SMEM_SPEC] + [ANY_SPEC] * 3,
        out_specs=VMEM_SPEC,
        out_shape=pltpu.VMEM(shape, BF16),
        scratch_shapes=[pltpu.SemaphoreType.DMA((12,))],
        cost_estimate=pl.CostEstimate(flops=0, bytes_accessed=4 * shape[0] * shape[1], transcendentals=0),
        compiler_params=pltpu.CompilerParams(vmem_limit_bytes=1 << 20),
        name="load_gate",
    )(place, in_hbm(gate), in_hbm(sgate), in_hbm(sup))


def load_up_kernel(up_ref, out_ref, sems):
    width = up_ref.shape[0]
    parts = 8
    piece = width // parts
    run_copies(
        [
            pltpu.make_async_copy(
                up_ref.at[pl.ds(i * piece, piece), :], out_ref.at[pl.ds(i * piece, piece), :], sems.at[i]
            )
            for i in range(parts)
        ]
    )


def load_up(up):
    width, hidden = up.shape
    return pl.pallas_call(
        load_up_kernel,
        in_specs=[ANY_SPEC],
        out_specs=VMEM_SPEC,
        out_shape=pltpu.VMEM((width, hidden), BF16),
        scratch_shapes=[pltpu.SemaphoreType.DMA((8,))],
        cost_estimate=pl.CostEstimate(flops=0, bytes_accessed=4 * width * hidden, transcendentals=0),
        compiler_params=pltpu.CompilerParams(vmem_limit_bytes=1 << 20),
        name="load_up",
    )(in_hbm(up))


def silu(v):
    return v / (1.0 + jnp.exp(-v))


def row_weight(node, dense):
    lane = lax.broadcasted_iota(jnp.int32, dense.shape, 1)
    return jnp.sum(jnp.where(lane == node, dense.astype(F32), 0.0), axis=1, keepdims=True)


DOWN_PARTS = 4


def down_scratch(rows, hidden, width):
    return [
        pltpu.VMEM((rows, hidden + LANES), BF16),
        pltpu.VMEM((hidden + LANES, width), BF16),
        pltpu.SemaphoreType.DMA((2 * DOWN_PARTS,)),
    ]


def down_copies(share, place_ref, down_ref, sdown_ref, second, sems):
    hidden, width = down_ref.shape
    column = pl.multiple_of((place_ref[0] // share) * LANES, LANES)
    piece = width // DOWN_PARTS
    groups = []
    for i in range(DOWN_PARTS):
        at = pl.ds(i * piece, piece)
        groups.append(
            [
                pltpu.make_async_copy(down_ref.at[:, at], second.at[pl.ds(0, hidden), at], sems.at[2 * i]),
                pltpu.make_async_copy(
                    sdown_ref.at[pl.ds(column, LANES), at],
                    second.at[pl.ds(hidden, LANES), at],
                    sems.at[2 * i + 1],
                ),
            ]
        )
    return groups


def start_group(groups, i):
    for copy in groups[i]:
        copy.start()


def wait_group(groups, i):
    for copy in groups[i]:
        copy.wait()


def shared_units(share, node, both):
    shared = silu(both[:, :LANES]) * both[:, LANES:]
    if share > 1:
        lane = lax.broadcasted_iota(jnp.int32, shared.shape, 1)
        shared = jnp.where(lane // (LANES // share) == node % share, shared, 0.0)
    return shared.astype(BF16)


def ffn(share, place_ref, x, first_ref, up_ref, act, second, take, store):
    width, hidden = up_ref.shape
    node = place_ref[0]
    rows = x[:, :width]
    weight = row_weight(node, x[:, width:])
    tile, piece = min(2 * LANES, hidden), width // DOWN_PARTS
    for at in range(0, hidden, tile):
        gate = jnp.dot(rows, first_ref[:, at : at + tile], preferred_element_type=F32)
        up = jnp.dot(rows, up_ref[:, at : at + tile], preferred_element_type=F32)
        act[:, at : at + tile] = (silu(gate) * up * weight).astype(BF16)
    both = jnp.dot(rows, first_ref[:, hidden:], preferred_element_type=F32)
    act[:, hidden:] = shared_units(share, node, both)
    for i in range(DOWN_PARTS):
        at = slice(i * piece, (i + 1) * piece)
        take(i)
        store(at, jnp.dot(act[...], second[:, at], preferred_element_type=F32))


def regroup(value, outer, inner):
    rows = value.shape[0] // (outer * inner)
    return jnp.concatenate(
        [
            value[(o * inner + i) * rows : (o * inner + i + 1) * rows]
            for i in range(inner)
            for o in range(outer)
        ],
        axis=0,
    )


def reorder(value, turn):
    value = value.astype(F32)
    return jnp.where(turn == 1, regroup(value, 2, 4), regroup(value, 4, 2)).astype(BF16)


def half_down_copies(share, place_ref, down_ref, sdown_ref, out_ref, lower, sems):
    hidden = down_ref.shape[0]
    column = pl.multiple_of((place_ref[0] // share) * LANES, LANES)
    parts = 2
    piece = out_ref.shape[1] // parts
    copies = []
    for i in range(parts):
        source, target = pl.ds(lower + i * piece, piece), pl.ds(i * piece, piece)
        copies.append(
            pltpu.make_async_copy(
                down_ref.at[:, source], out_ref.at[pl.ds(0, hidden), target], sems.at[2 * i]
            )
        )
        copies.append(
            pltpu.make_async_copy(
                sdown_ref.at[pl.ds(column, LANES), source],
                out_ref.at[pl.ds(hidden, LANES), target],
                sems.at[2 * i + 1],
            )
        )
    return copies


def late_half_kernel(
    share, place_ref, own_ref, other_ref, first_ref, up_ref, down_ref, sdown_ref, acc_ref, second_ref, x, sems
):
    copies = half_down_copies(share, place_ref, down_ref, sdown_ref, second_ref, 0, sems)
    for copy in copies:
        copy.start()
    width, hidden = up_ref.shape
    half, columns = own_ref.shape
    cut = width + LANES - columns
    odd = place_ref[0] % 2
    x[:half, :] = reorder(own_ref[...], odd)
    x[half:, :] = reorder(other_ref[...], 1 - odd)
    rows = x[:, : width - cut]
    acc_ref[:, :hidden] = jnp.dot(rows, first_ref[cut:, :hidden], preferred_element_type=F32)
    acc_ref[:, hidden : 2 * hidden] = jnp.dot(rows, up_ref[cut:, :], preferred_element_type=F32)
    acc_ref[:, 2 * hidden : 2 * hidden + 2 * LANES] = jnp.dot(
        rows, first_ref[cut:, hidden:], preferred_element_type=F32
    )
    weight = row_weight(place_ref[0], x[:, width - cut :])
    acc_ref[:, 2 * hidden + 2 * LANES :] = jnp.broadcast_to(weight, (2 * half, LANES))
    for copy in copies:
        copy.wait()


def early_half_kernel(
    share, place_ref, own_ref, other_ref, first_ref, up_ref, acc_ref, second_ref, down_ref, sdown_ref,
    own_out_ref, other_out_ref, act_ref, later_ref, x, sems,
):
    half, cut = own_ref.shape
    copies = half_down_copies(share, place_ref, down_ref, sdown_ref, later_ref, cut, sems)
    for copy in copies:
        copy.start()
    hidden = up_ref.shape[1]
    x[:half, :] = own_ref[...]
    x[half:, :] = other_ref[...]
    rows = x[...]
    tile = min(2 * LANES, hidden)
    weight = acc_ref[:, 2 * hidden + 2 * LANES :][:, :1]
    for at in range(0, hidden, tile):
        gate = acc_ref[:, at : at + tile] + jnp.dot(
            rows, first_ref[:cut, at : at + tile], preferred_element_type=F32
        )
        up = acc_ref[:, hidden + at : hidden + at + tile] + jnp.dot(
            rows, up_ref[:cut, at : at + tile], preferred_element_type=F32
        )
        act_ref[:, at : at + tile] = (silu(gate) * up * weight).astype(BF16)
    both = acc_ref[:, 2 * hidden : 2 * hidden + 2 * LANES] + jnp.dot(
        rows, first_ref[:cut, hidden:], preferred_element_type=F32
    )
    act_ref[:, hidden:] = shared_units(share, place_ref[0], both)
    piece = cut // 2
    for i in range(2):
        at = slice(i * piece, (i + 1) * piece)
        total = jnp.dot(act_ref[...], second_ref[:, at], preferred_element_type=F32).astype(BF16)
        own_out_ref[:, at] = total[:half]
        other_out_ref[:, at] = total[half:]
    for copy in copies:
        copy.wait()


def last_half_kernel(place_ref, act_ref, second_ref, own_out_ref, other_out_ref):
    half, columns = own_out_ref.shape
    odd = place_ref[0] % 2
    piece = columns // 2
    for i in range(2):
        at = slice(i * piece, (i + 1) * piece)
        total = jnp.dot(act_ref[...], second_ref[:, at], preferred_element_type=F32)
        own_out_ref[:, at] = reorder(total[:half], 1 - odd)
        other_out_ref[:, at] = reorder(total[half:], odd)


def estimate(rows, depth, columns):
    return pl.CostEstimate(
        flops=2 * rows * depth * columns, bytes_accessed=2 * depth * columns, transcendentals=0
    )


def pair_rows(place, own, other, first, up, down, sdown, share):
    half, cut = own[0].shape
    hidden, width = down.shape
    down, sdown = in_hbm(down), in_hbm(sdown)
    units = hidden + LANES
    acc, second = pl.pallas_call(
        functools.partial(late_half_kernel, share),
        in_specs=[SMEM_SPEC] + [VMEM_SPEC] * 4 + [ANY_SPEC] * 2,
        out_specs=[VMEM_SPEC] * 2,
        out_shape=[pltpu.VMEM((2 * half, 2 * units + LANES), F32), pltpu.VMEM((units, cut), BF16)],
        scratch_shapes=[pltpu.VMEM((2 * half, own[1].shape[1]), BF16), pltpu.SemaphoreType.DMA((4,))],
        cost_estimate=estimate(2 * half, width - cut, 2 * units),
        compiler_params=pltpu.CompilerParams(vmem_limit_bytes=10 << 20),
        name="late_half",
    )(place, own[1], other[1], first, up, down, sdown)
    own_out, other_out, act, later = pl.pallas_call(
        functools.partial(early_half_kernel, share),
        in_specs=[SMEM_SPEC] + [VMEM_SPEC] * 6 + [ANY_SPEC] * 2,
        out_specs=[VMEM_SPEC] * 4,
        out_shape=[
            pltpu.VMEM((half, cut), BF16),
            pltpu.VMEM((half, cut), BF16),
            pltpu.VMEM((2 * half, units), BF16),
            pltpu.VMEM((units, width - cut), BF16),
        ],
        scratch_shapes=[pltpu.VMEM((2 * half, cut), BF16), pltpu.SemaphoreType.DMA((4,))],
        cost_estimate=estimate(2 * half, cut, 3 * units),
        compiler_params=pltpu.CompilerParams(vmem_limit_bytes=10 << 20),
        name="early_half",
    )(place, own[0], other[0], first, up, acc, second, down, sdown)
    last = pl.pallas_call(
        last_half_kernel,
        in_specs=[SMEM_SPEC] + [VMEM_SPEC] * 2,
        out_specs=[VMEM_SPEC] * 2,
        out_shape=[pltpu.VMEM((half, width - cut), BF16)] * 2,
        cost_estimate=estimate(2 * half, width - cut, units),
        compiler_params=pltpu.CompilerParams(vmem_limit_bytes=10 << 20),
        name="last_half",
    )(place, act, later)
    return own_out, last[0], other_out, last[1]


def block_kernel(
    share, place_ref, x_ref, first_ref, up_ref, down_ref, sdown_ref, out_ref, act, second, sems
):
    groups = down_copies(share, place_ref, down_ref, sdown_ref, second, sems)

    @pl.when(pl.program_id(0) == 0)
    def _():
        for i in range(DOWN_PARTS):
            start_group(groups, i)
        for i in range(DOWN_PARTS):
            wait_group(groups, i)

    def store(at, total):
        out_ref[:, at] = total.astype(BF16)

    ffn(share, place_ref, x_ref, first_ref, up_ref, act, second, lambda i: None, store)


def block_rows(place, x, first, up, down, sdown, share):
    rows, packed = x.shape
    hidden, width = down.shape
    block = min(rows, ROW_BLOCK)
    return pl.pallas_call(
        functools.partial(block_kernel, share),
        grid=(rows // block,),
        in_specs=[SMEM_SPEC, pl.BlockSpec((block, packed), lambda i: (i, 0))] + [VMEM_SPEC] * 2 + [ANY_SPEC] * 2,
        out_specs=pl.BlockSpec((block, width), lambda i: (i, 0)),
        out_shape=jax.ShapeDtypeStruct((rows, width), BF16),
        scratch_shapes=down_scratch(block, hidden, width),
        compiler_params=pltpu.CompilerParams(vmem_limit_bytes=24 << 20),
        name="block_rows",
    )(place, x, first, up, in_hbm(down), in_hbm(sdown))


def f32_sum(*terms):
    return functools.reduce(lambda a, b: a + b, (t.astype(F32) for t in terms))


def flipped(value, even, odd):
    pairs = []
    for node in range(4):
        for local in range(4):
            node_bits, local_bits = odd if node % 2 else even
            pairs.append((node * 4 + local, (node ^ node_bits) * 4 + (local ^ local_bits)))
    return lax.ppermute(value, ("node", "local"), pairs)


X, Z1, Z2, CORE = (2, 0), (0, 1), (0, 2), (1, 0)
PHASES = ((Z2, X), (Z1, Z2), (X, Z1))


def stack(*values):
    return jnp.concatenate(values, axis=0)


def per_device(
    tokens,
    group_ids,
    route_weights,
    gate_experts,
    up_experts,
    down_experts,
    gate_shared,
    up_shared,
    down_shared,
):
    rows, width = tokens.shape
    node_count = lax.axis_size("node")
    local_count = lax.axis_size("local")
    share = max(1, LANES * node_count // gate_shared.shape[1])
    place = lax.axis_index("node").reshape(1)
    gate, up, down = gate_experts[0], up_experts[0], down_experts[0]
    packed = pack_rows(tokens, group_ids, route_weights)

    if node_count != 4 or local_count != 4:
        x = lax.all_gather(packed, ("node", "local"), axis=0, tiled=True)
        first = load_gate(place, gate, gate_shared, up_shared, share)
        part = block_rows(place, x, first, load_up(up), down, down_shared, share)
        return lax.psum_scatter(part, ("node", "local"), scatter_dimension=0, tiled=True)

    cut = width // 2
    own = [packed[:, :cut], packed[:, cut:]]
    loads = (
        lambda *ready: None,
        lambda *ready: load_gate(after(place, *ready), gate, gate_shared, up_shared, share),
        lambda *ready: load_up(after(up, *ready)),
    )
    loaded = []
    for phase, load in zip(PHASES, loads):
        got = [flipped(part, *pairs) for part, pairs in zip(own, (phase, phase[::-1]))]
        weights = load(*own)
        if weights is not None:
            got, weights = lax.optimization_barrier((got, weights))
            loaded.append(weights)
        own = [stack(part, add) for part, add in zip(own, got)]
    first, up = loaded
    other = [flipped(part, CORE, CORE) for part in own]

    outs = pair_rows(place, own, other, first, up, down, down_shared, share)

    totals = [[own, flipped(other, CORE, CORE)] for own, other in zip(outs[:2], outs[2:])]
    for phase in reversed(PHASES):
        for i, pairs in enumerate((phase, phase[::-1])):
            total = totals[i]
            half = total[0].shape[0] // 2
            sent = f32_sum(*(t[half:] for t in total)).astype(BF16)
            totals[i] = [f32_sum(*(t[:half] for t in total)), flipped(sent, *pairs)]
    return jnp.concatenate([f32_sum(*total).astype(BF16) for total in totals], axis=1)


def solution(mesh):
    in_specs = (
        P(("rep", "node", "local"), None),
        P(("rep", "node", "local"), None),
        P(("rep", "node", "local"), None),
        P("node", None, "local"),
        P("node", None, "local"),
        P("node", "local", None),
        P(None, "local"),
        P(None, "local"),
        P("local", None),
    )
    out_specs = P(("rep", "node", "local"), None)
    return jax.shard_map(
        per_device, mesh=mesh, in_specs=in_specs, out_specs=out_specs, check_vma=False
    )
```

```python
import functools

import jax
import jax.numpy as jnp
from jax import lax
from jax.experimental import pallas as pl
from jax.experimental.pallas import tpu as pltpu
from jax.sharding import PartitionSpec as P

LANES = 128
ROW_BLOCK = 128
F32 = jnp.float32
BF16 = jnp.bfloat16
VMEM_SPEC = pl.BlockSpec(memory_space=pltpu.VMEM)
SMEM_SPEC = pl.BlockSpec(memory_space=pltpu.SMEM)
ANY_SPEC = pl.BlockSpec(memory_space=pl.ANY)


def in_hbm(value):
    return pltpu.with_memory_space_constraint(value, pltpu.HBM)


def run_copies(copies):
    for copy in copies:
        copy.start()
    for copy in copies:
        copy.wait()


def after(value, *done):
    return lax.optimization_barrier((value, *done))[0]


def pack_kernel(tokens_ref, groups_ref, weights_ref, packed_ref):
    rows, width = tokens_ref.shape
    packed_ref[:, :width] = tokens_ref[...]
    groups = groups_ref[...].T
    weights = weights_ref[...].astype(F32).T
    lane = lax.broadcasted_iota(jnp.int32, (rows, LANES), 1)
    dense = jnp.zeros((rows, LANES), F32)
    for k in range(groups.shape[1]):
        dense += jnp.where(lane == groups[:, k : k + 1], weights[:, k : k + 1], 0.0)
    packed_ref[:, width:] = dense.astype(BF16)


def pack_rows(tokens, group_ids, route_weights):
    rows, width = tokens.shape
    return pl.pallas_call(
        pack_kernel,
        out_specs=VMEM_SPEC,
        out_shape=pltpu.VMEM((rows, width + LANES), BF16),
        name="pack_rows",
    )(tokens, group_ids.T, route_weights.T)


def load_gate_kernel(share, place_ref, gate_ref, sgate_ref, sup_ref, out_ref, sems):
    width, hidden = gate_ref.shape
    column = pl.multiple_of((place_ref[0] // share) * LANES, LANES)
    parts = 4
    piece = width // parts
    copies = []
    for i in range(parts):
        at = pl.ds(i * piece, piece)
        for source, lower, size in (
            (gate_ref.at[at, :], 0, hidden),
            (sgate_ref.at[at, pl.ds(column, LANES)], hidden, LANES),
            (sup_ref.at[at, pl.ds(column, LANES)], hidden + LANES, LANES),
        ):
            copies.append(
                pltpu.make_async_copy(source, out_ref.at[at, pl.ds(lower, size)], sems.at[len(copies)])
            )
    run_copies(copies)


def load_gate(place, gate, sgate, sup, share):
    width, hidden = gate.shape
    shape = (width, hidden + 2 * LANES)
    return pl.pallas_call(
        functools.partial(load_gate_kernel, share),
        in_specs=[SMEM_SPEC] + [ANY_SPEC] * 3,
        out_specs=VMEM_SPEC,
        out_shape=pltpu.VMEM(shape, BF16),
        scratch_shapes=[pltpu.SemaphoreType.DMA((12,))],
        cost_estimate=pl.CostEstimate(flops=0, bytes_accessed=4 * shape[0] * shape[1], transcendentals=0),
        compiler_params=pltpu.CompilerParams(vmem_limit_bytes=1 << 20),
        name="load_gate",
    )(place, in_hbm(gate), in_hbm(sgate), in_hbm(sup))


def load_up_kernel(up_ref, out_ref, sems):
    width = up_ref.shape[0]
    parts = 8
    piece = width // parts
    run_copies(
        [
            pltpu.make_async_copy(
                up_ref.at[pl.ds(i * piece, piece), :], out_ref.at[pl.ds(i * piece, piece), :], sems.at[i]
            )
            for i in range(parts)
        ]
    )


def load_up(up):
    width, hidden = up.shape
    return pl.pallas_call(
        load_up_kernel,
        in_specs=[ANY_SPEC],
        out_specs=VMEM_SPEC,
        out_shape=pltpu.VMEM((width, hidden), BF16),
        scratch_shapes=[pltpu.SemaphoreType.DMA((8,))],
        cost_estimate=pl.CostEstimate(flops=0, bytes_accessed=4 * width * hidden, transcendentals=0),
        compiler_params=pltpu.CompilerParams(vmem_limit_bytes=1 << 20),
        name="load_up",
    )(in_hbm(up))


def silu(v):
    return v / (1.0 + jnp.exp(-v))


def row_weight(node, dense):
    lane = lax.broadcasted_iota(jnp.int32, dense.shape, 1)
    return jnp.sum(jnp.where(lane == node, dense.astype(F32), 0.0), axis=1, keepdims=True)


DOWN_PARTS = 4


def down_scratch(rows, hidden, width):
    return [
        pltpu.VMEM((rows, hidden + LANES), BF16),
        pltpu.VMEM((hidden + LANES, width), BF16),
        pltpu.SemaphoreType.DMA((2 * DOWN_PARTS,)),
    ]


def down_copies(share, place_ref, down_ref, sdown_ref, second, sems):
    hidden, width = down_ref.shape
    column = pl.multiple_of((place_ref[0] // share) * LANES, LANES)
    piece = width // DOWN_PARTS
    groups = []
    for i in range(DOWN_PARTS):
        at = pl.ds(i * piece, piece)
        groups.append(
            [
                pltpu.make_async_copy(down_ref.at[:, at], second.at[pl.ds(0, hidden), at], sems.at[2 * i]),
                pltpu.make_async_copy(
                    sdown_ref.at[pl.ds(column, LANES), at],
                    second.at[pl.ds(hidden, LANES), at],
                    sems.at[2 * i + 1],
                ),
            ]
        )
    return groups


def start_group(groups, i):
    for copy in groups[i]:
        copy.start()


def wait_group(groups, i):
    for copy in groups[i]:
        copy.wait()


def shared_units(share, node, both):
    shared = silu(both[:, :LANES]) * both[:, LANES:]
    if share > 1:
        lane = lax.broadcasted_iota(jnp.int32, shared.shape, 1)
        shared = jnp.where(lane // (LANES // share) == node % share, shared, 0.0)
    return shared.astype(BF16)


def ffn(share, place_ref, x, first_ref, up_ref, act, second, take, store):
    width, hidden = up_ref.shape
    node = place_ref[0]
    rows = x[:, :width]
    weight = row_weight(node, x[:, width:])
    tile, piece = min(2 * LANES, hidden), width // DOWN_PARTS
    for at in range(0, hidden, tile):
        gate = jnp.dot(rows, first_ref[:, at : at + tile], preferred_element_type=F32)
        up = jnp.dot(rows, up_ref[:, at : at + tile], preferred_element_type=F32)
        act[:, at : at + tile] = (silu(gate) * up * weight).astype(BF16)
    both = jnp.dot(rows, first_ref[:, hidden:], preferred_element_type=F32)
    act[:, hidden:] = shared_units(share, node, both)
    for i in range(DOWN_PARTS):
        at = slice(i * piece, (i + 1) * piece)
        take(i)
        store(at, jnp.dot(act[...], second[:, at], preferred_element_type=F32))


def regroup(value, outer, inner):
    rows = value.shape[0] // (outer * inner)
    return jnp.concatenate(
        [
            value[(o * inner + i) * rows : (o * inner + i + 1) * rows]
            for i in range(inner)
            for o in range(outer)
        ],
        axis=0,
    )


def swap_quarters(value):
    quarter = value.shape[0] // 4
    return jnp.concatenate([value[i * quarter : (i + 1) * quarter] for i in (0, 2, 1, 3)], axis=0)


def half_down_copies(share, place_ref, down_ref, sdown_ref, out_ref, lower, sems):
    hidden = down_ref.shape[0]
    column = pl.multiple_of((place_ref[0] // share) * LANES, LANES)
    parts = 2
    piece = out_ref.shape[1] // parts
    copies = []
    for i in range(parts):
        source, target = pl.ds(lower + i * piece, piece), pl.ds(i * piece, piece)
        copies.append(
            pltpu.make_async_copy(
                down_ref.at[:, source], out_ref.at[pl.ds(0, hidden), target], sems.at[2 * i]
            )
        )
        copies.append(
            pltpu.make_async_copy(
                sdown_ref.at[pl.ds(column, LANES), source],
                out_ref.at[pl.ds(hidden, LANES), target],
                sems.at[2 * i + 1],
            )
        )
    return copies


def load_down_kernel(share, place_ref, down_ref, sdown_ref, out_ref, sems):
    run_copies(half_down_copies(share, place_ref, down_ref, sdown_ref, out_ref, 0, sems))


def load_down(place, down, sdown, cut, share):
    units = down.shape[0] + LANES
    return pl.pallas_call(
        functools.partial(load_down_kernel, share),
        in_specs=[SMEM_SPEC] + [ANY_SPEC] * 2,
        out_specs=VMEM_SPEC,
        out_shape=pltpu.VMEM((units, cut), BF16),
        scratch_shapes=[pltpu.SemaphoreType.DMA((4,))],
        cost_estimate=pl.CostEstimate(flops=0, bytes_accessed=4 * units * cut, transcendentals=0),
        compiler_params=pltpu.CompilerParams(vmem_limit_bytes=1 << 20),
        name="load_down",
    )(place, in_hbm(down), in_hbm(sdown))


def late_half_kernel(
    share, place_ref, own_ref, other_ref, first_ref, up_ref, down_ref, sdown_ref, acc_ref, later_ref, x, sems
):
    width, hidden = up_ref.shape
    half, columns = own_ref.shape
    cut = width + LANES - columns
    copies = half_down_copies(share, place_ref, down_ref, sdown_ref, later_ref, cut, sems)
    for copy in copies:
        copy.start()
    x[:half, :] = own_ref[...]
    x[half:, :] = other_ref[...]
    rows = x[:, : width - cut]
    tile = min(2 * LANES, hidden)
    for at in range(0, hidden, tile):
        acc_ref[:, at : at + tile] = jnp.dot(rows, first_ref[cut:, at : at + tile], preferred_element_type=F32)
        acc_ref[:, hidden + at : hidden + at + tile] = jnp.dot(
            rows, up_ref[cut:, at : at + tile], preferred_element_type=F32
        )
    acc_ref[:, 2 * hidden : 2 * hidden + 2 * LANES] = jnp.dot(
        rows, first_ref[cut:, hidden:], preferred_element_type=F32
    )
    weight = row_weight(place_ref[0], x[:, width - cut :])
    acc_ref[:, 2 * hidden + 2 * LANES :] = jnp.broadcast_to(weight, (2 * half, LANES))
    for copy in copies:
        copy.wait()


def early_half_kernel(
    share, place_ref, own_ref, other_ref, first_ref, up_ref, acc_ref, second_ref,
    own_out_ref, other_out_ref, act_ref, x,
):
    half, cut = own_ref.shape
    hidden = up_ref.shape[1]
    x[:half, :] = own_ref[...]
    x[half:, :] = other_ref[...]
    rows = x[...]
    tile = min(2 * LANES, hidden)
    weight = acc_ref[:, 2 * hidden + 2 * LANES :][:, :1]
    for at in range(0, hidden, tile):
        gate = acc_ref[:, at : at + tile] + jnp.dot(
            rows, first_ref[:cut, at : at + tile], preferred_element_type=F32
        )
        up = acc_ref[:, hidden + at : hidden + at + tile] + jnp.dot(
            rows, up_ref[:cut, at : at + tile], preferred_element_type=F32
        )
        act_ref[:, at : at + tile] = (silu(gate) * up * weight).astype(BF16)
    both = acc_ref[:, 2 * hidden : 2 * hidden + 2 * LANES] + jnp.dot(
        rows, first_ref[:cut, hidden:], preferred_element_type=F32
    )
    act_ref[:, hidden:] = shared_units(share, place_ref[0], both)
    piece = cut // 2
    for i in range(2):
        at = slice(i * piece, (i + 1) * piece)
        total = jnp.dot(act_ref[...], second_ref[:, at], preferred_element_type=F32).astype(BF16)
        own_out_ref[:, at] = total[:half]
        other_out_ref[:, at] = total[half:]


def last_half_kernel(act_ref, second_ref, own_out_ref, other_out_ref):
    half, columns = own_out_ref.shape
    piece = columns // 2
    for i in range(2):
        at = slice(i * piece, (i + 1) * piece)
        total = jnp.dot(act_ref[...], second_ref[:, at], preferred_element_type=F32).astype(BF16)
        own_out_ref[:, at] = swap_quarters(total[:half])
        other_out_ref[:, at] = swap_quarters(total[half:])


def estimate(rows, depth, columns):
    return pl.CostEstimate(
        flops=2 * rows * depth * columns, bytes_accessed=2 * depth * columns, transcendentals=0
    )


def pair_rows(place, own, other, first, up, second, down, sdown, share):
    half, cut = own[0].shape
    hidden, width = down.shape
    units = hidden + LANES
    acc, later = pl.pallas_call(
        functools.partial(late_half_kernel, share),
        in_specs=[SMEM_SPEC] + [VMEM_SPEC] * 4 + [ANY_SPEC] * 2,
        out_specs=[VMEM_SPEC] * 2,
        out_shape=[pltpu.VMEM((2 * half, 2 * units + LANES), F32), pltpu.VMEM((units, width - cut), BF16)],
        scratch_shapes=[pltpu.VMEM((2 * half, own[1].shape[1]), BF16), pltpu.SemaphoreType.DMA((4,))],
        cost_estimate=estimate(2 * half, width - cut, 2 * units),
        compiler_params=pltpu.CompilerParams(vmem_limit_bytes=10 << 20),
        name="late_half",
    )(place, own[1], other[1], first, up, in_hbm(down), in_hbm(sdown))
    own_out, other_out, act = pl.pallas_call(
        functools.partial(early_half_kernel, share),
        in_specs=[SMEM_SPEC] + [VMEM_SPEC] * 6,
        out_specs=[VMEM_SPEC] * 3,
        out_shape=[
            pltpu.VMEM((half, cut), BF16),
            pltpu.VMEM((half, cut), BF16),
            pltpu.VMEM((2 * half, units), BF16),
        ],
        scratch_shapes=[pltpu.VMEM((2 * half, cut), BF16)],
        cost_estimate=estimate(2 * half, cut, 3 * units),
        compiler_params=pltpu.CompilerParams(vmem_limit_bytes=10 << 20),
        name="early_half",
    )(place, own[0], other[0], first, up, acc, second)
    last = pl.pallas_call(
        last_half_kernel,
        in_specs=[VMEM_SPEC] * 2,
        out_specs=[VMEM_SPEC] * 2,
        out_shape=[pltpu.VMEM((half, width - cut), BF16)] * 2,
        cost_estimate=estimate(2 * half, width - cut, units),
        compiler_params=pltpu.CompilerParams(vmem_limit_bytes=10 << 20),
        name="last_half",
    )(act, later)
    return own_out, last[0], other_out, last[1]


def block_kernel(
    share, place_ref, x_ref, first_ref, up_ref, down_ref, sdown_ref, out_ref, act, second, sems
):
    groups = down_copies(share, place_ref, down_ref, sdown_ref, second, sems)

    @pl.when(pl.program_id(0) == 0)
    def _():
        for i in range(DOWN_PARTS):
            start_group(groups, i)
        for i in range(DOWN_PARTS):
            wait_group(groups, i)

    def store(at, total):
        out_ref[:, at] = total.astype(BF16)

    ffn(share, place_ref, x_ref, first_ref, up_ref, act, second, lambda i: None, store)


def block_rows(place, x, first, up, down, sdown, share):
    rows, packed = x.shape
    hidden, width = down.shape
    block = min(rows, ROW_BLOCK)
    return pl.pallas_call(
        functools.partial(block_kernel, share),
        grid=(rows // block,),
        in_specs=[SMEM_SPEC, pl.BlockSpec((block, packed), lambda i: (i, 0))] + [VMEM_SPEC] * 2 + [ANY_SPEC] * 2,
        out_specs=pl.BlockSpec((block, width), lambda i: (i, 0)),
        out_shape=jax.ShapeDtypeStruct((rows, width), BF16),
        scratch_shapes=down_scratch(block, hidden, width),
        compiler_params=pltpu.CompilerParams(vmem_limit_bytes=24 << 20),
        name="block_rows",
    )(place, x, first, up, in_hbm(down), in_hbm(sdown))


def f32_sum(*terms):
    return functools.reduce(lambda a, b: a + b, (t.astype(F32) for t in terms))


def flipped(value, even, odd):
    pairs = []
    for node in range(4):
        for local in range(4):
            node_bits, local_bits = odd if node % 2 else even
            pairs.append((node * 4 + local, (node ^ node_bits) * 4 + (local ^ local_bits)))
    return lax.ppermute(value, ("node", "local"), pairs)


X, Z1, Z2, CORE = (2, 0), (0, 1), (0, 2), (1, 0)
GATHER = ((Z2, X), (Z1, Z2), (X, Z1))
SCATTER = ((X, Z1), (Z1, X), (Z2, Z2))


def stack(*values):
    return jnp.concatenate(values, axis=0)


def per_device(
    tokens,
    group_ids,
    route_weights,
    gate_experts,
    up_experts,
    down_experts,
    gate_shared,
    up_shared,
    down_shared,
):
    rows, width = tokens.shape
    node_count = lax.axis_size("node")
    local_count = lax.axis_size("local")
    share = max(1, LANES * node_count // gate_shared.shape[1])
    place = lax.axis_index("node").reshape(1)
    gate, up, down = gate_experts[0], up_experts[0], down_experts[0]
    packed = pack_rows(tokens, group_ids, route_weights)

    if node_count != 4 or local_count != 4:
        x = lax.all_gather(packed, ("node", "local"), axis=0, tiled=True)
        first = load_gate(place, gate, gate_shared, up_shared, share)
        part = block_rows(place, x, first, load_up(up), down, down_shared, share)
        return lax.psum_scatter(part, ("node", "local"), scatter_dimension=0, tiled=True)

    cut = width // 2
    own = [packed[:, :cut], packed[:, cut:]]
    loads = (
        lambda *ready: load_down(after(place, *ready), down, down_shared, cut, share),
        lambda *ready: load_gate(after(place, *ready), gate, gate_shared, up_shared, share),
        lambda *ready: load_up(after(up, *ready)),
    )
    loaded = []
    for phase, load in zip(GATHER, loads):
        got = [flipped(part, *pairs) for part, pairs in zip(own, (phase, phase[::-1]))]
        got[0], weights = lax.optimization_barrier((got[0], load(*own)))
        loaded.append(weights)
        own = [stack(part, add) for part, add in zip(own, got)]
    second, first, up = loaded
    odd = place[0] % 2
    own = [jnp.where(odd == i, part, regroup(part, 4, 2)) for i, part in enumerate(own)]
    other = [flipped(part, CORE, CORE) for part in own]

    outs = pair_rows(place, own, other, first, up, second, down, down_shared, share)

    totals = [[own, flipped(other, CORE, CORE)] for own, other in zip(outs[:2], outs[2:])]
    for phase in SCATTER:
        for i, bits in enumerate(phase):
            total = totals[i]
            half = total[0].shape[0] // 2
            sent = f32_sum(*(t[half:] for t in total)).astype(BF16)
            totals[i] = [f32_sum(*(t[:half] for t in total)), flipped(sent, bits, bits)]
    return jnp.concatenate([f32_sum(*total).astype(BF16) for total in totals], axis=1)


def solution(mesh):
    in_specs = (
        P(("rep", "node", "local"), None),
        P(("rep", "node", "local"), None),
        P(("rep", "node", "local"), None),
        P("node", None, "local"),
        P("node", None, "local"),
        P("node", "local", None),
        P(None, "local"),
        P(None, "local"),
        P("local", None),
    )
    out_specs = P(("rep", "node", "local"), None)
    return jax.shard_map(
        per_device, mesh=mesh, in_specs=in_specs, out_specs=out_specs, check_vma=False
    )
```

```python
import functools

import jax
import jax.numpy as jnp
from jax import lax
from jax.experimental import pallas as pl
from jax.experimental.pallas import tpu as pltpu
from jax.sharding import PartitionSpec as P

LANES = 128
ROW_BLOCK = 128
F32 = jnp.float32
BF16 = jnp.bfloat16
VMEM_SPEC = pl.BlockSpec(memory_space=pltpu.VMEM)
SMEM_SPEC = pl.BlockSpec(memory_space=pltpu.SMEM)
ANY_SPEC = pl.BlockSpec(memory_space=pl.ANY)


def in_hbm(value):
    return pltpu.with_memory_space_constraint(value, pltpu.HBM)


def run_copies(copies):
    for copy in copies:
        copy.start()
    for copy in copies:
        copy.wait()


def after(value, *done):
    return lax.optimization_barrier((value, *done))[0]


def pack_kernel(tokens_ref, groups_ref, weights_ref, packed_ref):
    rows, width = tokens_ref.shape
    packed_ref[:, :width] = tokens_ref[...]
    groups = groups_ref[...].T
    weights = weights_ref[...].astype(F32).T
    lane = lax.broadcasted_iota(jnp.int32, (rows, LANES), 1)
    dense = jnp.zeros((rows, LANES), F32)
    for k in range(groups.shape[1]):
        dense += jnp.where(lane == groups[:, k : k + 1], weights[:, k : k + 1], 0.0)
    packed_ref[:, width:] = dense.astype(BF16)


def pack_rows(tokens, group_ids, route_weights):
    rows, width = tokens.shape
    return pl.pallas_call(
        pack_kernel,
        out_specs=VMEM_SPEC,
        out_shape=pltpu.VMEM((rows, width + LANES), BF16),
        name="pack_rows",
    )(tokens, group_ids.T, route_weights.T)


def load_kernel(share, place_ref, routed_ref, shared_ref, out_ref, sems):
    width, hidden = routed_ref.shape
    column = pl.multiple_of((place_ref[0] // share) * LANES, LANES)
    parts = sems.shape[0] // 2
    piece = width // parts
    copies = []
    for i in range(parts):
        at = pl.ds(i * piece, piece)
        for source, lower, size in (
            (routed_ref.at[at, :], 0, hidden),
            (shared_ref.at[at, pl.ds(column, LANES)], hidden, LANES),
        ):
            copies.append(
                pltpu.make_async_copy(source, out_ref.at[at, pl.ds(lower, size)], sems.at[len(copies)])
            )
    run_copies(copies)


def load_weights(place, routed, shared, share):
    width, hidden = routed.shape
    shape = (width, hidden + LANES)
    return pl.pallas_call(
        functools.partial(load_kernel, share),
        in_specs=[SMEM_SPEC] + [ANY_SPEC] * 2,
        out_specs=VMEM_SPEC,
        out_shape=pltpu.VMEM(shape, BF16),
        scratch_shapes=[pltpu.SemaphoreType.DMA((8,))],
        cost_estimate=pl.CostEstimate(flops=0, bytes_accessed=4 * shape[0] * shape[1], transcendentals=0),
        compiler_params=pltpu.CompilerParams(vmem_limit_bytes=1 << 20),
        name="load_weights",
    )(place, in_hbm(routed), in_hbm(shared))


def silu(v):
    return v / (1.0 + jnp.exp(-v))


def row_weight(node, dense):
    lane = lax.broadcasted_iota(jnp.int32, dense.shape, 1)
    return jnp.sum(jnp.where(lane == node, dense.astype(F32), 0.0), axis=1, keepdims=True)


DOWN_PARTS = 4


def down_scratch(rows, hidden, width):
    return [
        pltpu.VMEM((rows, hidden + LANES), BF16),
        pltpu.VMEM((hidden + LANES, width), BF16),
        pltpu.SemaphoreType.DMA((2 * DOWN_PARTS,)),
    ]


def down_copies(share, place_ref, down_ref, sdown_ref, second, sems):
    hidden, width = down_ref.shape
    column = pl.multiple_of((place_ref[0] // share) * LANES, LANES)
    piece = width // DOWN_PARTS
    groups = []
    for i in range(DOWN_PARTS):
        at = pl.ds(i * piece, piece)
        groups.append(
            [
                pltpu.make_async_copy(down_ref.at[:, at], second.at[pl.ds(0, hidden), at], sems.at[2 * i]),
                pltpu.make_async_copy(
                    sdown_ref.at[pl.ds(column, LANES), at],
                    second.at[pl.ds(hidden, LANES), at],
                    sems.at[2 * i + 1],
                ),
            ]
        )
    return groups


def start_group(groups, i):
    for copy in groups[i]:
        copy.start()


def wait_group(groups, i):
    for copy in groups[i]:
        copy.wait()


def shared_units(share, node, gate, up):
    shared = silu(gate) * up
    if share > 1:
        lane = lax.broadcasted_iota(jnp.int32, shared.shape, 1)
        shared = jnp.where(lane // (LANES // share) == node % share, shared, 0.0)
    return shared.astype(BF16)


def tiles_of(units):
    tile = 2 * LANES
    return [slice(at, min(at + tile, units)) for at in range(0, units, tile)]


def ffn(share, place_ref, x, gate_ref, up_ref, act, second, take, store):
    width, units = gate_ref.shape
    hidden = units - LANES
    node = place_ref[0]
    rows = x[:, :width]
    weight = row_weight(node, x[:, width:])
    gate = jnp.dot(rows, gate_ref[...], preferred_element_type=F32)
    up = jnp.dot(rows, up_ref[...], preferred_element_type=F32)
    act[:, :hidden] = (silu(gate[:, :hidden]) * up[:, :hidden] * weight).astype(BF16)
    act[:, hidden:] = shared_units(share, node, gate[:, hidden:], up[:, hidden:])
    piece = width // DOWN_PARTS
    for i in range(DOWN_PARTS):
        at = slice(i * piece, (i + 1) * piece)
        take(i)
        store(at, jnp.dot(act[...], second[:, at], preferred_element_type=F32))


def regroup(value, outer, inner):
    rows = value.shape[0] // (outer * inner)
    return jnp.concatenate(
        [
            value[(o * inner + i) * rows : (o * inner + i + 1) * rows]
            for i in range(inner)
            for o in range(outer)
        ],
        axis=0,
    )


def swap_quarters(value):
    quarter = value.shape[0] // 4
    return jnp.concatenate([value[i * quarter : (i + 1) * quarter] for i in (0, 2, 1, 3)], axis=0)


def half_down_copies(share, place_ref, down_ref, sdown_ref, out_ref, lower, sems):
    hidden = down_ref.shape[0]
    column = pl.multiple_of((place_ref[0] // share) * LANES, LANES)
    parts = 2
    piece = out_ref.shape[1] // parts
    copies = []
    for i in range(parts):
        source, target = pl.ds(lower + i * piece, piece), pl.ds(i * piece, piece)
        copies.append(
            pltpu.make_async_copy(
                down_ref.at[:, source], out_ref.at[pl.ds(0, hidden), target], sems.at[2 * i]
            )
        )
        copies.append(
            pltpu.make_async_copy(
                sdown_ref.at[pl.ds(column, LANES), source],
                out_ref.at[pl.ds(hidden, LANES), target],
                sems.at[2 * i + 1],
            )
        )
    return copies


def load_down_kernel(share, place_ref, down_ref, sdown_ref, out_ref, sems):
    run_copies(half_down_copies(share, place_ref, down_ref, sdown_ref, out_ref, 0, sems))


def load_down(place, down, sdown, cut, share):
    units = down.shape[0] + LANES
    return pl.pallas_call(
        functools.partial(load_down_kernel, share),
        in_specs=[SMEM_SPEC] + [ANY_SPEC] * 2,
        out_specs=VMEM_SPEC,
        out_shape=pltpu.VMEM((units, cut), BF16),
        scratch_shapes=[pltpu.SemaphoreType.DMA((4,))],
        cost_estimate=pl.CostEstimate(flops=0, bytes_accessed=4 * units * cut, transcendentals=0),
        compiler_params=pltpu.CompilerParams(vmem_limit_bytes=1 << 20),
        name="load_down",
    )(place, in_hbm(down), in_hbm(sdown))


def late_half_kernel(place_ref, own_ref, other_ref, gate_ref, up_ref, gate_acc_ref, up_acc_ref, weight_ref, x):
    width, units = gate_ref.shape
    half, columns = own_ref.shape
    cut = width + LANES - columns
    x[:half, :] = own_ref[...]
    x[half:, :] = other_ref[...]
    rows = x[:, : width - cut]
    for at in tiles_of(units):
        gate_acc_ref[:, at] = jnp.dot(rows, gate_ref[cut:, at], preferred_element_type=F32)
        up_acc_ref[:, at] = jnp.dot(rows, up_ref[cut:, at], preferred_element_type=F32)
    weight = row_weight(place_ref[0], x[:, width - cut :])
    weight_ref[...] = jnp.broadcast_to(weight, weight_ref.shape)


def early_half_kernel(
    share, place_ref, own_ref, other_ref, gate_ref, up_ref, gate_acc_ref, up_acc_ref, weight_ref, second_ref,
    down_ref, sdown_ref, own_out_ref, other_out_ref, act_ref, later_ref, x, sems,
):
    half, cut = own_ref.shape
    copies = half_down_copies(share, place_ref, down_ref, sdown_ref, later_ref, cut, sems)
    for copy in copies:
        copy.start()
    units = gate_ref.shape[1]
    hidden = units - LANES
    x[:half, :] = own_ref[...]
    x[half:, :] = other_ref[...]
    rows = x[...]
    weight = weight_ref[:, :1]
    for at in tiles_of(units):
        gate = gate_acc_ref[:, at] + jnp.dot(rows, gate_ref[:cut, at], preferred_element_type=F32)
        up = up_acc_ref[:, at] + jnp.dot(rows, up_ref[:cut, at], preferred_element_type=F32)
        if at.start < hidden:
            act_ref[:, at] = (silu(gate) * up * weight).astype(BF16)
        else:
            act_ref[:, at] = shared_units(share, place_ref[0], gate, up)
    piece = cut // 2
    for i in range(2):
        at = slice(i * piece, (i + 1) * piece)
        total = jnp.dot(act_ref[...], second_ref[:, at], preferred_element_type=F32).astype(BF16)
        own_out_ref[:, at] = total[:half]
        other_out_ref[:, at] = total[half:]
    for copy in copies:
        copy.wait()


def last_half_kernel(act_ref, second_ref, own_out_ref, other_out_ref):
    half, columns = own_out_ref.shape
    piece = columns // 2
    for i in range(2):
        at = slice(i * piece, (i + 1) * piece)
        total = jnp.dot(act_ref[...], second_ref[:, at], preferred_element_type=F32).astype(BF16)
        own_out_ref[:, at] = swap_quarters(total[:half])
        other_out_ref[:, at] = swap_quarters(total[half:])


def estimate(rows, depth, columns):
    return pl.CostEstimate(
        flops=2 * rows * depth * columns, bytes_accessed=2 * depth * columns, transcendentals=0
    )


def pair_rows(place, own, other, gate, up, second, down, sdown, share):
    half, cut = own[0].shape
    hidden, width = down.shape
    units = hidden + LANES
    partial = pl.pallas_call(
        late_half_kernel,
        in_specs=[SMEM_SPEC] + [VMEM_SPEC] * 4,
        out_specs=[VMEM_SPEC] * 3,
        out_shape=[pltpu.VMEM((2 * half, columns), F32) for columns in (units, units, LANES)],
        scratch_shapes=[pltpu.VMEM((2 * half, own[1].shape[1]), BF16)],
        cost_estimate=estimate(2 * half, width - cut, 2 * units),
        compiler_params=pltpu.CompilerParams(vmem_limit_bytes=10 << 20),
        name="late_half",
    )(place, own[1], other[1], gate, up)
    own_out, other_out, act, later = pl.pallas_call(
        functools.partial(early_half_kernel, share),
        in_specs=[SMEM_SPEC] + [VMEM_SPEC] * 8 + [ANY_SPEC] * 2,
        out_specs=[VMEM_SPEC] * 4,
        out_shape=[
            pltpu.VMEM((half, cut), BF16),
            pltpu.VMEM((half, cut), BF16),
            pltpu.VMEM((2 * half, units), BF16),
            pltpu.VMEM((units, width - cut), BF16),
        ],
        scratch_shapes=[pltpu.VMEM((2 * half, cut), BF16), pltpu.SemaphoreType.DMA((4,))],
        cost_estimate=estimate(2 * half, cut, 3 * units),
        compiler_params=pltpu.CompilerParams(vmem_limit_bytes=10 << 20),
        name="early_half",
    )(place, own[0], other[0], gate, up, *partial, second, in_hbm(down), in_hbm(sdown))
    last = pl.pallas_call(
        last_half_kernel,
        in_specs=[VMEM_SPEC] * 2,
        out_specs=[VMEM_SPEC] * 2,
        out_shape=[pltpu.VMEM((half, width - cut), BF16)] * 2,
        cost_estimate=estimate(2 * half, width - cut, units),
        compiler_params=pltpu.CompilerParams(vmem_limit_bytes=10 << 20),
        name="last_half",
    )(act, later)
    return own_out, last[0], other_out, last[1]


def block_kernel(
    share, place_ref, x_ref, gate_ref, up_ref, down_ref, sdown_ref, out_ref, act, second, sems
):
    groups = down_copies(share, place_ref, down_ref, sdown_ref, second, sems)

    @pl.when(pl.program_id(0) == 0)
    def _():
        for i in range(DOWN_PARTS):
            start_group(groups, i)
        for i in range(DOWN_PARTS):
            wait_group(groups, i)

    def store(at, total):
        out_ref[:, at] = total.astype(BF16)

    ffn(share, place_ref, x_ref, gate_ref, up_ref, act, second, lambda i: None, store)


def block_rows(place, x, gate, up, down, sdown, share):
    rows, packed = x.shape
    hidden, width = down.shape
    block = min(rows, ROW_BLOCK)
    return pl.pallas_call(
        functools.partial(block_kernel, share),
        grid=(rows // block,),
        in_specs=[SMEM_SPEC, pl.BlockSpec((block, packed), lambda i: (i, 0))] + [VMEM_SPEC] * 2 + [ANY_SPEC] * 2,
        out_specs=pl.BlockSpec((block, width), lambda i: (i, 0)),
        out_shape=jax.ShapeDtypeStruct((rows, width), BF16),
        scratch_shapes=down_scratch(block, hidden, width),
        compiler_params=pltpu.CompilerParams(vmem_limit_bytes=24 << 20),
        name="block_rows",
    )(place, x, gate, up, in_hbm(down), in_hbm(sdown))


def f32_sum(*terms):
    return functools.reduce(lambda a, b: a + b, (t.astype(F32) for t in terms))


def flipped(value, even, odd):
    pairs = []
    for node in range(4):
        for local in range(4):
            node_bits, local_bits = odd if node % 2 else even
            pairs.append((node * 4 + local, (node ^ node_bits) * 4 + (local ^ local_bits)))
    return lax.ppermute(value, ("node", "local"), pairs)


X, Z1, Z2, CORE = (2, 0), (0, 1), (0, 2), (1, 0)
GATHER = ((Z2, X), (Z1, Z2), (X, Z1))
SCATTER = ((X, Z1), (Z1, X), (Z2, Z2))


def stack(*values):
    return jnp.concatenate(values, axis=0)


def per_device(
    tokens,
    group_ids,
    route_weights,
    gate_experts,
    up_experts,
    down_experts,
    gate_shared,
    up_shared,
    down_shared,
):
    rows, width = tokens.shape
    node_count = lax.axis_size("node")
    local_count = lax.axis_size("local")
    share = max(1, LANES * node_count // gate_shared.shape[1])
    place = lax.axis_index("node").reshape(1)
    gate, up, down = gate_experts[0], up_experts[0], down_experts[0]
    packed = pack_rows(tokens, group_ids, route_weights)

    if node_count != 4 or local_count != 4:
        x = lax.all_gather(packed, ("node", "local"), axis=0, tiled=True)
        gate = load_weights(place, gate, gate_shared, share)
        up = load_weights(place, up, up_shared, share)
        part = block_rows(place, x, gate, up, down, down_shared, share)
        return lax.psum_scatter(part, ("node", "local"), scatter_dimension=0, tiled=True)

    cut = width // 2
    own = [packed[:, :cut], packed[:, cut:]]
    loads = (
        lambda *ready: load_down(after(place, *ready), down, down_shared, cut, share),
        lambda *ready: load_weights(after(place, *ready), gate, gate_shared, share),
        lambda *ready: load_weights(after(place, *ready), up, up_shared, share),
    )
    loaded = []
    for phase, load in zip(GATHER, loads):
        got = [flipped(part, *pairs) for part, pairs in zip(own, (phase[::-1], phase))]
        got[1], weights = lax.optimization_barrier((got[1], load(*own)))
        loaded.append(weights)
        own = [stack(part, add) for part, add in zip(own, got)]
    second, gate, up = loaded
    odd = place[0] % 2
    own = [jnp.where(odd == 1 - i, part, regroup(part, 4, 2)) for i, part in enumerate(own)]
    other = [flipped(part, CORE, CORE) for part in own]

    outs = pair_rows(place, own, other, gate, up, second, down, down_shared, share)

    totals = [[own, flipped(other, CORE, CORE)] for own, other in zip(outs[:2], outs[2:])]
    for phase in SCATTER:
        for i, bits in enumerate(phase):
            total = totals[i]
            half = total[0].shape[0] // 2
            sent = f32_sum(*(t[half:] for t in total)).astype(BF16)
            totals[i] = [f32_sum(*(t[:half] for t in total)), flipped(sent, bits, bits)]
    return jnp.concatenate([f32_sum(*total).astype(BF16) for total in totals], axis=1)


def solution(mesh):
    in_specs = (
        P(("rep", "node", "local"), None),
        P(("rep", "node", "local"), None),
        P(("rep", "node", "local"), None),
        P("node", None, "local"),
        P("node", None, "local"),
        P("node", "local", None),
        P(None, "local"),
        P(None, "local"),
        P("local", None),
    )
    out_specs = P(("rep", "node", "local"), None)
    return jax.shard_map(
        per_device, mesh=mesh, in_specs=in_specs, out_specs=out_specs, check_vma=False
    )
```

```python
import functools

import jax
import jax.numpy as jnp
from jax import lax
from jax.experimental import pallas as pl
from jax.experimental.pallas import tpu as pltpu
from jax.sharding import PartitionSpec as P

LANES = 128
ROW_BLOCK = 128
F32 = jnp.float32
BF16 = jnp.bfloat16
VMEM_SPEC = pl.BlockSpec(memory_space=pltpu.VMEM)
SMEM_SPEC = pl.BlockSpec(memory_space=pltpu.SMEM)
ANY_SPEC = pl.BlockSpec(memory_space=pl.ANY)


def in_hbm(value):
    return pltpu.with_memory_space_constraint(value, pltpu.HBM)


def run_copies(copies):
    for copy in copies:
        copy.start()
    for copy in copies:
        copy.wait()


def after(value, *done):
    return lax.optimization_barrier((value, *done))[0]


def pack_kernel(tokens_ref, groups_ref, weights_ref, packed_ref):
    rows, width = tokens_ref.shape
    packed_ref[:, :width] = tokens_ref[...]
    groups = groups_ref[...].T
    weights = weights_ref[...].astype(F32).T
    lane = lax.broadcasted_iota(jnp.int32, (rows, LANES), 1)
    dense = jnp.zeros((rows, LANES), F32)
    for k in range(groups.shape[1]):
        dense += jnp.where(lane == groups[:, k : k + 1], weights[:, k : k + 1], 0.0)
    packed_ref[:, width:] = dense.astype(BF16)


def pack_rows(tokens, group_ids, route_weights):
    rows, width = tokens.shape
    return pl.pallas_call(
        pack_kernel,
        out_specs=VMEM_SPEC,
        out_shape=pltpu.VMEM((rows, width + LANES), BF16),
        name="pack_rows",
    )(tokens, group_ids.T, route_weights.T)


def weight_copies(share, place_ref, routed_ref, shared_ref, out_ref, sems, parts):
    width, hidden = routed_ref.shape
    column = pl.multiple_of((place_ref[0] // share) * LANES, LANES)
    piece = width // parts
    copies = []
    for i in range(parts):
        at = pl.ds(i * piece, piece)
        for source, lower, size in (
            (routed_ref.at[at, :], 0, hidden),
            (shared_ref.at[at, pl.ds(column, LANES)], hidden, LANES),
        ):
            copies.append(
                pltpu.make_async_copy(source, out_ref.at[at, pl.ds(lower, size)], sems.at[len(copies)])
            )
    return copies


def load_kernel(share, place_ref, routed_ref, shared_ref, out_ref, sems):
    run_copies(weight_copies(share, place_ref, routed_ref, shared_ref, out_ref, sems, sems.shape[0] // 2))


def load_weights(place, routed, shared, share):
    width, hidden = routed.shape
    shape = (width, hidden + LANES)
    return pl.pallas_call(
        functools.partial(load_kernel, share),
        in_specs=[SMEM_SPEC] + [ANY_SPEC] * 2,
        out_specs=VMEM_SPEC,
        out_shape=pltpu.VMEM(shape, BF16),
        scratch_shapes=[pltpu.SemaphoreType.DMA((8,))],
        cost_estimate=pl.CostEstimate(flops=0, bytes_accessed=4 * shape[0] * shape[1], transcendentals=0),
        compiler_params=pltpu.CompilerParams(vmem_limit_bytes=1 << 20),
        name="load_weights",
    )(place, in_hbm(routed), in_hbm(shared))


def silu(v):
    return v / (1.0 + jnp.exp(-v))


def row_weight(node, dense):
    lane = lax.broadcasted_iota(jnp.int32, dense.shape, 1)
    return jnp.sum(jnp.where(lane == node, dense.astype(F32), 0.0), axis=1, keepdims=True)


DOWN_PARTS = 4


def down_scratch(rows, hidden, width):
    return [
        pltpu.VMEM((rows, hidden + LANES), BF16),
        pltpu.VMEM((hidden + LANES, width), BF16),
        pltpu.SemaphoreType.DMA((2 * DOWN_PARTS,)),
    ]


def down_copies(share, place_ref, down_ref, sdown_ref, second, sems):
    hidden, width = down_ref.shape
    column = pl.multiple_of((place_ref[0] // share) * LANES, LANES)
    piece = width // DOWN_PARTS
    groups = []
    for i in range(DOWN_PARTS):
        at = pl.ds(i * piece, piece)
        groups.append(
            [
                pltpu.make_async_copy(down_ref.at[:, at], second.at[pl.ds(0, hidden), at], sems.at[2 * i]),
                pltpu.make_async_copy(
                    sdown_ref.at[pl.ds(column, LANES), at],
                    second.at[pl.ds(hidden, LANES), at],
                    sems.at[2 * i + 1],
                ),
            ]
        )
    return groups


def start_group(groups, i):
    for copy in groups[i]:
        copy.start()


def wait_group(groups, i):
    for copy in groups[i]:
        copy.wait()


def shared_units(share, node, gate, up):
    shared = silu(gate) * up
    if share > 1:
        lane = lax.broadcasted_iota(jnp.int32, shared.shape, 1)
        shared = jnp.where(lane // (LANES // share) == node % share, shared, 0.0)
    return shared.astype(BF16)


def tiles_of(units):
    tile = 2 * LANES
    return [slice(at, min(at + tile, units)) for at in range(0, units, tile)]


def ffn(share, place_ref, x, gate_ref, up_ref, act, second, take, store):
    width, units = gate_ref.shape
    hidden = units - LANES
    node = place_ref[0]
    rows = x[:, :width]
    weight = row_weight(node, x[:, width:])
    gate = jnp.dot(rows, gate_ref[...], preferred_element_type=F32)
    up = jnp.dot(rows, up_ref[...], preferred_element_type=F32)
    act[:, :hidden] = (silu(gate[:, :hidden]) * up[:, :hidden] * weight).astype(BF16)
    act[:, hidden:] = shared_units(share, node, gate[:, hidden:], up[:, hidden:])
    piece = width // DOWN_PARTS
    for i in range(DOWN_PARTS):
        at = slice(i * piece, (i + 1) * piece)
        take(i)
        store(at, jnp.dot(act[...], second[:, at], preferred_element_type=F32))


def regroup(value, outer, inner):
    rows = value.shape[0] // (outer * inner)
    return jnp.concatenate(
        [
            value[(o * inner + i) * rows : (o * inner + i + 1) * rows]
            for i in range(inner)
            for o in range(outer)
        ],
        axis=0,
    )


def swap_quarters(value):
    quarter = value.shape[0] // 4
    return jnp.concatenate([value[i * quarter : (i + 1) * quarter] for i in (0, 2, 1, 3)], axis=0)


def down_range_copies(share, place_ref, down_ref, sdown_ref, out_ref, lower, sems, parts):
    hidden = down_ref.shape[0]
    column = pl.multiple_of((place_ref[0] // share) * LANES, LANES)
    piece = out_ref.shape[1] // parts
    copies = []
    for i in range(parts):
        source, target = pl.ds(lower + i * piece, piece), pl.ds(i * piece, piece)
        copies.append(
            pltpu.make_async_copy(
                down_ref.at[:, source], out_ref.at[pl.ds(0, hidden), target], sems.at[2 * i]
            )
        )
        copies.append(
            pltpu.make_async_copy(
                sdown_ref.at[pl.ds(column, LANES), source],
                out_ref.at[pl.ds(hidden, LANES), target],
                sems.at[2 * i + 1],
            )
        )
    return copies


def load_late_kernel(share, place_ref, up_ref, sup_ref, down_ref, sdown_ref, up_out_ref, down_out_ref, sems):
    parts = (sems.shape[0] - 4) // 2
    run_copies(
        weight_copies(share, place_ref, up_ref, sup_ref, up_out_ref, sems, parts)
        + down_range_copies(share, place_ref, down_ref, sdown_ref, down_out_ref, 0, sems.at[2 * parts :], 2)
    )


def load_late(place, up, sup, down, sdown, cut, share):
    width, hidden = up.shape
    units = hidden + LANES
    return pl.pallas_call(
        functools.partial(load_late_kernel, share),
        in_specs=[SMEM_SPEC] + [ANY_SPEC] * 4,
        out_specs=[VMEM_SPEC] * 2,
        out_shape=[pltpu.VMEM((width, units), BF16), pltpu.VMEM((units, cut), BF16)],
        scratch_shapes=[pltpu.SemaphoreType.DMA((12,))],
        cost_estimate=pl.CostEstimate(flops=0, bytes_accessed=4 * units * (width + cut), transcendentals=0),
        compiler_params=pltpu.CompilerParams(vmem_limit_bytes=1 << 20),
        name="load_late",
    )(place, *(in_hbm(w) for w in (up, sup, down, sdown)))


def late_half_kernel(
    share, place_ref, own_ref, other_ref, gate_ref, up_ref, down_ref, sdown_ref,
    gate_acc_ref, up_acc_ref, weight_ref, later_ref, x, sems,
):
    width, units = gate_ref.shape
    half, columns = own_ref.shape
    cut = width + LANES - columns
    copies = down_range_copies(share, place_ref, down_ref, sdown_ref, later_ref, cut, sems, 1)
    for copy in copies:
        copy.start()
    x[:half, :] = own_ref[...]
    x[half:, :] = other_ref[...]
    rows = x[:, : width - cut]
    for at in tiles_of(units):
        gate_acc_ref[:, at] = jnp.dot(rows, gate_ref[cut:, at], preferred_element_type=F32)
        up_acc_ref[:, at] = jnp.dot(rows, up_ref[cut:, at], preferred_element_type=F32)
    weight = row_weight(place_ref[0], x[:, width - cut :])
    weight_ref[...] = jnp.broadcast_to(weight, weight_ref.shape)
    for copy in copies:
        copy.wait()


def early_half_kernel(
    share, place_ref, own_ref, other_ref, gate_ref, up_ref, gate_acc_ref, up_acc_ref, weight_ref, second_ref,
    down_ref, sdown_ref, own_out_ref, other_out_ref, act_ref, later_ref, x, sems,
):
    half, cut = own_ref.shape
    lower = down_ref.shape[1] - later_ref.shape[1]
    copies = down_range_copies(share, place_ref, down_ref, sdown_ref, later_ref, lower, sems, 1)
    for copy in copies:
        copy.start()
    units = gate_ref.shape[1]
    hidden = units - LANES
    x[:half, :] = own_ref[...]
    x[half:, :] = other_ref[...]
    rows = x[...]
    weight = weight_ref[:, :1]
    for at in tiles_of(units):
        gate = gate_acc_ref[:, at] + jnp.dot(rows, gate_ref[:cut, at], preferred_element_type=F32)
        up = up_acc_ref[:, at] + jnp.dot(rows, up_ref[:cut, at], preferred_element_type=F32)
        if at.start < hidden:
            act_ref[:, at] = (silu(gate) * up * weight).astype(BF16)
        else:
            act_ref[:, at] = shared_units(share, place_ref[0], gate, up)
    piece = cut // 2
    for i in range(2):
        at = slice(i * piece, (i + 1) * piece)
        total = jnp.dot(act_ref[...], second_ref[:, at], preferred_element_type=F32).astype(BF16)
        own_out_ref[:, at] = total[:half]
        other_out_ref[:, at] = total[half:]
    for copy in copies:
        copy.wait()


def last_half_kernel(act_ref, third_ref, fourth_ref, own_out_ref, other_out_ref):
    half, columns = own_out_ref.shape
    piece = columns // 2
    for i, later_ref in enumerate((third_ref, fourth_ref)):
        at = slice(i * piece, (i + 1) * piece)
        total = jnp.dot(act_ref[...], later_ref[...], preferred_element_type=F32).astype(BF16)
        own_out_ref[:, at] = swap_quarters(total[:half])
        other_out_ref[:, at] = swap_quarters(total[half:])


def estimate(rows, depth, columns):
    return pl.CostEstimate(
        flops=2 * rows * depth * columns, bytes_accessed=2 * depth * columns, transcendentals=0
    )


def pair_rows(place, own, other, gate, up, second, down, sdown, share):
    half, cut = own[0].shape
    hidden, width = down.shape
    units = hidden + LANES
    down, sdown = in_hbm(down), in_hbm(sdown)
    quarter = pltpu.VMEM((units, (width - cut) // 2), BF16)
    *partial, third = pl.pallas_call(
        functools.partial(late_half_kernel, share),
        in_specs=[SMEM_SPEC] + [VMEM_SPEC] * 4 + [ANY_SPEC] * 2,
        out_specs=[VMEM_SPEC] * 4,
        out_shape=[pltpu.VMEM((2 * half, columns), F32) for columns in (units, units, LANES)] + [quarter],
        scratch_shapes=[pltpu.VMEM((2 * half, own[1].shape[1]), BF16), pltpu.SemaphoreType.DMA((2,))],
        cost_estimate=estimate(2 * half, width - cut, 2 * units),
        compiler_params=pltpu.CompilerParams(vmem_limit_bytes=10 << 20),
        name="late_half",
    )(place, own[1], other[1], gate, up, down, sdown)
    own_out, other_out, act, fourth = pl.pallas_call(
        functools.partial(early_half_kernel, share),
        in_specs=[SMEM_SPEC] + [VMEM_SPEC] * 8 + [ANY_SPEC] * 2,
        out_specs=[VMEM_SPEC] * 4,
        out_shape=[
            pltpu.VMEM((half, cut), BF16),
            pltpu.VMEM((half, cut), BF16),
            pltpu.VMEM((2 * half, units), BF16),
            quarter,
        ],
        scratch_shapes=[pltpu.VMEM((2 * half, cut), BF16), pltpu.SemaphoreType.DMA((2,))],
        cost_estimate=estimate(2 * half, cut, 3 * units),
        compiler_params=pltpu.CompilerParams(vmem_limit_bytes=10 << 20),
        name="early_half",
    )(place, own[0], other[0], gate, up, *partial, second, down, sdown)
    last = pl.pallas_call(
        last_half_kernel,
        in_specs=[VMEM_SPEC] * 3,
        out_specs=[VMEM_SPEC] * 2,
        out_shape=[pltpu.VMEM((half, width - cut), BF16)] * 2,
        cost_estimate=estimate(2 * half, width - cut, units),
        compiler_params=pltpu.CompilerParams(vmem_limit_bytes=10 << 20),
        name="last_half",
    )(act, third, fourth)
    return own_out, last[0], other_out, last[1]


def block_kernel(
    share, place_ref, x_ref, gate_ref, up_ref, down_ref, sdown_ref, out_ref, act, second, sems
):
    groups = down_copies(share, place_ref, down_ref, sdown_ref, second, sems)

    @pl.when(pl.program_id(0) == 0)
    def _():
        for i in range(DOWN_PARTS):
            start_group(groups, i)
        for i in range(DOWN_PARTS):
            wait_group(groups, i)

    def store(at, total):
        out_ref[:, at] = total.astype(BF16)

    ffn(share, place_ref, x_ref, gate_ref, up_ref, act, second, lambda i: None, store)


def block_rows(place, x, gate, up, down, sdown, share):
    rows, packed = x.shape
    hidden, width = down.shape
    block = min(rows, ROW_BLOCK)
    return pl.pallas_call(
        functools.partial(block_kernel, share),
        grid=(rows // block,),
        in_specs=[SMEM_SPEC, pl.BlockSpec((block, packed), lambda i: (i, 0))] + [VMEM_SPEC] * 2 + [ANY_SPEC] * 2,
        out_specs=pl.BlockSpec((block, width), lambda i: (i, 0)),
        out_shape=jax.ShapeDtypeStruct((rows, width), BF16),
        scratch_shapes=down_scratch(block, hidden, width),
        compiler_params=pltpu.CompilerParams(vmem_limit_bytes=24 << 20),
        name="block_rows",
    )(place, x, gate, up, in_hbm(down), in_hbm(sdown))


def f32_sum(*terms):
    return functools.reduce(lambda a, b: a + b, (t.astype(F32) for t in terms))


def flipped(value, even, odd):
    pairs = []
    for node in range(4):
        for local in range(4):
            node_bits, local_bits = odd if node % 2 else even
            pairs.append((node * 4 + local, (node ^ node_bits) * 4 + (local ^ local_bits)))
    return lax.ppermute(value, ("node", "local"), pairs)


X, Z1, Z2, CORE = (2, 0), (0, 1), (0, 2), (1, 0)
GATHER = ((Z2, X), (Z1, Z2), (X, Z1))
SCATTER = ((X, Z1), (Z1, X), (Z2, Z2))


def stack(*values):
    return jnp.concatenate(values, axis=0)


def per_device(
    tokens,
    group_ids,
    route_weights,
    gate_experts,
    up_experts,
    down_experts,
    gate_shared,
    up_shared,
    down_shared,
):
    rows, width = tokens.shape
    node_count = lax.axis_size("node")
    local_count = lax.axis_size("local")
    share = max(1, LANES * node_count // gate_shared.shape[1])
    place = lax.axis_index("node").reshape(1)
    gate, up, down = gate_experts[0], up_experts[0], down_experts[0]
    packed = pack_rows(tokens, group_ids, route_weights)

    if node_count != 4 or local_count != 4:
        x = lax.all_gather(packed, ("node", "local"), axis=0, tiled=True)
        gate = load_weights(place, gate, gate_shared, share)
        up = load_weights(place, up, up_shared, share)
        part = block_rows(place, x, gate, up, down, down_shared, share)
        return lax.psum_scatter(part, ("node", "local"), scatter_dimension=0, tiled=True)

    cut = width // 2
    own = [packed[:, :cut], packed[:, cut:]]
    loads = (
        lambda *ready: (),
        lambda *ready: (load_weights(after(place, *ready), gate, gate_shared, share),),
        lambda *ready: load_late(after(place, *ready), up, up_shared, down, down_shared, cut, share),
    )
    loaded = ()
    for phase, load in zip(GATHER, loads):
        got = [flipped(part, *pairs) for part, pairs in zip(own, (phase, phase[::-1]))]
        weights = tuple(load(*own))
        if weights:
            got, weights = lax.optimization_barrier((got, weights))
        loaded += weights
        own = [stack(part, add) for part, add in zip(own, got)]
    gate, up, second = loaded
    odd = place[0] % 2
    own = [jnp.where(odd == i, part, regroup(part, 4, 2)) for i, part in enumerate(own)]
    other = [flipped(part, CORE, CORE) for part in own]

    outs = pair_rows(place, own, other, gate, up, second, down, down_shared, share)

    totals = [[own, flipped(other, CORE, CORE)] for own, other in zip(outs[:2], outs[2:])]
    for phase in SCATTER:
        for i, bits in enumerate(phase):
            total = totals[i]
            half = total[0].shape[0] // 2
            sent = f32_sum(*(t[half:] for t in total)).astype(BF16)
            totals[i] = [f32_sum(*(t[:half] for t in total)), flipped(sent, bits, bits)]
    return jnp.concatenate([f32_sum(*total).astype(BF16) for total in totals], axis=1)


def solution(mesh):
    in_specs = (
        P(("rep", "node", "local"), None),
        P(("rep", "node", "local"), None),
        P(("rep", "node", "local"), None),
        P("node", None, "local"),
        P("node", None, "local"),
        P("node", "local", None),
        P(None, "local"),
        P(None, "local"),
        P("local", None),
    )
    out_specs = P(("rep", "node", "local"), None)
    return jax.shard_map(
        per_device, mesh=mesh, in_specs=in_specs, out_specs=out_specs, check_vma=False
    )
```

```python
import functools

import jax
import jax.numpy as jnp
from jax import lax
from jax.experimental import pallas as pl
from jax.experimental.pallas import tpu as pltpu
from jax.sharding import PartitionSpec as P

LANES = 128
ROW_BLOCK = 128
F32 = jnp.float32
BF16 = jnp.bfloat16
VMEM_SPEC = pl.BlockSpec(memory_space=pltpu.VMEM)
SMEM_SPEC = pl.BlockSpec(memory_space=pltpu.SMEM)
ANY_SPEC = pl.BlockSpec(memory_space=pl.ANY)


def in_hbm(value):
    return pltpu.with_memory_space_constraint(value, pltpu.HBM)


def run_copies(copies):
    for copy in copies:
        copy.start()
    for copy in copies:
        copy.wait()


def after(value, *done):
    return lax.optimization_barrier((value, *done))[0]


def pack_kernel(tokens_ref, groups_ref, weights_ref, packed_ref):
    rows, width = tokens_ref.shape
    packed_ref[:, :width] = tokens_ref[...]
    groups = groups_ref[...].T
    weights = weights_ref[...].astype(F32).T
    lane = lax.broadcasted_iota(jnp.int32, (rows, LANES), 1)
    dense = jnp.zeros((rows, LANES), F32)
    for k in range(groups.shape[1]):
        dense += jnp.where(lane == groups[:, k : k + 1], weights[:, k : k + 1], 0.0)
    packed_ref[:, width:] = dense.astype(BF16)


def pack_rows(tokens, group_ids, route_weights):
    rows, width = tokens.shape
    return pl.pallas_call(
        pack_kernel,
        out_specs=VMEM_SPEC,
        out_shape=pltpu.VMEM((rows, width + LANES), BF16),
        name="pack_rows",
    )(tokens, group_ids.T, route_weights.T)


def weight_copies(share, place_ref, routed_ref, shared_ref, out_ref, sems, parts):
    width, hidden = routed_ref.shape
    column = pl.multiple_of((place_ref[0] // share) * LANES, LANES)
    piece = width // parts
    copies = []
    for i in range(parts):
        at = pl.ds(i * piece, piece)
        for source, lower, size in (
            (routed_ref.at[at, :], 0, hidden),
            (shared_ref.at[at, pl.ds(column, LANES)], hidden, LANES),
        ):
            copies.append(
                pltpu.make_async_copy(source, out_ref.at[at, pl.ds(lower, size)], sems.at[len(copies)])
            )
    return copies


def load_kernel(share, place_ref, routed_ref, shared_ref, out_ref, sems):
    run_copies(weight_copies(share, place_ref, routed_ref, shared_ref, out_ref, sems, sems.shape[0] // 2))


def load_weights(place, routed, shared, share):
    width, hidden = routed.shape
    shape = (width, hidden + LANES)
    return pl.pallas_call(
        functools.partial(load_kernel, share),
        in_specs=[SMEM_SPEC] + [ANY_SPEC] * 2,
        out_specs=VMEM_SPEC,
        out_shape=pltpu.VMEM(shape, BF16),
        scratch_shapes=[pltpu.SemaphoreType.DMA((8,))],
        cost_estimate=pl.CostEstimate(flops=0, bytes_accessed=4 * shape[0] * shape[1], transcendentals=0),
        compiler_params=pltpu.CompilerParams(vmem_limit_bytes=1 << 20),
        name="load_weights",
    )(place, in_hbm(routed), in_hbm(shared))


def silu(v):
    return v / (1.0 + jnp.exp(-v))


def row_weight(node, dense):
    lane = lax.broadcasted_iota(jnp.int32, dense.shape, 1)
    return jnp.sum(jnp.where(lane == node, dense.astype(F32), 0.0), axis=1, keepdims=True)


DOWN_PARTS = 4


def down_scratch(rows, hidden, width):
    return [
        pltpu.VMEM((rows, hidden + LANES), BF16),
        pltpu.VMEM((hidden + LANES, width), BF16),
        pltpu.SemaphoreType.DMA((2 * DOWN_PARTS,)),
    ]


def down_copies(share, place_ref, down_ref, sdown_ref, second, sems):
    hidden, width = down_ref.shape
    column = pl.multiple_of((place_ref[0] // share) * LANES, LANES)
    piece = width // DOWN_PARTS
    groups = []
    for i in range(DOWN_PARTS):
        at = pl.ds(i * piece, piece)
        groups.append(
            [
                pltpu.make_async_copy(down_ref.at[:, at], second.at[pl.ds(0, hidden), at], sems.at[2 * i]),
                pltpu.make_async_copy(
                    sdown_ref.at[pl.ds(column, LANES), at],
                    second.at[pl.ds(hidden, LANES), at],
                    sems.at[2 * i + 1],
                ),
            ]
        )
    return groups


def start_group(groups, i):
    for copy in groups[i]:
        copy.start()


def wait_group(groups, i):
    for copy in groups[i]:
        copy.wait()


def shared_units(share, node, gate, up):
    shared = silu(gate) * up
    if share > 1:
        lane = lax.broadcasted_iota(jnp.int32, shared.shape, 1)
        shared = jnp.where(lane // (LANES // share) == node % share, shared, 0.0)
    return shared.astype(BF16)


def tiles_of(units):
    tile = 2 * LANES
    return [slice(at, min(at + tile, units)) for at in range(0, units, tile)]


def ffn(share, place_ref, x, gate_ref, up_ref, act, second, take, store):
    width, units = gate_ref.shape
    hidden = units - LANES
    node = place_ref[0]
    rows = x[:, :width]
    weight = row_weight(node, x[:, width:])
    gate = jnp.dot(rows, gate_ref[...], preferred_element_type=F32)
    up = jnp.dot(rows, up_ref[...], preferred_element_type=F32)
    act[:, :hidden] = (silu(gate[:, :hidden]) * up[:, :hidden] * weight).astype(BF16)
    act[:, hidden:] = shared_units(share, node, gate[:, hidden:], up[:, hidden:])
    piece = width // DOWN_PARTS
    for i in range(DOWN_PARTS):
        at = slice(i * piece, (i + 1) * piece)
        take(i)
        store(at, jnp.dot(act[...], second[:, at], preferred_element_type=F32))


def regroup(value, outer, inner):
    rows = value.shape[0] // (outer * inner)
    return jnp.concatenate(
        [
            value[(o * inner + i) * rows : (o * inner + i + 1) * rows]
            for i in range(inner)
            for o in range(outer)
        ],
        axis=0,
    )


def swap_quarters(value):
    quarter = value.shape[0] // 4
    return jnp.concatenate([value[i * quarter : (i + 1) * quarter] for i in (0, 2, 1, 3)], axis=0)


DOWN_ROWS = 64


def down_range_copies(share, place_ref, down_ref, sdown_ref, out_ref, lower, sems):
    hidden = down_ref.shape[0]
    column = pl.multiple_of((place_ref[0] // share) * LANES, LANES)
    columns = pl.ds(lower, out_ref.shape[1])
    copies = []
    for at in range(0, hidden + LANES, DOWN_ROWS):
        if at < hidden:
            source = down_ref.at[pl.ds(at, DOWN_ROWS), columns]
        else:
            source = sdown_ref.at[pl.ds(column + (at - hidden), DOWN_ROWS), columns]
        copies.append(
            pltpu.make_async_copy(source, out_ref.at[pl.ds(at, DOWN_ROWS), :], sems.at[len(copies)])
        )
    return copies


def load_late_kernel(share, place_ref, up_ref, sup_ref, down_ref, sdown_ref, up_out_ref, down_out_ref, sems):
    parts = 4
    run_copies(
        weight_copies(share, place_ref, up_ref, sup_ref, up_out_ref, sems, parts)
        + down_range_copies(share, place_ref, down_ref, sdown_ref, down_out_ref, 0, sems.at[2 * parts :])
    )


def load_late(place, up, sup, down, sdown, cut, share):
    width, hidden = up.shape
    units = hidden + LANES
    return pl.pallas_call(
        functools.partial(load_late_kernel, share),
        in_specs=[SMEM_SPEC] + [ANY_SPEC] * 4,
        out_specs=[VMEM_SPEC] * 2,
        out_shape=[pltpu.VMEM((width, units), BF16), pltpu.VMEM((units, cut), BF16)],
        scratch_shapes=[pltpu.SemaphoreType.DMA((8 + units // DOWN_ROWS,))],
        cost_estimate=pl.CostEstimate(flops=0, bytes_accessed=4 * units * (width + cut), transcendentals=0),
        compiler_params=pltpu.CompilerParams(vmem_limit_bytes=1 << 20),
        name="load_late",
    )(place, *(in_hbm(w) for w in (up, sup, down, sdown)))


def late_half_kernel(
    share, place_ref, own_ref, other_ref, gate_ref, up_ref, down_ref, sdown_ref,
    gate_acc_ref, up_acc_ref, weight_ref, later_ref, x, sems,
):
    width, units = gate_ref.shape
    half, columns = own_ref.shape
    cut = width + LANES - columns
    copies = down_range_copies(share, place_ref, down_ref, sdown_ref, later_ref, cut, sems)
    for copy in copies:
        copy.start()
    x[:half, :] = own_ref[...]
    x[half:, :] = other_ref[...]
    rows = x[:, : width - cut]
    for at in tiles_of(units):
        gate_acc_ref[:, at] = jnp.dot(rows, gate_ref[cut:, at], preferred_element_type=F32)
        up_acc_ref[:, at] = jnp.dot(rows, up_ref[cut:, at], preferred_element_type=F32)
    weight = row_weight(place_ref[0], x[:, width - cut :])
    weight_ref[...] = jnp.broadcast_to(weight, weight_ref.shape)
    for copy in copies:
        copy.wait()


def early_half_kernel(
    share, place_ref, own_ref, other_ref, gate_ref, up_ref, gate_acc_ref, up_acc_ref, weight_ref, second_ref,
    down_ref, sdown_ref, own_out_ref, other_out_ref, act_ref, later_ref, x, sems,
):
    half, cut = own_ref.shape
    lower = down_ref.shape[1] - later_ref.shape[1]
    copies = down_range_copies(share, place_ref, down_ref, sdown_ref, later_ref, lower, sems)
    for copy in copies:
        copy.start()
    units = gate_ref.shape[1]
    hidden = units - LANES
    x[:half, :] = own_ref[...]
    x[half:, :] = other_ref[...]
    rows = x[...]
    weight = weight_ref[:, :1]
    for at in tiles_of(units):
        gate = gate_acc_ref[:, at] + jnp.dot(rows, gate_ref[:cut, at], preferred_element_type=F32)
        up = up_acc_ref[:, at] + jnp.dot(rows, up_ref[:cut, at], preferred_element_type=F32)
        if at.start < hidden:
            act_ref[:, at] = (silu(gate) * up * weight).astype(BF16)
        else:
            act_ref[:, at] = shared_units(share, place_ref[0], gate, up)
    piece = cut // 2
    for i in range(2):
        at = slice(i * piece, (i + 1) * piece)
        total = jnp.dot(act_ref[...], second_ref[:, at], preferred_element_type=F32).astype(BF16)
        own_out_ref[:, at] = total[:half]
        other_out_ref[:, at] = total[half:]
    for copy in copies:
        copy.wait()


def last_half_kernel(act_ref, third_ref, fourth_ref, own_out_ref, other_out_ref):
    half, columns = own_out_ref.shape
    piece = columns // 2
    for i, later_ref in enumerate((third_ref, fourth_ref)):
        at = slice(i * piece, (i + 1) * piece)
        total = jnp.dot(act_ref[...], later_ref[...], preferred_element_type=F32).astype(BF16)
        own_out_ref[:, at] = swap_quarters(total[:half])
        other_out_ref[:, at] = swap_quarters(total[half:])


def estimate(rows, depth, columns):
    return pl.CostEstimate(
        flops=2 * rows * depth * columns, bytes_accessed=2 * depth * columns, transcendentals=0
    )


def pair_rows(place, own, other, gate, up, second, down, sdown, share):
    half, cut = own[0].shape
    hidden, width = down.shape
    units = hidden + LANES
    down, sdown = in_hbm(down), in_hbm(sdown)
    quarter = pltpu.VMEM((units, (width - cut) // 2), BF16)
    *partial, third = pl.pallas_call(
        functools.partial(late_half_kernel, share),
        in_specs=[SMEM_SPEC] + [VMEM_SPEC] * 4 + [ANY_SPEC] * 2,
        out_specs=[VMEM_SPEC] * 4,
        out_shape=[pltpu.VMEM((2 * half, columns), F32) for columns in (units, units, LANES)] + [quarter],
        scratch_shapes=[pltpu.VMEM((2 * half, own[1].shape[1]), BF16), pltpu.SemaphoreType.DMA((units // DOWN_ROWS,))],
        cost_estimate=estimate(2 * half, width - cut, 2 * units),
        compiler_params=pltpu.CompilerParams(vmem_limit_bytes=10 << 20),
        name="late_half",
    )(place, own[1], other[1], gate, up, down, sdown)
    own_out, other_out, act, fourth = pl.pallas_call(
        functools.partial(early_half_kernel, share),
        in_specs=[SMEM_SPEC] + [VMEM_SPEC] * 8 + [ANY_SPEC] * 2,
        out_specs=[VMEM_SPEC] * 4,
        out_shape=[
            pltpu.VMEM((half, cut), BF16),
            pltpu.VMEM((half, cut), BF16),
            pltpu.VMEM((2 * half, units), BF16),
            quarter,
        ],
        scratch_shapes=[pltpu.VMEM((2 * half, cut), BF16), pltpu.SemaphoreType.DMA((units // DOWN_ROWS,))],
        cost_estimate=estimate(2 * half, cut, 3 * units),
        compiler_params=pltpu.CompilerParams(vmem_limit_bytes=10 << 20),
        name="early_half",
    )(place, own[0], other[0], gate, up, *partial, second, down, sdown)
    last = pl.pallas_call(
        last_half_kernel,
        in_specs=[VMEM_SPEC] * 3,
        out_specs=[VMEM_SPEC] * 2,
        out_shape=[pltpu.VMEM((half, width - cut), BF16)] * 2,
        cost_estimate=estimate(2 * half, width - cut, units),
        compiler_params=pltpu.CompilerParams(vmem_limit_bytes=10 << 20),
        name="last_half",
    )(act, third, fourth)
    return own_out, last[0], other_out, last[1]


def block_kernel(
    share, place_ref, x_ref, gate_ref, up_ref, down_ref, sdown_ref, out_ref, act, second, sems
):
    groups = down_copies(share, place_ref, down_ref, sdown_ref, second, sems)

    @pl.when(pl.program_id(0) == 0)
    def _():
        for i in range(DOWN_PARTS):
            start_group(groups, i)
        for i in range(DOWN_PARTS):
            wait_group(groups, i)

    def store(at, total):
        out_ref[:, at] = total.astype(BF16)

    ffn(share, place_ref, x_ref, gate_ref, up_ref, act, second, lambda i: None, store)


def block_rows(place, x, gate, up, down, sdown, share):
    rows, packed = x.shape
    hidden, width = down.shape
    block = min(rows, ROW_BLOCK)
    return pl.pallas_call(
        functools.partial(block_kernel, share),
        grid=(rows // block,),
        in_specs=[SMEM_SPEC, pl.BlockSpec((block, packed), lambda i: (i, 0))] + [VMEM_SPEC] * 2 + [ANY_SPEC] * 2,
        out_specs=pl.BlockSpec((block, width), lambda i: (i, 0)),
        out_shape=jax.ShapeDtypeStruct((rows, width), BF16),
        scratch_shapes=down_scratch(block, hidden, width),
        compiler_params=pltpu.CompilerParams(vmem_limit_bytes=24 << 20),
        name="block_rows",
    )(place, x, gate, up, in_hbm(down), in_hbm(sdown))


def f32_sum(*terms):
    return functools.reduce(lambda a, b: a + b, (t.astype(F32) for t in terms))


def flipped(value, even, odd):
    pairs = []
    for node in range(4):
        for local in range(4):
            node_bits, local_bits = odd if node % 2 else even
            pairs.append((node * 4 + local, (node ^ node_bits) * 4 + (local ^ local_bits)))
    return lax.ppermute(value, ("node", "local"), pairs)


X, Z1, Z2, CORE = (2, 0), (0, 1), (0, 2), (1, 0)
GATHER = ((Z2, X), (Z1, Z2), (X, Z1))
SCATTER = ((X, Z1), (Z1, X), (Z2, Z2))


def stack(*values):
    return jnp.concatenate(values, axis=0)


def per_device(
    tokens,
    group_ids,
    route_weights,
    gate_experts,
    up_experts,
    down_experts,
    gate_shared,
    up_shared,
    down_shared,
):
    rows, width = tokens.shape
    node_count = lax.axis_size("node")
    local_count = lax.axis_size("local")
    share = max(1, LANES * node_count // gate_shared.shape[1])
    place = lax.axis_index("node").reshape(1)
    gate, up, down = gate_experts[0], up_experts[0], down_experts[0]
    packed = pack_rows(tokens, group_ids, route_weights)

    if node_count != 4 or local_count != 4:
        x = lax.all_gather(packed, ("node", "local"), axis=0, tiled=True)
        gate = load_weights(place, gate, gate_shared, share)
        up = load_weights(place, up, up_shared, share)
        part = block_rows(place, x, gate, up, down, down_shared, share)
        return lax.psum_scatter(part, ("node", "local"), scatter_dimension=0, tiled=True)

    cut = width // 2
    own = [packed[:, :cut], packed[:, cut:]]
    loads = (
        lambda *ready: (),
        lambda *ready: (load_weights(after(place, *ready), gate, gate_shared, share),),
        lambda *ready: load_late(after(place, *ready), up, up_shared, down, down_shared, cut, share),
    )
    loaded = ()
    for phase, load in zip(GATHER, loads):
        got = [flipped(part, *pairs) for part, pairs in zip(own, (phase, phase[::-1]))]
        weights = tuple(load(*own))
        if weights:
            got, weights = lax.optimization_barrier((got, weights))
        loaded += weights
        own = [stack(part, add) for part, add in zip(own, got)]
    gate, up, second = loaded
    odd = place[0] % 2
    own = [jnp.where(odd == i, part, regroup(part, 4, 2)) for i, part in enumerate(own)]
    other = [flipped(part, CORE, CORE) for part in own]

    outs = pair_rows(place, own, other, gate, up, second, down, down_shared, share)

    totals = [[own, flipped(other, CORE, CORE)] for own, other in zip(outs[:2], outs[2:])]
    for phase in SCATTER:
        for i, bits in enumerate(phase):
            total = totals[i]
            half = total[0].shape[0] // 2
            sent = f32_sum(*(t[half:] for t in total)).astype(BF16)
            totals[i] = [f32_sum(*(t[:half] for t in total)), flipped(sent, bits, bits)]
    return jnp.concatenate([f32_sum(*total).astype(BF16) for total in totals], axis=1)


def solution(mesh):
    in_specs = (
        P(("rep", "node", "local"), None),
        P(("rep", "node", "local"), None),
        P(("rep", "node", "local"), None),
        P("node", None, "local"),
        P("node", None, "local"),
        P("node", "local", None),
        P(None, "local"),
        P(None, "local"),
        P("local", None),
    )
    out_specs = P(("rep", "node", "local"), None)
    return jax.shard_map(
        per_device, mesh=mesh, in_specs=in_specs, out_specs=out_specs, check_vma=False
    )
```

```python
import functools

import jax
import jax.numpy as jnp
from jax import lax
from jax.experimental import pallas as pl
from jax.experimental.pallas import tpu as pltpu
from jax.sharding import PartitionSpec as P

LANES = 128
ROW_BLOCK = 128
F32 = jnp.float32
BF16 = jnp.bfloat16
VMEM_SPEC = pl.BlockSpec(memory_space=pltpu.VMEM)
SMEM_SPEC = pl.BlockSpec(memory_space=pltpu.SMEM)
ANY_SPEC = pl.BlockSpec(memory_space=pl.ANY)


def in_hbm(value):
    return pltpu.with_memory_space_constraint(value, pltpu.HBM)


def run_copies(copies):
    for copy in copies:
        copy.start()
    for copy in copies:
        copy.wait()


def after(value, *done):
    return lax.optimization_barrier((value, *done))[0]


def pack_kernel(tokens_ref, groups_ref, weights_ref, packed_ref):
    rows, width = tokens_ref.shape
    packed_ref[:, :width] = tokens_ref[...]
    groups = groups_ref[...].T
    weights = weights_ref[...].astype(F32).T
    lane = lax.broadcasted_iota(jnp.int32, (rows, LANES), 1)
    dense = jnp.zeros((rows, LANES), F32)
    for k in range(groups.shape[1]):
        dense += jnp.where(lane == groups[:, k : k + 1], weights[:, k : k + 1], 0.0)
    packed_ref[:, width:] = dense.astype(BF16)


def pack_rows(tokens, group_ids, route_weights):
    rows, width = tokens.shape
    return pl.pallas_call(
        pack_kernel,
        out_specs=VMEM_SPEC,
        out_shape=pltpu.VMEM((rows, width + LANES), BF16),
        name="pack_rows",
    )(tokens, group_ids.T, route_weights.T)


def weight_copies(share, place_ref, routed_ref, shared_ref, out_ref, sems, parts):
    width, hidden = routed_ref.shape
    column = pl.multiple_of((place_ref[0] // share) * LANES, LANES)
    piece = width // parts
    copies = []
    for i in range(parts):
        at = pl.ds(i * piece, piece)
        for source, lower, size in (
            (routed_ref.at[at, :], 0, hidden),
            (shared_ref.at[at, pl.ds(column, LANES)], hidden, LANES),
        ):
            copies.append(
                pltpu.make_async_copy(source, out_ref.at[at, pl.ds(lower, size)], sems.at[len(copies)])
            )
    return copies


def load_kernel(share, place_ref, routed_ref, shared_ref, out_ref, sems):
    run_copies(weight_copies(share, place_ref, routed_ref, shared_ref, out_ref, sems, sems.shape[0] // 2))


def load_weights(place, routed, shared, share):
    width, hidden = routed.shape
    shape = (width, hidden + LANES)
    return pl.pallas_call(
        functools.partial(load_kernel, share),
        in_specs=[SMEM_SPEC] + [ANY_SPEC] * 2,
        out_specs=VMEM_SPEC,
        out_shape=pltpu.VMEM(shape, BF16),
        scratch_shapes=[pltpu.SemaphoreType.DMA((8,))],
        cost_estimate=pl.CostEstimate(flops=0, bytes_accessed=4 * shape[0] * shape[1], transcendentals=0),
        compiler_params=pltpu.CompilerParams(vmem_limit_bytes=1 << 20),
        name="load_weights",
    )(place, in_hbm(routed), in_hbm(shared))


def silu(v):
    return v / (1.0 + jnp.exp(-v))


def row_weight(node, dense):
    lane = lax.broadcasted_iota(jnp.int32, dense.shape, 1)
    return jnp.sum(jnp.where(lane == node, dense.astype(F32), 0.0), axis=1, keepdims=True)


DOWN_PARTS = 4


def down_scratch(rows, hidden, width):
    return [
        pltpu.VMEM((rows, hidden + LANES), BF16),
        pltpu.VMEM((hidden + LANES, width), BF16),
        pltpu.SemaphoreType.DMA((2 * DOWN_PARTS,)),
    ]


def down_copies(share, place_ref, down_ref, sdown_ref, second, sems):
    hidden, width = down_ref.shape
    column = pl.multiple_of((place_ref[0] // share) * LANES, LANES)
    piece = width // DOWN_PARTS
    groups = []
    for i in range(DOWN_PARTS):
        at = pl.ds(i * piece, piece)
        groups.append(
            [
                pltpu.make_async_copy(down_ref.at[:, at], second.at[pl.ds(0, hidden), at], sems.at[2 * i]),
                pltpu.make_async_copy(
                    sdown_ref.at[pl.ds(column, LANES), at],
                    second.at[pl.ds(hidden, LANES), at],
                    sems.at[2 * i + 1],
                ),
            ]
        )
    return groups


def start_group(groups, i):
    for copy in groups[i]:
        copy.start()


def wait_group(groups, i):
    for copy in groups[i]:
        copy.wait()


def shared_units(share, node, gate, up):
    shared = silu(gate) * up
    if share > 1:
        lane = lax.broadcasted_iota(jnp.int32, shared.shape, 1)
        shared = jnp.where(lane // (LANES // share) == node % share, shared, 0.0)
    return shared.astype(BF16)


def tiles_of(units):
    tile = 2 * LANES
    return [slice(at, min(at + tile, units)) for at in range(0, units, tile)]


def ffn(share, place_ref, x, gate_ref, up_ref, act, second, take, store):
    width, units = gate_ref.shape
    hidden = units - LANES
    node = place_ref[0]
    rows = x[:, :width]
    weight = row_weight(node, x[:, width:])
    gate = jnp.dot(rows, gate_ref[...], preferred_element_type=F32)
    up = jnp.dot(rows, up_ref[...], preferred_element_type=F32)
    act[:, :hidden] = (silu(gate[:, :hidden]) * up[:, :hidden] * weight).astype(BF16)
    act[:, hidden:] = shared_units(share, node, gate[:, hidden:], up[:, hidden:])
    piece = width // DOWN_PARTS
    for i in range(DOWN_PARTS):
        at = slice(i * piece, (i + 1) * piece)
        take(i)
        store(at, jnp.dot(act[...], second[:, at], preferred_element_type=F32))


def regroup(value, outer, inner):
    rows = value.shape[0] // (outer * inner)
    return jnp.concatenate(
        [
            value[(o * inner + i) * rows : (o * inner + i + 1) * rows]
            for i in range(inner)
            for o in range(outer)
        ],
        axis=0,
    )


def swap_quarters(value):
    quarter = value.shape[0] // 4
    return jnp.concatenate([value[i * quarter : (i + 1) * quarter] for i in (0, 2, 1, 3)], axis=0)


DOWN_ROWS = 128


def down_range_copies(share, place_ref, down_ref, sdown_ref, out_ref, lower, sems):
    hidden = down_ref.shape[0]
    column = pl.multiple_of((place_ref[0] // share) * LANES, LANES)
    columns = pl.ds(lower, out_ref.shape[1])
    copies = []
    for at in range(0, hidden + LANES, DOWN_ROWS):
        if at < hidden:
            source = down_ref.at[pl.ds(at, DOWN_ROWS), columns]
        else:
            source = sdown_ref.at[pl.ds(column + (at - hidden), DOWN_ROWS), columns]
        copies.append(
            pltpu.make_async_copy(source, out_ref.at[pl.ds(at, DOWN_ROWS), :], sems.at[len(copies)])
        )
    return copies


def load_both_kernel(
    share, lower, place_ref, routed_ref, shared_ref, down_ref, sdown_ref, out_ref, down_out_ref, sems
):
    parts = 4
    run_copies(
        weight_copies(share, place_ref, routed_ref, shared_ref, out_ref, sems, parts)
        + down_range_copies(
            share, place_ref, down_ref, sdown_ref, down_out_ref, lower, sems.at[2 * parts :]
        )
    )


def load_both(place, routed, shared, down, sdown, lower, columns, share):
    width, hidden = routed.shape
    units = hidden + LANES
    return pl.pallas_call(
        functools.partial(load_both_kernel, share, lower),
        in_specs=[SMEM_SPEC] + [ANY_SPEC] * 4,
        out_specs=[VMEM_SPEC] * 2,
        out_shape=[pltpu.VMEM((width, units), BF16), pltpu.VMEM((units, columns), BF16)],
        scratch_shapes=[pltpu.SemaphoreType.DMA((8 + units // DOWN_ROWS,))],
        cost_estimate=pl.CostEstimate(
            flops=0, bytes_accessed=4 * units * (width + columns), transcendentals=0
        ),
        compiler_params=pltpu.CompilerParams(vmem_limit_bytes=1 << 20),
        name="load_both",
    )(place, *(in_hbm(w) for w in (routed, shared, down, sdown)))


def load_down_kernel(share, lower, place_ref, down_ref, sdown_ref, out_ref, sems):
    run_copies(down_range_copies(share, place_ref, down_ref, sdown_ref, out_ref, lower, sems))


def load_down(place, down, sdown, lower, columns, share):
    units = down.shape[0] + LANES
    return pl.pallas_call(
        functools.partial(load_down_kernel, share, lower),
        in_specs=[SMEM_SPEC] + [ANY_SPEC] * 2,
        out_specs=VMEM_SPEC,
        out_shape=pltpu.VMEM((units, columns), BF16),
        scratch_shapes=[pltpu.SemaphoreType.DMA((units // DOWN_ROWS,))],
        cost_estimate=pl.CostEstimate(flops=0, bytes_accessed=4 * units * columns, transcendentals=0),
        compiler_params=pltpu.CompilerParams(vmem_limit_bytes=1 << 20),
        name="load_down",
    )(place, in_hbm(down), in_hbm(sdown))


def late_half_kernel(place_ref, own_ref, other_ref, gate_ref, up_ref, gate_acc_ref, up_acc_ref, weight_ref, x):
    width, units = gate_ref.shape
    half, columns = own_ref.shape
    cut = width + LANES - columns
    x[:half, :] = own_ref[...]
    x[half:, :] = other_ref[...]
    rows = x[:, : width - cut]
    for at in tiles_of(units):
        gate_acc_ref[:, at] = jnp.dot(rows, gate_ref[cut:, at], preferred_element_type=F32)
        up_acc_ref[:, at] = jnp.dot(rows, up_ref[cut:, at], preferred_element_type=F32)
    weight = row_weight(place_ref[0], x[:, width - cut :])
    weight_ref[...] = jnp.broadcast_to(weight, weight_ref.shape)


def early_half_kernel(
    share, place_ref, own_ref, other_ref, gate_ref, up_ref, gate_acc_ref, up_acc_ref, weight_ref, second_ref,
    own_out_ref, other_out_ref, act_ref, x,
):
    half, cut = own_ref.shape
    units = gate_ref.shape[1]
    hidden = units - LANES
    x[:half, :] = own_ref[...]
    x[half:, :] = other_ref[...]
    rows = x[...]
    weight = weight_ref[:, :1]
    for at in tiles_of(units):
        gate = gate_acc_ref[:, at] + jnp.dot(rows, gate_ref[:cut, at], preferred_element_type=F32)
        up = up_acc_ref[:, at] + jnp.dot(rows, up_ref[:cut, at], preferred_element_type=F32)
        if at.start < hidden:
            act_ref[:, at] = (silu(gate) * up * weight).astype(BF16)
        else:
            act_ref[:, at] = shared_units(share, place_ref[0], gate, up)
    piece = cut // 2
    for i in range(2):
        at = slice(i * piece, (i + 1) * piece)
        total = jnp.dot(act_ref[...], second_ref[:, at], preferred_element_type=F32).astype(BF16)
        own_out_ref[:, at] = total[:half]
        other_out_ref[:, at] = total[half:]


def last_half_kernel(act_ref, third_ref, fourth_ref, own_out_ref, other_out_ref):
    half, columns = own_out_ref.shape
    piece = columns // 2
    for i, later_ref in enumerate((third_ref, fourth_ref)):
        at = slice(i * piece, (i + 1) * piece)
        total = jnp.dot(act_ref[...], later_ref[...], preferred_element_type=F32).astype(BF16)
        own_out_ref[:, at] = swap_quarters(total[:half])
        other_out_ref[:, at] = swap_quarters(total[half:])


def estimate(rows, depth, columns):
    return pl.CostEstimate(
        flops=2 * rows * depth * columns, bytes_accessed=2 * depth * columns, transcendentals=0
    )


def pair_rows(place, own, other, gate, up, second, third, fourth, share):
    half, cut = own[0].shape
    width, units = gate.shape
    partial = pl.pallas_call(
        late_half_kernel,
        in_specs=[SMEM_SPEC] + [VMEM_SPEC] * 4,
        out_specs=[VMEM_SPEC] * 3,
        out_shape=[pltpu.VMEM((2 * half, columns), F32) for columns in (units, units, LANES)],
        scratch_shapes=[pltpu.VMEM((2 * half, own[1].shape[1]), BF16)],
        cost_estimate=estimate(2 * half, width - cut, 2 * units),
        compiler_params=pltpu.CompilerParams(vmem_limit_bytes=10 << 20),
        name="late_half",
    )(place, own[1], other[1], gate, up)
    own_out, other_out, act = pl.pallas_call(
        functools.partial(early_half_kernel, share),
        in_specs=[SMEM_SPEC] + [VMEM_SPEC] * 8,
        out_specs=[VMEM_SPEC] * 3,
        out_shape=[
            pltpu.VMEM((half, cut), BF16),
            pltpu.VMEM((half, cut), BF16),
            pltpu.VMEM((2 * half, units), BF16),
        ],
        scratch_shapes=[pltpu.VMEM((2 * half, cut), BF16)],
        cost_estimate=estimate(2 * half, cut, 3 * units),
        compiler_params=pltpu.CompilerParams(vmem_limit_bytes=10 << 20),
        name="early_half",
    )(place, own[0], other[0], gate, up, *partial, second)
    last = pl.pallas_call(
        last_half_kernel,
        in_specs=[VMEM_SPEC] * 3,
        out_specs=[VMEM_SPEC] * 2,
        out_shape=[pltpu.VMEM((half, width - cut), BF16)] * 2,
        cost_estimate=estimate(2 * half, width - cut, units),
        compiler_params=pltpu.CompilerParams(vmem_limit_bytes=10 << 20),
        name="last_half",
    )(act, third, fourth)
    return own_out, last[0], other_out, last[1]


def block_kernel(
    share, place_ref, x_ref, gate_ref, up_ref, down_ref, sdown_ref, out_ref, act, second, sems
):
    groups = down_copies(share, place_ref, down_ref, sdown_ref, second, sems)

    @pl.when(pl.program_id(0) == 0)
    def _():
        for i in range(DOWN_PARTS):
            start_group(groups, i)
        for i in range(DOWN_PARTS):
            wait_group(groups, i)

    def store(at, total):
        out_ref[:, at] = total.astype(BF16)

    ffn(share, place_ref, x_ref, gate_ref, up_ref, act, second, lambda i: None, store)


def block_rows(place, x, gate, up, down, sdown, share):
    rows, packed = x.shape
    hidden, width = down.shape
    block = min(rows, ROW_BLOCK)
    return pl.pallas_call(
        functools.partial(block_kernel, share),
        grid=(rows // block,),
        in_specs=[SMEM_SPEC, pl.BlockSpec((block, packed), lambda i: (i, 0))] + [VMEM_SPEC] * 2 + [ANY_SPEC] * 2,
        out_specs=pl.BlockSpec((block, width), lambda i: (i, 0)),
        out_shape=jax.ShapeDtypeStruct((rows, width), BF16),
        scratch_shapes=down_scratch(block, hidden, width),
        compiler_params=pltpu.CompilerParams(vmem_limit_bytes=24 << 20),
        name="block_rows",
    )(place, x, gate, up, in_hbm(down), in_hbm(sdown))


def f32_sum(*terms):
    return functools.reduce(lambda a, b: a + b, (t.astype(F32) for t in terms))


def flipped(value, even, odd):
    pairs = []
    for node in range(4):
        for local in range(4):
            node_bits, local_bits = odd if node % 2 else even
            pairs.append((node * 4 + local, (node ^ node_bits) * 4 + (local ^ local_bits)))
    return lax.ppermute(value, ("node", "local"), pairs)


X, Z1, Z2, CORE = (2, 0), (0, 1), (0, 2), (1, 0)
GATHER = ((Z2, X), (Z1, Z2), (X, Z1))
SCATTER = ((X, Z1), (Z1, X), (Z2, Z2))


def stack(*values):
    return jnp.concatenate(values, axis=0)


def per_device(
    tokens,
    group_ids,
    route_weights,
    gate_experts,
    up_experts,
    down_experts,
    gate_shared,
    up_shared,
    down_shared,
):
    rows, width = tokens.shape
    node_count = lax.axis_size("node")
    local_count = lax.axis_size("local")
    share = max(1, LANES * node_count // gate_shared.shape[1])
    place = lax.axis_index("node").reshape(1)
    gate, up, down = gate_experts[0], up_experts[0], down_experts[0]
    packed = pack_rows(tokens, group_ids, route_weights)

    if node_count != 4 or local_count != 4:
        x = lax.all_gather(packed, ("node", "local"), axis=0, tiled=True)
        gate = load_weights(place, gate, gate_shared, share)
        up = load_weights(place, up, up_shared, share)
        part = block_rows(place, x, gate, up, down, down_shared, share)
        return lax.psum_scatter(part, ("node", "local"), scatter_dimension=0, tiled=True)

    cut = width // 2
    own = [packed[:, :cut], packed[:, cut:]]
    quarter = (width - cut) // 2
    loads = (
        lambda *ready: (),
        lambda *ready: load_both(
            after(place, *ready), gate, gate_shared, down, down_shared, cut, quarter, share
        ),
        lambda *ready: load_both(after(place, *ready), up, up_shared, down, down_shared, 0, cut, share),
    )
    loaded = ()
    for phase, load in zip(GATHER, loads):
        got = [flipped(part, *pairs) for part, pairs in zip(own, (phase, phase[::-1]))]
        weights = tuple(load(*own))
        if weights:
            got, weights = lax.optimization_barrier((got, weights))
        loaded += weights
        own = [stack(part, add) for part, add in zip(own, got)]
    gate, third, up, second = loaded
    odd = place[0] % 2
    own = [jnp.where(odd == i, part, regroup(part, 4, 2)) for i, part in enumerate(own)]
    other = [flipped(part, CORE, CORE) for part in own]

    fourth = load_down(after(place, *own), down, down_shared, cut + quarter, quarter, share)
    other[1], fourth = lax.optimization_barrier((other[1], fourth))

    outs = pair_rows(place, own, other, gate, up, second, third, fourth, share)

    totals = [[own, flipped(other, CORE, CORE)] for own, other in zip(outs[:2], outs[2:])]
    for phase in SCATTER:
        for i, bits in enumerate(phase):
            total = totals[i]
            half = total[0].shape[0] // 2
            sent = f32_sum(*(t[half:] for t in total)).astype(BF16)
            totals[i] = [f32_sum(*(t[:half] for t in total)), flipped(sent, bits, bits)]
    return jnp.concatenate([f32_sum(*total).astype(BF16) for total in totals], axis=1)


def solution(mesh):
    in_specs = (
        P(("rep", "node", "local"), None),
        P(("rep", "node", "local"), None),
        P(("rep", "node", "local"), None),
        P("node", None, "local"),
        P("node", None, "local"),
        P("node", "local", None),
        P(None, "local"),
        P(None, "local"),
        P("local", None),
    )
    out_specs = P(("rep", "node", "local"), None)
    return jax.shard_map(
        per_device, mesh=mesh, in_specs=in_specs, out_specs=out_specs, check_vma=False
    )
```

```python
import functools

import jax
import jax.numpy as jnp
from jax import lax
from jax.experimental import pallas as pl
from jax.experimental.pallas import tpu as pltpu
from jax.sharding import PartitionSpec as P

LANES = 128
ROW_BLOCK = 128
F32 = jnp.float32
BF16 = jnp.bfloat16
VMEM_SPEC = pl.BlockSpec(memory_space=pltpu.VMEM)
SMEM_SPEC = pl.BlockSpec(memory_space=pltpu.SMEM)
ANY_SPEC = pl.BlockSpec(memory_space=pl.ANY)


def in_hbm(value):
    return pltpu.with_memory_space_constraint(value, pltpu.HBM)


def run_copies(copies):
    for copy in copies:
        copy.start()
    for copy in copies:
        copy.wait()


def after(value, *done):
    return lax.optimization_barrier((value, *done))[0]


def pack_kernel(tokens_ref, groups_ref, weights_ref, packed_ref):
    rows, width = tokens_ref.shape
    packed_ref[:, :width] = tokens_ref[...]
    groups = groups_ref[...].T
    weights = weights_ref[...].astype(F32).T
    lane = lax.broadcasted_iota(jnp.int32, (rows, LANES), 1)
    dense = jnp.zeros((rows, LANES), F32)
    for k in range(groups.shape[1]):
        dense += jnp.where(lane == groups[:, k : k + 1], weights[:, k : k + 1], 0.0)
    packed_ref[:, width:] = dense.astype(BF16)


def pack_rows(tokens, group_ids, route_weights):
    rows, width = tokens.shape
    return pl.pallas_call(
        pack_kernel,
        out_specs=VMEM_SPEC,
        out_shape=pltpu.VMEM((rows, width + LANES), BF16),
        name="pack_rows",
    )(tokens, group_ids.T, route_weights.T)


def weight_copies(share, place_ref, routed_ref, shared_ref, out_ref, sems, parts):
    width, hidden = routed_ref.shape
    column = pl.multiple_of((place_ref[0] // share) * LANES, LANES)
    piece = width // parts
    copies = []
    for i in range(parts):
        at = pl.ds(i * piece, piece)
        for source, lower, size in (
            (routed_ref.at[at, :], 0, hidden),
            (shared_ref.at[at, pl.ds(column, LANES)], hidden, LANES),
        ):
            copies.append(
                pltpu.make_async_copy(source, out_ref.at[at, pl.ds(lower, size)], sems.at[len(copies)])
            )
    return copies


def load_kernel(share, place_ref, routed_ref, shared_ref, out_ref, sems):
    run_copies(weight_copies(share, place_ref, routed_ref, shared_ref, out_ref, sems, sems.shape[0] // 2))


def load_weights(place, routed, shared, share):
    width, hidden = routed.shape
    shape = (width, hidden + LANES)
    return pl.pallas_call(
        functools.partial(load_kernel, share),
        in_specs=[SMEM_SPEC] + [ANY_SPEC] * 2,
        out_specs=VMEM_SPEC,
        out_shape=pltpu.VMEM(shape, BF16),
        scratch_shapes=[pltpu.SemaphoreType.DMA((8,))],
        cost_estimate=pl.CostEstimate(flops=0, bytes_accessed=4 * shape[0] * shape[1], transcendentals=0),
        compiler_params=pltpu.CompilerParams(vmem_limit_bytes=1 << 20),
        name="load_weights",
    )(place, in_hbm(routed), in_hbm(shared))


def silu(v):
    return v / (1.0 + jnp.exp(-v))


def row_weight(node, dense):
    lane = lax.broadcasted_iota(jnp.int32, dense.shape, 1)
    return jnp.sum(jnp.where(lane == node, dense.astype(F32), 0.0), axis=1, keepdims=True)


DOWN_PARTS = 4


def down_scratch(rows, hidden, width):
    return [
        pltpu.VMEM((rows, hidden + LANES), BF16),
        pltpu.VMEM((hidden + LANES, width), BF16),
        pltpu.SemaphoreType.DMA((2 * DOWN_PARTS,)),
    ]


def down_copies(share, place_ref, down_ref, sdown_ref, second, sems):
    hidden, width = down_ref.shape
    column = pl.multiple_of((place_ref[0] // share) * LANES, LANES)
    piece = width // DOWN_PARTS
    groups = []
    for i in range(DOWN_PARTS):
        at = pl.ds(i * piece, piece)
        groups.append(
            [
                pltpu.make_async_copy(down_ref.at[:, at], second.at[pl.ds(0, hidden), at], sems.at[2 * i]),
                pltpu.make_async_copy(
                    sdown_ref.at[pl.ds(column, LANES), at],
                    second.at[pl.ds(hidden, LANES), at],
                    sems.at[2 * i + 1],
                ),
            ]
        )
    return groups


def start_group(groups, i):
    for copy in groups[i]:
        copy.start()


def wait_group(groups, i):
    for copy in groups[i]:
        copy.wait()


def shared_units(share, node, gate, up):
    shared = silu(gate) * up
    if share > 1:
        lane = lax.broadcasted_iota(jnp.int32, shared.shape, 1)
        shared = jnp.where(lane // (LANES // share) == node % share, shared, 0.0)
    return shared.astype(BF16)


def tiles_of(units):
    tile = 2 * LANES
    return [slice(at, min(at + tile, units)) for at in range(0, units, tile)]


def ffn(share, place_ref, x, gate_ref, up_ref, act, second, take, store):
    width, units = gate_ref.shape
    hidden = units - LANES
    node = place_ref[0]
    rows = x[:, :width]
    weight = row_weight(node, x[:, width:])
    gate = jnp.dot(rows, gate_ref[...], preferred_element_type=F32)
    up = jnp.dot(rows, up_ref[...], preferred_element_type=F32)
    act[:, :hidden] = (silu(gate[:, :hidden]) * up[:, :hidden] * weight).astype(BF16)
    act[:, hidden:] = shared_units(share, node, gate[:, hidden:], up[:, hidden:])
    piece = width // DOWN_PARTS
    for i in range(DOWN_PARTS):
        at = slice(i * piece, (i + 1) * piece)
        take(i)
        store(at, jnp.dot(act[...], second[:, at], preferred_element_type=F32))


def regroup(value, outer, inner):
    rows = value.shape[0] // (outer * inner)
    return jnp.concatenate(
        [
            value[(o * inner + i) * rows : (o * inner + i + 1) * rows]
            for i in range(inner)
            for o in range(outer)
        ],
        axis=0,
    )


def swap_quarters(value):
    quarter = value.shape[0] // 4
    return jnp.concatenate([value[i * quarter : (i + 1) * quarter] for i in (0, 2, 1, 3)], axis=0)


DOWN_ROWS = 128


def down_range_copies(share, place_ref, down_ref, sdown_ref, out_ref, lower, sems):
    hidden = down_ref.shape[0]
    column = pl.multiple_of((place_ref[0] // share) * LANES, LANES)
    columns = pl.ds(lower, out_ref.shape[1])
    copies = []
    for at in range(0, hidden + LANES, DOWN_ROWS):
        if at < hidden:
            source = down_ref.at[pl.ds(at, DOWN_ROWS), columns]
        else:
            source = sdown_ref.at[pl.ds(column + (at - hidden), DOWN_ROWS), columns]
        copies.append(
            pltpu.make_async_copy(source, out_ref.at[pl.ds(at, DOWN_ROWS), :], sems.at[len(copies)])
        )
    return copies


def load_both_kernel(
    share, lower, place_ref, routed_ref, shared_ref, down_ref, sdown_ref, out_ref, down_out_ref, sems
):
    parts = 4
    run_copies(
        weight_copies(share, place_ref, routed_ref, shared_ref, out_ref, sems, parts)
        + down_range_copies(
            share, place_ref, down_ref, sdown_ref, down_out_ref, lower, sems.at[2 * parts :]
        )
    )


def load_both(place, routed, shared, down, sdown, lower, columns, share):
    width, hidden = routed.shape
    units = hidden + LANES
    return pl.pallas_call(
        functools.partial(load_both_kernel, share, lower),
        in_specs=[SMEM_SPEC] + [ANY_SPEC] * 4,
        out_specs=[VMEM_SPEC] * 2,
        out_shape=[pltpu.VMEM((width, units), BF16), pltpu.VMEM((units, columns), BF16)],
        scratch_shapes=[pltpu.SemaphoreType.DMA((8 + units // DOWN_ROWS,))],
        cost_estimate=pl.CostEstimate(
            flops=0, bytes_accessed=4 * units * (width + columns), transcendentals=0
        ),
        compiler_params=pltpu.CompilerParams(vmem_limit_bytes=1 << 20),
        name="load_both",
    )(place, *(in_hbm(w) for w in (routed, shared, down, sdown)))


def load_down_kernel(share, lower, place_ref, down_ref, sdown_ref, out_ref, sems):
    run_copies(down_range_copies(share, place_ref, down_ref, sdown_ref, out_ref, lower, sems))


def load_down(place, down, sdown, lower, columns, share):
    units = down.shape[0] + LANES
    return pl.pallas_call(
        functools.partial(load_down_kernel, share, lower),
        in_specs=[SMEM_SPEC] + [ANY_SPEC] * 2,
        out_specs=VMEM_SPEC,
        out_shape=pltpu.VMEM((units, columns), BF16),
        scratch_shapes=[pltpu.SemaphoreType.DMA((units // DOWN_ROWS,))],
        cost_estimate=pl.CostEstimate(flops=0, bytes_accessed=4 * units * columns, transcendentals=0),
        compiler_params=pltpu.CompilerParams(vmem_limit_bytes=1 << 20),
        name="load_down",
    )(place, in_hbm(down), in_hbm(sdown))


def late_half_kernel(place_ref, own_ref, other_ref, gate_ref, up_ref, gate_acc_ref, up_acc_ref, weight_ref, x):
    width, units = gate_ref.shape
    half, columns = own_ref.shape
    cut = width + LANES - columns
    x[:half, :] = own_ref[...]
    x[half:, :] = other_ref[...]
    rows = x[:, : width - cut]
    for at in tiles_of(units):
        gate_acc_ref[:, at] = jnp.dot(rows, gate_ref[cut:, at], preferred_element_type=F32)
        up_acc_ref[:, at] = jnp.dot(rows, up_ref[cut:, at], preferred_element_type=F32)
    weight = row_weight(place_ref[0], x[:, width - cut :])
    weight_ref[...] = jnp.broadcast_to(weight, weight_ref.shape)


def early_half_kernel(
    share, place_ref, own_ref, other_ref, gate_ref, up_ref, gate_acc_ref, up_acc_ref, weight_ref, second_ref,
    own_out_ref, other_out_ref, act_ref, x,
):
    half, cut = own_ref.shape
    units = gate_ref.shape[1]
    hidden = units - LANES
    x[:half, :] = own_ref[...]
    x[half:, :] = other_ref[...]
    rows = x[...]
    weight = weight_ref[:, :1]
    for at in tiles_of(units):
        gate = gate_acc_ref[:, at] + jnp.dot(rows, gate_ref[:cut, at], preferred_element_type=F32)
        up = up_acc_ref[:, at] + jnp.dot(rows, up_ref[:cut, at], preferred_element_type=F32)
        if at.start < hidden:
            act_ref[:, at] = (silu(gate) * up * weight).astype(BF16)
        else:
            act_ref[:, at] = shared_units(share, place_ref[0], gate, up)
    piece = cut // 2
    for i in range(2):
        at = slice(i * piece, (i + 1) * piece)
        total = jnp.dot(act_ref[...], second_ref[:, at], preferred_element_type=F32).astype(BF16)
        own_out_ref[:, at] = total[:half]
        other_out_ref[:, at] = total[half:]


def last_half_kernel(act_ref, later_ref, own_out_ref, other_out_ref):
    half, columns = own_out_ref.shape
    piece = columns // 2
    for i in range(2):
        at = slice(i * piece, (i + 1) * piece)
        total = jnp.dot(act_ref[...], later_ref[:, at], preferred_element_type=F32).astype(BF16)
        own_out_ref[:, at] = swap_quarters(total[:half])
        other_out_ref[:, at] = swap_quarters(total[half:])


def estimate(rows, depth, columns):
    return pl.CostEstimate(
        flops=2 * rows * depth * columns, bytes_accessed=2 * depth * columns, transcendentals=0
    )


def pair_rows(place, own, other, gate, up, second, later, share):
    half, cut = own[0].shape
    width, units = gate.shape
    partial = pl.pallas_call(
        late_half_kernel,
        in_specs=[SMEM_SPEC] + [VMEM_SPEC] * 4,
        out_specs=[VMEM_SPEC] * 3,
        out_shape=[pltpu.VMEM((2 * half, columns), F32) for columns in (units, units, LANES)],
        scratch_shapes=[pltpu.VMEM((2 * half, own[1].shape[1]), BF16)],
        cost_estimate=estimate(2 * half, width - cut, 2 * units),
        compiler_params=pltpu.CompilerParams(vmem_limit_bytes=10 << 20),
        name="late_half",
    )(place, own[1], other[1], gate, up)
    own_out, other_out, act = pl.pallas_call(
        functools.partial(early_half_kernel, share),
        in_specs=[SMEM_SPEC] + [VMEM_SPEC] * 8,
        out_specs=[VMEM_SPEC] * 3,
        out_shape=[
            pltpu.VMEM((half, cut), BF16),
            pltpu.VMEM((half, cut), BF16),
            pltpu.VMEM((2 * half, units), BF16),
        ],
        scratch_shapes=[pltpu.VMEM((2 * half, cut), BF16)],
        cost_estimate=estimate(2 * half, cut, 3 * units),
        compiler_params=pltpu.CompilerParams(vmem_limit_bytes=10 << 20),
        name="early_half",
    )(place, own[0], other[0], gate, up, *partial, second)
    last = pl.pallas_call(
        last_half_kernel,
        in_specs=[VMEM_SPEC] * 2,
        out_specs=[VMEM_SPEC] * 2,
        out_shape=[pltpu.VMEM((half, width - cut), BF16)] * 2,
        cost_estimate=estimate(2 * half, width - cut, units),
        compiler_params=pltpu.CompilerParams(vmem_limit_bytes=10 << 20),
        name="last_half",
    )(act, later)
    return own_out, last[0], other_out, last[1]


def block_kernel(
    share, place_ref, x_ref, gate_ref, up_ref, down_ref, sdown_ref, out_ref, act, second, sems
):
    groups = down_copies(share, place_ref, down_ref, sdown_ref, second, sems)

    @pl.when(pl.program_id(0) == 0)
    def _():
        for i in range(DOWN_PARTS):
            start_group(groups, i)
        for i in range(DOWN_PARTS):
            wait_group(groups, i)

    def store(at, total):
        out_ref[:, at] = total.astype(BF16)

    ffn(share, place_ref, x_ref, gate_ref, up_ref, act, second, lambda i: None, store)


def block_rows(place, x, gate, up, down, sdown, share):
    rows, packed = x.shape
    hidden, width = down.shape
    block = min(rows, ROW_BLOCK)
    return pl.pallas_call(
        functools.partial(block_kernel, share),
        grid=(rows // block,),
        in_specs=[SMEM_SPEC, pl.BlockSpec((block, packed), lambda i: (i, 0))] + [VMEM_SPEC] * 2 + [ANY_SPEC] * 2,
        out_specs=pl.BlockSpec((block, width), lambda i: (i, 0)),
        out_shape=jax.ShapeDtypeStruct((rows, width), BF16),
        scratch_shapes=down_scratch(block, hidden, width),
        compiler_params=pltpu.CompilerParams(vmem_limit_bytes=24 << 20),
        name="block_rows",
    )(place, x, gate, up, in_hbm(down), in_hbm(sdown))


def f32_sum(*terms):
    return functools.reduce(lambda a, b: a + b, (t.astype(F32) for t in terms))


def flipped(value, even, odd):
    pairs = []
    for node in range(4):
        for local in range(4):
            node_bits, local_bits = odd if node % 2 else even
            pairs.append((node * 4 + local, (node ^ node_bits) * 4 + (local ^ local_bits)))
    return lax.ppermute(value, ("node", "local"), pairs)


X, Z1, Z2, CORE = (2, 0), (0, 1), (0, 2), (1, 0)
GATHER = ((Z2, X), (Z1, Z2), (X, Z1))
SCATTER = ((X, Z1), (Z1, X), (Z2, Z2))


def stack(*values):
    return jnp.concatenate(values, axis=0)


def per_device(
    tokens,
    group_ids,
    route_weights,
    gate_experts,
    up_experts,
    down_experts,
    gate_shared,
    up_shared,
    down_shared,
):
    rows, width = tokens.shape
    node_count = lax.axis_size("node")
    local_count = lax.axis_size("local")
    share = max(1, LANES * node_count // gate_shared.shape[1])
    place = lax.axis_index("node").reshape(1)
    gate, up, down = gate_experts[0], up_experts[0], down_experts[0]
    packed = pack_rows(tokens, group_ids, route_weights)

    if node_count != 4 or local_count != 4:
        x = lax.all_gather(packed, ("node", "local"), axis=0, tiled=True)
        gate = load_weights(place, gate, gate_shared, share)
        up = load_weights(place, up, up_shared, share)
        part = block_rows(place, x, gate, up, down, down_shared, share)
        return lax.psum_scatter(part, ("node", "local"), scatter_dimension=0, tiled=True)

    cut = width // 2
    own = [packed[:, :cut], packed[:, cut:]]
    loads = (
        lambda *ready: (load_down(after(place, *ready), down, down_shared, cut, width - cut, share),),
        lambda *ready: (load_weights(after(place, *ready), gate, gate_shared, share),),
        lambda *ready: load_both(after(place, *ready), up, up_shared, down, down_shared, 0, cut, share),
    )
    loaded = ()
    for number, (phase, load) in enumerate(zip(GATHER, loads)):
        got = [flipped(part, *pairs) for part, pairs in zip(own, (phase[::-1], phase))]
        weights = tuple(load(*own))
        if number == 0:
            got[1], weights = lax.optimization_barrier((got[1], weights))
        else:
            got, weights = lax.optimization_barrier((got, weights))
        loaded += weights
        own = [stack(part, add) for part, add in zip(own, got)]
    later, gate, up, second = loaded
    odd = place[0] % 2
    own = [jnp.where(odd == 1 - i, part, regroup(part, 4, 2)) for i, part in enumerate(own)]
    other = [flipped(part, CORE, CORE) for part in own]


    outs = pair_rows(place, own, other, gate, up, second, later, share)

    totals = [[own, flipped(other, CORE, CORE)] for own, other in zip(outs[:2], outs[2:])]
    for phase in SCATTER:
        for i, bits in enumerate(phase):
            total = totals[i]
            half = total[0].shape[0] // 2
            sent = f32_sum(*(t[half:] for t in total)).astype(BF16)
            totals[i] = [f32_sum(*(t[:half] for t in total)), flipped(sent, bits, bits)]
    return jnp.concatenate([f32_sum(*total).astype(BF16) for total in totals], axis=1)


def solution(mesh):
    in_specs = (
        P(("rep", "node", "local"), None),
        P(("rep", "node", "local"), None),
        P(("rep", "node", "local"), None),
        P("node", None, "local"),
        P("node", None, "local"),
        P("node", "local", None),
        P(None, "local"),
        P(None, "local"),
        P("local", None),
    )
    out_specs = P(("rep", "node", "local"), None)
    return jax.shard_map(
        per_device, mesh=mesh, in_specs=in_specs, out_specs=out_specs, check_vma=False
    )
```

```python
import functools

import jax
import jax.numpy as jnp
from jax import lax
from jax.experimental import pallas as pl
from jax.experimental.pallas import tpu as pltpu
from jax.sharding import PartitionSpec as P

LANES = 128
ROW_BLOCK = 128
F32 = jnp.float32
BF16 = jnp.bfloat16
VMEM_SPEC = pl.BlockSpec(memory_space=pltpu.VMEM)
SMEM_SPEC = pl.BlockSpec(memory_space=pltpu.SMEM)
ANY_SPEC = pl.BlockSpec(memory_space=pl.ANY)


def in_hbm(value):
    return pltpu.with_memory_space_constraint(value, pltpu.HBM)


def run_copies(copies):
    for copy in copies:
        copy.start()
    for copy in copies:
        copy.wait()


def after(value, *done):
    return lax.optimization_barrier((value, *done))[0]


def pack_kernel(tokens_ref, groups_ref, weights_ref, packed_ref):
    rows, width = tokens_ref.shape
    packed_ref[:, :width] = tokens_ref[...]
    groups = groups_ref[...].T
    weights = weights_ref[...].astype(F32).T
    lane = lax.broadcasted_iota(jnp.int32, (rows, LANES), 1)
    dense = jnp.zeros((rows, LANES), F32)
    for k in range(groups.shape[1]):
        dense += jnp.where(lane == groups[:, k : k + 1], weights[:, k : k + 1], 0.0)
    packed_ref[:, width:] = dense.astype(BF16)


def pack_rows(tokens, group_ids, route_weights):
    rows, width = tokens.shape
    return pl.pallas_call(
        pack_kernel,
        out_specs=VMEM_SPEC,
        out_shape=pltpu.VMEM((rows, width + LANES), BF16),
        name="pack_rows",
    )(tokens, group_ids.T, route_weights.T)


def weight_copies(share, place_ref, routed_ref, shared_ref, out_ref, sems, parts):
    width, hidden = routed_ref.shape
    column = pl.multiple_of((place_ref[0] // share) * LANES, LANES)
    piece = width // parts
    copies = []
    for i in range(parts):
        at = pl.ds(i * piece, piece)
        for source, lower, size in (
            (routed_ref.at[at, :], 0, hidden),
            (shared_ref.at[at, pl.ds(column, LANES)], hidden, LANES),
        ):
            copies.append(
                pltpu.make_async_copy(source, out_ref.at[at, pl.ds(lower, size)], sems.at[len(copies)])
            )
    return copies


def load_kernel(share, place_ref, routed_ref, shared_ref, out_ref, sems):
    run_copies(weight_copies(share, place_ref, routed_ref, shared_ref, out_ref, sems, sems.shape[0] // 2))


def load_weights(place, routed, shared, share):
    width, hidden = routed.shape
    shape = (width, hidden + LANES)
    return pl.pallas_call(
        functools.partial(load_kernel, share),
        in_specs=[SMEM_SPEC] + [ANY_SPEC] * 2,
        out_specs=VMEM_SPEC,
        out_shape=pltpu.VMEM(shape, BF16),
        scratch_shapes=[pltpu.SemaphoreType.DMA((8,))],
        cost_estimate=pl.CostEstimate(flops=0, bytes_accessed=4 * shape[0] * shape[1], transcendentals=0),
        compiler_params=pltpu.CompilerParams(vmem_limit_bytes=1 << 20),
        name="load_weights",
    )(place, in_hbm(routed), in_hbm(shared))


def silu(v):
    return v / (1.0 + jnp.exp(-v))


def row_weight(node, dense):
    lane = lax.broadcasted_iota(jnp.int32, dense.shape, 1)
    return jnp.sum(jnp.where(lane == node, dense.astype(F32), 0.0), axis=1, keepdims=True)


DOWN_PARTS = 4


def down_scratch(rows, hidden, width):
    return [
        pltpu.VMEM((rows, hidden + LANES), BF16),
        pltpu.VMEM((hidden + LANES, width), BF16),
        pltpu.SemaphoreType.DMA((2 * DOWN_PARTS,)),
    ]


def down_copies(share, place_ref, down_ref, sdown_ref, second, sems):
    hidden, width = down_ref.shape
    column = pl.multiple_of((place_ref[0] // share) * LANES, LANES)
    piece = width // DOWN_PARTS
    groups = []
    for i in range(DOWN_PARTS):
        at = pl.ds(i * piece, piece)
        groups.append(
            [
                pltpu.make_async_copy(down_ref.at[:, at], second.at[pl.ds(0, hidden), at], sems.at[2 * i]),
                pltpu.make_async_copy(
                    sdown_ref.at[pl.ds(column, LANES), at],
                    second.at[pl.ds(hidden, LANES), at],
                    sems.at[2 * i + 1],
                ),
            ]
        )
    return groups


def start_group(groups, i):
    for copy in groups[i]:
        copy.start()


def wait_group(groups, i):
    for copy in groups[i]:
        copy.wait()


def shared_units(share, node, gate, up):
    shared = silu(gate) * up
    if share > 1:
        lane = lax.broadcasted_iota(jnp.int32, shared.shape, 1)
        shared = jnp.where(lane // (LANES // share) == node % share, shared, 0.0)
    return shared.astype(BF16)


def tiles_of(units):
    tile = 2 * LANES
    return [slice(at, min(at + tile, units)) for at in range(0, units, tile)]


def ffn(share, place_ref, x, gate_ref, up_ref, act, second, take, store):
    width, units = gate_ref.shape
    hidden = units - LANES
    node = place_ref[0]
    rows = x[:, :width]
    weight = row_weight(node, x[:, width:])
    gate = jnp.dot(rows, gate_ref[...], preferred_element_type=F32)
    up = jnp.dot(rows, up_ref[...], preferred_element_type=F32)
    act[:, :hidden] = (silu(gate[:, :hidden]) * up[:, :hidden] * weight).astype(BF16)
    act[:, hidden:] = shared_units(share, node, gate[:, hidden:], up[:, hidden:])
    piece = width // DOWN_PARTS
    for i in range(DOWN_PARTS):
        at = slice(i * piece, (i + 1) * piece)
        take(i)
        store(at, jnp.dot(act[...], second[:, at], preferred_element_type=F32))


def regroup(value, outer, inner):
    rows = value.shape[0] // (outer * inner)
    return jnp.concatenate(
        [
            value[(o * inner + i) * rows : (o * inner + i + 1) * rows]
            for i in range(inner)
            for o in range(outer)
        ],
        axis=0,
    )


def swap_quarters(value):
    quarter = value.shape[0] // 4
    return jnp.concatenate([value[i * quarter : (i + 1) * quarter] for i in (0, 2, 1, 3)], axis=0)


DOWN_ROWS = 128


def down_range_copies(share, place_ref, down_ref, sdown_ref, out_ref, lower, sems):
    hidden = down_ref.shape[0]
    column = pl.multiple_of((place_ref[0] // share) * LANES, LANES)
    columns = pl.ds(lower, out_ref.shape[1])
    copies = []
    for at in range(0, hidden + LANES, DOWN_ROWS):
        if at < hidden:
            source = down_ref.at[pl.ds(at, DOWN_ROWS), columns]
        else:
            source = sdown_ref.at[pl.ds(column + (at - hidden), DOWN_ROWS), columns]
        copies.append(
            pltpu.make_async_copy(source, out_ref.at[pl.ds(at, DOWN_ROWS), :], sems.at[len(copies)])
        )
    return copies


def load_both_kernel(
    share, lower, place_ref, routed_ref, shared_ref, down_ref, sdown_ref, out_ref, down_out_ref, sems
):
    parts = 4
    run_copies(
        weight_copies(share, place_ref, routed_ref, shared_ref, out_ref, sems, parts)
        + down_range_copies(
            share, place_ref, down_ref, sdown_ref, down_out_ref, lower, sems.at[2 * parts :]
        )
    )


def load_both(place, routed, shared, down, sdown, lower, columns, share):
    width, hidden = routed.shape
    units = hidden + LANES
    return pl.pallas_call(
        functools.partial(load_both_kernel, share, lower),
        in_specs=[SMEM_SPEC] + [ANY_SPEC] * 4,
        out_specs=[VMEM_SPEC] * 2,
        out_shape=[pltpu.VMEM((width, units), BF16), pltpu.VMEM((units, columns), BF16)],
        scratch_shapes=[pltpu.SemaphoreType.DMA((8 + units // DOWN_ROWS,))],
        cost_estimate=pl.CostEstimate(
            flops=0, bytes_accessed=4 * units * (width + columns), transcendentals=0
        ),
        compiler_params=pltpu.CompilerParams(vmem_limit_bytes=1 << 20),
        name="load_both",
    )(place, *(in_hbm(w) for w in (routed, shared, down, sdown)))


def load_down_kernel(share, lower, place_ref, down_ref, sdown_ref, out_ref, sems):
    run_copies(down_range_copies(share, place_ref, down_ref, sdown_ref, out_ref, lower, sems))


def load_down(place, down, sdown, lower, columns, share):
    units = down.shape[0] + LANES
    return pl.pallas_call(
        functools.partial(load_down_kernel, share, lower),
        in_specs=[SMEM_SPEC] + [ANY_SPEC] * 2,
        out_specs=VMEM_SPEC,
        out_shape=pltpu.VMEM((units, columns), BF16),
        scratch_shapes=[pltpu.SemaphoreType.DMA((units // DOWN_ROWS,))],
        cost_estimate=pl.CostEstimate(flops=0, bytes_accessed=4 * units * columns, transcendentals=0),
        compiler_params=pltpu.CompilerParams(vmem_limit_bytes=1 << 20),
        name="load_down",
    )(place, in_hbm(down), in_hbm(sdown))


def late_half_kernel(place_ref, own_ref, other_ref, gate_ref, up_ref, gate_acc_ref, up_acc_ref, weight_ref, x):
    width, units = gate_ref.shape
    half, columns = own_ref.shape
    cut = width + LANES - columns
    x[:half, :] = own_ref[...]
    x[half:, :] = other_ref[...]
    rows = x[:, : width - cut]
    for at in tiles_of(units):
        gate_acc_ref[:, at] = jnp.dot(rows, gate_ref[cut:, at], preferred_element_type=F32)
        up_acc_ref[:, at] = jnp.dot(rows, up_ref[cut:, at], preferred_element_type=F32)
    weight = row_weight(place_ref[0], x[:, width - cut :])
    weight_ref[...] = jnp.broadcast_to(weight, weight_ref.shape)


def early_half_kernel(
    share, place_ref, own_ref, other_ref, gate_ref, up_ref, gate_acc_ref, up_acc_ref, weight_ref, second_ref,
    own_out_ref, other_out_ref, act_ref, x,
):
    half, cut = own_ref.shape
    units = gate_ref.shape[1]
    hidden = units - LANES
    x[:half, :] = own_ref[...]
    x[half:, :] = other_ref[...]
    rows = x[...]
    weight = weight_ref[:, :1]
    for at in tiles_of(units):
        gate = gate_acc_ref[:, at] + jnp.dot(rows, gate_ref[:cut, at], preferred_element_type=F32)
        up = up_acc_ref[:, at] + jnp.dot(rows, up_ref[:cut, at], preferred_element_type=F32)
        if at.start < hidden:
            act_ref[:, at] = (silu(gate) * up * weight).astype(BF16)
        else:
            act_ref[:, at] = shared_units(share, place_ref[0], gate, up)
    piece = cut // 2
    for i in range(2):
        at = slice(i * piece, (i + 1) * piece)
        total = jnp.dot(act_ref[...], second_ref[:, at], preferred_element_type=F32).astype(BF16)
        own_out_ref[:, at] = total[:half]
        other_out_ref[:, at] = total[half:]


def last_half_kernel(act_ref, later_ref, own_out_ref, other_out_ref):
    half, columns = own_out_ref.shape
    piece = columns // 2
    for i in range(2):
        at = slice(i * piece, (i + 1) * piece)
        total = jnp.dot(act_ref[...], later_ref[:, at], preferred_element_type=F32).astype(BF16)
        own_out_ref[:, at] = swap_quarters(total[:half])
        other_out_ref[:, at] = swap_quarters(total[half:])


def estimate(rows, depth, columns):
    return pl.CostEstimate(
        flops=2 * rows * depth * columns, bytes_accessed=2 * depth * columns, transcendentals=0
    )


def pair_rows(place, own, other, gate, up, second, later, share):
    half, cut = own[0].shape
    width, units = gate.shape
    partial = pl.pallas_call(
        late_half_kernel,
        in_specs=[SMEM_SPEC] + [VMEM_SPEC] * 4,
        out_specs=[VMEM_SPEC] * 3,
        out_shape=[pltpu.VMEM((2 * half, columns), F32) for columns in (units, units, LANES)],
        scratch_shapes=[pltpu.VMEM((2 * half, own[1].shape[1]), BF16)],
        cost_estimate=estimate(2 * half, width - cut, 2 * units),
        compiler_params=pltpu.CompilerParams(vmem_limit_bytes=10 << 20),
        name="late_half",
    )(place, own[1], other[1], gate, up)
    own_out, other_out, act = pl.pallas_call(
        functools.partial(early_half_kernel, share),
        in_specs=[SMEM_SPEC] + [VMEM_SPEC] * 8,
        out_specs=[VMEM_SPEC] * 3,
        out_shape=[
            pltpu.VMEM((half, cut), BF16),
            pltpu.VMEM((half, cut), BF16),
            pltpu.VMEM((2 * half, units), BF16),
        ],
        scratch_shapes=[pltpu.VMEM((2 * half, cut), BF16)],
        cost_estimate=estimate(2 * half, cut, 3 * units),
        compiler_params=pltpu.CompilerParams(vmem_limit_bytes=10 << 20),
        name="early_half",
    )(place, own[0], other[0], gate, up, *partial, second)
    last = pl.pallas_call(
        last_half_kernel,
        in_specs=[VMEM_SPEC] * 2,
        out_specs=[VMEM_SPEC] * 2,
        out_shape=[pltpu.VMEM((half, width - cut), BF16)] * 2,
        cost_estimate=estimate(2 * half, width - cut, units),
        compiler_params=pltpu.CompilerParams(vmem_limit_bytes=10 << 20),
        name="last_half",
    )(act, later)
    return own_out, last[0], other_out, last[1]


def block_kernel(
    share, place_ref, x_ref, gate_ref, up_ref, down_ref, sdown_ref, out_ref, act, second, sems
):
    groups = down_copies(share, place_ref, down_ref, sdown_ref, second, sems)

    @pl.when(pl.program_id(0) == 0)
    def _():
        for i in range(DOWN_PARTS):
            start_group(groups, i)
        for i in range(DOWN_PARTS):
            wait_group(groups, i)

    def store(at, total):
        out_ref[:, at] = total.astype(BF16)

    ffn(share, place_ref, x_ref, gate_ref, up_ref, act, second, lambda i: None, store)


def block_rows(place, x, gate, up, down, sdown, share):
    rows, packed = x.shape
    hidden, width = down.shape
    block = min(rows, ROW_BLOCK)
    return pl.pallas_call(
        functools.partial(block_kernel, share),
        grid=(rows // block,),
        in_specs=[SMEM_SPEC, pl.BlockSpec((block, packed), lambda i: (i, 0))] + [VMEM_SPEC] * 2 + [ANY_SPEC] * 2,
        out_specs=pl.BlockSpec((block, width), lambda i: (i, 0)),
        out_shape=jax.ShapeDtypeStruct((rows, width), BF16),
        scratch_shapes=down_scratch(block, hidden, width),
        compiler_params=pltpu.CompilerParams(vmem_limit_bytes=24 << 20),
        name="block_rows",
    )(place, x, gate, up, in_hbm(down), in_hbm(sdown))


def f32_sum(*terms):
    return functools.reduce(lambda a, b: a + b, (t.astype(F32) for t in terms))


def flipped(value, even, odd):
    pairs = []
    for node in range(4):
        for local in range(4):
            node_bits, local_bits = odd if node % 2 else even
            pairs.append((node * 4 + local, (node ^ node_bits) * 4 + (local ^ local_bits)))
    return lax.ppermute(value, ("node", "local"), pairs)


X, Z1, Z2, CORE = (2, 0), (0, 1), (0, 2), (1, 0)
GATHER = ((Z2, X), (Z1, Z2), (X, Z1))
SCATTER = ((X, Z1), (Z1, X), (Z2, Z2))


def stack(*values):
    return jnp.concatenate(values, axis=0)


def per_device(
    tokens,
    group_ids,
    route_weights,
    gate_experts,
    up_experts,
    down_experts,
    gate_shared,
    up_shared,
    down_shared,
):
    rows, width = tokens.shape
    node_count = lax.axis_size("node")
    local_count = lax.axis_size("local")
    share = max(1, LANES * node_count // gate_shared.shape[1])
    place = lax.axis_index("node").reshape(1)
    gate, up, down = gate_experts[0], up_experts[0], down_experts[0]
    packed = pack_rows(tokens, group_ids, route_weights)

    if node_count != 4 or local_count != 4:
        x = lax.all_gather(packed, ("node", "local"), axis=0, tiled=True)
        gate = load_weights(place, gate, gate_shared, share)
        up = load_weights(place, up, up_shared, share)
        part = block_rows(place, x, gate, up, down, down_shared, share)
        return lax.psum_scatter(part, ("node", "local"), scatter_dimension=0, tiled=True)

    cut = width // 2
    own = [packed[:, :cut], packed[:, cut:]]
    loads = (
        lambda *ready: (load_down(after(place, *ready), down, down_shared, 0, cut, share),),
        lambda *ready: (load_weights(after(place, *ready), gate, gate_shared, share),),
        lambda *ready: load_both(
            after(place, *ready), up, up_shared, down, down_shared, cut, width - cut, share
        ),
    )
    loaded = ()
    for number, (phase, load) in enumerate(zip(GATHER, loads)):
        got = [flipped(part, *pairs) for part, pairs in zip(own, (phase, phase[::-1]))]
        weights = tuple(load(*own))
        if number == 0:
            got[1], weights = lax.optimization_barrier((got[1], weights))
        else:
            got, weights = lax.optimization_barrier((got, weights))
        loaded += weights
        own = [stack(part, add) for part, add in zip(own, got)]
    second, gate, up, later = loaded
    odd = place[0] % 2
    own = [jnp.where(odd == i, part, regroup(part, 4, 2)) for i, part in enumerate(own)]
    other = [flipped(part, CORE, CORE) for part in own]


    outs = pair_rows(place, own, other, gate, up, second, later, share)

    totals = [[own, flipped(other, CORE, CORE)] for own, other in zip(outs[:2], outs[2:])]
    for phase in SCATTER:
        for i, bits in enumerate(phase):
            total = totals[i]
            half = total[0].shape[0] // 2
            sent = f32_sum(*(t[half:] for t in total)).astype(BF16)
            totals[i] = [f32_sum(*(t[:half] for t in total)), flipped(sent, bits, bits)]
    return jnp.concatenate([f32_sum(*total).astype(BF16) for total in totals], axis=1)


def solution(mesh):
    in_specs = (
        P(("rep", "node", "local"), None),
        P(("rep", "node", "local"), None),
        P(("rep", "node", "local"), None),
        P("node", None, "local"),
        P("node", None, "local"),
        P("node", "local", None),
        P(None, "local"),
        P(None, "local"),
        P("local", None),
    )
    out_specs = P(("rep", "node", "local"), None)
    return jax.shard_map(
        per_device, mesh=mesh, in_specs=in_specs, out_specs=out_specs, check_vma=False
    )
```

```python
import functools

import jax
import jax.numpy as jnp
from jax import lax
from jax.experimental import pallas as pl
from jax.experimental.pallas import tpu as pltpu
from jax.sharding import PartitionSpec as P

LANES = 128
ROW_BLOCK = 128
F32 = jnp.float32
BF16 = jnp.bfloat16
VMEM_SPEC = pl.BlockSpec(memory_space=pltpu.VMEM)
SMEM_SPEC = pl.BlockSpec(memory_space=pltpu.SMEM)
ANY_SPEC = pl.BlockSpec(memory_space=pl.ANY)


def in_hbm(value):
    return pltpu.with_memory_space_constraint(value, pltpu.HBM)


def run_copies(copies):
    for copy in copies:
        copy.start()
    for copy in copies:
        copy.wait()


def after(value, *done):
    return lax.optimization_barrier((value, *done))[0]


def pack_kernel(tokens_ref, groups_ref, weights_ref, packed_ref):
    rows, width = tokens_ref.shape
    packed_ref[:, :width] = tokens_ref[...]
    groups = groups_ref[...].T
    weights = weights_ref[...].astype(F32).T
    lane = lax.broadcasted_iota(jnp.int32, (rows, LANES), 1)
    dense = jnp.zeros((rows, LANES), F32)
    for k in range(groups.shape[1]):
        dense += jnp.where(lane == groups[:, k : k + 1], weights[:, k : k + 1], 0.0)
    packed_ref[:, width:] = dense.astype(BF16)


def pack_rows(tokens, group_ids, route_weights):
    rows, width = tokens.shape
    return pl.pallas_call(
        pack_kernel,
        out_specs=VMEM_SPEC,
        out_shape=pltpu.VMEM((rows, width + LANES), BF16),
        name="pack_rows",
    )(tokens, group_ids.T, route_weights.T)


def weight_copies(share, place_ref, routed_ref, shared_ref, out_ref, sems, parts):
    width, hidden = routed_ref.shape
    column = pl.multiple_of((place_ref[0] // share) * LANES, LANES)
    piece = width // parts
    copies = []
    for i in range(parts):
        at = pl.ds(i * piece, piece)
        for source, lower, size in (
            (routed_ref.at[at, :], 0, hidden),
            (shared_ref.at[at, pl.ds(column, LANES)], hidden, LANES),
        ):
            copies.append(
                pltpu.make_async_copy(source, out_ref.at[at, pl.ds(lower, size)], sems.at[len(copies)])
            )
    return copies


def load_kernel(share, place_ref, routed_ref, shared_ref, out_ref, sems):
    run_copies(weight_copies(share, place_ref, routed_ref, shared_ref, out_ref, sems, sems.shape[0] // 2))


def load_weights(place, routed, shared, share):
    width, hidden = routed.shape
    shape = (width, hidden + LANES)
    return pl.pallas_call(
        functools.partial(load_kernel, share),
        in_specs=[SMEM_SPEC] + [ANY_SPEC] * 2,
        out_specs=VMEM_SPEC,
        out_shape=pltpu.VMEM(shape, BF16),
        scratch_shapes=[pltpu.SemaphoreType.DMA((8,))],
        cost_estimate=pl.CostEstimate(flops=0, bytes_accessed=4 * shape[0] * shape[1], transcendentals=0),
        compiler_params=pltpu.CompilerParams(vmem_limit_bytes=1 << 20),
        name="load_weights",
    )(place, in_hbm(routed), in_hbm(shared))


def silu(v):
    return v / (1.0 + jnp.exp(-v))


def row_weight(node, dense):
    lane = lax.broadcasted_iota(jnp.int32, dense.shape, 1)
    return jnp.sum(jnp.where(lane == node, dense.astype(F32), 0.0), axis=1, keepdims=True)


DOWN_PARTS = 4


def down_scratch(rows, hidden, width):
    return [
        pltpu.VMEM((rows, hidden + LANES), BF16),
        pltpu.VMEM((hidden + LANES, width), BF16),
        pltpu.SemaphoreType.DMA((2 * DOWN_PARTS,)),
    ]


def down_copies(share, place_ref, down_ref, sdown_ref, second, sems):
    hidden, width = down_ref.shape
    column = pl.multiple_of((place_ref[0] // share) * LANES, LANES)
    piece = width // DOWN_PARTS
    groups = []
    for i in range(DOWN_PARTS):
        at = pl.ds(i * piece, piece)
        groups.append(
            [
                pltpu.make_async_copy(down_ref.at[:, at], second.at[pl.ds(0, hidden), at], sems.at[2 * i]),
                pltpu.make_async_copy(
                    sdown_ref.at[pl.ds(column, LANES), at],
                    second.at[pl.ds(hidden, LANES), at],
                    sems.at[2 * i + 1],
                ),
            ]
        )
    return groups


def start_group(groups, i):
    for copy in groups[i]:
        copy.start()


def wait_group(groups, i):
    for copy in groups[i]:
        copy.wait()


def shared_units(share, node, gate, up):
    shared = silu(gate) * up
    if share > 1:
        lane = lax.broadcasted_iota(jnp.int32, shared.shape, 1)
        shared = jnp.where(lane // (LANES // share) == node % share, shared, 0.0)
    return shared.astype(BF16)


def tiles_of(units):
    tile = 2 * LANES
    return [slice(at, min(at + tile, units)) for at in range(0, units, tile)]


def ffn(share, place_ref, x, gate_ref, up_ref, act, second, take, store):
    width, units = gate_ref.shape
    hidden = units - LANES
    node = place_ref[0]
    rows = x[:, :width]
    weight = row_weight(node, x[:, width:])
    gate = jnp.dot(rows, gate_ref[...], preferred_element_type=F32)
    up = jnp.dot(rows, up_ref[...], preferred_element_type=F32)
    act[:, :hidden] = (silu(gate[:, :hidden]) * up[:, :hidden] * weight).astype(BF16)
    act[:, hidden:] = shared_units(share, node, gate[:, hidden:], up[:, hidden:])
    piece = width // DOWN_PARTS
    for i in range(DOWN_PARTS):
        at = slice(i * piece, (i + 1) * piece)
        take(i)
        store(at, jnp.dot(act[...], second[:, at], preferred_element_type=F32))


def regroup(value, outer, inner):
    rows = value.shape[0] // (outer * inner)
    return jnp.concatenate(
        [
            value[(o * inner + i) * rows : (o * inner + i + 1) * rows]
            for i in range(inner)
            for o in range(outer)
        ],
        axis=0,
    )


def swap_quarters(value):
    quarter = value.shape[0] // 4
    return jnp.concatenate([value[i * quarter : (i + 1) * quarter] for i in (0, 2, 1, 3)], axis=0)


DOWN_ROWS = 128


def down_range_copies(share, place_ref, down_ref, sdown_ref, out_ref, lower, sems):
    hidden = down_ref.shape[0]
    column = pl.multiple_of((place_ref[0] // share) * LANES, LANES)
    columns = pl.ds(lower, out_ref.shape[1])
    copies = []
    for at in range(0, hidden + LANES, DOWN_ROWS):
        if at < hidden:
            source = down_ref.at[pl.ds(at, DOWN_ROWS), columns]
        else:
            source = sdown_ref.at[pl.ds(column + (at - hidden), DOWN_ROWS), columns]
        copies.append(
            pltpu.make_async_copy(source, out_ref.at[pl.ds(at, DOWN_ROWS), :], sems.at[len(copies)])
        )
    return copies


def load_both_kernel(
    share, lower, place_ref, routed_ref, shared_ref, down_ref, sdown_ref, out_ref, down_out_ref, sems
):
    parts = 4
    run_copies(
        weight_copies(share, place_ref, routed_ref, shared_ref, out_ref, sems, parts)
        + down_range_copies(
            share, place_ref, down_ref, sdown_ref, down_out_ref, lower, sems.at[2 * parts :]
        )
    )


def load_both(place, routed, shared, down, sdown, lower, columns, share):
    width, hidden = routed.shape
    units = hidden + LANES
    return pl.pallas_call(
        functools.partial(load_both_kernel, share, lower),
        in_specs=[SMEM_SPEC] + [ANY_SPEC] * 4,
        out_specs=[VMEM_SPEC] * 2,
        out_shape=[pltpu.VMEM((width, units), BF16), pltpu.VMEM((units, columns), BF16)],
        scratch_shapes=[pltpu.SemaphoreType.DMA((8 + units // DOWN_ROWS,))],
        cost_estimate=pl.CostEstimate(
            flops=0, bytes_accessed=4 * units * (width + columns), transcendentals=0
        ),
        compiler_params=pltpu.CompilerParams(vmem_limit_bytes=1 << 20),
        name="load_both",
    )(place, *(in_hbm(w) for w in (routed, shared, down, sdown)))


def load_first_kernel(share, lower, place_ref, routed_ref, shared_ref, sdown_ref, out_ref, rows_ref, sems):
    parts = 4
    column = pl.multiple_of((place_ref[0] // share) * LANES, LANES)
    rows = pltpu.make_async_copy(
        sdown_ref.at[pl.ds(column, LANES), pl.ds(lower, rows_ref.shape[1])], rows_ref, sems.at[2 * parts]
    )
    run_copies(weight_copies(share, place_ref, routed_ref, shared_ref, out_ref, sems, parts) + [rows])


def load_first(place, routed, shared, sdown, lower, share):
    width, hidden = routed.shape
    units = hidden + LANES
    return pl.pallas_call(
        functools.partial(load_first_kernel, share, lower),
        in_specs=[SMEM_SPEC] + [ANY_SPEC] * 3,
        out_specs=[VMEM_SPEC] * 2,
        out_shape=[pltpu.VMEM((width, units), BF16), pltpu.VMEM((LANES, sdown.shape[1] - lower), BF16)],
        scratch_shapes=[pltpu.SemaphoreType.DMA((9,))],
        cost_estimate=pl.CostEstimate(flops=0, bytes_accessed=4 * units * width, transcendentals=0),
        compiler_params=pltpu.CompilerParams(vmem_limit_bytes=1 << 20),
        name="load_first",
    )(place, *(in_hbm(w) for w in (routed, shared, sdown)))


def late_half_kernel(place_ref, own_ref, other_ref, gate_ref, up_ref, gate_acc_ref, up_acc_ref, weight_ref, x):
    width, units = gate_ref.shape
    half, columns = own_ref.shape
    cut = width + LANES - columns
    x[:half, :] = own_ref[...]
    x[half:, :] = other_ref[...]
    rows = x[:, : width - cut]
    for at in tiles_of(units):
        gate_acc_ref[:, at] = jnp.dot(rows, gate_ref[cut:, at], preferred_element_type=F32)
        up_acc_ref[:, at] = jnp.dot(rows, up_ref[cut:, at], preferred_element_type=F32)
    weight = row_weight(place_ref[0], x[:, width - cut :])
    weight_ref[...] = jnp.broadcast_to(weight, weight_ref.shape)


def early_half_kernel(
    share, place_ref, own_ref, other_ref, gate_ref, up_ref, gate_acc_ref, up_acc_ref, weight_ref, second_ref,
    own_out_ref, other_out_ref, act_ref, x,
):
    half, cut = own_ref.shape
    units = gate_ref.shape[1]
    hidden = units - LANES
    x[:half, :] = own_ref[...]
    x[half:, :] = other_ref[...]
    rows = x[...]
    weight = weight_ref[:, :1]
    for at in tiles_of(units):
        gate = gate_acc_ref[:, at] + jnp.dot(rows, gate_ref[:cut, at], preferred_element_type=F32)
        up = up_acc_ref[:, at] + jnp.dot(rows, up_ref[:cut, at], preferred_element_type=F32)
        if at.start < hidden:
            act_ref[:, at] = (silu(gate) * up * weight).astype(BF16)
        else:
            act_ref[:, at] = shared_units(share, place_ref[0], gate, up)
    piece = cut // 2
    for i in range(2):
        at = slice(i * piece, (i + 1) * piece)
        total = jnp.dot(act_ref[...], second_ref[:, at], preferred_element_type=F32).astype(BF16)
        own_out_ref[:, at] = total[:half]
        other_out_ref[:, at] = total[half:]


def last_half_kernel(act_ref, down_ref, rows_ref, own_out_ref, other_out_ref):
    half, columns = own_out_ref.shape
    hidden, width = down_ref.shape
    piece = columns // 2
    for i in range(2):
        at = slice(i * piece, (i + 1) * piece)
        whole = slice(width - columns + i * piece, width - columns + (i + 1) * piece)
        total = jnp.dot(act_ref[:, :hidden], down_ref[:, whole], preferred_element_type=F32)
        total += jnp.dot(act_ref[:, hidden:], rows_ref[:, at], preferred_element_type=F32)
        total = total.astype(BF16)
        own_out_ref[:, at] = swap_quarters(total[:half])
        other_out_ref[:, at] = swap_quarters(total[half:])


def estimate(rows, depth, columns):
    return pl.CostEstimate(
        flops=2 * rows * depth * columns, bytes_accessed=2 * depth * columns, transcendentals=0
    )


def pair_rows(place, own, other, gate, up, second, down, rows, share):
    half, cut = own[0].shape
    width, units = gate.shape
    partial = pl.pallas_call(
        late_half_kernel,
        in_specs=[SMEM_SPEC] + [VMEM_SPEC] * 4,
        out_specs=[VMEM_SPEC] * 3,
        out_shape=[pltpu.VMEM((2 * half, columns), F32) for columns in (units, units, LANES)],
        scratch_shapes=[pltpu.VMEM((2 * half, own[1].shape[1]), BF16)],
        cost_estimate=estimate(2 * half, width - cut, 2 * units),
        compiler_params=pltpu.CompilerParams(vmem_limit_bytes=10 << 20),
        name="late_half",
    )(place, own[1], other[1], gate, up)
    own_out, other_out, act = pl.pallas_call(
        functools.partial(early_half_kernel, share),
        in_specs=[SMEM_SPEC] + [VMEM_SPEC] * 8,
        out_specs=[VMEM_SPEC] * 3,
        out_shape=[
            pltpu.VMEM((half, cut), BF16),
            pltpu.VMEM((half, cut), BF16),
            pltpu.VMEM((2 * half, units), BF16),
        ],
        scratch_shapes=[pltpu.VMEM((2 * half, cut), BF16)],
        cost_estimate=estimate(2 * half, cut, 3 * units),
        compiler_params=pltpu.CompilerParams(vmem_limit_bytes=10 << 20),
        name="early_half",
    )(place, own[0], other[0], gate, up, *partial, second)
    last = pl.pallas_call(
        last_half_kernel,
        in_specs=[VMEM_SPEC] * 3,
        out_specs=[VMEM_SPEC] * 2,
        out_shape=[pltpu.VMEM((half, width - cut), BF16)] * 2,
        cost_estimate=estimate(2 * half, width - cut, units),
        compiler_params=pltpu.CompilerParams(vmem_limit_bytes=10 << 20),
        name="last_half",
    )(act, pltpu.with_memory_space_constraint(down, pltpu.VMEM), rows)
    return own_out, last[0], other_out, last[1]


def block_kernel(
    share, place_ref, x_ref, gate_ref, up_ref, down_ref, sdown_ref, out_ref, act, second, sems
):
    groups = down_copies(share, place_ref, down_ref, sdown_ref, second, sems)

    @pl.when(pl.program_id(0) == 0)
    def _():
        for i in range(DOWN_PARTS):
            start_group(groups, i)
        for i in range(DOWN_PARTS):
            wait_group(groups, i)

    def store(at, total):
        out_ref[:, at] = total.astype(BF16)

    ffn(share, place_ref, x_ref, gate_ref, up_ref, act, second, lambda i: None, store)


def block_rows(place, x, gate, up, down, sdown, share):
    rows, packed = x.shape
    hidden, width = down.shape
    block = min(rows, ROW_BLOCK)
    return pl.pallas_call(
        functools.partial(block_kernel, share),
        grid=(rows // block,),
        in_specs=[SMEM_SPEC, pl.BlockSpec((block, packed), lambda i: (i, 0))] + [VMEM_SPEC] * 2 + [ANY_SPEC] * 2,
        out_specs=pl.BlockSpec((block, width), lambda i: (i, 0)),
        out_shape=jax.ShapeDtypeStruct((rows, width), BF16),
        scratch_shapes=down_scratch(block, hidden, width),
        compiler_params=pltpu.CompilerParams(vmem_limit_bytes=24 << 20),
        name="block_rows",
    )(place, x, gate, up, in_hbm(down), in_hbm(sdown))


def f32_sum(*terms):
    return functools.reduce(lambda a, b: a + b, (t.astype(F32) for t in terms))


def flipped(value, even, odd):
    pairs = []
    for node in range(4):
        for local in range(4):
            node_bits, local_bits = odd if node % 2 else even
            pairs.append((node * 4 + local, (node ^ node_bits) * 4 + (local ^ local_bits)))
    return lax.ppermute(value, ("node", "local"), pairs)


X, Z1, Z2, CORE = (2, 0), (0, 1), (0, 2), (1, 0)
GATHER = ((Z2, X), (Z1, Z2), (X, Z1))
SCATTER = ((X, Z1), (Z1, X), (Z2, Z2))


def stack(*values):
    return jnp.concatenate(values, axis=0)


def per_device(
    tokens,
    group_ids,
    route_weights,
    gate_experts,
    up_experts,
    down_experts,
    gate_shared,
    up_shared,
    down_shared,
):
    rows, width = tokens.shape
    node_count = lax.axis_size("node")
    local_count = lax.axis_size("local")
    share = max(1, LANES * node_count // gate_shared.shape[1])
    place = lax.axis_index("node").reshape(1)
    gate, up, down = gate_experts[0], up_experts[0], down_experts[0]
    packed = pack_rows(tokens, group_ids, route_weights)

    if node_count != 4 or local_count != 4:
        x = lax.all_gather(packed, ("node", "local"), axis=0, tiled=True)
        gate = load_weights(place, gate, gate_shared, share)
        up = load_weights(place, up, up_shared, share)
        part = block_rows(place, x, gate, up, down, down_shared, share)
        return lax.psum_scatter(part, ("node", "local"), scatter_dimension=0, tiled=True)

    cut = width // 2
    own = [packed[:, :cut], packed[:, cut:]]
    loads = (
        lambda *ready: (),
        lambda *ready: load_first(after(place, *ready), gate, gate_shared, down_shared, cut, share),
        lambda *ready: load_both(after(place, *ready), up, up_shared, down, down_shared, 0, cut, share),
    )
    loaded = ()
    for phase, load in zip(GATHER, loads):
        got = [flipped(part, *pairs) for part, pairs in zip(own, (phase, phase[::-1]))]
        weights = tuple(load(*own))
        if weights:
            got, weights = lax.optimization_barrier((got, weights))
        loaded += weights
        own = [stack(part, add) for part, add in zip(own, got)]
    gate, late_rows, up, second = loaded
    odd = place[0] % 2
    own = [jnp.where(odd == i, part, regroup(part, 4, 2)) for i, part in enumerate(own)]
    other = [flipped(part, CORE, CORE) for part in own]

    outs = pair_rows(place, own, other, gate, up, second, down, late_rows, share)

    totals = [[own, flipped(other, CORE, CORE)] for own, other in zip(outs[:2], outs[2:])]
    for phase in SCATTER:
        for i, bits in enumerate(phase):
            total = totals[i]
            half = total[0].shape[0] // 2
            sent = f32_sum(*(t[half:] for t in total)).astype(BF16)
            totals[i] = [f32_sum(*(t[:half] for t in total)), flipped(sent, bits, bits)]
    return jnp.concatenate([f32_sum(*total).astype(BF16) for total in totals], axis=1)


def solution(mesh):
    in_specs = (
        P(("rep", "node", "local"), None),
        P(("rep", "node", "local"), None),
        P(("rep", "node", "local"), None),
        P("node", None, "local"),
        P("node", None, "local"),
        P("node", "local", None),
        P(None, "local"),
        P(None, "local"),
        P("local", None),
    )
    out_specs = P(("rep", "node", "local"), None)
    return jax.shard_map(
        per_device, mesh=mesh, in_specs=in_specs, out_specs=out_specs, check_vma=False
    )
```

```python
import functools

import jax
import jax.numpy as jnp
from jax import lax
from jax.experimental import pallas as pl
from jax.experimental.pallas import tpu as pltpu
from jax.sharding import PartitionSpec as P

LANES = 128
ROW_BLOCK = 128
F32 = jnp.float32
BF16 = jnp.bfloat16
VMEM_SPEC = pl.BlockSpec(memory_space=pltpu.VMEM)
SMEM_SPEC = pl.BlockSpec(memory_space=pltpu.SMEM)
ANY_SPEC = pl.BlockSpec(memory_space=pl.ANY)


def in_hbm(value):
    return pltpu.with_memory_space_constraint(value, pltpu.HBM)


def run_copies(copies):
    for copy in copies:
        copy.start()
    for copy in copies:
        copy.wait()


def after(value, *done):
    return lax.optimization_barrier((value, *done))[0]


def pack_kernel(tokens_ref, groups_ref, weights_ref, packed_ref):
    rows, width = tokens_ref.shape
    packed_ref[:, :width] = tokens_ref[...]
    groups = groups_ref[...].T
    weights = weights_ref[...].astype(F32).T
    lane = lax.broadcasted_iota(jnp.int32, (rows, LANES), 1)
    dense = jnp.zeros((rows, LANES), F32)
    for k in range(groups.shape[1]):
        dense += jnp.where(lane == groups[:, k : k + 1], weights[:, k : k + 1], 0.0)
    packed_ref[:, width:] = dense.astype(BF16)


def pack_rows(tokens, group_ids, route_weights):
    rows, width = tokens.shape
    return pl.pallas_call(
        pack_kernel,
        out_specs=VMEM_SPEC,
        out_shape=pltpu.VMEM((rows, width + LANES), BF16),
        name="pack_rows",
    )(tokens, group_ids.T, route_weights.T)


def weight_copies(share, place_ref, routed_ref, shared_ref, out_ref, sems, parts):
    width, hidden = routed_ref.shape
    column = pl.multiple_of((place_ref[0] // share) * LANES, LANES)
    piece = width // parts
    copies = []
    for i in range(parts):
        at = pl.ds(i * piece, piece)
        for source, lower, size in (
            (routed_ref.at[at, :], 0, hidden),
            (shared_ref.at[at, pl.ds(column, LANES)], hidden, LANES),
        ):
            copies.append(
                pltpu.make_async_copy(source, out_ref.at[at, pl.ds(lower, size)], sems.at[len(copies)])
            )
    return copies


def load_kernel(share, place_ref, routed_ref, shared_ref, out_ref, sems):
    run_copies(weight_copies(share, place_ref, routed_ref, shared_ref, out_ref, sems, sems.shape[0] // 2))


def load_weights(place, routed, shared, share):
    width, hidden = routed.shape
    shape = (width, hidden + LANES)
    return pl.pallas_call(
        functools.partial(load_kernel, share),
        in_specs=[SMEM_SPEC] + [ANY_SPEC] * 2,
        out_specs=VMEM_SPEC,
        out_shape=pltpu.VMEM(shape, BF16),
        scratch_shapes=[pltpu.SemaphoreType.DMA((8,))],
        cost_estimate=pl.CostEstimate(flops=0, bytes_accessed=4 * shape[0] * shape[1], transcendentals=0),
        compiler_params=pltpu.CompilerParams(vmem_limit_bytes=1 << 20),
        name="load_weights",
    )(place, in_hbm(routed), in_hbm(shared))


def silu(v):
    return v / (1.0 + jnp.exp(-v))


def row_weight(node, dense):
    lane = lax.broadcasted_iota(jnp.int32, dense.shape, 1)
    return jnp.sum(jnp.where(lane == node, dense.astype(F32), 0.0), axis=1, keepdims=True)


DOWN_PARTS = 4


def down_scratch(rows, hidden, width):
    return [
        pltpu.VMEM((rows, hidden + LANES), BF16),
        pltpu.VMEM((hidden + LANES, width), BF16),
        pltpu.SemaphoreType.DMA((2 * DOWN_PARTS,)),
    ]


def down_copies(share, place_ref, down_ref, sdown_ref, second, sems):
    hidden, width = down_ref.shape
    column = pl.multiple_of((place_ref[0] // share) * LANES, LANES)
    piece = width // DOWN_PARTS
    groups = []
    for i in range(DOWN_PARTS):
        at = pl.ds(i * piece, piece)
        groups.append(
            [
                pltpu.make_async_copy(down_ref.at[:, at], second.at[pl.ds(0, hidden), at], sems.at[2 * i]),
                pltpu.make_async_copy(
                    sdown_ref.at[pl.ds(column, LANES), at],
                    second.at[pl.ds(hidden, LANES), at],
                    sems.at[2 * i + 1],
                ),
            ]
        )
    return groups


def start_group(groups, i):
    for copy in groups[i]:
        copy.start()


def wait_group(groups, i):
    for copy in groups[i]:
        copy.wait()


def shared_units(share, node, gate, up):
    shared = silu(gate) * up
    if share > 1:
        lane = lax.broadcasted_iota(jnp.int32, shared.shape, 1)
        shared = jnp.where(lane // (LANES // share) == node % share, shared, 0.0)
    return shared.astype(BF16)


def tiles_of(units):
    tile = 2 * LANES
    return [slice(at, min(at + tile, units)) for at in range(0, units, tile)]


def ffn(share, place_ref, x, gate_ref, up_ref, act, second, take, store):
    width, units = gate_ref.shape
    hidden = units - LANES
    node = place_ref[0]
    rows = x[:, :width]
    weight = row_weight(node, x[:, width:])
    gate = jnp.dot(rows, gate_ref[...], preferred_element_type=F32)
    up = jnp.dot(rows, up_ref[...], preferred_element_type=F32)
    act[:, :hidden] = (silu(gate[:, :hidden]) * up[:, :hidden] * weight).astype(BF16)
    act[:, hidden:] = shared_units(share, node, gate[:, hidden:], up[:, hidden:])
    piece = width // DOWN_PARTS
    for i in range(DOWN_PARTS):
        at = slice(i * piece, (i + 1) * piece)
        take(i)
        store(at, jnp.dot(act[...], second[:, at], preferred_element_type=F32))


def regroup(value, outer, inner):
    rows = value.shape[0] // (outer * inner)
    return jnp.concatenate(
        [
            value[(o * inner + i) * rows : (o * inner + i + 1) * rows]
            for i in range(inner)
            for o in range(outer)
        ],
        axis=0,
    )


def swap_quarters(value):
    quarter = value.shape[0] // 4
    return jnp.concatenate([value[i * quarter : (i + 1) * quarter] for i in (0, 2, 1, 3)], axis=0)


DOWN_ROWS = 128


def down_range_copies(share, place_ref, down_ref, sdown_ref, out_ref, lower, sems):
    hidden = down_ref.shape[0]
    column = pl.multiple_of((place_ref[0] // share) * LANES, LANES)
    columns = pl.ds(lower, out_ref.shape[1])
    copies = []
    for at in range(0, hidden + LANES, DOWN_ROWS):
        if at < hidden:
            source = down_ref.at[pl.ds(at, DOWN_ROWS), columns]
        else:
            source = sdown_ref.at[pl.ds(column + (at - hidden), DOWN_ROWS), columns]
        copies.append(
            pltpu.make_async_copy(source, out_ref.at[pl.ds(at, DOWN_ROWS), :], sems.at[len(copies)])
        )
    return copies


def load_both_kernel(
    share, lower, place_ref, routed_ref, shared_ref, down_ref, sdown_ref, out_ref, down_out_ref, sems
):
    parts = 4
    run_copies(
        weight_copies(share, place_ref, routed_ref, shared_ref, out_ref, sems, parts)
        + down_range_copies(
            share, place_ref, down_ref, sdown_ref, down_out_ref, lower, sems.at[2 * parts :]
        )
    )


def load_both(place, routed, shared, down, sdown, lower, columns, share):
    width, hidden = routed.shape
    units = hidden + LANES
    return pl.pallas_call(
        functools.partial(load_both_kernel, share, lower),
        in_specs=[SMEM_SPEC] + [ANY_SPEC] * 4,
        out_specs=[VMEM_SPEC] * 2,
        out_shape=[pltpu.VMEM((width, units), BF16), pltpu.VMEM((units, columns), BF16)],
        scratch_shapes=[pltpu.SemaphoreType.DMA((8 + units // DOWN_ROWS,))],
        cost_estimate=pl.CostEstimate(
            flops=0, bytes_accessed=4 * units * (width + columns), transcendentals=0
        ),
        compiler_params=pltpu.CompilerParams(vmem_limit_bytes=1 << 20),
        name="load_both",
    )(place, *(in_hbm(w) for w in (routed, shared, down, sdown)))


def load_first_kernel(share, lower, place_ref, routed_ref, shared_ref, sdown_ref, out_ref, rows_ref, sems):
    parts = 4
    column = pl.multiple_of((place_ref[0] // share) * LANES, LANES)
    rows = pltpu.make_async_copy(
        sdown_ref.at[pl.ds(column, LANES), pl.ds(lower, rows_ref.shape[1])], rows_ref, sems.at[2 * parts]
    )
    run_copies(weight_copies(share, place_ref, routed_ref, shared_ref, out_ref, sems, parts) + [rows])


def load_first(place, routed, shared, sdown, lower, share):
    width, hidden = routed.shape
    units = hidden + LANES
    return pl.pallas_call(
        functools.partial(load_first_kernel, share, lower),
        in_specs=[SMEM_SPEC] + [ANY_SPEC] * 3,
        out_specs=[VMEM_SPEC] * 2,
        out_shape=[pltpu.VMEM((width, units), BF16), pltpu.VMEM((LANES, sdown.shape[1] - lower), BF16)],
        scratch_shapes=[pltpu.SemaphoreType.DMA((9,))],
        cost_estimate=pl.CostEstimate(flops=0, bytes_accessed=4 * units * width, transcendentals=0),
        compiler_params=pltpu.CompilerParams(vmem_limit_bytes=1 << 20),
        name="load_first",
    )(place, *(in_hbm(w) for w in (routed, shared, sdown)))


def late_half_kernel(place_ref, own_ref, other_ref, gate_ref, up_ref, gate_acc_ref, up_acc_ref, weight_ref, x):
    width, units = gate_ref.shape
    half, columns = own_ref.shape
    cut = width + LANES - columns
    x[:half, :] = own_ref[...]
    x[half:, :] = other_ref[...]
    rows = x[:, : width - cut]
    for at in tiles_of(units):
        gate_acc_ref[:, at] = jnp.dot(rows, gate_ref[cut:, at], preferred_element_type=F32)
        up_acc_ref[:, at] = jnp.dot(rows, up_ref[cut:, at], preferred_element_type=F32)
    weight = row_weight(place_ref[0], x[:, width - cut :])
    weight_ref[...] = jnp.broadcast_to(weight, weight_ref.shape)


def early_half_kernel(
    share, place_ref, own_ref, other_ref, gate_ref, up_ref, gate_acc_ref, up_acc_ref, weight_ref, second_ref,
    own_out_ref, other_out_ref, act_ref, x,
):
    half, cut = own_ref.shape
    units = gate_ref.shape[1]
    hidden = units - LANES
    x[:half, :] = own_ref[...]
    x[half:, :] = other_ref[...]
    rows = x[...]
    weight = weight_ref[:, :1]
    for at in tiles_of(units):
        gate = gate_acc_ref[:, at] + jnp.dot(rows, gate_ref[:cut, at], preferred_element_type=F32)
        up = up_acc_ref[:, at] + jnp.dot(rows, up_ref[:cut, at], preferred_element_type=F32)
        if at.start < hidden:
            act_ref[:, at] = (silu(gate) * up * weight).astype(BF16)
        else:
            act_ref[:, at] = shared_units(share, place_ref[0], gate, up)
    piece = cut // 2
    for i in range(2):
        at = slice(i * piece, (i + 1) * piece)
        total = jnp.dot(act_ref[...], second_ref[:, at], preferred_element_type=F32).astype(BF16)
        own_out_ref[:, at] = total[:half]
        other_out_ref[:, at] = total[half:]


def last_half_kernel(act_ref, down_ref, rows_ref, own_out_ref, other_out_ref):
    half, columns = own_out_ref.shape
    hidden, width = down_ref.shape
    piece = columns // 2
    for i in range(2):
        at = slice(i * piece, (i + 1) * piece)
        whole = slice(width - columns + i * piece, width - columns + (i + 1) * piece)
        total = jnp.dot(act_ref[:, :hidden], down_ref[:, whole], preferred_element_type=F32)
        total += jnp.dot(act_ref[:, hidden:], rows_ref[:, at], preferred_element_type=F32)
        total = total.astype(BF16)
        own_out_ref[:, at] = swap_quarters(total[:half])
        other_out_ref[:, at] = swap_quarters(total[half:])


def estimate(rows, depth, columns):
    return pl.CostEstimate(
        flops=2 * rows * depth * columns, bytes_accessed=2 * depth * columns, transcendentals=0
    )


def pair_rows(place, own, other, gate, up, second, down, rows, share):
    half, cut = own[0].shape
    width, units = gate.shape
    partial = pl.pallas_call(
        late_half_kernel,
        in_specs=[SMEM_SPEC] + [VMEM_SPEC] * 4,
        out_specs=[VMEM_SPEC] * 3,
        out_shape=[pltpu.VMEM((2 * half, columns), F32) for columns in (units, units, LANES)],
        scratch_shapes=[pltpu.VMEM((2 * half, own[1].shape[1]), BF16)],
        cost_estimate=estimate(2 * half, width - cut, 2 * units),
        compiler_params=pltpu.CompilerParams(vmem_limit_bytes=10 << 20),
        name="late_half",
    )(place, own[1], other[1], gate, up)
    own_out, other_out, act = pl.pallas_call(
        functools.partial(early_half_kernel, share),
        in_specs=[SMEM_SPEC] + [VMEM_SPEC] * 8,
        out_specs=[VMEM_SPEC] * 3,
        out_shape=[
            pltpu.VMEM((half, cut), BF16),
            pltpu.VMEM((half, cut), BF16),
            pltpu.VMEM((2 * half, units), BF16),
        ],
        scratch_shapes=[pltpu.VMEM((2 * half, cut), BF16)],
        cost_estimate=estimate(2 * half, cut, 3 * units),
        compiler_params=pltpu.CompilerParams(vmem_limit_bytes=10 << 20),
        name="early_half",
    )(place, own[0], other[0], gate, up, *partial, second)
    last = pl.pallas_call(
        last_half_kernel,
        in_specs=[VMEM_SPEC] * 3,
        out_specs=[VMEM_SPEC] * 2,
        out_shape=[pltpu.VMEM((half, width - cut), BF16)] * 2,
        cost_estimate=estimate(2 * half, width - cut, units),
        compiler_params=pltpu.CompilerParams(vmem_limit_bytes=10 << 20),
        name="last_half",
    )(act, pltpu.with_memory_space_constraint(down, pltpu.VMEM), rows)
    return own_out, last[0], other_out, last[1]


def block_kernel(
    share, place_ref, x_ref, gate_ref, up_ref, down_ref, sdown_ref, out_ref, act, second, sems
):
    groups = down_copies(share, place_ref, down_ref, sdown_ref, second, sems)

    @pl.when(pl.program_id(0) == 0)
    def _():
        for i in range(DOWN_PARTS):
            start_group(groups, i)
        for i in range(DOWN_PARTS):
            wait_group(groups, i)

    def store(at, total):
        out_ref[:, at] = total.astype(BF16)

    ffn(share, place_ref, x_ref, gate_ref, up_ref, act, second, lambda i: None, store)


def block_rows(place, x, gate, up, down, sdown, share):
    rows, packed = x.shape
    hidden, width = down.shape
    block = min(rows, ROW_BLOCK)
    return pl.pallas_call(
        functools.partial(block_kernel, share),
        grid=(rows // block,),
        in_specs=[SMEM_SPEC, pl.BlockSpec((block, packed), lambda i: (i, 0))] + [VMEM_SPEC] * 2 + [ANY_SPEC] * 2,
        out_specs=pl.BlockSpec((block, width), lambda i: (i, 0)),
        out_shape=jax.ShapeDtypeStruct((rows, width), BF16),
        scratch_shapes=down_scratch(block, hidden, width),
        compiler_params=pltpu.CompilerParams(vmem_limit_bytes=24 << 20),
        name="block_rows",
    )(place, x, gate, up, in_hbm(down), in_hbm(sdown))


def f32_sum(*terms):
    return functools.reduce(lambda a, b: a + b, (t.astype(F32) for t in terms))


def flipped(value, even, odd):
    pairs = []
    for node in range(4):
        for local in range(4):
            node_bits, local_bits = odd if node % 2 else even
            pairs.append((node * 4 + local, (node ^ node_bits) * 4 + (local ^ local_bits)))
    return lax.ppermute(value, ("node", "local"), pairs)


X, Z1, Z2, CORE = (2, 0), (0, 1), (0, 2), (1, 0)
GATHER = ((Z2, X), (Z1, Z2), (X, Z1))
SCATTER = ((X, Z1), (Z1, X), (Z2, Z2))


def stack(*values):
    return jnp.concatenate(values, axis=0)


def per_device(
    tokens,
    group_ids,
    route_weights,
    gate_experts,
    up_experts,
    down_experts,
    gate_shared,
    up_shared,
    down_shared,
):
    rows, width = tokens.shape
    node_count = lax.axis_size("node")
    local_count = lax.axis_size("local")
    share = max(1, LANES * node_count // gate_shared.shape[1])
    place = lax.axis_index("node").reshape(1)
    gate, up, down = gate_experts[0], up_experts[0], down_experts[0]
    packed = pack_rows(tokens, group_ids, route_weights)

    if node_count != 4 or local_count != 4:
        x = lax.all_gather(packed, ("node", "local"), axis=0, tiled=True)
        gate = load_weights(place, gate, gate_shared, share)
        up = load_weights(place, up, up_shared, share)
        part = block_rows(place, x, gate, up, down, down_shared, share)
        return lax.psum_scatter(part, ("node", "local"), scatter_dimension=0, tiled=True)

    cut = width // 2
    own = [packed[:, :cut], packed[:, cut:]]
    loads = (
        lambda *ready: (),
        lambda *ready: load_first(after(place, *ready), gate, gate_shared, down_shared, cut, share),
        lambda *ready: load_both(after(place, *ready), up, up_shared, down, down_shared, 0, cut, share),
    )
    loaded = ()
    for phase, load in zip(GATHER, loads):
        got = [flipped(part, *pairs) for part, pairs in zip(own, (phase, phase[::-1]))]
        weights = tuple(load(*own))
        if weights:
            got, weights = lax.optimization_barrier((got, weights))
        loaded += weights
        own = [stack(part, add) for part, add in zip(own, got)]
    gate, late_rows, up, second = loaded
    odd = place[0] % 2
    own = [jnp.where(odd == i, part, regroup(part, 4, 2)) for i, part in enumerate(own)]
    other = [flipped(part, CORE, CORE) for part in own]

    outs = pair_rows(place, own, other, gate, up, second, down, late_rows, share)

    swapped = flipped(outs[2], CORE, CORE)
    totals = [[outs[0], swapped], [outs[1], flipped(after(outs[3], swapped), CORE, CORE)]]
    for phase in SCATTER:
        for i, bits in enumerate(phase):
            total = totals[i]
            half = total[0].shape[0] // 2
            sent = f32_sum(*(t[half:] for t in total)).astype(BF16)
            totals[i] = [f32_sum(*(t[:half] for t in total)), flipped(sent, bits, bits)]
    return jnp.concatenate([f32_sum(*total).astype(BF16) for total in totals], axis=1)


def solution(mesh):
    in_specs = (
        P(("rep", "node", "local"), None),
        P(("rep", "node", "local"), None),
        P(("rep", "node", "local"), None),
        P("node", None, "local"),
        P("node", None, "local"),
        P("node", "local", None),
        P(None, "local"),
        P(None, "local"),
        P("local", None),
    )
    out_specs = P(("rep", "node", "local"), None)
    return jax.shard_map(
        per_device, mesh=mesh, in_specs=in_specs, out_specs=out_specs, check_vma=False
    )
```

```python
import functools

import jax
import jax.numpy as jnp
from jax import lax
from jax.experimental import pallas as pl
from jax.experimental.pallas import tpu as pltpu
from jax.sharding import PartitionSpec as P

LANES = 128
ROW_BLOCK = 128
F32 = jnp.float32
BF16 = jnp.bfloat16
VMEM_SPEC = pl.BlockSpec(memory_space=pltpu.VMEM)
SMEM_SPEC = pl.BlockSpec(memory_space=pltpu.SMEM)
ANY_SPEC = pl.BlockSpec(memory_space=pl.ANY)


def in_hbm(value):
    return pltpu.with_memory_space_constraint(value, pltpu.HBM)


def run_copies(copies):
    for copy in copies:
        copy.start()
    for copy in copies:
        copy.wait()


def after(value, *done):
    return lax.optimization_barrier((value, *done))[0]


def pack_kernel(tokens_ref, groups_ref, weights_ref, packed_ref):
    rows, width = tokens_ref.shape
    packed_ref[:, :width] = tokens_ref[...]
    groups = groups_ref[...].T
    weights = weights_ref[...].astype(F32).T
    lane = lax.broadcasted_iota(jnp.int32, (rows, LANES), 1)
    dense = jnp.zeros((rows, LANES), F32)
    for k in range(groups.shape[1]):
        dense += jnp.where(lane == groups[:, k : k + 1], weights[:, k : k + 1], 0.0)
    packed_ref[:, width:] = dense.astype(BF16)


def pack_rows(tokens, group_ids, route_weights):
    rows, width = tokens.shape
    return pl.pallas_call(
        pack_kernel,
        out_specs=VMEM_SPEC,
        out_shape=pltpu.VMEM((rows, width + LANES), BF16),
        name="pack_rows",
    )(tokens, group_ids.T, route_weights.T)


def weight_copies(share, place_ref, routed_ref, shared_ref, out_ref, sems, parts, first_row=0):
    hidden = routed_ref.shape[1]
    column = pl.multiple_of((place_ref[0] // share) * LANES, LANES)
    piece = out_ref.shape[0] // parts
    copies = []
    for i in range(parts):
        at = pl.ds(i * piece, piece)
        rows = pl.ds(first_row + i * piece, piece)
        for source, lower, size in (
            (routed_ref.at[rows, :], 0, hidden),
            (shared_ref.at[rows, pl.ds(column, LANES)], hidden, LANES),
        ):
            copies.append(
                pltpu.make_async_copy(source, out_ref.at[at, pl.ds(lower, size)], sems.at[len(copies)])
            )
    return copies


def load_kernel(share, first_row, place_ref, routed_ref, shared_ref, out_ref, sems):
    run_copies(
        weight_copies(
            share, place_ref, routed_ref, shared_ref, out_ref, sems, sems.shape[0] // 2, first_row
        )
    )


def load_weights(place, routed, shared, share, first_row=0, rows=None):
    width, hidden = routed.shape
    shape = (width if rows is None else rows, hidden + LANES)
    return pl.pallas_call(
        functools.partial(load_kernel, share, first_row),
        in_specs=[SMEM_SPEC] + [ANY_SPEC] * 2,
        out_specs=VMEM_SPEC,
        out_shape=pltpu.VMEM(shape, BF16),
        scratch_shapes=[pltpu.SemaphoreType.DMA((8,))],
        cost_estimate=pl.CostEstimate(flops=0, bytes_accessed=4 * shape[0] * shape[1], transcendentals=0),
        compiler_params=pltpu.CompilerParams(vmem_limit_bytes=1 << 20),
        name="load_weights",
    )(place, in_hbm(routed), in_hbm(shared))


def silu(v):
    return v / (1.0 + jnp.exp(-v))


def row_weight(node, dense):
    lane = lax.broadcasted_iota(jnp.int32, dense.shape, 1)
    return jnp.sum(jnp.where(lane == node, dense.astype(F32), 0.0), axis=1, keepdims=True)


DOWN_PARTS = 4


def down_scratch(rows, hidden, width):
    return [
        pltpu.VMEM((rows, hidden + LANES), BF16),
        pltpu.VMEM((hidden + LANES, width), BF16),
        pltpu.SemaphoreType.DMA((2 * DOWN_PARTS,)),
    ]


def down_copies(share, place_ref, down_ref, sdown_ref, second, sems):
    hidden, width = down_ref.shape
    column = pl.multiple_of((place_ref[0] // share) * LANES, LANES)
    piece = width // DOWN_PARTS
    groups = []
    for i in range(DOWN_PARTS):
        at = pl.ds(i * piece, piece)
        groups.append(
            [
                pltpu.make_async_copy(down_ref.at[:, at], second.at[pl.ds(0, hidden), at], sems.at[2 * i]),
                pltpu.make_async_copy(
                    sdown_ref.at[pl.ds(column, LANES), at],
                    second.at[pl.ds(hidden, LANES), at],
                    sems.at[2 * i + 1],
                ),
            ]
        )
    return groups


def start_group(groups, i):
    for copy in groups[i]:
        copy.start()


def wait_group(groups, i):
    for copy in groups[i]:
        copy.wait()


def shared_units(share, node, gate, up):
    shared = silu(gate) * up
    if share > 1:
        lane = lax.broadcasted_iota(jnp.int32, shared.shape, 1)
        shared = jnp.where(lane // (LANES // share) == node % share, shared, 0.0)
    return shared.astype(BF16)


def tiles_of(units):
    tile = 2 * LANES
    return [slice(at, min(at + tile, units)) for at in range(0, units, tile)]


def ffn(share, place_ref, x, gate_ref, up_ref, act, second, take, store):
    width, units = gate_ref.shape
    hidden = units - LANES
    node = place_ref[0]
    rows = x[:, :width]
    weight = row_weight(node, x[:, width:])
    gate = jnp.dot(rows, gate_ref[...], preferred_element_type=F32)
    up = jnp.dot(rows, up_ref[...], preferred_element_type=F32)
    act[:, :hidden] = (silu(gate[:, :hidden]) * up[:, :hidden] * weight).astype(BF16)
    act[:, hidden:] = shared_units(share, node, gate[:, hidden:], up[:, hidden:])
    piece = width // DOWN_PARTS
    for i in range(DOWN_PARTS):
        at = slice(i * piece, (i + 1) * piece)
        take(i)
        store(at, jnp.dot(act[...], second[:, at], preferred_element_type=F32))


def swap_quarters(value):
    quarter = value.shape[0] // 4
    return jnp.concatenate([value[i * quarter : (i + 1) * quarter] for i in (0, 2, 1, 3)], axis=0)


DOWN_ROWS = 128


def down_range_copies(share, place_ref, down_ref, sdown_ref, out_ref, lower, sems):
    hidden = down_ref.shape[0]
    column = pl.multiple_of((place_ref[0] // share) * LANES, LANES)
    columns = pl.ds(lower, out_ref.shape[1])
    copies = []
    for at in range(0, hidden + LANES, DOWN_ROWS):
        if at < hidden:
            source = down_ref.at[pl.ds(at, DOWN_ROWS), columns]
        else:
            source = sdown_ref.at[pl.ds(column + (at - hidden), DOWN_ROWS), columns]
        copies.append(
            pltpu.make_async_copy(source, out_ref.at[pl.ds(at, DOWN_ROWS), :], sems.at[len(copies)])
        )
    return copies


def load_both_kernel(
    share, lower, place_ref, routed_ref, shared_ref, down_ref, sdown_ref, out_ref, down_out_ref, sems
):
    parts = 4
    run_copies(
        weight_copies(share, place_ref, routed_ref, shared_ref, out_ref, sems, parts)
        + down_range_copies(
            share, place_ref, down_ref, sdown_ref, down_out_ref, lower, sems.at[2 * parts :]
        )
    )


def load_both(place, routed, shared, down, sdown, lower, columns, share):
    width, hidden = routed.shape
    units = hidden + LANES
    return pl.pallas_call(
        functools.partial(load_both_kernel, share, lower),
        in_specs=[SMEM_SPEC] + [ANY_SPEC] * 4,
        out_specs=[VMEM_SPEC] * 2,
        out_shape=[pltpu.VMEM((width, units), BF16), pltpu.VMEM((units, columns), BF16)],
        scratch_shapes=[pltpu.SemaphoreType.DMA((8 + units // DOWN_ROWS,))],
        cost_estimate=pl.CostEstimate(
            flops=0, bytes_accessed=4 * units * (width + columns), transcendentals=0
        ),
        compiler_params=pltpu.CompilerParams(vmem_limit_bytes=1 << 20),
        name="load_both",
    )(place, *(in_hbm(w) for w in (routed, shared, down, sdown)))


def load_first_kernel(share, lower, place_ref, routed_ref, shared_ref, sdown_ref, out_ref, rows_ref, sems):
    parts = 4
    column = pl.multiple_of((place_ref[0] // share) * LANES, LANES)
    rows = pltpu.make_async_copy(
        sdown_ref.at[pl.ds(column, LANES), pl.ds(lower, rows_ref.shape[1])], rows_ref, sems.at[2 * parts]
    )
    run_copies(weight_copies(share, place_ref, routed_ref, shared_ref, out_ref, sems, parts) + [rows])


def load_first(place, routed, shared, sdown, lower, share):
    width, units = lower, routed.shape[1] + LANES
    return pl.pallas_call(
        functools.partial(load_first_kernel, share, lower),
        in_specs=[SMEM_SPEC] + [ANY_SPEC] * 3,
        out_specs=[VMEM_SPEC] * 2,
        out_shape=[pltpu.VMEM((width, units), BF16), pltpu.VMEM((LANES, sdown.shape[1] - lower), BF16)],
        scratch_shapes=[pltpu.SemaphoreType.DMA((9,))],
        cost_estimate=pl.CostEstimate(flops=0, bytes_accessed=4 * units * width, transcendentals=0),
        compiler_params=pltpu.CompilerParams(vmem_limit_bytes=1 << 20),
        name="load_first",
    )(place, *(in_hbm(w) for w in (routed, shared, sdown)))


def late_half_kernel(place_ref, own_ref, other_ref, gate_ref, up_ref, gate_acc_ref, up_acc_ref, weight_ref, x):
    width, units = up_ref.shape
    half, columns = own_ref.shape
    cut = width + LANES - columns
    x[:half, :] = own_ref[...]
    x[half:, :] = other_ref[...]
    rows = x[:, : width - cut]
    for at in tiles_of(units):
        gate_acc_ref[:, at] = jnp.dot(rows, gate_ref[:, at], preferred_element_type=F32)
        up_acc_ref[:, at] = jnp.dot(rows, up_ref[cut:, at], preferred_element_type=F32)
    weight = row_weight(place_ref[0], x[:, width - cut :])
    weight_ref[...] = jnp.broadcast_to(weight, weight_ref.shape)


def early_half_kernel(
    share, place_ref, own_ref, other_ref, gate_ref, up_ref, gate_acc_ref, up_acc_ref, weight_ref, second_ref,
    own_out_ref, other_out_ref, act_ref, x,
):
    half, cut = own_ref.shape
    units = gate_ref.shape[1]
    hidden = units - LANES
    x[:half, :] = own_ref[...]
    x[half:, :] = other_ref[...]
    rows = x[...]
    weight = weight_ref[:, :1]
    for at in tiles_of(units):
        gate = gate_acc_ref[:, at] + jnp.dot(rows, gate_ref[:, at], preferred_element_type=F32)
        up = up_acc_ref[:, at] + jnp.dot(rows, up_ref[:cut, at], preferred_element_type=F32)
        if at.start < hidden:
            act_ref[:, at] = (silu(gate) * up * weight).astype(BF16)
        else:
            act_ref[:, at] = shared_units(share, place_ref[0], gate, up)
    piece = cut // 2
    for i in range(2):
        at = slice(i * piece, (i + 1) * piece)
        total = jnp.dot(act_ref[...], second_ref[:, at], preferred_element_type=F32).astype(BF16)
        own_out_ref[:, at] = total[:half]
        other_out_ref[:, at] = total[half:]


def last_half_kernel(act_ref, down_ref, rows_ref, own_out_ref, other_out_ref):
    half, columns = own_out_ref.shape
    hidden, width = down_ref.shape
    piece = columns // 2
    for i in range(2):
        at = slice(i * piece, (i + 1) * piece)
        whole = slice(width - columns + i * piece, width - columns + (i + 1) * piece)
        total = jnp.dot(act_ref[:, :hidden], down_ref[:, whole], preferred_element_type=F32)
        total += jnp.dot(act_ref[:, hidden:], rows_ref[:, at], preferred_element_type=F32)
        total = total.astype(BF16)
        own_out_ref[:, at] = swap_quarters(total[:half])
        other_out_ref[:, at] = swap_quarters(total[half:])


def estimate(rows, depth, columns):
    return pl.CostEstimate(
        flops=2 * rows * depth * columns, bytes_accessed=2 * depth * columns, transcendentals=0
    )


def pair_rows(place, own, other, gate, late_gate, up, second, down, rows, share):
    half, cut = own[0].shape
    width, units = up.shape
    partial = pl.pallas_call(
        late_half_kernel,
        in_specs=[SMEM_SPEC] + [VMEM_SPEC] * 4,
        out_specs=[VMEM_SPEC] * 3,
        out_shape=[pltpu.VMEM((2 * half, columns), F32) for columns in (units, units, LANES)],
        scratch_shapes=[pltpu.VMEM((2 * half, own[1].shape[1]), BF16)],
        cost_estimate=estimate(2 * half, width - cut, 2 * units),
        compiler_params=pltpu.CompilerParams(vmem_limit_bytes=10 << 20),
        name="late_half",
    )(place, own[1], other[1], late_gate, up)
    own_out, other_out, act = pl.pallas_call(
        functools.partial(early_half_kernel, share),
        in_specs=[SMEM_SPEC] + [VMEM_SPEC] * 8,
        out_specs=[VMEM_SPEC] * 3,
        out_shape=[
            pltpu.VMEM((half, cut), BF16),
            pltpu.VMEM((half, cut), BF16),
            pltpu.VMEM((2 * half, units), BF16),
        ],
        scratch_shapes=[pltpu.VMEM((2 * half, cut), BF16)],
        cost_estimate=estimate(2 * half, cut, 3 * units),
        compiler_params=pltpu.CompilerParams(vmem_limit_bytes=10 << 20),
        name="early_half",
    )(place, own[0], other[0], gate, up, *partial, second)
    last = pl.pallas_call(
        last_half_kernel,
        in_specs=[VMEM_SPEC] * 3,
        out_specs=[VMEM_SPEC] * 2,
        out_shape=[pltpu.VMEM((half, width - cut), BF16)] * 2,
        cost_estimate=estimate(2 * half, width - cut, units),
        compiler_params=pltpu.CompilerParams(vmem_limit_bytes=10 << 20),
        name="last_half",
    )(act, pltpu.with_memory_space_constraint(down, pltpu.VMEM), rows)
    return own_out, last[0], other_out, last[1]


def block_kernel(
    share, place_ref, x_ref, gate_ref, up_ref, down_ref, sdown_ref, out_ref, act, second, sems
):
    groups = down_copies(share, place_ref, down_ref, sdown_ref, second, sems)

    @pl.when(pl.program_id(0) == 0)
    def _():
        for i in range(DOWN_PARTS):
            start_group(groups, i)
        for i in range(DOWN_PARTS):
            wait_group(groups, i)

    def store(at, total):
        out_ref[:, at] = total.astype(BF16)

    ffn(share, place_ref, x_ref, gate_ref, up_ref, act, second, lambda i: None, store)


def block_rows(place, x, gate, up, down, sdown, share):
    rows, packed = x.shape
    hidden, width = down.shape
    block = min(rows, ROW_BLOCK)
    return pl.pallas_call(
        functools.partial(block_kernel, share),
        grid=(rows // block,),
        in_specs=[SMEM_SPEC, pl.BlockSpec((block, packed), lambda i: (i, 0))] + [VMEM_SPEC] * 2 + [ANY_SPEC] * 2,
        out_specs=pl.BlockSpec((block, width), lambda i: (i, 0)),
        out_shape=jax.ShapeDtypeStruct((rows, width), BF16),
        scratch_shapes=down_scratch(block, hidden, width),
        compiler_params=pltpu.CompilerParams(vmem_limit_bytes=24 << 20),
        name="block_rows",
    )(place, x, gate, up, in_hbm(down), in_hbm(sdown))


def f32_sum(*terms):
    return functools.reduce(lambda a, b: a + b, (t.astype(F32) for t in terms))


def flipped(value, bits):
    axis = 0 if bits[0] else 1
    return lax.ppermute(value, ("node", "local")[axis], [(i, i ^ bits[axis]) for i in range(4)])


X, Z1, Z2, CORE = (2, 0), (0, 1), (0, 2), (1, 0)
GATHER = ((Z2, Z2), (Z1, X), (X, Z1))
SCATTER = GATHER[::-1]


def stack(*values):
    return jnp.concatenate(values, axis=0)


def per_device(
    tokens,
    group_ids,
    route_weights,
    gate_experts,
    up_experts,
    down_experts,
    gate_shared,
    up_shared,
    down_shared,
):
    rows, width = tokens.shape
    node_count = lax.axis_size("node")
    local_count = lax.axis_size("local")
    share = max(1, LANES * node_count // gate_shared.shape[1])
    place = lax.axis_index("node").reshape(1)
    gate, up, down = gate_experts[0], up_experts[0], down_experts[0]
    packed = pack_rows(tokens, group_ids, route_weights)

    if node_count != 4 or local_count != 4:
        x = lax.all_gather(packed, ("node", "local"), axis=0, tiled=True)
        gate = load_weights(place, gate, gate_shared, share)
        up = load_weights(place, up, up_shared, share)
        part = block_rows(place, x, gate, up, down, down_shared, share)
        return lax.psum_scatter(part, ("node", "local"), scatter_dimension=0, tiled=True)

    cut = width // 2
    own = [packed[:, :cut], packed[:, cut:]]
    loads = (
        lambda *ready: (load_weights(after(place, *ready), gate, gate_shared, share, cut, width - cut),),
        lambda *ready: load_first(after(place, *ready), gate, gate_shared, down_shared, cut, share),
        lambda *ready: load_both(after(place, *ready), up, up_shared, down, down_shared, 0, cut, share),
    )
    loaded = ()
    for number, (phase, load) in enumerate(zip(GATHER, loads)):
        got = [flipped(part, bits) for part, bits in zip(own, phase)]
        weights = tuple(load(*own))
        if number == 0:
            got[1], weights = lax.optimization_barrier((got[1], weights))
        else:
            got, weights = lax.optimization_barrier((got, weights))
        loaded += weights
        own = [stack(part, add) for part, add in zip(own, got)]
    late_gate, gate, late_rows, up, second = loaded
    own[1] = swap_quarters(own[1])
    other = [flipped(part, CORE) for part in own]

    outs = pair_rows(place, own, other, gate, late_gate, up, second, down, late_rows, share)

    swapped = flipped(outs[2], CORE)
    totals = [[outs[0], swapped], [outs[1], flipped(after(outs[3], swapped), CORE)]]
    for phase in SCATTER:
        for i, bits in enumerate(phase):
            total = totals[i]
            half = total[0].shape[0] // 2
            sent = f32_sum(*(t[half:] for t in total)).astype(BF16)
            totals[i] = [f32_sum(*(t[:half] for t in total)), flipped(sent, bits)]
    return jnp.concatenate([f32_sum(*total).astype(BF16) for total in totals], axis=1)


def solution(mesh):
    in_specs = (
        P(("rep", "node", "local"), None),
        P(("rep", "node", "local"), None),
        P(("rep", "node", "local"), None),
        P("node", None, "local"),
        P("node", None, "local"),
        P("node", "local", None),
        P(None, "local"),
        P(None, "local"),
        P("local", None),
    )
    out_specs = P(("rep", "node", "local"), None)
    return jax.shard_map(
        per_device, mesh=mesh, in_specs=in_specs, out_specs=out_specs, check_vma=False
    )
```

```python
import functools

import jax
import jax.numpy as jnp
from jax import lax
from jax.experimental import pallas as pl
from jax.experimental.pallas import tpu as pltpu
from jax.sharding import PartitionSpec as P

LANES = 128
ROW_BLOCK = 128
F32 = jnp.float32
BF16 = jnp.bfloat16
VMEM_SPEC = pl.BlockSpec(memory_space=pltpu.VMEM)
SMEM_SPEC = pl.BlockSpec(memory_space=pltpu.SMEM)
ANY_SPEC = pl.BlockSpec(memory_space=pl.ANY)


def in_hbm(value):
    return pltpu.with_memory_space_constraint(value, pltpu.HBM)


def run_copies(copies):
    for copy in copies:
        copy.start()
    for copy in copies:
        copy.wait()


def after(value, *done):
    return lax.optimization_barrier((value, *done))[0]


def pack_kernel(tokens_ref, groups_ref, weights_ref, packed_ref):
    rows, width = tokens_ref.shape
    packed_ref[:, :width] = tokens_ref[...]
    groups = groups_ref[...].T
    weights = weights_ref[...].astype(F32).T
    lane = lax.broadcasted_iota(jnp.int32, (rows, LANES), 1)
    dense = jnp.zeros((rows, LANES), F32)
    for k in range(groups.shape[1]):
        dense += jnp.where(lane == groups[:, k : k + 1], weights[:, k : k + 1], 0.0)
    packed_ref[:, width:] = dense.astype(BF16)


def pack_rows(tokens, group_ids, route_weights):
    rows, width = tokens.shape
    return pl.pallas_call(
        pack_kernel,
        out_specs=VMEM_SPEC,
        out_shape=pltpu.VMEM((rows, width + LANES), BF16),
        name="pack_rows",
    )(tokens, group_ids.T, route_weights.T)


def weight_copies(share, place_ref, routed_ref, shared_ref, out_ref, sems, parts, first_row=0):
    hidden = routed_ref.shape[1]
    column = pl.multiple_of((place_ref[0] // share) * LANES, LANES)
    piece = out_ref.shape[0] // parts
    copies = []
    for i in range(parts):
        at = pl.ds(i * piece, piece)
        rows = pl.ds(first_row + i * piece, piece)
        for source, lower, size in (
            (routed_ref.at[rows, :], 0, hidden),
            (shared_ref.at[rows, pl.ds(column, LANES)], hidden, LANES),
        ):
            copies.append(
                pltpu.make_async_copy(source, out_ref.at[at, pl.ds(lower, size)], sems.at[len(copies)])
            )
    return copies


def load_kernel(share, first_row, place_ref, routed_ref, shared_ref, out_ref, sems):
    run_copies(
        weight_copies(
            share, place_ref, routed_ref, shared_ref, out_ref, sems, sems.shape[0] // 2, first_row
        )
    )


def load_weights(place, routed, shared, share, first_row=0, rows=None):
    width, hidden = routed.shape
    shape = (width if rows is None else rows, hidden + LANES)
    return pl.pallas_call(
        functools.partial(load_kernel, share, first_row),
        in_specs=[SMEM_SPEC] + [ANY_SPEC] * 2,
        out_specs=VMEM_SPEC,
        out_shape=pltpu.VMEM(shape, BF16),
        scratch_shapes=[pltpu.SemaphoreType.DMA((8,))],
        cost_estimate=pl.CostEstimate(flops=0, bytes_accessed=4 * shape[0] * shape[1], transcendentals=0),
        compiler_params=pltpu.CompilerParams(vmem_limit_bytes=1 << 20),
        name="load_weights",
    )(place, in_hbm(routed), in_hbm(shared))


def silu(v):
    return v / (1.0 + jnp.exp(-v))


def row_weight(node, dense):
    lane = lax.broadcasted_iota(jnp.int32, dense.shape, 1)
    return jnp.sum(jnp.where(lane == node, dense.astype(F32), 0.0), axis=1, keepdims=True)


DOWN_PARTS = 4


def down_scratch(rows, hidden, width):
    return [
        pltpu.VMEM((rows, hidden + LANES), BF16),
        pltpu.VMEM((hidden + LANES, width), BF16),
        pltpu.SemaphoreType.DMA((2 * DOWN_PARTS,)),
    ]


def down_copies(share, place_ref, down_ref, sdown_ref, second, sems):
    hidden, width = down_ref.shape
    column = pl.multiple_of((place_ref[0] // share) * LANES, LANES)
    piece = width // DOWN_PARTS
    groups = []
    for i in range(DOWN_PARTS):
        at = pl.ds(i * piece, piece)
        groups.append(
            [
                pltpu.make_async_copy(down_ref.at[:, at], second.at[pl.ds(0, hidden), at], sems.at[2 * i]),
                pltpu.make_async_copy(
                    sdown_ref.at[pl.ds(column, LANES), at],
                    second.at[pl.ds(hidden, LANES), at],
                    sems.at[2 * i + 1],
                ),
            ]
        )
    return groups


def start_group(groups, i):
    for copy in groups[i]:
        copy.start()


def wait_group(groups, i):
    for copy in groups[i]:
        copy.wait()


def shared_units(share, node, gate, up):
    shared = silu(gate) * up
    if share > 1:
        lane = lax.broadcasted_iota(jnp.int32, shared.shape, 1)
        shared = jnp.where(lane // (LANES // share) == node % share, shared, 0.0)
    return shared.astype(BF16)


def tiles_of(units):
    tile = 2 * LANES
    return [slice(at, min(at + tile, units)) for at in range(0, units, tile)]


def ffn(share, place_ref, x, gate_ref, up_ref, act, second, take, store):
    width, units = gate_ref.shape
    hidden = units - LANES
    node = place_ref[0]
    rows = x[:, :width]
    weight = row_weight(node, x[:, width:])
    gate = jnp.dot(rows, gate_ref[...], preferred_element_type=F32)
    up = jnp.dot(rows, up_ref[...], preferred_element_type=F32)
    act[:, :hidden] = (silu(gate[:, :hidden]) * up[:, :hidden] * weight).astype(BF16)
    act[:, hidden:] = shared_units(share, node, gate[:, hidden:], up[:, hidden:])
    piece = width // DOWN_PARTS
    for i in range(DOWN_PARTS):
        at = slice(i * piece, (i + 1) * piece)
        take(i)
        store(at, jnp.dot(act[...], second[:, at], preferred_element_type=F32))


def swap_quarters(value):
    quarter = value.shape[0] // 4
    return jnp.concatenate([value[i * quarter : (i + 1) * quarter] for i in (0, 2, 1, 3)], axis=0)


DOWN_ROWS = 128


def down_range_copies(share, place_ref, down_ref, sdown_ref, out_ref, lower, sems):
    hidden = down_ref.shape[0]
    column = pl.multiple_of((place_ref[0] // share) * LANES, LANES)
    columns = pl.ds(lower, out_ref.shape[1])
    copies = []
    for at in range(0, hidden + LANES, DOWN_ROWS):
        if at < hidden:
            source = down_ref.at[pl.ds(at, DOWN_ROWS), columns]
        else:
            source = sdown_ref.at[pl.ds(column + (at - hidden), DOWN_ROWS), columns]
        copies.append(
            pltpu.make_async_copy(source, out_ref.at[pl.ds(at, DOWN_ROWS), :], sems.at[len(copies)])
        )
    return copies


def load_late_kernel(share, place_ref, shared_ref, down_ref, sdown_ref, out_ref, down_out_ref, sems):
    parts = 4
    column = pl.multiple_of((place_ref[0] // share) * LANES, LANES)
    piece = shared_ref.shape[0] // parts
    copies = [
        pltpu.make_async_copy(
            shared_ref.at[pl.ds(i * piece, piece), pl.ds(column, LANES)],
            out_ref.at[pl.ds(i * piece, piece), :],
            sems.at[i],
        )
        for i in range(parts)
    ]
    run_copies(
        copies
        + down_range_copies(share, place_ref, down_ref, sdown_ref, down_out_ref, 0, sems.at[parts:])
    )


def load_late(place, shared, down, sdown, columns, share):
    width = shared.shape[0]
    units = down.shape[0] + LANES
    return pl.pallas_call(
        functools.partial(load_late_kernel, share),
        in_specs=[SMEM_SPEC] + [ANY_SPEC] * 3,
        out_specs=[VMEM_SPEC] * 2,
        out_shape=[pltpu.VMEM((width, LANES), BF16), pltpu.VMEM((units, columns), BF16)],
        scratch_shapes=[pltpu.SemaphoreType.DMA((4 + units // DOWN_ROWS,))],
        cost_estimate=pl.CostEstimate(
            flops=0, bytes_accessed=4 * (units * columns + width * LANES), transcendentals=0
        ),
        compiler_params=pltpu.CompilerParams(vmem_limit_bytes=1 << 20),
        name="load_late",
    )(place, *(in_hbm(w) for w in (shared, down, sdown)))


def load_first_kernel(share, lower, place_ref, routed_ref, shared_ref, sdown_ref, out_ref, rows_ref, sems):
    parts = 4
    column = pl.multiple_of((place_ref[0] // share) * LANES, LANES)
    rows = pltpu.make_async_copy(
        sdown_ref.at[pl.ds(column, LANES), pl.ds(lower, rows_ref.shape[1])], rows_ref, sems.at[2 * parts]
    )
    run_copies(weight_copies(share, place_ref, routed_ref, shared_ref, out_ref, sems, parts) + [rows])


def load_first(place, routed, shared, sdown, lower, share):
    width, units = lower, routed.shape[1] + LANES
    return pl.pallas_call(
        functools.partial(load_first_kernel, share, lower),
        in_specs=[SMEM_SPEC] + [ANY_SPEC] * 3,
        out_specs=[VMEM_SPEC] * 2,
        out_shape=[pltpu.VMEM((width, units), BF16), pltpu.VMEM((LANES, sdown.shape[1] - lower), BF16)],
        scratch_shapes=[pltpu.SemaphoreType.DMA((9,))],
        cost_estimate=pl.CostEstimate(flops=0, bytes_accessed=4 * units * width, transcendentals=0),
        compiler_params=pltpu.CompilerParams(vmem_limit_bytes=1 << 20),
        name="load_first",
    )(place, *(in_hbm(w) for w in (routed, shared, sdown)))


def late_half_kernel(
    place_ref, own_ref, other_ref, gate_ref, up_ref, sup_ref, gate_acc_ref, up_acc_ref, weight_ref, x
):
    width, hidden = up_ref.shape
    units = hidden + LANES
    half, columns = own_ref.shape
    cut = width + LANES - columns
    x[:half, :] = own_ref[...]
    x[half:, :] = other_ref[...]
    rows = x[:, : width - cut]
    for at in tiles_of(units):
        gate_acc_ref[:, at] = jnp.dot(rows, gate_ref[:, at], preferred_element_type=F32)
        up = up_ref[cut:, at] if at.start < hidden else sup_ref[cut:, :]
        up_acc_ref[:, at] = jnp.dot(rows, up, preferred_element_type=F32)
    weight = row_weight(place_ref[0], x[:, width - cut :])
    weight_ref[...] = jnp.broadcast_to(weight, weight_ref.shape)


def early_half_kernel(
    share, place_ref, own_ref, other_ref, gate_ref, up_ref, sup_ref, gate_acc_ref, up_acc_ref, weight_ref, second_ref,
    own_out_ref, other_out_ref, act_ref, x,
):
    half, cut = own_ref.shape
    units = gate_ref.shape[1]
    hidden = units - LANES
    x[:half, :] = own_ref[...]
    x[half:, :] = other_ref[...]
    rows = x[...]
    weight = weight_ref[:, :1]
    for at in tiles_of(units):
        gate = gate_acc_ref[:, at] + jnp.dot(rows, gate_ref[:, at], preferred_element_type=F32)
        up = up_ref[:cut, at] if at.start < hidden else sup_ref[:cut, :]
        up = up_acc_ref[:, at] + jnp.dot(rows, up, preferred_element_type=F32)
        if at.start < hidden:
            act_ref[:, at] = (silu(gate) * up * weight).astype(BF16)
        else:
            act_ref[:, at] = shared_units(share, place_ref[0], gate, up)
    piece = cut // 2
    for i in range(2):
        at = slice(i * piece, (i + 1) * piece)
        total = jnp.dot(act_ref[...], second_ref[:, at], preferred_element_type=F32).astype(BF16)
        own_out_ref[:, at] = total[:half]
        other_out_ref[:, at] = total[half:]


def last_half_kernel(act_ref, down_ref, rows_ref, own_out_ref, other_out_ref):
    half, columns = own_out_ref.shape
    hidden, width = down_ref.shape
    piece = columns // 2
    for i in range(2):
        at = slice(i * piece, (i + 1) * piece)
        whole = slice(width - columns + i * piece, width - columns + (i + 1) * piece)
        total = jnp.dot(act_ref[:, :hidden], down_ref[:, whole], preferred_element_type=F32)
        total += jnp.dot(act_ref[:, hidden:], rows_ref[:, at], preferred_element_type=F32)
        total = total.astype(BF16)
        own_out_ref[:, at] = swap_quarters(total[:half])
        other_out_ref[:, at] = swap_quarters(total[half:])


def estimate(rows, depth, columns):
    return pl.CostEstimate(
        flops=2 * rows * depth * columns, bytes_accessed=2 * depth * columns, transcendentals=0
    )


def pair_rows(place, own, other, gate, late_gate, up, sup, second, down, rows, share):
    half, cut = own[0].shape
    width, hidden = up.shape
    units = hidden + LANES
    up = pltpu.with_memory_space_constraint(up, pltpu.VMEM)
    partial = pl.pallas_call(
        late_half_kernel,
        in_specs=[SMEM_SPEC] + [VMEM_SPEC] * 5,
        out_specs=[VMEM_SPEC] * 3,
        out_shape=[pltpu.VMEM((2 * half, columns), F32) for columns in (units, units, LANES)],
        scratch_shapes=[pltpu.VMEM((2 * half, own[1].shape[1]), BF16)],
        cost_estimate=estimate(2 * half, width - cut, 2 * units),
        compiler_params=pltpu.CompilerParams(vmem_limit_bytes=10 << 20),
        name="late_half",
    )(place, own[1], other[1], late_gate, up, sup)
    own_out, other_out, act = pl.pallas_call(
        functools.partial(early_half_kernel, share),
        in_specs=[SMEM_SPEC] + [VMEM_SPEC] * 9,
        out_specs=[VMEM_SPEC] * 3,
        out_shape=[
            pltpu.VMEM((half, cut), BF16),
            pltpu.VMEM((half, cut), BF16),
            pltpu.VMEM((2 * half, units), BF16),
        ],
        scratch_shapes=[pltpu.VMEM((2 * half, cut), BF16)],
        cost_estimate=estimate(2 * half, cut, 3 * units),
        compiler_params=pltpu.CompilerParams(vmem_limit_bytes=10 << 20),
        name="early_half",
    )(place, own[0], other[0], gate, up, sup, *partial, second)
    last = pl.pallas_call(
        last_half_kernel,
        in_specs=[VMEM_SPEC] * 3,
        out_specs=[VMEM_SPEC] * 2,
        out_shape=[pltpu.VMEM((half, width - cut), BF16)] * 2,
        cost_estimate=estimate(2 * half, width - cut, units),
        compiler_params=pltpu.CompilerParams(vmem_limit_bytes=10 << 20),
        name="last_half",
    )(act, pltpu.with_memory_space_constraint(down, pltpu.VMEM), rows)
    return own_out, last[0], other_out, last[1]


def block_kernel(
    share, place_ref, x_ref, gate_ref, up_ref, down_ref, sdown_ref, out_ref, act, second, sems
):
    groups = down_copies(share, place_ref, down_ref, sdown_ref, second, sems)

    @pl.when(pl.program_id(0) == 0)
    def _():
        for i in range(DOWN_PARTS):
            start_group(groups, i)
        for i in range(DOWN_PARTS):
            wait_group(groups, i)

    def store(at, total):
        out_ref[:, at] = total.astype(BF16)

    ffn(share, place_ref, x_ref, gate_ref, up_ref, act, second, lambda i: None, store)


def block_rows(place, x, gate, up, down, sdown, share):
    rows, packed = x.shape
    hidden, width = down.shape
    block = min(rows, ROW_BLOCK)
    return pl.pallas_call(
        functools.partial(block_kernel, share),
        grid=(rows // block,),
        in_specs=[SMEM_SPEC, pl.BlockSpec((block, packed), lambda i: (i, 0))] + [VMEM_SPEC] * 2 + [ANY_SPEC] * 2,
        out_specs=pl.BlockSpec((block, width), lambda i: (i, 0)),
        out_shape=jax.ShapeDtypeStruct((rows, width), BF16),
        scratch_shapes=down_scratch(block, hidden, width),
        compiler_params=pltpu.CompilerParams(vmem_limit_bytes=24 << 20),
        name="block_rows",
    )(place, x, gate, up, in_hbm(down), in_hbm(sdown))


def f32_sum(*terms):
    return functools.reduce(lambda a, b: a + b, (t.astype(F32) for t in terms))


def flipped(value, bits):
    axis = 0 if bits[0] else 1
    return lax.ppermute(value, ("node", "local")[axis], [(i, i ^ bits[axis]) for i in range(4)])


X, Z1, Z2, CORE = (2, 0), (0, 1), (0, 2), (1, 0)
GATHER = ((Z2, Z2), (Z1, X), (X, Z1))
SCATTER = GATHER[::-1]


def stack(*values):
    return jnp.concatenate(values, axis=0)


def per_device(
    tokens,
    group_ids,
    route_weights,
    gate_experts,
    up_experts,
    down_experts,
    gate_shared,
    up_shared,
    down_shared,
):
    rows, width = tokens.shape
    node_count = lax.axis_size("node")
    local_count = lax.axis_size("local")
    share = max(1, LANES * node_count // gate_shared.shape[1])
    place = lax.axis_index("node").reshape(1)
    gate, up, down = gate_experts[0], up_experts[0], down_experts[0]
    packed = pack_rows(tokens, group_ids, route_weights)

    if node_count != 4 or local_count != 4:
        x = lax.all_gather(packed, ("node", "local"), axis=0, tiled=True)
        gate = load_weights(place, gate, gate_shared, share)
        up = load_weights(place, up, up_shared, share)
        part = block_rows(place, x, gate, up, down, down_shared, share)
        return lax.psum_scatter(part, ("node", "local"), scatter_dimension=0, tiled=True)

    cut = width // 2
    own = [packed[:, :cut], packed[:, cut:]]
    loads = (
        lambda *ready: (load_weights(after(place, *ready), gate, gate_shared, share, cut, width - cut),),
        lambda *ready: load_first(after(place, *ready), gate, gate_shared, down_shared, cut, share),
        lambda *ready: load_late(after(place, *ready), up_shared, down, down_shared, cut, share),
    )
    loaded = ()
    for number, (phase, load) in enumerate(zip(GATHER, loads)):
        got = [flipped(part, bits) for part, bits in zip(own, phase)]
        weights = tuple(load(*own))
        if number == 0:
            got[1], weights = lax.optimization_barrier((got[1], weights))
        else:
            got, weights = lax.optimization_barrier((got, weights))
        loaded += weights
        own = [stack(part, add) for part, add in zip(own, got)]
    late_gate, gate, late_rows, sup, second = loaded
    own[1] = swap_quarters(own[1])
    other = [flipped(part, CORE) for part in own]

    outs = pair_rows(place, own, other, gate, late_gate, up, sup, second, down, late_rows, share)

    swapped = flipped(outs[2], CORE)
    totals = [[outs[0], swapped], [outs[1], flipped(after(outs[3], swapped), CORE)]]
    for phase in SCATTER:
        for i, bits in enumerate(phase):
            total = totals[i]
            half = total[0].shape[0] // 2
            sent = f32_sum(*(t[half:] for t in total)).astype(BF16)
            totals[i] = [f32_sum(*(t[:half] for t in total)), flipped(sent, bits)]
    return jnp.concatenate([f32_sum(*total).astype(BF16) for total in totals], axis=1)


def solution(mesh):
    in_specs = (
        P(("rep", "node", "local"), None),
        P(("rep", "node", "local"), None),
        P(("rep", "node", "local"), None),
        P("node", None, "local"),
        P("node", None, "local"),
        P("node", "local", None),
        P(None, "local"),
        P(None, "local"),
        P("local", None),
    )
    out_specs = P(("rep", "node", "local"), None)
    return jax.shard_map(
        per_device, mesh=mesh, in_specs=in_specs, out_specs=out_specs, check_vma=False
    )
```

```python
import functools

import jax
import jax.numpy as jnp
from jax import lax
from jax.experimental import pallas as pl
from jax.experimental.pallas import tpu as pltpu
from jax.sharding import PartitionSpec as P

LANES = 128
ROW_BLOCK = 128
F32 = jnp.float32
BF16 = jnp.bfloat16
VMEM_SPEC = pl.BlockSpec(memory_space=pltpu.VMEM)
SMEM_SPEC = pl.BlockSpec(memory_space=pltpu.SMEM)
ANY_SPEC = pl.BlockSpec(memory_space=pl.ANY)


def in_hbm(value):
    return pltpu.with_memory_space_constraint(value, pltpu.HBM)


def run_copies(copies):
    for copy in copies:
        copy.start()
    for copy in copies:
        copy.wait()


def after(value, *done):
    return lax.optimization_barrier((value, *done))[0]


def pack_kernel(tokens_ref, groups_ref, weights_ref, packed_ref):
    rows, width = tokens_ref.shape
    packed_ref[:, :width] = tokens_ref[...]
    groups = groups_ref[...].T
    weights = weights_ref[...].astype(F32).T
    lane = lax.broadcasted_iota(jnp.int32, (rows, LANES), 1)
    dense = jnp.zeros((rows, LANES), F32)
    for k in range(groups.shape[1]):
        dense += jnp.where(lane == groups[:, k : k + 1], weights[:, k : k + 1], 0.0)
    packed_ref[:, width:] = dense.astype(BF16)


def pack_rows(tokens, group_ids, route_weights):
    rows, width = tokens.shape
    return pl.pallas_call(
        pack_kernel,
        out_specs=VMEM_SPEC,
        out_shape=pltpu.VMEM((rows, width + LANES), BF16),
        name="pack_rows",
    )(tokens, group_ids.T, route_weights.T)


def weight_copies(share, place_ref, routed_ref, shared_ref, out_ref, sems, parts, first_row=0):
    hidden = routed_ref.shape[1]
    column = pl.multiple_of((place_ref[0] // share) * LANES, LANES)
    piece = out_ref.shape[0] // parts
    copies = []
    for i in range(parts):
        at = pl.ds(i * piece, piece)
        rows = pl.ds(first_row + i * piece, piece)
        for source, lower, size in (
            (routed_ref.at[rows, :], 0, hidden),
            (shared_ref.at[rows, pl.ds(column, LANES)], hidden, LANES),
        ):
            copies.append(
                pltpu.make_async_copy(source, out_ref.at[at, pl.ds(lower, size)], sems.at[len(copies)])
            )
    return copies


def load_kernel(share, first_row, place_ref, routed_ref, shared_ref, out_ref, sems):
    run_copies(
        weight_copies(
            share, place_ref, routed_ref, shared_ref, out_ref, sems, sems.shape[0] // 2, first_row
        )
    )


def load_weights(place, routed, shared, share, first_row=0, rows=None):
    width, hidden = routed.shape
    shape = (width if rows is None else rows, hidden + LANES)
    return pl.pallas_call(
        functools.partial(load_kernel, share, first_row),
        in_specs=[SMEM_SPEC] + [ANY_SPEC] * 2,
        out_specs=VMEM_SPEC,
        out_shape=pltpu.VMEM(shape, BF16),
        scratch_shapes=[pltpu.SemaphoreType.DMA((8,))],
        cost_estimate=pl.CostEstimate(flops=0, bytes_accessed=4 * shape[0] * shape[1], transcendentals=0),
        compiler_params=pltpu.CompilerParams(vmem_limit_bytes=1 << 20),
        name="load_weights",
    )(place, in_hbm(routed), in_hbm(shared))


def silu(v):
    return v / (1.0 + jnp.exp(-v))


def row_weight(node, dense):
    lane = lax.broadcasted_iota(jnp.int32, dense.shape, 1)
    return jnp.sum(jnp.where(lane == node, dense.astype(F32), 0.0), axis=1, keepdims=True)


DOWN_PARTS = 4


def down_scratch(rows, hidden, width):
    return [
        pltpu.VMEM((rows, hidden + LANES), BF16),
        pltpu.VMEM((hidden + LANES, width), BF16),
        pltpu.SemaphoreType.DMA((2 * DOWN_PARTS,)),
    ]


def down_copies(share, place_ref, down_ref, sdown_ref, second, sems):
    hidden, width = down_ref.shape
    column = pl.multiple_of((place_ref[0] // share) * LANES, LANES)
    piece = width // DOWN_PARTS
    groups = []
    for i in range(DOWN_PARTS):
        at = pl.ds(i * piece, piece)
        groups.append(
            [
                pltpu.make_async_copy(down_ref.at[:, at], second.at[pl.ds(0, hidden), at], sems.at[2 * i]),
                pltpu.make_async_copy(
                    sdown_ref.at[pl.ds(column, LANES), at],
                    second.at[pl.ds(hidden, LANES), at],
                    sems.at[2 * i + 1],
                ),
            ]
        )
    return groups


def start_group(groups, i):
    for copy in groups[i]:
        copy.start()


def wait_group(groups, i):
    for copy in groups[i]:
        copy.wait()


def shared_units(share, node, gate, up):
    shared = silu(gate) * up
    if share > 1:
        lane = lax.broadcasted_iota(jnp.int32, shared.shape, 1)
        shared = jnp.where(lane // (LANES // share) == node % share, shared, 0.0)
    return shared.astype(BF16)


def tiles_of(units):
    tile = 2 * LANES
    return [slice(at, min(at + tile, units)) for at in range(0, units, tile)]


def ffn(share, place_ref, x, gate_ref, up_ref, act, second, take, store):
    width, units = gate_ref.shape
    hidden = units - LANES
    node = place_ref[0]
    rows = x[:, :width]
    weight = row_weight(node, x[:, width:])
    gate = jnp.dot(rows, gate_ref[...], preferred_element_type=F32)
    up = jnp.dot(rows, up_ref[...], preferred_element_type=F32)
    act[:, :hidden] = (silu(gate[:, :hidden]) * up[:, :hidden] * weight).astype(BF16)
    act[:, hidden:] = shared_units(share, node, gate[:, hidden:], up[:, hidden:])
    piece = width // DOWN_PARTS
    for i in range(DOWN_PARTS):
        at = slice(i * piece, (i + 1) * piece)
        take(i)
        store(at, jnp.dot(act[...], second[:, at], preferred_element_type=F32))


def swap_quarters(value):
    quarter = value.shape[0] // 4
    return jnp.concatenate([value[i * quarter : (i + 1) * quarter] for i in (0, 2, 1, 3)], axis=0)


DOWN_ROWS = 128


def down_range_copies(share, place_ref, down_ref, sdown_ref, out_ref, lower, sems):
    hidden = down_ref.shape[0]
    column = pl.multiple_of((place_ref[0] // share) * LANES, LANES)
    columns = pl.ds(lower, out_ref.shape[1])
    copies = []
    for at in range(0, hidden + LANES, DOWN_ROWS):
        if at < hidden:
            source = down_ref.at[pl.ds(at, DOWN_ROWS), columns]
        else:
            source = sdown_ref.at[pl.ds(column + (at - hidden), DOWN_ROWS), columns]
        copies.append(
            pltpu.make_async_copy(source, out_ref.at[pl.ds(at, DOWN_ROWS), :], sems.at[len(copies)])
        )
    return copies


def load_late_kernel(share, place_ref, shared_ref, down_ref, sdown_ref, out_ref, down_out_ref, sems):
    parts = 4
    column = pl.multiple_of((place_ref[0] // share) * LANES, LANES)
    piece = shared_ref.shape[0] // parts
    copies = [
        pltpu.make_async_copy(
            shared_ref.at[pl.ds(i * piece, piece), pl.ds(column, LANES)],
            out_ref.at[pl.ds(i * piece, piece), :],
            sems.at[i],
        )
        for i in range(parts)
    ]
    run_copies(
        copies
        + down_range_copies(share, place_ref, down_ref, sdown_ref, down_out_ref, 0, sems.at[parts:])
    )


def load_late(place, shared, down, sdown, columns, share):
    width = shared.shape[0]
    units = down.shape[0] + LANES
    return pl.pallas_call(
        functools.partial(load_late_kernel, share),
        in_specs=[SMEM_SPEC] + [ANY_SPEC] * 3,
        out_specs=[VMEM_SPEC] * 2,
        out_shape=[pltpu.VMEM((width, LANES), BF16), pltpu.VMEM((units, columns), BF16)],
        scratch_shapes=[pltpu.SemaphoreType.DMA((4 + units // DOWN_ROWS,))],
        cost_estimate=pl.CostEstimate(
            flops=0, bytes_accessed=4 * (units * columns + width * LANES), transcendentals=0
        ),
        compiler_params=pltpu.CompilerParams(vmem_limit_bytes=1 << 20),
        name="load_late",
    )(place, *(in_hbm(w) for w in (shared, down, sdown)))


def load_first_kernel(share, lower, place_ref, routed_ref, shared_ref, sdown_ref, out_ref, rows_ref, sems):
    parts = 4
    column = pl.multiple_of((place_ref[0] // share) * LANES, LANES)
    rows = pltpu.make_async_copy(
        sdown_ref.at[pl.ds(column, LANES), pl.ds(lower, rows_ref.shape[1])], rows_ref, sems.at[2 * parts]
    )
    run_copies(weight_copies(share, place_ref, routed_ref, shared_ref, out_ref, sems, parts) + [rows])


def load_first(place, routed, shared, sdown, lower, share):
    width, units = lower, routed.shape[1] + LANES
    return pl.pallas_call(
        functools.partial(load_first_kernel, share, lower),
        in_specs=[SMEM_SPEC] + [ANY_SPEC] * 3,
        out_specs=[VMEM_SPEC] * 2,
        out_shape=[pltpu.VMEM((width, units), BF16), pltpu.VMEM((LANES, sdown.shape[1] - lower), BF16)],
        scratch_shapes=[pltpu.SemaphoreType.DMA((9,))],
        cost_estimate=pl.CostEstimate(flops=0, bytes_accessed=4 * units * width, transcendentals=0),
        compiler_params=pltpu.CompilerParams(vmem_limit_bytes=1 << 20),
        name="load_first",
    )(place, *(in_hbm(w) for w in (routed, shared, sdown)))


def late_half_kernel(
    place_ref, own_ref, other_ref, gate_ref, up_ref, sup_ref, gate_acc_ref, up_acc_ref, weight_ref, x
):
    width, hidden = up_ref.shape
    units = hidden + LANES
    half, columns = own_ref.shape
    cut = width + LANES - columns
    x[:half, :] = own_ref[...]
    x[half:, :] = other_ref[...]
    rows = x[:, : width - cut]
    for at in tiles_of(units):
        gate_acc_ref[:, at] = jnp.dot(rows, gate_ref[:, at], preferred_element_type=F32)
        up = up_ref[cut:, at] if at.start < hidden else sup_ref[cut:, :]
        up_acc_ref[:, at] = jnp.dot(rows, up, preferred_element_type=F32)
    weight = row_weight(place_ref[0], x[:, width - cut :])
    weight_ref[...] = jnp.broadcast_to(weight, weight_ref.shape)


def early_half_kernel(
    share, place_ref, own_ref, other_ref, gate_ref, up_ref, sup_ref, gate_acc_ref, up_acc_ref, weight_ref, second_ref,
    own_out_ref, other_out_ref, act_ref, x,
):
    half, cut = own_ref.shape
    units = gate_ref.shape[1]
    hidden = units - LANES
    x[:half, :] = own_ref[...]
    x[half:, :] = other_ref[...]
    rows = x[...]
    weight = weight_ref[:, :1]
    for at in tiles_of(units):
        gate = gate_acc_ref[:, at] + jnp.dot(rows, gate_ref[:, at], preferred_element_type=F32)
        up = up_ref[:cut, at] if at.start < hidden else sup_ref[:cut, :]
        up = up_acc_ref[:, at] + jnp.dot(rows, up, preferred_element_type=F32)
        if at.start < hidden:
            act_ref[:, at] = (silu(gate) * up * weight).astype(BF16)
        else:
            act_ref[:, at] = shared_units(share, place_ref[0], gate, up)
    piece = cut // 2
    for i in range(2):
        at = slice(i * piece, (i + 1) * piece)
        total = jnp.dot(act_ref[...], second_ref[:, at], preferred_element_type=F32).astype(BF16)
        own_out_ref[:, at] = total[:half]
        other_out_ref[:, at] = total[half:]


def last_half_kernel(act_ref, down_ref, rows_ref, own_out_ref, other_out_ref):
    half, columns = own_out_ref.shape
    hidden, width = down_ref.shape
    piece = columns // 2
    for i in range(2):
        at = slice(i * piece, (i + 1) * piece)
        whole = slice(width - columns + i * piece, width - columns + (i + 1) * piece)
        total = jnp.dot(act_ref[:, :hidden], down_ref[:, whole], preferred_element_type=F32)
        total += jnp.dot(act_ref[:, hidden:], rows_ref[:, at], preferred_element_type=F32)
        total = total.astype(BF16)
        own_out_ref[:, at] = swap_quarters(total[:half])
        other_out_ref[:, at] = swap_quarters(total[half:])


def estimate(rows, depth, columns):
    return pl.CostEstimate(
        flops=2 * rows * depth * columns, bytes_accessed=2 * depth * columns, transcendentals=0
    )


def pair_rows(place, own, other, gate, late_gate, up, sup, second, down, rows, share):
    half, cut = own[0].shape
    width, hidden = up.shape
    units = hidden + LANES
    up = pltpu.with_memory_space_constraint(up, pltpu.VMEM)
    partial = pl.pallas_call(
        late_half_kernel,
        in_specs=[SMEM_SPEC] + [VMEM_SPEC] * 5,
        out_specs=[VMEM_SPEC] * 3,
        out_shape=[pltpu.VMEM((2 * half, columns), F32) for columns in (units, units, LANES)],
        scratch_shapes=[pltpu.VMEM((2 * half, own[1].shape[1]), BF16)],
        cost_estimate=estimate(2 * half, width - cut, 2 * units),
        compiler_params=pltpu.CompilerParams(vmem_limit_bytes=10 << 20),
        name="late_half",
    )(place, own[1], other[1], late_gate, up, sup)
    own_out, other_out, act = pl.pallas_call(
        functools.partial(early_half_kernel, share),
        in_specs=[SMEM_SPEC] + [VMEM_SPEC] * 9,
        out_specs=[VMEM_SPEC] * 3,
        out_shape=[
            pltpu.VMEM((half, cut), BF16),
            pltpu.VMEM((half, cut), BF16),
            pltpu.VMEM((2 * half, units), BF16),
        ],
        scratch_shapes=[pltpu.VMEM((2 * half, cut), BF16)],
        cost_estimate=estimate(2 * half, cut, 3 * units),
        compiler_params=pltpu.CompilerParams(vmem_limit_bytes=10 << 20),
        name="early_half",
    )(place, own[0], other[0], gate, up, sup, *partial, second)
    last = pl.pallas_call(
        last_half_kernel,
        in_specs=[VMEM_SPEC] * 3,
        out_specs=[VMEM_SPEC] * 2,
        out_shape=[pltpu.VMEM((half, width - cut), BF16)] * 2,
        cost_estimate=estimate(2 * half, width - cut, units),
        compiler_params=pltpu.CompilerParams(vmem_limit_bytes=10 << 20),
        name="last_half",
    )(act, pltpu.with_memory_space_constraint(down, pltpu.VMEM), rows)
    return own_out, last[0], other_out, last[1]


def block_kernel(
    share, place_ref, x_ref, gate_ref, up_ref, down_ref, sdown_ref, out_ref, act, second, sems
):
    groups = down_copies(share, place_ref, down_ref, sdown_ref, second, sems)

    @pl.when(pl.program_id(0) == 0)
    def _():
        for i in range(DOWN_PARTS):
            start_group(groups, i)
        for i in range(DOWN_PARTS):
            wait_group(groups, i)

    def store(at, total):
        out_ref[:, at] = total.astype(BF16)

    ffn(share, place_ref, x_ref, gate_ref, up_ref, act, second, lambda i: None, store)


def block_rows(place, x, gate, up, down, sdown, share):
    rows, packed = x.shape
    hidden, width = down.shape
    block = min(rows, ROW_BLOCK)
    return pl.pallas_call(
        functools.partial(block_kernel, share),
        grid=(rows // block,),
        in_specs=[SMEM_SPEC, pl.BlockSpec((block, packed), lambda i: (i, 0))] + [VMEM_SPEC] * 2 + [ANY_SPEC] * 2,
        out_specs=pl.BlockSpec((block, width), lambda i: (i, 0)),
        out_shape=jax.ShapeDtypeStruct((rows, width), BF16),
        scratch_shapes=down_scratch(block, hidden, width),
        compiler_params=pltpu.CompilerParams(vmem_limit_bytes=24 << 20),
        name="block_rows",
    )(place, x, gate, up, in_hbm(down), in_hbm(sdown))


def f32_sum(*terms):
    return functools.reduce(lambda a, b: a + b, (t.astype(F32) for t in terms))


def flipped(value, bits):
    axis = 0 if bits[0] else 1
    return lax.ppermute(value, ("node", "local")[axis], [(i, i ^ bits[axis]) for i in range(4)])


X, Z1, Z2, CORE = (2, 0), (0, 1), (0, 2), (1, 0)
GATHER = ((Z1, X), (X, Z1))
SCATTER = ((X, Z1), (Z1, X), (Z2, Z2))


def stack(*values):
    return jnp.concatenate(values, axis=0)


def per_device(
    tokens,
    group_ids,
    route_weights,
    gate_experts,
    up_experts,
    down_experts,
    gate_shared,
    up_shared,
    down_shared,
):
    rows, width = tokens.shape
    node_count = lax.axis_size("node")
    local_count = lax.axis_size("local")
    share = max(1, LANES * node_count // gate_shared.shape[1])
    place = lax.axis_index("node").reshape(1)
    gate, up, down = gate_experts[0], up_experts[0], down_experts[0]
    packed = pack_rows(tokens, group_ids, route_weights)

    if node_count != 4 or local_count != 4:
        x = lax.all_gather(packed, ("node", "local"), axis=0, tiled=True)
        gate = load_weights(place, gate, gate_shared, share)
        up = load_weights(place, up, up_shared, share)
        part = block_rows(place, x, gate, up, down, down_shared, share)
        return lax.psum_scatter(part, ("node", "local"), scatter_dimension=0, tiled=True)

    cut = width // 2
    got = flipped(packed, Z2)
    late_gate = load_weights(after(place, packed), gate, gate_shared, share, cut, width - cut)
    got, late_gate = lax.optimization_barrier((got, late_gate))
    packed = stack(packed, got)
    own = [packed[:, :cut], packed[:, cut:]]
    loads = (
        lambda *ready: load_first(after(place, *ready), gate, gate_shared, down_shared, cut, share),
        lambda *ready: load_late(after(place, *ready), up_shared, down, down_shared, cut, share),
    )
    loaded = ()
    for phase, load in zip(GATHER, loads):
        got = [flipped(part, bits) for part, bits in zip(own, phase)]
        got, weights = lax.optimization_barrier((got, tuple(load(*own))))
        loaded += weights
        own = [stack(part, add) for part, add in zip(own, got)]
    gate, late_rows, sup, second = loaded
    own[1] = swap_quarters(own[1])
    other = [flipped(part, CORE) for part in own]

    outs = pair_rows(place, own, other, gate, late_gate, up, sup, second, down, late_rows, share)

    swapped = flipped(outs[2], CORE)
    totals = [[outs[0], swapped], [outs[1], flipped(after(outs[3], swapped), CORE)]]
    for phase in SCATTER:
        for i, bits in enumerate(phase):
            total = totals[i]
            half = total[0].shape[0] // 2
            sent = f32_sum(*(t[half:] for t in total)).astype(BF16)
            totals[i] = [f32_sum(*(t[:half] for t in total)), flipped(sent, bits)]
    return jnp.concatenate([f32_sum(*total).astype(BF16) for total in totals], axis=1)


def solution(mesh):
    in_specs = (
        P(("rep", "node", "local"), None),
        P(("rep", "node", "local"), None),
        P(("rep", "node", "local"), None),
        P("node", None, "local"),
        P("node", None, "local"),
        P("node", "local", None),
        P(None, "local"),
        P(None, "local"),
        P("local", None),
    )
    out_specs = P(("rep", "node", "local"), None)
    return jax.shard_map(
        per_device, mesh=mesh, in_specs=in_specs, out_specs=out_specs, check_vma=False
    )
```

```python
import functools

import jax
import jax.numpy as jnp
from jax import lax
from jax.experimental import pallas as pl
from jax.experimental.pallas import tpu as pltpu
from jax.sharding import PartitionSpec as P

LANES = 128
ROW_BLOCK = 128
F32 = jnp.float32
BF16 = jnp.bfloat16
VMEM_SPEC = pl.BlockSpec(memory_space=pltpu.VMEM)
SMEM_SPEC = pl.BlockSpec(memory_space=pltpu.SMEM)
ANY_SPEC = pl.BlockSpec(memory_space=pl.ANY)


def in_hbm(value):
    return pltpu.with_memory_space_constraint(value, pltpu.HBM)


def run_copies(copies):
    for copy in copies:
        copy.start()
    for copy in copies:
        copy.wait()


def after(value, *done):
    return lax.optimization_barrier((value, *done))[0]


def pack_kernel(tokens_ref, groups_ref, weights_ref, packed_ref):
    rows, width = tokens_ref.shape
    packed_ref[:, :width] = tokens_ref[...]
    groups = groups_ref[...].T
    weights = weights_ref[...].astype(F32).T
    lane = lax.broadcasted_iota(jnp.int32, (rows, LANES), 1)
    dense = jnp.zeros((rows, LANES), F32)
    for k in range(groups.shape[1]):
        dense += jnp.where(lane == groups[:, k : k + 1], weights[:, k : k + 1], 0.0)
    packed_ref[:, width:] = dense.astype(BF16)


def pack_rows(tokens, group_ids, route_weights):
    rows, width = tokens.shape
    return pl.pallas_call(
        pack_kernel,
        out_specs=VMEM_SPEC,
        out_shape=pltpu.VMEM((rows, width + LANES), BF16),
        name="pack_rows",
    )(tokens, group_ids.T, route_weights.T)


def weight_copies(share, place_ref, routed_ref, shared_ref, out_ref, sems, parts, first_row=0):
    hidden = routed_ref.shape[1]
    column = pl.multiple_of((place_ref[0] // share) * LANES, LANES)
    piece = out_ref.shape[0] // parts
    copies = []
    for i in range(parts):
        at = pl.ds(i * piece, piece)
        rows = pl.ds(first_row + i * piece, piece)
        for source, lower, size in (
            (routed_ref.at[rows, :], 0, hidden),
            (shared_ref.at[rows, pl.ds(column, LANES)], hidden, LANES),
        ):
            copies.append(
                pltpu.make_async_copy(source, out_ref.at[at, pl.ds(lower, size)], sems.at[len(copies)])
            )
    return copies


def load_kernel(share, first_row, place_ref, routed_ref, shared_ref, out_ref, sems):
    run_copies(
        weight_copies(
            share, place_ref, routed_ref, shared_ref, out_ref, sems, sems.shape[0] // 2, first_row
        )
    )


def load_weights(place, routed, shared, share, first_row=0, rows=None):
    width, hidden = routed.shape
    shape = (width if rows is None else rows, hidden + LANES)
    return pl.pallas_call(
        functools.partial(load_kernel, share, first_row),
        in_specs=[SMEM_SPEC] + [ANY_SPEC] * 2,
        out_specs=VMEM_SPEC,
        out_shape=pltpu.VMEM(shape, BF16),
        scratch_shapes=[pltpu.SemaphoreType.DMA((8,))],
        cost_estimate=pl.CostEstimate(flops=0, bytes_accessed=4 * shape[0] * shape[1], transcendentals=0),
        compiler_params=pltpu.CompilerParams(vmem_limit_bytes=1 << 20),
        name="load_weights",
    )(place, in_hbm(routed), in_hbm(shared))


def silu(v):
    return v / (1.0 + jnp.exp(-v))


def row_weight(node, dense):
    lane = lax.broadcasted_iota(jnp.int32, dense.shape, 1)
    return jnp.sum(jnp.where(lane == node, dense.astype(F32), 0.0), axis=1, keepdims=True)


DOWN_PARTS = 4


def down_scratch(rows, hidden, width):
    return [
        pltpu.VMEM((rows, hidden + LANES), BF16),
        pltpu.VMEM((hidden + LANES, width), BF16),
        pltpu.SemaphoreType.DMA((2 * DOWN_PARTS,)),
    ]


def down_copies(share, place_ref, down_ref, sdown_ref, second, sems):
    hidden, width = down_ref.shape
    column = pl.multiple_of((place_ref[0] // share) * LANES, LANES)
    piece = width // DOWN_PARTS
    groups = []
    for i in range(DOWN_PARTS):
        at = pl.ds(i * piece, piece)
        groups.append(
            [
                pltpu.make_async_copy(down_ref.at[:, at], second.at[pl.ds(0, hidden), at], sems.at[2 * i]),
                pltpu.make_async_copy(
                    sdown_ref.at[pl.ds(column, LANES), at],
                    second.at[pl.ds(hidden, LANES), at],
                    sems.at[2 * i + 1],
                ),
            ]
        )
    return groups


def start_group(groups, i):
    for copy in groups[i]:
        copy.start()


def wait_group(groups, i):
    for copy in groups[i]:
        copy.wait()


def shared_units(share, node, gate, up):
    shared = silu(gate) * up
    if share > 1:
        lane = lax.broadcasted_iota(jnp.int32, shared.shape, 1)
        shared = jnp.where(lane // (LANES // share) == node % share, shared, 0.0)
    return shared.astype(BF16)


def tiles_of(units):
    tile = 2 * LANES
    return [slice(at, min(at + tile, units)) for at in range(0, units, tile)]


def ffn(share, place_ref, x, gate_ref, up_ref, act, second, take, store):
    width, units = gate_ref.shape
    hidden = units - LANES
    node = place_ref[0]
    rows = x[:, :width]
    weight = row_weight(node, x[:, width:])
    gate = jnp.dot(rows, gate_ref[...], preferred_element_type=F32)
    up = jnp.dot(rows, up_ref[...], preferred_element_type=F32)
    act[:, :hidden] = (silu(gate[:, :hidden]) * up[:, :hidden] * weight).astype(BF16)
    act[:, hidden:] = shared_units(share, node, gate[:, hidden:], up[:, hidden:])
    piece = width // DOWN_PARTS
    for i in range(DOWN_PARTS):
        at = slice(i * piece, (i + 1) * piece)
        take(i)
        store(at, jnp.dot(act[...], second[:, at], preferred_element_type=F32))


def swap_quarters(value):
    quarter = value.shape[0] // 4
    return jnp.concatenate([value[i * quarter : (i + 1) * quarter] for i in (0, 2, 1, 3)], axis=0)


DOWN_ROWS = 128


def down_range_copies(share, place_ref, down_ref, sdown_ref, out_ref, lower, sems):
    hidden = down_ref.shape[0]
    column = pl.multiple_of((place_ref[0] // share) * LANES, LANES)
    columns = pl.ds(lower, out_ref.shape[1])
    copies = []
    for at in range(0, hidden + LANES, DOWN_ROWS):
        if at < hidden:
            source = down_ref.at[pl.ds(at, DOWN_ROWS), columns]
        else:
            source = sdown_ref.at[pl.ds(column + (at - hidden), DOWN_ROWS), columns]
        copies.append(
            pltpu.make_async_copy(source, out_ref.at[pl.ds(at, DOWN_ROWS), :], sems.at[len(copies)])
        )
    return copies


def load_late_kernel(
    share, place_ref, shared_ref, down_ref, sdown_ref, out_ref, down_out_ref, rows_ref, sems
):
    parts = 4
    column = pl.multiple_of((place_ref[0] // share) * LANES, LANES)
    piece = shared_ref.shape[0] // parts
    copies = [
        pltpu.make_async_copy(
            shared_ref.at[pl.ds(i * piece, piece), pl.ds(column, LANES)],
            out_ref.at[pl.ds(i * piece, piece), :],
            sems.at[i],
        )
        for i in range(parts)
    ]
    rows = pltpu.make_async_copy(
        sdown_ref.at[pl.ds(column, LANES), pl.ds(down_out_ref.shape[1], rows_ref.shape[1])],
        rows_ref,
        sems.at[parts],
    )
    run_copies(
        copies
        + [rows]
        + down_range_copies(share, place_ref, down_ref, sdown_ref, down_out_ref, 0, sems.at[parts + 1 :])
    )


def load_late(place, shared, down, sdown, columns, share):
    width = shared.shape[0]
    units = down.shape[0] + LANES
    return pl.pallas_call(
        functools.partial(load_late_kernel, share),
        in_specs=[SMEM_SPEC] + [ANY_SPEC] * 3,
        out_specs=[VMEM_SPEC] * 3,
        out_shape=[
            pltpu.VMEM((width, LANES), BF16),
            pltpu.VMEM((units, columns), BF16),
            pltpu.VMEM((LANES, sdown.shape[1] - columns), BF16),
        ],
        scratch_shapes=[pltpu.SemaphoreType.DMA((5 + units // DOWN_ROWS,))],
        cost_estimate=pl.CostEstimate(
            flops=0, bytes_accessed=4 * (units * columns + width * LANES), transcendentals=0
        ),
        compiler_params=pltpu.CompilerParams(vmem_limit_bytes=1 << 20),
        name="load_late",
    )(place, *(in_hbm(w) for w in (shared, down, sdown)))


def late_half_kernel(
    place_ref, own_ref, other_ref, gate_ref, up_ref, sup_ref, gate_acc_ref, up_acc_ref, weight_ref, x
):
    width, hidden = up_ref.shape
    units = hidden + LANES
    half, columns = own_ref.shape
    cut = width + LANES - columns
    x[:half, :] = own_ref[...]
    x[half:, :] = other_ref[...]
    rows = x[:, : width - cut]
    for at in tiles_of(units):
        gate_acc_ref[:, at] = jnp.dot(rows, gate_ref[:, at], preferred_element_type=F32)
        up = up_ref[cut:, at] if at.start < hidden else sup_ref[cut:, :]
        up_acc_ref[:, at] = jnp.dot(rows, up, preferred_element_type=F32)
    weight = row_weight(place_ref[0], x[:, width - cut :])
    weight_ref[...] = jnp.broadcast_to(weight, weight_ref.shape)


def early_half_kernel(
    share, place_ref, own_ref, other_ref, gate_ref, up_ref, sup_ref, gate_acc_ref, up_acc_ref, weight_ref, second_ref,
    own_out_ref, other_out_ref, act_ref, x,
):
    half, cut = own_ref.shape
    units = gate_ref.shape[1]
    hidden = units - LANES
    x[:half, :] = own_ref[...]
    x[half:, :] = other_ref[...]
    rows = x[...]
    weight = weight_ref[:, :1]
    for at in tiles_of(units):
        gate = gate_acc_ref[:, at] + jnp.dot(rows, gate_ref[:, at], preferred_element_type=F32)
        up = up_ref[:cut, at] if at.start < hidden else sup_ref[:cut, :]
        up = up_acc_ref[:, at] + jnp.dot(rows, up, preferred_element_type=F32)
        if at.start < hidden:
            act_ref[:, at] = (silu(gate) * up * weight).astype(BF16)
        else:
            act_ref[:, at] = shared_units(share, place_ref[0], gate, up)
    piece = cut // 2
    for i in range(2):
        at = slice(i * piece, (i + 1) * piece)
        total = jnp.dot(act_ref[...], second_ref[:, at], preferred_element_type=F32).astype(BF16)
        own_out_ref[:, at] = total[:half]
        other_out_ref[:, at] = total[half:]


def last_half_kernel(act_ref, down_ref, rows_ref, own_out_ref, other_out_ref):
    half, columns = own_out_ref.shape
    hidden, width = down_ref.shape
    piece = columns // 2
    for i in range(2):
        at = slice(i * piece, (i + 1) * piece)
        whole = slice(width - columns + i * piece, width - columns + (i + 1) * piece)
        total = jnp.dot(act_ref[:, :hidden], down_ref[:, whole], preferred_element_type=F32)
        total += jnp.dot(act_ref[:, hidden:], rows_ref[:, at], preferred_element_type=F32)
        total = total.astype(BF16)
        own_out_ref[:, at] = swap_quarters(total[:half])
        other_out_ref[:, at] = swap_quarters(total[half:])


def estimate(rows, depth, columns):
    return pl.CostEstimate(
        flops=2 * rows * depth * columns, bytes_accessed=2 * depth * columns, transcendentals=0
    )


def pair_rows(place, own, other, gate, late_gate, up, sup, second, down, rows, share):
    half, cut = own[0].shape
    width, hidden = up.shape
    units = hidden + LANES
    up = pltpu.with_memory_space_constraint(up, pltpu.VMEM)
    partial = pl.pallas_call(
        late_half_kernel,
        in_specs=[SMEM_SPEC] + [VMEM_SPEC] * 5,
        out_specs=[VMEM_SPEC] * 3,
        out_shape=[pltpu.VMEM((2 * half, columns), F32) for columns in (units, units, LANES)],
        scratch_shapes=[pltpu.VMEM((2 * half, own[1].shape[1]), BF16)],
        cost_estimate=estimate(2 * half, width - cut, 2 * units),
        compiler_params=pltpu.CompilerParams(vmem_limit_bytes=10 << 20),
        name="late_half",
    )(place, own[1], other[1], late_gate, up, sup)
    own_out, other_out, act = pl.pallas_call(
        functools.partial(early_half_kernel, share),
        in_specs=[SMEM_SPEC] + [VMEM_SPEC] * 9,
        out_specs=[VMEM_SPEC] * 3,
        out_shape=[
            pltpu.VMEM((half, cut), BF16),
            pltpu.VMEM((half, cut), BF16),
            pltpu.VMEM((2 * half, units), BF16),
        ],
        scratch_shapes=[pltpu.VMEM((2 * half, cut), BF16)],
        cost_estimate=estimate(2 * half, cut, 3 * units),
        compiler_params=pltpu.CompilerParams(vmem_limit_bytes=10 << 20),
        name="early_half",
    )(place, own[0], other[0], gate, up, sup, *partial, second)
    last = pl.pallas_call(
        last_half_kernel,
        in_specs=[VMEM_SPEC] * 3,
        out_specs=[VMEM_SPEC] * 2,
        out_shape=[pltpu.VMEM((half, width - cut), BF16)] * 2,
        cost_estimate=estimate(2 * half, width - cut, units),
        compiler_params=pltpu.CompilerParams(vmem_limit_bytes=10 << 20),
        name="last_half",
    )(act, pltpu.with_memory_space_constraint(down, pltpu.VMEM), rows)
    return own_out, last[0], other_out, last[1]


def block_kernel(
    share, place_ref, x_ref, gate_ref, up_ref, down_ref, sdown_ref, out_ref, act, second, sems
):
    groups = down_copies(share, place_ref, down_ref, sdown_ref, second, sems)

    @pl.when(pl.program_id(0) == 0)
    def _():
        for i in range(DOWN_PARTS):
            start_group(groups, i)
        for i in range(DOWN_PARTS):
            wait_group(groups, i)

    def store(at, total):
        out_ref[:, at] = total.astype(BF16)

    ffn(share, place_ref, x_ref, gate_ref, up_ref, act, second, lambda i: None, store)


def block_rows(place, x, gate, up, down, sdown, share):
    rows, packed = x.shape
    hidden, width = down.shape
    block = min(rows, ROW_BLOCK)
    return pl.pallas_call(
        functools.partial(block_kernel, share),
        grid=(rows // block,),
        in_specs=[SMEM_SPEC, pl.BlockSpec((block, packed), lambda i: (i, 0))] + [VMEM_SPEC] * 2 + [ANY_SPEC] * 2,
        out_specs=pl.BlockSpec((block, width), lambda i: (i, 0)),
        out_shape=jax.ShapeDtypeStruct((rows, width), BF16),
        scratch_shapes=down_scratch(block, hidden, width),
        compiler_params=pltpu.CompilerParams(vmem_limit_bytes=24 << 20),
        name="block_rows",
    )(place, x, gate, up, in_hbm(down), in_hbm(sdown))


def f32_sum(*terms):
    return functools.reduce(lambda a, b: a + b, (t.astype(F32) for t in terms))


def flipped(value, bits):
    axis = 0 if bits[0] else 1
    return lax.ppermute(value, ("node", "local")[axis], [(i, i ^ bits[axis]) for i in range(4)])


X, Z1, Z2, CORE = (2, 0), (0, 1), (0, 2), (1, 0)
GATHER = ((Z2, Z2), (Z1, X), (X, Z1))
SCATTER = GATHER[::-1]


def stack(*values):
    return jnp.concatenate(values, axis=0)


def per_device(
    tokens,
    group_ids,
    route_weights,
    gate_experts,
    up_experts,
    down_experts,
    gate_shared,
    up_shared,
    down_shared,
):
    rows, width = tokens.shape
    node_count = lax.axis_size("node")
    local_count = lax.axis_size("local")
    share = max(1, LANES * node_count // gate_shared.shape[1])
    place = lax.axis_index("node").reshape(1)
    gate, up, down = gate_experts[0], up_experts[0], down_experts[0]
    packed = pack_rows(tokens, group_ids, route_weights)

    if node_count != 4 or local_count != 4:
        x = lax.all_gather(packed, ("node", "local"), axis=0, tiled=True)
        gate = load_weights(place, gate, gate_shared, share)
        up = load_weights(place, up, up_shared, share)
        part = block_rows(place, x, gate, up, down, down_shared, share)
        return lax.psum_scatter(part, ("node", "local"), scatter_dimension=0, tiled=True)

    cut = width // 2
    own = [packed[:, :cut], packed[:, cut:]]
    loads = (
        lambda *ready: (load_weights(after(place, *ready), gate, gate_shared, share, cut, width - cut),),
        lambda *ready: (load_weights(after(place, *ready), gate, gate_shared, share, 0, cut),),
        lambda *ready: load_late(after(place, *ready), up_shared, down, down_shared, cut, share),
    )
    loaded = ()
    for number, (phase, load) in enumerate(zip(GATHER, loads)):
        got = [flipped(part, bits) for part, bits in zip(own, phase)]
        weights = tuple(load(*own))
        if number == 0:
            got[1], weights = lax.optimization_barrier((got[1], weights))
        else:
            got, weights = lax.optimization_barrier((got, weights))
        loaded += weights
        own = [stack(part, add) for part, add in zip(own, got)]
    late_gate, gate, sup, second, late_rows = loaded
    own[1] = swap_quarters(own[1])
    other = [flipped(part, CORE) for part in own]

    outs = pair_rows(place, own, other, gate, late_gate, up, sup, second, down, late_rows, share)

    swapped = flipped(outs[2], CORE)
    totals = [[outs[0], swapped], [outs[1], flipped(after(outs[3], swapped), CORE)]]
    for phase in SCATTER:
        for i, bits in enumerate(phase):
            total = totals[i]
            half = total[0].shape[0] // 2
            sent = f32_sum(*(t[half:] for t in total)).astype(BF16)
            totals[i] = [f32_sum(*(t[:half] for t in total)), flipped(sent, bits)]
    return jnp.concatenate([f32_sum(*total).astype(BF16) for total in totals], axis=1)


def solution(mesh):
    in_specs = (
        P(("rep", "node", "local"), None),
        P(("rep", "node", "local"), None),
        P(("rep", "node", "local"), None),
        P("node", None, "local"),
        P("node", None, "local"),
        P("node", "local", None),
        P(None, "local"),
        P(None, "local"),
        P("local", None),
    )
    out_specs = P(("rep", "node", "local"), None)
    return jax.shard_map(
        per_device, mesh=mesh, in_specs=in_specs, out_specs=out_specs, check_vma=False
    )
```

```python
import functools

import jax
import jax.numpy as jnp
from jax import lax
from jax.experimental import pallas as pl
from jax.experimental.pallas import tpu as pltpu
from jax.sharding import PartitionSpec as P

LANES = 128
ROW_BLOCK = 128
F32 = jnp.float32
BF16 = jnp.bfloat16
VMEM_SPEC = pl.BlockSpec(memory_space=pltpu.VMEM)
SMEM_SPEC = pl.BlockSpec(memory_space=pltpu.SMEM)
ANY_SPEC = pl.BlockSpec(memory_space=pl.ANY)


def in_hbm(value):
    return pltpu.with_memory_space_constraint(value, pltpu.HBM)


def run_copies(copies):
    for copy in copies:
        copy.start()
    for copy in copies:
        copy.wait()


def after(value, *done):
    return lax.optimization_barrier((value, *done))[0]


def pack_kernel(tokens_ref, groups_ref, weights_ref, packed_ref):
    rows, width = tokens_ref.shape
    packed_ref[:, :width] = tokens_ref[...]
    groups = groups_ref[...].T
    weights = weights_ref[...].astype(F32).T
    lane = lax.broadcasted_iota(jnp.int32, (rows, LANES), 1)
    dense = jnp.zeros((rows, LANES), F32)
    for k in range(groups.shape[1]):
        dense += jnp.where(lane == groups[:, k : k + 1], weights[:, k : k + 1], 0.0)
    packed_ref[:, width:] = dense.astype(BF16)


def pack_rows(tokens, group_ids, route_weights):
    rows, width = tokens.shape
    return pl.pallas_call(
        pack_kernel,
        out_specs=VMEM_SPEC,
        out_shape=pltpu.VMEM((rows, width + LANES), BF16),
        name="pack_rows",
    )(tokens, group_ids.T, route_weights.T)


def weight_copies(share, place_ref, routed_ref, shared_ref, out_ref, sems, parts, first_row=0):
    hidden = routed_ref.shape[1]
    column = pl.multiple_of((place_ref[0] // share) * LANES, LANES)
    piece = out_ref.shape[0] // parts
    copies = []
    for i in range(parts):
        at = pl.ds(i * piece, piece)
        rows = pl.ds(first_row + i * piece, piece)
        for source, lower, size in (
            (routed_ref.at[rows, :], 0, hidden),
            (shared_ref.at[rows, pl.ds(column, LANES)], hidden, LANES),
        ):
            copies.append(
                pltpu.make_async_copy(source, out_ref.at[at, pl.ds(lower, size)], sems.at[len(copies)])
            )
    return copies


def load_kernel(share, first_row, place_ref, routed_ref, shared_ref, out_ref, sems):
    run_copies(
        weight_copies(
            share, place_ref, routed_ref, shared_ref, out_ref, sems, sems.shape[0] // 2, first_row
        )
    )


def load_weights(place, routed, shared, share, first_row=0, rows=None):
    width, hidden = routed.shape
    shape = (width if rows is None else rows, hidden + LANES)
    return pl.pallas_call(
        functools.partial(load_kernel, share, first_row),
        in_specs=[SMEM_SPEC] + [ANY_SPEC] * 2,
        out_specs=VMEM_SPEC,
        out_shape=pltpu.VMEM(shape, BF16),
        scratch_shapes=[pltpu.SemaphoreType.DMA((8,))],
        cost_estimate=pl.CostEstimate(flops=0, bytes_accessed=4 * shape[0] * shape[1], transcendentals=0),
        compiler_params=pltpu.CompilerParams(vmem_limit_bytes=1 << 20),
        name="load_weights",
    )(place, in_hbm(routed), in_hbm(shared))


def silu(v):
    return v / (1.0 + jnp.exp(-v))


def row_weight(node, dense):
    lane = lax.broadcasted_iota(jnp.int32, dense.shape, 1)
    return jnp.sum(jnp.where(lane == node, dense.astype(F32), 0.0), axis=1, keepdims=True)


DOWN_PARTS = 4


def down_scratch(rows, hidden, width):
    return [
        pltpu.VMEM((rows, hidden + LANES), BF16),
        pltpu.VMEM((hidden + LANES, width), BF16),
        pltpu.SemaphoreType.DMA((2 * DOWN_PARTS,)),
    ]


def down_copies(share, place_ref, down_ref, sdown_ref, second, sems):
    hidden, width = down_ref.shape
    column = pl.multiple_of((place_ref[0] // share) * LANES, LANES)
    piece = width // DOWN_PARTS
    groups = []
    for i in range(DOWN_PARTS):
        at = pl.ds(i * piece, piece)
        groups.append(
            [
                pltpu.make_async_copy(down_ref.at[:, at], second.at[pl.ds(0, hidden), at], sems.at[2 * i]),
                pltpu.make_async_copy(
                    sdown_ref.at[pl.ds(column, LANES), at],
                    second.at[pl.ds(hidden, LANES), at],
                    sems.at[2 * i + 1],
                ),
            ]
        )
    return groups


def start_group(groups, i):
    for copy in groups[i]:
        copy.start()


def wait_group(groups, i):
    for copy in groups[i]:
        copy.wait()


def shared_units(share, node, gate, up):
    shared = silu(gate) * up
    if share > 1:
        lane = lax.broadcasted_iota(jnp.int32, shared.shape, 1)
        shared = jnp.where(lane // (LANES // share) == node % share, shared, 0.0)
    return shared.astype(BF16)


def tiles_of(units):
    tile = 2 * LANES
    return [slice(at, min(at + tile, units)) for at in range(0, units, tile)]


def ffn(share, place_ref, x, gate_ref, up_ref, act, second, take, store):
    width, units = gate_ref.shape
    hidden = units - LANES
    node = place_ref[0]
    rows = x[:, :width]
    weight = row_weight(node, x[:, width:])
    gate = jnp.dot(rows, gate_ref[...], preferred_element_type=F32)
    up = jnp.dot(rows, up_ref[...], preferred_element_type=F32)
    act[:, :hidden] = (silu(gate[:, :hidden]) * up[:, :hidden] * weight).astype(BF16)
    act[:, hidden:] = shared_units(share, node, gate[:, hidden:], up[:, hidden:])
    piece = width // DOWN_PARTS
    for i in range(DOWN_PARTS):
        at = slice(i * piece, (i + 1) * piece)
        take(i)
        store(at, jnp.dot(act[...], second[:, at], preferred_element_type=F32))


def swap_quarters(value):
    quarter = value.shape[0] // 4
    return jnp.concatenate([value[i * quarter : (i + 1) * quarter] for i in (0, 2, 1, 3)], axis=0)


DOWN_ROWS = 128


def down_range_copies(share, place_ref, down_ref, sdown_ref, out_ref, lower, sems):
    hidden = down_ref.shape[0]
    column = pl.multiple_of((place_ref[0] // share) * LANES, LANES)
    columns = pl.ds(lower, out_ref.shape[1])
    copies = []
    for at in range(0, hidden + LANES, DOWN_ROWS):
        if at < hidden:
            source = down_ref.at[pl.ds(at, DOWN_ROWS), columns]
        else:
            source = sdown_ref.at[pl.ds(column + (at - hidden), DOWN_ROWS), columns]
        copies.append(
            pltpu.make_async_copy(source, out_ref.at[pl.ds(at, DOWN_ROWS), :], sems.at[len(copies)])
        )
    return copies


def load_late_kernel(
    share, place_ref, shared_ref, down_ref, sdown_ref, out_ref, down_out_ref, rows_ref, sems
):
    parts = 4
    column = pl.multiple_of((place_ref[0] // share) * LANES, LANES)
    piece = shared_ref.shape[0] // parts
    copies = [
        pltpu.make_async_copy(
            shared_ref.at[pl.ds(i * piece, piece), pl.ds(column, LANES)],
            out_ref.at[pl.ds(i * piece, piece), :],
            sems.at[i],
        )
        for i in range(parts)
    ]
    rows = pltpu.make_async_copy(
        sdown_ref.at[pl.ds(column, LANES), pl.ds(down_out_ref.shape[1], rows_ref.shape[1])],
        rows_ref,
        sems.at[parts],
    )
    run_copies(
        copies
        + [rows]
        + down_range_copies(share, place_ref, down_ref, sdown_ref, down_out_ref, 0, sems.at[parts + 1 :])
    )


def load_late(place, shared, down, sdown, columns, share):
    width = shared.shape[0]
    units = down.shape[0] + LANES
    return pl.pallas_call(
        functools.partial(load_late_kernel, share),
        in_specs=[SMEM_SPEC] + [ANY_SPEC] * 3,
        out_specs=[VMEM_SPEC] * 3,
        out_shape=[
            pltpu.VMEM((width, LANES), BF16),
            pltpu.VMEM((units, columns), BF16),
            pltpu.VMEM((LANES, sdown.shape[1] - columns), BF16),
        ],
        scratch_shapes=[pltpu.SemaphoreType.DMA((5 + units // DOWN_ROWS,))],
        cost_estimate=pl.CostEstimate(
            flops=0, bytes_accessed=4 * (units * columns + width * LANES), transcendentals=0
        ),
        compiler_params=pltpu.CompilerParams(vmem_limit_bytes=1 << 20),
        name="load_late",
    )(place, *(in_hbm(w) for w in (shared, down, sdown)))


def late_half_kernel(
    place_ref, own_ref, other_ref, gate_ref, up_ref, sup_ref, gate_acc_ref, up_acc_ref, weight_ref, x
):
    width, hidden = up_ref.shape
    units = hidden + LANES
    half, columns = own_ref.shape
    cut = width + LANES - columns
    x[:half, :] = own_ref[...]
    x[half:, :] = other_ref[...]
    rows = x[:, : width - cut]
    for at in tiles_of(units):
        gate_acc_ref[:, at] = jnp.dot(rows, gate_ref[:, at], preferred_element_type=F32)
        up = up_ref[cut:, at] if at.start < hidden else sup_ref[cut:, :]
        up_acc_ref[:, at] = jnp.dot(rows, up, preferred_element_type=F32)
    weight = row_weight(place_ref[0], x[:, width - cut :])
    weight_ref[...] = jnp.broadcast_to(weight, weight_ref.shape)


def early_half_kernel(
    share, place_ref, own_ref, other_ref, gate_ref, up_ref, sup_ref, gate_acc_ref, up_acc_ref, weight_ref, second_ref,
    own_out_ref, other_out_ref, act_ref, x,
):
    half, cut = own_ref.shape
    units = gate_ref.shape[1]
    hidden = units - LANES
    x[:half, :] = own_ref[...]
    x[half:, :] = other_ref[...]
    rows = x[...]
    weight = weight_ref[:, :1]
    for at in tiles_of(units):
        gate = gate_acc_ref[:, at] + jnp.dot(rows, gate_ref[:, at], preferred_element_type=F32)
        up = up_ref[:cut, at] if at.start < hidden else sup_ref[:cut, :]
        up = up_acc_ref[:, at] + jnp.dot(rows, up, preferred_element_type=F32)
        if at.start < hidden:
            act_ref[:, at] = (silu(gate) * up * weight).astype(BF16)
        else:
            act_ref[:, at] = shared_units(share, place_ref[0], gate, up)
    piece = cut // 2
    for i in range(2):
        at = slice(i * piece, (i + 1) * piece)
        total = jnp.dot(act_ref[...], second_ref[:, at], preferred_element_type=F32).astype(BF16)
        own_out_ref[:, at] = swap_quarters(total[:half])
        other_out_ref[:, at] = swap_quarters(total[half:])


def last_half_kernel(act_ref, down_ref, rows_ref, own_out_ref, other_out_ref):
    half, columns = own_out_ref.shape
    hidden, width = down_ref.shape
    piece = columns // 2
    for i in range(2):
        at = slice(i * piece, (i + 1) * piece)
        whole = slice(width - columns + i * piece, width - columns + (i + 1) * piece)
        total = jnp.dot(act_ref[:, :hidden], down_ref[:, whole], preferred_element_type=F32)
        total += jnp.dot(act_ref[:, hidden:], rows_ref[:, at], preferred_element_type=F32)
        total = total.astype(BF16)
        own_out_ref[:, at] = total[:half]
        other_out_ref[:, at] = total[half:]


def estimate(rows, depth, columns):
    return pl.CostEstimate(
        flops=2 * rows * depth * columns, bytes_accessed=2 * depth * columns, transcendentals=0
    )


def pair_rows(place, own, other, gate, late_gate, up, sup, second, down, rows, share):
    half, cut = own[0].shape
    width, hidden = up.shape
    units = hidden + LANES
    up = pltpu.with_memory_space_constraint(up, pltpu.VMEM)
    partial = pl.pallas_call(
        late_half_kernel,
        in_specs=[SMEM_SPEC] + [VMEM_SPEC] * 5,
        out_specs=[VMEM_SPEC] * 3,
        out_shape=[pltpu.VMEM((2 * half, columns), F32) for columns in (units, units, LANES)],
        scratch_shapes=[pltpu.VMEM((2 * half, own[1].shape[1]), BF16)],
        cost_estimate=estimate(2 * half, width - cut, 2 * units),
        compiler_params=pltpu.CompilerParams(vmem_limit_bytes=10 << 20),
        name="late_half",
    )(place, own[1], other[1], late_gate, up, sup)
    own_out, other_out, act = pl.pallas_call(
        functools.partial(early_half_kernel, share),
        in_specs=[SMEM_SPEC] + [VMEM_SPEC] * 9,
        out_specs=[VMEM_SPEC] * 3,
        out_shape=[
            pltpu.VMEM((half, cut), BF16),
            pltpu.VMEM((half, cut), BF16),
            pltpu.VMEM((2 * half, units), BF16),
        ],
        scratch_shapes=[pltpu.VMEM((2 * half, cut), BF16)],
        cost_estimate=estimate(2 * half, cut, 3 * units),
        compiler_params=pltpu.CompilerParams(vmem_limit_bytes=10 << 20),
        name="early_half",
    )(place, own[0], other[0], gate, up, sup, *partial, second)
    last = pl.pallas_call(
        last_half_kernel,
        in_specs=[VMEM_SPEC] * 3,
        out_specs=[VMEM_SPEC] * 2,
        out_shape=[pltpu.VMEM((half, width - cut), BF16)] * 2,
        cost_estimate=estimate(2 * half, width - cut, units),
        compiler_params=pltpu.CompilerParams(vmem_limit_bytes=10 << 20),
        name="last_half",
    )(act, pltpu.with_memory_space_constraint(down, pltpu.VMEM), rows)
    return own_out, last[0], other_out, last[1]


def block_kernel(
    share, place_ref, x_ref, gate_ref, up_ref, down_ref, sdown_ref, out_ref, act, second, sems
):
    groups = down_copies(share, place_ref, down_ref, sdown_ref, second, sems)

    @pl.when(pl.program_id(0) == 0)
    def _():
        for i in range(DOWN_PARTS):
            start_group(groups, i)
        for i in range(DOWN_PARTS):
            wait_group(groups, i)

    def store(at, total):
        out_ref[:, at] = total.astype(BF16)

    ffn(share, place_ref, x_ref, gate_ref, up_ref, act, second, lambda i: None, store)


def block_rows(place, x, gate, up, down, sdown, share):
    rows, packed = x.shape
    hidden, width = down.shape
    block = min(rows, ROW_BLOCK)
    return pl.pallas_call(
        functools.partial(block_kernel, share),
        grid=(rows // block,),
        in_specs=[SMEM_SPEC, pl.BlockSpec((block, packed), lambda i: (i, 0))] + [VMEM_SPEC] * 2 + [ANY_SPEC] * 2,
        out_specs=pl.BlockSpec((block, width), lambda i: (i, 0)),
        out_shape=jax.ShapeDtypeStruct((rows, width), BF16),
        scratch_shapes=down_scratch(block, hidden, width),
        compiler_params=pltpu.CompilerParams(vmem_limit_bytes=24 << 20),
        name="block_rows",
    )(place, x, gate, up, in_hbm(down), in_hbm(sdown))


def f32_sum(*terms):
    return functools.reduce(lambda a, b: a + b, (t.astype(F32) for t in terms))


def flipped(value, bits):
    axis = 0 if bits[0] else 1
    return lax.ppermute(value, ("node", "local")[axis], [(i, i ^ bits[axis]) for i in range(4)])


X, Z1, Z2, CORE = (2, 0), (0, 1), (0, 2), (1, 0)
GATHER = ((Z2, Z2), (X, Z1), (Z1, X))
SCATTER = ((X, Z1), (Z1, X), (Z2, Z2))


def stack(*values):
    return jnp.concatenate(values, axis=0)


def per_device(
    tokens,
    group_ids,
    route_weights,
    gate_experts,
    up_experts,
    down_experts,
    gate_shared,
    up_shared,
    down_shared,
):
    rows, width = tokens.shape
    node_count = lax.axis_size("node")
    local_count = lax.axis_size("local")
    share = max(1, LANES * node_count // gate_shared.shape[1])
    place = lax.axis_index("node").reshape(1)
    gate, up, down = gate_experts[0], up_experts[0], down_experts[0]
    packed = pack_rows(tokens, group_ids, route_weights)

    if node_count != 4 or local_count != 4:
        x = lax.all_gather(packed, ("node", "local"), axis=0, tiled=True)
        gate = load_weights(place, gate, gate_shared, share)
        up = load_weights(place, up, up_shared, share)
        part = block_rows(place, x, gate, up, down, down_shared, share)
        return lax.psum_scatter(part, ("node", "local"), scatter_dimension=0, tiled=True)

    cut = width // 2
    own = [packed[:, :cut], packed[:, cut:]]
    loads = (
        lambda *ready: (load_weights(after(place, *ready), gate, gate_shared, share, cut, width - cut),),
        lambda *ready: (load_weights(after(place, *ready), gate, gate_shared, share, 0, cut),),
        lambda *ready: load_late(after(place, *ready), up_shared, down, down_shared, cut, share),
    )
    loaded = ()
    for number, (phase, load) in enumerate(zip(GATHER, loads)):
        got = [flipped(part, bits) for part, bits in zip(own, phase)]
        weights = tuple(load(*own))
        if number == 0:
            got[1], weights = lax.optimization_barrier((got[1], weights))
        else:
            got, weights = lax.optimization_barrier((got, weights))
        loaded += weights
        own = [stack(part, add) for part, add in zip(own, got)]
    late_gate, gate, sup, second, late_rows = loaded
    own[1] = swap_quarters(own[1])
    other = [flipped(part, CORE) for part in own]

    outs = pair_rows(place, own, other, gate, late_gate, up, sup, second, down, late_rows, share)

    swapped = flipped(outs[2], CORE)
    totals = [[outs[0], swapped], [outs[1], flipped(after(outs[3], swapped), CORE)]]
    for phase in SCATTER:
        for i, bits in enumerate(phase):
            total = totals[i]
            half = total[0].shape[0] // 2
            sent = f32_sum(*(t[half:] for t in total)).astype(BF16)
            totals[i] = [f32_sum(*(t[:half] for t in total)), flipped(sent, bits)]
    return jnp.concatenate([f32_sum(*total).astype(BF16) for total in totals], axis=1)


def solution(mesh):
    in_specs = (
        P(("rep", "node", "local"), None),
        P(("rep", "node", "local"), None),
        P(("rep", "node", "local"), None),
        P("node", None, "local"),
        P("node", None, "local"),
        P("node", "local", None),
        P(None, "local"),
        P(None, "local"),
        P("local", None),
    )
    out_specs = P(("rep", "node", "local"), None)
    return jax.shard_map(
        per_device, mesh=mesh, in_specs=in_specs, out_specs=out_specs, check_vma=False
    )
```
